32 devices in a mesh: groups: 2 (over x), tm: 16 (over z, y, core).
Axes of the slice: x: 2, y: 2, z: 4, core: 2. Of those that a mesh axis runs over, the one named last changes fastest.
Arguments:
- links: float32 [4, 2, 3, 3, 2, 64, 512], P(None, None, None, None, 'groups', 'tm'), parts along dimension 4, may hold values from -1 to 1, as said below
- cotangent: bfloat16 [4, 2, 3, 3, 2, 64, 512], P(None, None, None, None, 'groups', 'tm'), parts along dimension 4, may hold values from -0.078125 to 0.078125
- parity: int32 [2, 64], P('groups', 'tm'), parts along dimension 0, may hold values from 0 to 1
- link_subset: int32 [2, 64], P('groups', 'tm'), parts along dimension 0, may hold values from 1 to 15
- w_first: bfloat16 [3456], P('tm'), may hold values from -0.75 to 0.75
- w_second: bfloat16 [20736], P('tm'), may hold values from -0.3125 to 0.3125
- w_third: bfloat16 [20736], P('tm'), may hold values from -0.3125 to 0.3125
- w_last: bfloat16 [1728], P('tm'), may hold values from -0.3125 to 0.3125
Outputs:
- new_links: float32 [4, 2, 3, 3, 2, 64, 512], P(None, None, None, None, 'groups', 'tm'), parts along dimension 4
- grad_first: float32 [2, 3456], P('groups', 'tm'), parts along dimension 0
- grad_second: float32 [2, 20736], P('groups', 'tm'), parts along dimension 0
- grad_third: float32 [2, 20736], P('groups', 'tm'), parts along dimension 0
- grad_last: float32 [2, 1728], P('groups', 'tm'), parts along dimension 0
The draws below stay inside these ranges and needn't reach their ends.
There are 2 independent parts, one for each index of `groups`. The reference program is written for one: setup_inputs(seed, part) draws one part's arguments, and reference() takes and returns one part's arrays. A program takes and returns all parts, laid end to end along the dimension named above; an argument that names none is the same for every part. Nothing has to cross between parts.
Inputs may be any that keep to these rules, and one draw needn't show every extreme that they name: `links`: each link is a special unitary 3 x 3 matrix.
All inputs are finite; a program needn't handle non-finite values.
Results may differ from the reference program's by a relative error of at most 0.028.
Values may be sent and summed in bfloat16 or wider, within the bound.
No kernel may reach another device: no remote copies, remote signals or barrier semaphores. Data moves between devices by JAX's collectives and lax.ppermute only.
A program may use at most 128 MiB of HBM per device.

```python
import jax
import jax.numpy as jnp
from jax import lax

LS = 8
SITES = 512
CONF = 1
NT = 64
H = 48
NF = 8
NO = 4
TAPS = 9


def unit_rows(first_re, first_im, second_re, second_im):
    scale = jax.lax.rsqrt(jnp.sum(first_re * first_re + first_im * first_im, axis=1, keepdims=True))
    first_re = first_re * scale
    first_im = first_im * scale
    inner_re = jnp.sum(first_re * second_re + first_im * second_im, axis=1, keepdims=True)
    inner_im = jnp.sum(first_re * second_im - first_im * second_re, axis=1, keepdims=True)
    second_re = second_re - (inner_re * first_re - inner_im * first_im)
    second_im = second_im - (inner_re * first_im + inner_im * first_re)
    scale = jax.lax.rsqrt(jnp.sum(second_re * second_re + second_im * second_im, axis=1, keepdims=True))
    return (first_re, first_im, second_re * scale, second_im * scale)


def draw_links(key, part):
    key = jax.random.fold_in(key, 11)
    shape = (4, 3, 3, CONF, NT, LS ** 3)
    key_re, key_im = jax.random.split(key)
    real_part = jax.random.normal(key_re, shape, jnp.float32)
    imag_part = jax.random.normal(key_im, shape, jnp.float32)
    lift = 0.3
    eye_three = jnp.eye(3, dtype=jnp.float32).reshape(1, 3, 3, 1, 1, 1)
    real_part = real_part + lift * eye_three
    row_re, row_im, next_re, next_im = unit_rows(real_part[:, 0], imag_part[:, 0], real_part[:, 1], imag_part[:, 1])
    cross_re = []
    cross_im = []
    for column in range(3):
        left = (column + 1) % 3
        right = (column + 2) % 3
        prod_re = row_re[:, left] * next_re[:, right] - row_im[:, left] * next_im[:, right]
        prod_im = row_re[:, left] * next_im[:, right] + row_im[:, left] * next_re[:, right]
        back_re = row_re[:, right] * next_re[:, left] - row_im[:, right] * next_im[:, left]
        back_im = row_re[:, right] * next_im[:, left] + row_im[:, right] * next_re[:, left]
        cross_re.append(prod_re - back_re)
        cross_im.append(-(prod_im - back_im))
    third_re = jnp.stack(cross_re, axis=1)
    third_im = jnp.stack(cross_im, axis=1)
    real_rows = jnp.stack([row_re, next_re, third_re], axis=1)
    imag_rows = jnp.stack([row_im, next_im, third_im], axis=1)
    return jnp.stack([real_rows, imag_rows], axis=1)


def with_ends(values, rng, smallest, top_value):
    longest = values.shape.index(max(values.shape))
    spots = []
    for shift in (0, 1):
        where = [jax.random.randint(jax.random.fold_in(rng, axis), (), 0, length) for axis, length in enumerate(values.shape)]
        where[longest] = (where[longest] + shift) % values.shape[longest]
        spots.append(tuple(where))
    return values.at[spots[0]].set(smallest).at[spots[1]].set(top_value)


def block_scale(stream_key, dims, cuts, least, largest):
    gain, own = 1.0, jax.random.fold_in(stream_key, 6)
    for dim, blocks in cuts:
        draws = jnp.exp(jax.random.uniform(jax.random.fold_in(own, dim), (blocks,), jnp.float32, least / len(cuts), largest / len(cuts)))
        gain = gain * jnp.repeat(draws, dims[dim] // blocks).reshape([-1 if axis == dim else 1 for axis in range(len(dims))])
    return gain


def normal_values(own_key, shape, deviation, bound, cuts=(), kind=jnp.bfloat16):
    entries = jax.random.normal(own_key, shape, jnp.float32) * deviation
    if len(cuts) > 0:
        entries = block_scale(own_key, shape, cuts, -0.22, 0.18) * entries
    return jnp.clip(entries, min=-bound, max=bound).astype(kind)


def setup_inputs(seed: int = 0, part: int = 0) -> dict:
    seeds = jax.random.split(jax.random.key(seed), 9)
    part_keys = jax.random.split(jax.random.fold_in(seeds[8], part), 9)
    return {
        "links": draw_links(jax.random.fold_in(jax.random.fold_in(seeds[8], part), 71), part),
        "cotangent": normal_values(part_keys[1], (4, 2, 3, 3, CONF, NT, SITES), (1.0 / (CONF * NT * SITES) ** 0.5), 0.078125, ((5, 16),)),
        "parity": with_ends(jax.random.randint(part_keys[2], (CONF, NT), 0, 2), jax.random.fold_in(part_keys[2], 1), 0, 1).astype(jnp.int32),
        "link_subset": with_ends(jax.random.randint(part_keys[3], (CONF, NT), 1, 16), jax.random.fold_in(part_keys[3], 1), 1, 15).astype(jnp.int32),
        "w_first": normal_values(seeds[4], (TAPS * H * NF,), (TAPS * NF) ** -0.5, 0.75, ((0, 16),)),
        "w_second": normal_values(seeds[5], (TAPS * H * H,), (TAPS * H) ** -0.5, 0.3125, ((0, 16),)),
        "w_third": normal_values(seeds[6], (TAPS * H * H,), (TAPS * H) ** -0.5, 0.3125, ((0, 16),)),
        "w_last": normal_values(seeds[7], (TAPS * NO * H,), (TAPS * H) ** -0.5, 0.3125, ((0, 16),)),
    }


OFFSETS = ((0, 0, 0, 0), (1, 0, 0, 0), (-1, 0, 0, 0), (0, 1, 0, 0), (0, -1, 0, 0), (0, 0, 1, 0), (0, 0, -1, 0), (0, 0, 0, 1), (0, 0, 0, -1))
PLANES = ((0, 1), (0, 2), (0, 3), (1, 2), (1, 3), (2, 3))

def real_product(left, right):
    return lax.optimization_barrier(jnp.sum(left[:, :, None] * right[None], axis=1))

def complex_mul(left, right):
    real_part = real_product(left[0], right[0]) - real_product(left[1], right[1])
    imag_part = real_product(left[0], right[1]) + real_product(left[1], right[0])
    return jnp.stack([real_part, imag_part])

def dagger(matrix):
    return jnp.stack([jnp.swapaxes(matrix[0], 0, 1), -jnp.swapaxes(matrix[1], 0, 1)])

def trace_of(matrix):
    return matrix[:, 0, 0] + matrix[:, 1, 1] + matrix[:, 2, 2]

def unit_step(direction, amount):
    return tuple((amount if index == direction else 0 for index in range(4)))

def step_sum(first, second):
    return tuple((first[index] + second[index] for index in range(4)))

def moved(field, disp):
    rolled = field
    if disp[3] != 0:
        rolled = jnp.roll(rolled, -disp[3], axis=rolled.ndim - 2)
    lattice = rolled.reshape(rolled.shape[:-1] + (LS, LS, LS))
    for space_axis in range(3):
        if disp[space_axis] != 0:
            lattice = jnp.roll(lattice, -disp[space_axis], axis=lattice.ndim - 3 + space_axis)
    return lattice.reshape(rolled.shape)

def gauge_terms(fields, locate):
    anchor = (0, 0, 0, 0)

    def link(direction, disp):
        return locate(fields[direction], disp)
    plaquettes = []
    for first_dir, second_dir in PLANES:
        loop = complex_mul(complex_mul(link(first_dir, anchor), link(second_dir, unit_step(first_dir, 1))), complex_mul(dagger(link(first_dir, unit_step(second_dir, 1))), dagger(link(second_dir, anchor))))
        plaquettes.append(trace_of(loop)[0] / 3.0)
    forces = []
    for direction in range(4):
        staple = None
        for other in range(4):
            if other == direction:
                continue
            upper = complex_mul(complex_mul(link(other, unit_step(direction, 1)), dagger(link(direction, unit_step(other, 1)))), dagger(link(other, anchor)))
            lower = complex_mul(complex_mul(dagger(link(other, step_sum(unit_step(direction, 1), unit_step(other, -1)))), dagger(link(direction, unit_step(other, -1)))), link(other, unit_step(other, -1)))
            staple = upper + lower if staple is None else staple + upper + lower
        current = link(direction, anchor)
        omega = complex_mul(current, staple)
        anti = 0.5 * (omega - dagger(omega))
        diag_mean = trace_of(anti) / 3.0
        eye_three = jnp.eye(3, dtype=anti.dtype)
        generator = (anti - diag_mean[:, None, None] * eye_three[None, :, :, None, None, None]) / 6.0
        applied = complex_mul(generator, current)
        twice = complex_mul(generator, applied)
        forces.append((current, applied, twice))
    return (plaquettes, forces)

def identity_like(sample):
    eye_three = jnp.eye(3, dtype=sample.dtype)[:, :, None, None]
    real_part = jnp.broadcast_to(eye_three, sample.shape[1:])
    return jnp.stack([real_part, jnp.zeros_like(real_part)])

def activity(parity, link_subset, times, sites):
    site_ids = jnp.arange(sites, dtype=jnp.int32)
    coord_sum = site_ids // (LS * LS) + site_ids // LS % LS + site_ids % LS
    colour = (times[:, None] + coord_sum[None, :]) % 2
    on_site = colour[None] == parity[:, :, None]
    masks = []
    for direction in range(4):
        chosen = (jnp.right_shift(link_subset, direction) % 2 == 1)[:, :, None]
        masks.append(jnp.logical_and(on_site, chosen))
    return jnp.stack(masks)

def conv_forward(weight, act, outputs):
    inputs = act.shape[0]
    panel = weight.reshape(len(OFFSETS), outputs, inputs)
    total = jnp.zeros((outputs, act[0].size), jnp.float32)
    for tap, offset in enumerate(OFFSETS):
        total = total + jnp.dot(panel[tap], moved(act, offset).reshape(inputs, -1), preferred_element_type=jnp.float32)
    return total.reshape((outputs,) + act.shape[1:])

def conv_back(weight, grad, inputs):
    outputs = grad.shape[0]
    panel = weight.reshape(len(OFFSETS), outputs, inputs)
    total = jnp.zeros((inputs, grad[0].size), jnp.float32)
    for tap, offset in enumerate(OFFSETS):
        back = tuple((-value for value in offset))
        total = total + jnp.dot(panel[tap].T, moved(grad, back).reshape(outputs, -1), preferred_element_type=jnp.float32)
    return total.reshape((inputs,) + grad.shape[1:])

def weight_grad(grad, act):
    outputs = grad.shape[0]
    inputs = act.shape[0]
    flat_grad = grad.reshape(outputs, -1)
    pieces = []
    for offset in OFFSETS:
        pieces.append(lax.dot_general(flat_grad, moved(act, offset).reshape(inputs, -1), (((1,), (1,)), ((), ())), preferred_element_type=jnp.float32))
    return jnp.stack(pieces).reshape(1, -1)

def reference(links, cotangent, parity, link_subset, w_first, w_second, w_third, w_last):
    fields = [links[index] for index in range(4)]
    plaquettes, forces = gauge_terms(fields, moved)
    time_links = links[3]
    steps_count = time_links.shape[4]

    def advance(index, product):
        return complex_mul(product, lax.dynamic_index_in_dim(time_links, index, axis=4, keepdims=False))
    whole = lax.fori_loop(0, steps_count, advance, identity_like(time_links[:, :, :, :, 0]))
    loop_trace = trace_of(whole) / 3.0
    conf_count = links.shape[4]
    sites = links.shape[6]
    polyakov = jnp.broadcast_to(loop_trace[:, :, None, :], (2, conf_count, steps_count, sites))
    features = jnp.concatenate([jnp.stack(plaquettes), polyakov], axis=0).astype(jnp.bfloat16)
    hidden = w_first.shape[0] // (len(OFFSETS) * features.shape[0])
    hidden_one = jnp.tanh(conv_forward(w_first, features, hidden)).astype(jnp.bfloat16)
    hidden_two = jnp.tanh(conv_forward(w_second, hidden_one, hidden)).astype(jnp.bfloat16)
    hidden_three = jnp.tanh(conv_forward(w_third, hidden_two, hidden)).astype(jnp.bfloat16)
    coeff = jnp.tanh(conv_forward(w_last, hidden_three, 4))
    times = jnp.arange(steps_count, dtype=jnp.int32)
    masks = activity(parity, link_subset, times, sites).astype(coeff.dtype)
    new_fields = []
    coeff_grads = []
    for direction in range(4):
        current, applied, twice = forces[direction]
        factor = coeff[direction]
        gate = masks[direction]
        new_fields.append(current + gate * (factor * applied + 0.5 * factor * factor * twice))
        incoming = cotangent[direction].astype(coeff.dtype)
        slope = applied + factor * twice
        coeff_grads.append(gate * lax.optimization_barrier(jnp.sum(incoming * slope, axis=(0, 1, 2))))
    new_links = jnp.stack(new_fields)
    coeff_grad = jnp.stack(coeff_grads)
    last_pre = (coeff_grad * (1.0 - coeff * coeff)).astype(jnp.bfloat16)
    three = hidden_three.astype(coeff.dtype)
    third_pre = (conv_back(w_last, last_pre, hidden) * (1.0 - three * three)).astype(jnp.bfloat16)
    two = hidden_two.astype(coeff.dtype)
    second_pre = (conv_back(w_third, third_pre, hidden) * (1.0 - two * two)).astype(jnp.bfloat16)
    one = hidden_one.astype(coeff.dtype)
    first_pre = (conv_back(w_second, second_pre, hidden) * (1.0 - one * one)).astype(jnp.bfloat16)
    grad_last = weight_grad(last_pre, hidden_three)
    grad_third = weight_grad(third_pre, hidden_two)
    grad_second = weight_grad(second_pre, hidden_one)
    grad_first = weight_grad(first_pre, features)
    return (new_links, grad_first, grad_second, grad_third, grad_last)
```

```python
import functools

import jax
import jax.numpy as jnp
from jax import lax
from jax.experimental import pallas as pl
from jax.experimental.pallas import tpu as pltpu
from jax.sharding import PartitionSpec as P

F32 = jnp.float32
BF16 = jnp.bfloat16
TAPS = 9
H = 48
LANES = 128
SITES = 512
PAIRS = ((0, 1), (0, 2), (0, 3), (1, 2), (1, 3), (2, 3))
SWAP = (0, 2, 1, 4, 3, 6, 5, 8, 7)
ENTRIES = tuple((c, i, j) for c in range(2) for i in range(3) for j in range(3))
SLABROWS = 80
BLOCKROWS = 112
LIMIT = 40 * 1024 * 1024


def lane_iota(rows):
    return lax.broadcasted_iota(jnp.int32, (rows, LANES), 1)


def row_iota():
    return lax.broadcasted_iota(jnp.int32, (8, LANES), 0)


def roll_lanes(value, amount):
    return pltpu.roll(value, amount % LANES, 1)


def shift_z(chunk, sign, lanes):
    z = lanes % 8
    if sign > 0:
        return jnp.where(z == 7, roll_lanes(chunk, 7), roll_lanes(chunk, -1))
    return jnp.where(z == 0, roll_lanes(chunk, -7), roll_lanes(chunk, 1))


def shift_y(chunk, sign, lanes):
    y = lanes // 8 % 8
    if sign > 0:
        return jnp.where(y == 7, roll_lanes(chunk, 56), roll_lanes(chunk, -8))
    return jnp.where(y == 0, roll_lanes(chunk, -56), roll_lanes(chunk, 8))


def dense_shift(pair, axis, sign):
    lanes = lane_iota(8)
    if axis == 2:
        return [shift_z(chunk, sign, lanes) for chunk in pair]
    if axis == 1:
        return [shift_y(chunk, sign, lanes) for chunk in pair]
    low = lanes < 64
    first, second = [roll_lanes(chunk, 64) for chunk in pair]
    if sign > 0:
        return [jnp.where(low, first, second), jnp.where(low, second, pltpu.roll(first, 4, 0))]
    return [jnp.where(low, pltpu.roll(second, 4, 0), first), jnp.where(low, first, second)]


def pack_pair(value):
    return [
        jnp.concatenate([value[:, c * 128:c * 128 + 128], value[:, 256 + c * 128:384 + c * 128]], axis=0)
        for c in range(2)
    ]


def halo_pair(ref, index):
    top = row_iota() < 4
    pair = []
    for c in range(2):
        low = jnp.broadcast_to(ref[index, c:c + 1, :], (8, LANES))
        high = jnp.broadcast_to(ref[index, 2 + c:3 + c, :], (8, LANES))
        pair.append(jnp.where(top, low, high))
    return pair


def load_matrix(read):
    real = [[read(3 * i + j) for j in range(3)] for i in range(3)]
    imag = [[read(9 + 3 * i + j) for j in range(3)] for i in range(3)]
    return (real, imag, 1)


def dagger(matrix):
    real, imag, sign = matrix
    return (
        [[real[j][i] for j in range(3)] for i in range(3)],
        [[imag[j][i] for j in range(3)] for i in range(3)],
        -sign,
    )


def total(terms, signs):
    value = None
    for term, sign in zip(terms, signs):
        if value is None:
            value = term if sign > 0 else -term
        else:
            value = value + term if sign > 0 else value - term
    return value


def mat_mul(left, right):
    lr, li, ls = left
    rr, ri, rs = right
    same = ls == rs
    real = [[None] * 3 for _ in range(3)]
    imag = [[None] * 3 for _ in range(3)]
    for i in range(3):
        for j in range(3):
            real[i][j] = total(
                [lr[i][k] * rr[k][j] for k in range(3)] + [li[i][k] * ri[k][j] for k in range(3)],
                [1, 1, 1] + [-1 if same else 1] * 3,
            )
            imag[i][j] = total(
                [lr[i][k] * ri[k][j] for k in range(3)] + [li[i][k] * rr[k][j] for k in range(3)],
                [1, 1, 1] + [1 if same else -1] * 3,
            )
    return (real, imag, ls if same else rs)


def imag_of(matrix, i, j):
    return matrix[1][i][j] if matrix[2] > 0 else -matrix[1][i][j]


def store_matrix(matrix, write):
    for i in range(3):
        for j in range(3):
            write(3 * i + j, matrix[0][i][j])
            write(9 + 3 * i + j, imag_of(matrix, i, j))


def anti_parts(matrix):
    parts = [2.0 * imag_of(matrix, i, i) for i in range(3)]
    for i, j in ((0, 1), (0, 2), (1, 2)):
        parts.append(matrix[0][i][j] - matrix[0][j][i])
        parts.append(imag_of(matrix, i, j) + imag_of(matrix, j, i))
    return parts


def anti_matrix(parts):
    zero = jnp.zeros_like(parts[0])
    real = [[zero, parts[3], parts[5]], [-parts[3], zero, parts[7]], [-parts[5], -parts[7], zero]]
    imag = [[parts[0], parts[4], parts[6]], [parts[4], parts[1], parts[8]], [parts[6], parts[8], parts[2]]]
    return real, imag


def anti_mul(parts, right):
    real, imag = anti_matrix(parts)
    rr, ri, _ = right
    out_r = [[None] * 3 for _ in range(3)]
    out_i = [[None] * 3 for _ in range(3)]
    for i in range(3):
        for j in range(3):
            value_r = -(imag[i][i] * ri[i][j])
            value_i = imag[i][i] * rr[i][j]
            for k in range(3):
                if k != i:
                    value_r = value_r + real[i][k] * rr[k][j] - imag[i][k] * ri[k][j]
                    value_i = value_i + real[i][k] * ri[k][j] + imag[i][k] * rr[k][j]
            out_r[i][j] = value_r
            out_i[i][j] = value_i
    return (out_r, out_i, 1)


def pack_links(links_ref, dense):
    def body(mu, carry):
        for e, (c, i, j) in enumerate(ENTRIES):
            low, high = pack_pair(links_ref[mu, c, i, j, 0].astype(F32))
            dense[mu, e, 0] = low
            dense[mu, e, 1] = high
        return carry

    lax.fori_loop(0, 4, body, 0)


def first_kernel(widths, links_ref, w1_ref, w2_ref, w3_ref, w4_ref, up_ref, down_ref, block_ref, dense, moved, rows, block):
    pack_links(links_ref, dense)

    def shift_body(e, carry):
        pair = [dense[3, e, 0], dense[3, e, 1]]
        for mu in range(3):
            low, high = dense_shift(pair, mu, 1)
            moved[mu, e, 0] = low
            moved[mu, e, 1] = high
        return carry

    lax.fori_loop(0, 18, shift_body, 0)

    for mu in range(3):
        def staple_body(c, carry):
            u_mu = load_matrix(lambda e: dense[mu, e, c])
            u_t = load_matrix(lambda e: dense[3, e, c])
            edge = mat_mul(u_mu, load_matrix(lambda e: moved[mu, e, c]))
            staple = mat_mul(dagger(edge), u_t)

            def write(e, value):
                rows[mu * 18 + e, pl.ds(c, 1)] = value[3:4]
                rows[mu * 18 + e, pl.ds(2 + c, 1)] = value[7:8]

            store_matrix(staple, write)
            return carry

        lax.fori_loop(0, 2, staple_body, 0)
    for q in range(4):
        up_ref[:, q * 128:q * 128 + 128] = rows[:, q, :].astype(BF16)
    for mu in range(3):
        for e in range(18):
            for c in range(2):
                value = dense[mu, e, c]
                rows[mu * 18 + e, c:c + 1] = value[0:1]
                rows[mu * 18 + e, 2 + c:3 + c] = value[4:5]
    for q in range(4):
        down_ref[:, q * 128:q * 128 + 128] = rows[:, q, :].astype(BF16)

    block[...] = jnp.zeros_like(block)

    def slab_body(c, carry):
        u_t = load_matrix(lambda e: dense[3, e, c])
        ahead = load_matrix(lambda e: pltpu.roll(dense[3, e, c], 7, 0))
        two = mat_mul(u_t, ahead)
        later = tuple(
            [[pltpu.roll(part[i][j], 6, 0) for j in range(3)] for i in range(3)] for part in two[:2]
        ) + (two[2],)
        four = mat_mul(two, later)

        def write(e, value):
            block[pl.ds(4 * e + c, 1), :] = value[0:1]
            block[pl.ds(4 * e + 2 + c, 1), :] = value[4:5]

        store_matrix(four, write)
        return carry

    lax.fori_loop(0, 2, slab_body, 0)
    offset = 0
    for ref, width in zip((w2_ref, w3_ref, w1_ref, w4_ref), widths):
        flat = ref[...].astype(F32)
        for r in range(27):
            block[SLABROWS + r:SLABROWS + r + 1, offset:offset + width] = flat[:, width * r:width * r + width]
        offset += width
    block_ref[...] = block[...].astype(BF16)


def gauge_kernel(
    links_ref, cot_ref, up_ref, down_ref, parity_ref, subset_ref,
    fm_ref, fup_ref, fdown_ref, w1_ref, w2_ref,
    dense, cots, moved, staples, sums, halo_up, halo_down, forces, rows,
):
    pack_links(links_ref, dense)
    pack_links(cot_ref, cots)
    for q in range(4):
        halo_up[:, q, :] = up_ref[:, q * 128:q * 128 + 128].astype(F32)
        halo_down[:, q, :] = down_ref[:, q * 128:q * 128 + 128].astype(F32)
    rows[...] = jnp.zeros_like(rows)
    forces[...] = jnp.zeros_like(forces)
    steps = row_iota() % 4
    lanes = lane_iota(8)

    def shift_body(e, carry):
        for nu in range(4):
            pair = [dense[nu, e, 0], dense[nu, e, 1]]
            for mu in range(3):
                if mu != nu:
                    low, high = dense_shift(pair, mu, 1)
                    moved[mu, nu, e, 0] = low
                    moved[mu, nu, e, 1] = high
            if nu < 3:
                halo = halo_pair(halo_down, nu * 18 + e)
                for c in range(2):
                    moved[3, nu, e, c] = jnp.where(steps == 3, halo[c], pltpu.roll(pair[c], 7, 0))
        return carry

    lax.fori_loop(0, 18, shift_body, 0)

    def put_row(channel, c, value):
        for t in range(4):
            rows[t, c, pl.ds(channel, 1), :] = value[t:t + 1]
            rows[t, 2 + c, pl.ds(channel, 1), :] = value[4 + t:5 + t]

    def plane_body(step, carry):
        plane = step // 2
        c = step % 2
        mu = jnp.where(plane < 3, 0, jnp.where(plane < 5, 1, 2))
        nu = jnp.where(plane < 3, plane + 1, jnp.where(plane < 5, plane - 1, 3))
        u_mu = load_matrix(lambda e: dense[mu, e, c])
        u_nu = load_matrix(lambda e: dense[nu, e, c])
        one = mat_mul(u_mu, load_matrix(lambda e: moved[mu, nu, e, c]))
        two = mat_mul(u_nu, load_matrix(lambda e: moved[nu, mu, e, c]))
        loop = mat_mul(one, dagger(two))
        put_row(plane, c, (loop[0][0][0] + loop[0][1][1] + loop[0][2][2]) / 3.0)
        for e, part in enumerate(anti_parts(loop)):
            forces[mu, e, c] += part
            forces[nu, e, c] -= part

        def write_mu(e, value):
            staples[mu, nu, e, c] = value

        def write_nu(e, value):
            staples[nu, mu, e, c] = value

        store_matrix(mat_mul(dagger(one), u_nu), write_mu)
        store_matrix(mat_mul(dagger(two), u_mu), write_nu)
        return carry

    lax.fori_loop(0, 12, plane_body, 0)

    def lower_body(e, carry):
        for mu in range(4):
            acc = [None, None]
            for nu in range(4):
                if nu == mu:
                    continue
                pair = [staples[mu, nu, e, 0], staples[mu, nu, e, 1]]
                if nu < 3:
                    pair = dense_shift(pair, nu, -1)
                else:
                    halo = halo_pair(halo_up, mu * 18 + e)
                    pair = [jnp.where(steps == 0, halo[c], pltpu.roll(pair[c], 1, 0)) for c in range(2)]
                acc = [pair[c] if acc[c] is None else acc[c] + pair[c] for c in range(2)]
            sums[mu, e, 0] = acc[0]
            sums[mu, e, 1] = acc[1]
        return carry

    lax.fori_loop(0, 18, lower_body, 0)

    colour = (lanes // 64 + lanes // 8 % 8 + lanes % 8 + steps) % 2
    parity = jnp.zeros_like(steps)
    subset = jnp.zeros_like(steps)
    for t in range(4):
        parity = jnp.where(steps == t, parity_ref[0, t], parity)
        subset = jnp.where(steps == t, subset_ref[0, t], subset)
    on_site = colour == parity

    def force_body(step, carry):
        mu = step // 2
        c = step % 2
        current = load_matrix(lambda e: dense[mu, e, c])
        omega = mat_mul(current, load_matrix(lambda e: sums[mu, e, c]))
        parts = [part + forces[mu, e, c] for e, part in enumerate(anti_parts(omega))]
        mean = (parts[0] + parts[1] + parts[2]) * (1.0 / 3.0)
        parts = [parts[e] - mean if e < 3 else parts[e] for e in range(9)]
        parts = [part * (1.0 / 12.0) for part in parts]
        applied = anti_mul(parts, current)
        twice = anti_mul(parts, applied)
        gate = jnp.where(jnp.logical_and(on_site, jnp.right_shift(subset, mu) % 2 == 1), 1.0, 0.0)
        slope = jnp.zeros_like(gate)
        curve = jnp.zeros_like(gate)
        for e, (part, i, j) in enumerate(ENTRIES):
            weight = cots[mu, e, c]
            slope = slope + weight * applied[part][i][j]
            curve = curve + weight * twice[part][i][j]
            w1_ref[mu, e, c] = gate * applied[part][i][j]
            w2_ref[mu, e, c] = gate * twice[part][i][j]
        put_row(8 + mu, c, gate * slope)
        put_row(12 + mu, c, gate * curve)
        return carry

    lax.fori_loop(0, 8, force_body, 0)
    for t in range(4):
        for q in range(4):
            value = rows[t, q]
            fm_ref[t, :, q * 128:q * 128 + 128] = value.astype(BF16)
            if t > 0:
                fup_ref[t - 1, :, q * 128:q * 128 + 128] = value[0:8].astype(BF16)
            if t < 3:
                fdown_ref[t, :, q * 128:q * 128 + 128] = value[0:8].astype(BF16)


def selectors():
    row = lax.broadcasted_iota(jnp.int32, (432, 72), 0)
    col = lax.broadcasted_iota(jnp.int32, (432, 72), 1)
    group = row // 12
    spread = (group // 4 * 8 + group % 4 == col).astype(F32).astype(BF16)
    keep = (
        lax.broadcasted_iota(jnp.int32, (432, H), 1) // 4 == lax.broadcasted_iota(jnp.int32, (432, H), 0) % 12
    )
    return spread, keep


def panel_kernel(gathered_ref, weights_ref, loops_ref, p1_ref, p2_ref, p3_ref, p4_ref, b2_ref, b3_ref, b4_ref, weights):
    count = gathered_ref.shape[0]

    def read(d):
        return load_matrix(lambda e: slabs[4 * e:4 * e + 4, :])

    slabs = gathered_ref[0, 0:SLABROWS, :].astype(F32)
    product = read(0)
    state = tuple(product[0][i][j] for i in range(3) for j in range(3)) + tuple(
        product[1][i][j] for i in range(3) for j in range(3)
    )

    def chain(d, state):
        slab = gathered_ref[d, 0:SLABROWS, :].astype(F32)
        left = load_matrix(lambda e: state[e])
        product = mat_mul(left, load_matrix(lambda e: slab[4 * e:4 * e + 4, :]))
        out = []
        store_matrix(product, lambda e, value: out.append((e, value)))
        return tuple(value for _, value in sorted(out, key=lambda item: item[0]))

    state = lax.fori_loop(1, count, chain, state)
    loops_ref[0] = (state[0] + state[4] + state[8]) / 3.0
    loops_ref[1] = (state[9] + state[13] + state[17]) / 3.0

    if weights_ref is None:
        for d in range(count):
            block = gathered_ref[d, SLABROWS:BLOCKROWS, :].astype(F32)
            weights[27 * d:27 * d + 27, :] = block[0:27]
    else:
        weights[...] = weights_ref[...].astype(F32)
    for k in range(TAPS):
        rows = slice(H * k, H * k + H)
        back = slice(H * SWAP[k], H * SWAP[k] + H)
        p2_ref[:, rows] = weights[rows, 0:48].astype(BF16)
        p3_ref[:, rows] = weights[rows, 48:96].astype(BF16)
        p1_ref[:, 8 * k:8 * k + 8] = weights[rows, 96:104].astype(BF16)
        turned = weights[back, :].T
        b2_ref[:, rows] = turned[0:48].astype(BF16)
        b3_ref[:, rows] = turned[48:96].astype(BF16)
    spread, keep = selectors()
    place = (
        lax.broadcasted_iota(jnp.int32, (LANES, H), 0) == 104 + lax.broadcasted_iota(jnp.int32, (LANES, H), 1) % 4
    ).astype(F32).astype(BF16)
    wide = jnp.dot(weights[...].astype(BF16), place, preferred_element_type=F32)
    wide = jnp.where(keep, wide, 0.0).astype(BF16)
    last = lax.dot_general(spread, wide, (((0,), (0,)), ((), ())), preferred_element_type=F32)
    p4_ref[...] = last.astype(BF16)
    for k in range(TAPS):
        b4_ref[:, 8 * k:8 * k + 8] = last[8 * SWAP[k]:8 * SWAP[k] + 8, :].T.astype(BF16)


def panel_kernel_plain(gathered_ref, *rest):
    panel_kernel(gathered_ref, None, *rest)


def chunks_of(value):
    return [value[:, q * 128:q * 128 + 128] for q in range(4)]


def one_shift(chunks, position):
    if position == 0:
        return chunks
    lanes = lane_iota(chunks[0].shape[0])
    sign = 1 if position % 2 == 1 else -1
    if position > 4:
        return [shift_z(chunk, sign, lanes) for chunk in chunks]
    if position > 2:
        return [shift_y(chunk, sign, lanes) for chunk in chunks]
    low = lanes < 64
    rolled = [roll_lanes(chunk, 64) for chunk in chunks]
    if sign > 0:
        return [jnp.where(low, rolled[q], rolled[(q + 1) % 4]) for q in range(4)]
    return [jnp.where(low, rolled[(q + 3) % 4], rolled[q]) for q in range(4)]


def span(slice_index, count=1):
    if isinstance(slice_index, int):
        return slice(slice_index * SITES, (slice_index + count) * SITES)
    return pl.ds(pl.multiple_of(slice_index * SITES, SITES), count * SITES)


def stack_wide(source, target, first, count):
    for s in range(count):
        chunks = chunks_of(source[:, span(first + s)])
        for position in range(7):
            shifted = one_shift(chunks, position)
            for q in range(4):
                lanes = slice(s * SITES + q * 128, s * SITES + q * 128 + 128)
                target[H * position:H * position + H, lanes] = shifted[q]
    width = slice(0, count * SITES)
    target[7 * H:8 * H, width] = source[:, span(first + 1, count)]
    target[8 * H:9 * H, width] = source[:, span(first - 1, count)]


def stack_thin(source, target, first, count):
    for s in range(count):
        chunks = chunks_of(source[:, span(first + s)])
        ahead = chunks_of(source[:, span(first + s + 1)])
        behind = chunks_of(source[:, span(first + s - 1)])
        columns = [one_shift(chunks, position) for position in range(7)] + [ahead, behind]
        for q in range(4):
            lanes = slice(s * SITES + q * 128, s * SITES + q * 128 + 128)
            target[0:72, lanes] = jnp.concatenate([column[q] for column in columns], axis=0).astype(BF16)


def one_minus_square(value):
    value = value.astype(F32)
    return 1.0 - value * value


def conv_kernel(
    split, fm_ref, below_ref, above_ref, fbelow_ref, fabove_ref, loops_ref,
    p1_ref, p2_ref, p3_ref, p4_ref, b2_ref, b3_ref, b4_ref,
    coeff_ref, grads_ref,
    feats, mixed, h1, h2, h3, parts, lasts, g3, g2, wide, thin, packed,
):
    row8 = lax.broadcasted_iota(jnp.int32, (8, SITES), 0)
    loop_re = jnp.concatenate([loops_ref[0, q:q + 1, :] for q in range(4)], axis=1)
    loop_im = jnp.concatenate([loops_ref[1, q:q + 1, :] for q in range(4)], axis=1)
    loops = jnp.where(row8 == 6, loop_re, jnp.where(row8 == 7, loop_im, 0.0))
    loops = loops.astype(BF16).astype(F32)
    for j in range(3):
        feats[:, span(j)] = fbelow_ref[j].astype(F32) + loops
        feats[:, span(15 + j)] = fabove_ref[j].astype(F32) + loops
    for base, ref in ((3, below_ref), (7, fm_ref), (11, above_ref)):
        for j in range(4):
            value = ref[j].astype(F32)
            feats[:, span(base + j)] = value[0:8] + loops
            mixed[:, span(base + j)] = value[8:16]

    def layer_one(step, carry):
        first = 1 + 4 * step
        stack_thin(feats, thin, first, 4)
        out = jnp.dot(p1_ref[...], thin[...], preferred_element_type=F32)
        h1[:, span(first, 4)] = jnp.tanh(out).astype(BF16)
        return carry

    lax.fori_loop(0, 4, layer_one, 0)

    def layer_two(step, carry):
        first = 2 + 2 * step
        stack_wide(h1, wide, first, 2)
        out = jnp.dot(p2_ref[...], wide[:, 0:1024], preferred_element_type=F32)
        h2[:, span(first, 2)] = jnp.tanh(out).astype(BF16)
        return carry

    lax.fori_loop(0, 7, layer_two, 0)

    def layer_three(step, carry):
        first = 3 + 2 * step
        stack_wide(h2, wide, first, 2)
        out = jnp.dot(p3_ref[...], wide[:, 0:1024], preferred_element_type=F32)
        out = jnp.tanh(out).astype(BF16)
        h3[:, span(first, 2)] = out
        taps = jnp.dot(p4_ref[...], out, preferred_element_type=F32)
        for s in range(2):
            acc = None
            for position in range(7):
                shifted = one_shift(
                    chunks_of(taps[8 * position:8 * position + 8, s * SITES:(s + 1) * SITES]), position
                )
                acc = shifted if acc is None else [a + b for a, b in zip(acc, shifted)]
            parts[0, :, span(first + s)] = jnp.concatenate(acc, axis=1)
            parts[1, :, span(first + s)] = taps[56:64, s * SITES:(s + 1) * SITES]
            parts[2, :, span(first + s)] = taps[64:72, s * SITES:(s + 1) * SITES]
        return carry

    lax.fori_loop(0, 6, layer_three, 0)

    def last_layer(step, carry):
        for s in range(2):
            index = 4 + 2 * step + s
            coeff = jnp.tanh(parts[0, :, span(index)] + parts[1, :, span(index + 1)] + parts[2, :, span(index - 1)])
            blend = mixed[:, span(index)]
            value = (blend + coeff * pltpu.roll(blend, 4, 0)) * (1.0 - coeff * coeff)
            lasts[:, span(index)] = jnp.where(row8 < 4, value, 0.0).astype(BF16).astype(F32)
            parts[0, :, span(index)] = coeff
        return carry

    lax.fori_loop(0, 5, last_layer, 0)
    for t in range(4):
        coeff_ref[t] = parts[0, :, span(7 + t)]

    def back_three(first, count):
        stack_thin(lasts, thin, first, count)
        out = jnp.dot(b4_ref[...], thin[:, 0:count * SITES], preferred_element_type=F32)
        g3[:, span(first, count)] = (out * one_minus_square(h3[:, span(first, count)])).astype(BF16)

    back_three(5, 2)
    back_three(11, 2)
    back_three(7, 4)
    own = span(7, 4)
    contract = (((1,), (1,)), ((), ()))
    grad_last = lax.dot_general(thin[...], h3[:, own], contract, preferred_element_type=F32)

    stack_wide(g3, wide, 6, 1)
    out = jnp.dot(b3_ref[...], wide[:, 0:SITES], preferred_element_type=F32)
    g2[:, span(6)] = (out * one_minus_square(h2[:, span(6)])).astype(BF16)
    stack_wide(g3, wide, 11, 1)
    out = jnp.dot(b3_ref[...], wide[:, 0:SITES], preferred_element_type=F32)
    g2[:, span(11)] = (out * one_minus_square(h2[:, span(11)])).astype(BF16)
    stack_wide(g3, wide, 7, 4)
    out = jnp.dot(b3_ref[...], wide[...], preferred_element_type=F32)
    g2[:, own] = (out * one_minus_square(h2[:, own])).astype(BF16)
    grad_third = lax.dot_general(wide[...], h2[:, own], contract, preferred_element_type=F32)

    stack_wide(g2, wide, 7, 4)
    out = jnp.dot(b2_ref[...], wide[...], preferred_element_type=F32)
    g1 = (out * one_minus_square(h1[:, own])).astype(BF16)
    grad_second = lax.dot_general(wide[...], h1[:, own], contract, preferred_element_type=F32)

    stack_thin(feats, thin, 7, 4)
    grad_first = lax.dot_general(g1, thin[...], contract, preferred_element_type=F32)

    spread, keep = selectors()
    ordered = jnp.concatenate([grad_last[8 * SWAP[k]:8 * SWAP[k] + 8] for k in range(TAPS)], axis=0)
    broad = jnp.dot(spread, ordered.astype(BF16), preferred_element_type=F32)
    broad = jnp.where(keep, broad, 0.0).astype(BF16)
    place = (
        lax.broadcasted_iota(jnp.int32, (H, LANES), 1) == 104 + lax.broadcasted_iota(jnp.int32, (H, LANES), 0) % 4
    ).astype(F32).astype(BF16)
    packed[...] = jnp.dot(broad, place, preferred_element_type=F32)
    for k in range(TAPS):
        rows = slice(H * k, H * k + H)
        back = slice(H * SWAP[k], H * SWAP[k] + H)
        packed[rows, 0:48] = grad_second[back]
        packed[rows, 48:96] = grad_third[back]
        packed[rows, 96:104] = grad_first[:, 8 * k:8 * k + 8]
    if split:
        for d in range(16):
            grads_ref[d] = packed[27 * d:27 * d + 27, :].astype(BF16)
    else:
        grads_ref[...] = packed[...].astype(BF16)


def update_kernel(links_ref, w1_ref, w2_ref, coeff_ref, out_ref, factors):
    for mu in range(4):
        for t in range(4):
            for c in range(2):
                factors[mu, c, t:t + 1, :] = coeff_ref[t, mu:mu + 1, c * 128:c * 128 + 128]
                factors[mu, c, 4 + t:5 + t, :] = coeff_ref[t, mu:mu + 1, 256 + c * 128:384 + c * 128]

    def body(mu, carry):
        factor = [factors[mu, c] for c in range(2)]
        half = [0.5 * value * value for value in factor]
        for e, (part, i, j) in enumerate(ENTRIES):
            pair = pack_pair(links_ref[mu, part, i, j, 0])
            new = [pair[c] + factor[c] * w1_ref[mu, e, c] + half[c] * w2_ref[mu, e, c] for c in range(2)]
            out_ref[mu, part, i, j, 0] = jnp.concatenate(
                [new[0][0:4], new[1][0:4], new[0][4:8], new[1][4:8]], axis=1
            )
        return carry

    lax.fori_loop(0, 4, body, 0)


def sum_kernel(widths, parts_ref, first_ref, second_ref, third_ref, last_ref):
    value = parts_ref[0].astype(F32)
    for d in range(1, parts_ref.shape[0]):
        value = value + parts_ref[d].astype(F32)
    offset = 0
    for ref, width in zip((second_ref, third_ref, first_ref, last_ref), widths):
        for r in range(27):
            ref[:, width * r:width * r + width] = value[r:r + 1, offset:offset + width]
        offset += width


def call(body, outs, scratch, smem=(), count=0):
    specs = {}
    if smem:
        specs["in_specs"] = [
            pl.BlockSpec(memory_space=pltpu.SMEM if i in smem else pltpu.VMEM) for i in range(count)
        ]
    return pl.pallas_call(
        body,
        out_shape=[jax.ShapeDtypeStruct(shape, dtype) for shape, dtype in outs],
        scratch_shapes=[pltpu.VMEM(shape, dtype) for shape, dtype in scratch],
        compiler_params=pltpu.CompilerParams(vmem_limit_bytes=LIMIT),
        **specs,
    )


def on_device(links, cotangent, parity, link_subset, w_first, w_second, w_third, w_last):
    count = lax.axis_size("tm")

    def send(value, distance):
        return lax.ppermute(value, "tm", [(i, (i + distance) % count) for i in range(count)])

    widths = (768 // count, 768 // count, 128 // count, 64 // count)
    up, down, block = call(
        functools.partial(first_kernel, widths),
        [((54, SITES), BF16), ((54, SITES), BF16), ((BLOCKROWS, LANES), BF16)],
        [((4, 18, 2, 8, LANES), F32), ((3, 18, 2, 8, LANES), F32), ((54, 4, LANES), F32), ((BLOCKROWS, LANES), F32)],
    )(links, w_first[None], w_second[None], w_third[None], w_last[None])
    up = send(up, 1)
    down = send(down, -1)
    gathered = lax.all_to_all(
        jnp.broadcast_to(block[None], (count,) + block.shape), "tm", split_axis=0, concat_axis=0, tiled=True
    )
    fm, fup, fdown, applied, twice = call(
        gauge_kernel,
        [
            ((4, 16, SITES), BF16), ((3, 8, SITES), BF16), ((3, 8, SITES), BF16),
            ((4, 18, 2, 8, LANES), F32), ((4, 18, 2, 8, LANES), F32),
        ],
        [
            ((4, 18, 2, 8, LANES), F32), ((4, 18, 2, 8, LANES), F32), ((4, 4, 18, 2, 8, LANES), F32),
            ((4, 4, 18, 2, 8, LANES), F32), ((4, 18, 2, 8, LANES), F32), ((54, 4, LANES), F32), ((54, 4, LANES), F32),
            ((4, 9, 2, 8, LANES), F32), ((4, 4, 16, LANES), F32),
        ],
        smem=(4, 5), count=6,
    )(links, cotangent, up, down, parity, link_subset)
    below = send(fm, 1)
    above = send(fm, -1)
    fbelow = send(fup, 2)
    fabove = send(fdown, -2)

    panel_outs = [
        ((2, 4, LANES), F32), ((H, 72), BF16), ((H, 432), BF16), ((H, 432), BF16), ((72, H), BF16),
        ((H, 432), BF16), ((H, 432), BF16), ((H, 72), BF16),
    ]
    panel_scratch = [((432, LANES), F32)]
    if count == 16:
        loops, p1, p2, p3, p4, b2, b3, b4 = call(panel_kernel_plain, panel_outs, panel_scratch)(gathered)
    else:
        pieces = []
        offset = 0
        for width, full in zip(widths, (48, 48, 8, 4)):
            piece = gathered[:, SLABROWS:SLABROWS + 27, offset:offset + width]
            pieces.append(piece.reshape(432, full))
            offset += width
        pieces.append(jnp.zeros((432, 20), BF16))
        loops, p1, p2, p3, p4, b2, b3, b4 = call(panel_kernel, panel_outs, panel_scratch)(
            gathered, jnp.concatenate(pieces, axis=1)
        )

    window = 18 * SITES
    coeff, grads = call(
        functools.partial(conv_kernel, count == 16),
        [((4, 8, SITES), F32), ((16, 27, LANES) if count == 16 else (432, LANES), BF16)],
        [
            ((8, window), F32), ((8, window), F32), ((H, window), BF16), ((H, window), BF16), ((H, window), BF16),
            ((3, 8, window), F32), ((8, window), F32), ((H, window), BF16), ((H, window), BF16),
            ((432, 4 * SITES), BF16), ((72, 4 * SITES), BF16), ((432, LANES), F32),
        ],
    )(fm, below, above, fbelow, fabove, loops, p1, p2, p3, p4, b2, b3, b4)
    if count != 16:
        offset = 0
        pieces = []
        for width, full in zip(widths, (48, 48, 8, 4)):
            pieces.append(grads[:, offset:offset + full].reshape(count, 27, width))
            offset += full
        grads = jnp.concatenate(pieces, axis=2)
    grads = lax.all_to_all(grads, "tm", split_axis=0, concat_axis=0, tiled=True)
    (new_links,) = call(
        update_kernel, [(links.shape, F32)], [((4, 2, 8, LANES), F32)]
    )(links, applied, twice, coeff)
    grad_first, grad_second, grad_third, grad_last = call(
        functools.partial(sum_kernel, widths),
        [((1, 27 * width), F32) for width in (widths[2], widths[0], widths[1], widths[3])],
        [],
    )(grads)
    return (new_links, grad_first, grad_second, grad_third, grad_last)


def solution(mesh):
    placed = (
        P(None, None, None, None, "groups", "tm", None),
        P(None, None, None, None, "groups", "tm", None),
        P("groups", "tm"),
        P("groups", "tm"),
        P("tm"),
        P("tm"),
        P("tm"),
        P("tm"),
    )
    return jax.shard_map(
        on_device,
        mesh=mesh,
        in_specs=placed,
        out_specs=(
            P(None, None, None, None, "groups", "tm", None),
            P("groups", "tm"),
            P("groups", "tm"),
            P("groups", "tm"),
            P("groups", "tm"),
        ),
        check_vma=False,
    )
```

```python
import functools

import jax
import jax.numpy as jnp
from jax import lax
from jax.experimental import pallas as pl
from jax.experimental.pallas import tpu as pltpu
from jax.sharding import PartitionSpec as P

F32 = jnp.float32
BF16 = jnp.bfloat16
TAPS = 9
H = 48
LANES = 128
SITES = 512
PAIRS = ((0, 1), (0, 2), (0, 3), (1, 2), (1, 3), (2, 3))
SWAP = (0, 2, 1, 4, 3, 6, 5, 8, 7)
ENTRIES = tuple((c, i, j) for c in range(2) for i in range(3) for j in range(3))
SLABROWS = 48
BLOCKROWS = 80
LIMIT = 40 * 1024 * 1024


def lane_iota(rows):
    return lax.broadcasted_iota(jnp.int32, (rows, LANES), 1)


def row_iota():
    return lax.broadcasted_iota(jnp.int32, (8, LANES), 0)


def roll_lanes(value, amount):
    return pltpu.roll(value, amount % LANES, 1)


def shift_z(chunk, sign, lanes):
    z = lanes % 8
    if sign > 0:
        return jnp.where(z == 7, roll_lanes(chunk, 7), roll_lanes(chunk, -1))
    return jnp.where(z == 0, roll_lanes(chunk, -7), roll_lanes(chunk, 1))


def shift_y(chunk, sign, lanes):
    y = lanes // 8 % 8
    if sign > 0:
        return jnp.where(y == 7, roll_lanes(chunk, 56), roll_lanes(chunk, -8))
    return jnp.where(y == 0, roll_lanes(chunk, -56), roll_lanes(chunk, 8))


def dense_shift(pair, axis, sign):
    lanes = lane_iota(8)
    if axis == 2:
        return [shift_z(chunk, sign, lanes) for chunk in pair]
    if axis == 1:
        return [shift_y(chunk, sign, lanes) for chunk in pair]
    low = lanes < 64
    first, second = [roll_lanes(chunk, 64) for chunk in pair]
    if sign > 0:
        return [jnp.where(low, first, second), jnp.where(low, second, pltpu.roll(first, 4, 0))]
    return [jnp.where(low, pltpu.roll(second, 4, 0), first), jnp.where(low, first, second)]


def pack_pair(value):
    return [
        jnp.concatenate([value[:, c * 128:c * 128 + 128], value[:, 256 + c * 128:384 + c * 128]], axis=0)
        for c in range(2)
    ]


def halo_pair(ref, index):
    top = row_iota() < 4
    pair = []
    for c in range(2):
        low = jnp.broadcast_to(ref[index, c:c + 1, :], (8, LANES))
        high = jnp.broadcast_to(ref[index, 2 + c:3 + c, :], (8, LANES))
        pair.append(jnp.where(top, low, high))
    return pair


def load_matrix(read):
    real = [[read(3 * i + j) for j in range(3)] for i in range(3)]
    imag = [[read(9 + 3 * i + j) for j in range(3)] for i in range(3)]
    return (real, imag, 1)


def dagger(matrix):
    real, imag, sign = matrix
    return (
        [[real[j][i] for j in range(3)] for i in range(3)],
        [[imag[j][i] for j in range(3)] for i in range(3)],
        -sign,
    )


def total(terms, signs):
    value = None
    for term, sign in zip(terms, signs):
        if value is None:
            value = term if sign > 0 else -term
        else:
            value = value + term if sign > 0 else value - term
    return value


def mat_mul(left, right):
    lr, li, ls = left
    rr, ri, rs = right
    same = ls == rs
    real = [[None] * 3 for _ in range(3)]
    imag = [[None] * 3 for _ in range(3)]
    for i in range(3):
        for j in range(3):
            real[i][j] = total(
                [lr[i][k] * rr[k][j] for k in range(3)] + [li[i][k] * ri[k][j] for k in range(3)],
                [1, 1, 1] + [-1 if same else 1] * 3,
            )
            imag[i][j] = total(
                [lr[i][k] * ri[k][j] for k in range(3)] + [li[i][k] * rr[k][j] for k in range(3)],
                [1, 1, 1] + [1 if same else -1] * 3,
            )
    return (real, imag, ls if same else rs)


def imag_of(matrix, i, j):
    return matrix[1][i][j] if matrix[2] > 0 else -matrix[1][i][j]


def store_matrix(matrix, write):
    for i in range(3):
        for j in range(3):
            write(3 * i + j, matrix[0][i][j])
            write(9 + 3 * i + j, imag_of(matrix, i, j))


def anti_parts(matrix):
    parts = [2.0 * imag_of(matrix, i, i) for i in range(3)]
    for i, j in ((0, 1), (0, 2), (1, 2)):
        parts.append(matrix[0][i][j] - matrix[0][j][i])
        parts.append(imag_of(matrix, i, j) + imag_of(matrix, j, i))
    return parts


def anti_matrix(parts):
    zero = jnp.zeros_like(parts[0])
    real = [[zero, parts[3], parts[5]], [-parts[3], zero, parts[7]], [-parts[5], -parts[7], zero]]
    imag = [[parts[0], parts[4], parts[6]], [parts[4], parts[1], parts[8]], [parts[6], parts[8], parts[2]]]
    return real, imag


def anti_mul(parts, right):
    real, imag = anti_matrix(parts)
    rr, ri, _ = right
    out_r = [[None] * 3 for _ in range(3)]
    out_i = [[None] * 3 for _ in range(3)]
    for i in range(3):
        for j in range(3):
            value_r = -(imag[i][i] * ri[i][j])
            value_i = imag[i][i] * rr[i][j]
            for k in range(3):
                if k != i:
                    value_r = value_r + real[i][k] * rr[k][j] - imag[i][k] * ri[k][j]
                    value_i = value_i + real[i][k] * ri[k][j] + imag[i][k] * rr[k][j]
            out_r[i][j] = value_r
            out_i[i][j] = value_i
    return (out_r, out_i, 1)


def pack_links(links_ref, dense):
    def body(mu, carry):
        for e, (c, i, j) in enumerate(ENTRIES):
            low, high = pack_pair(links_ref[mu, c, i, j, 0].astype(F32))
            dense[mu, e, 0] = low
            dense[mu, e, 1] = high
        return carry

    lax.fori_loop(0, 4, body, 0)


def face_kernel(links_ref, up_ref, down_ref, dense, moved, rows):
    pack_links(links_ref, dense)

    def shift_body(e, carry):
        pair = [dense[3, e, 0], dense[3, e, 1]]
        for mu in range(3):
            low, high = dense_shift(pair, mu, 1)
            moved[mu, e, 0] = low
            moved[mu, e, 1] = high
        return carry

    lax.fori_loop(0, 18, shift_body, 0)

    def staple_body(step, carry):
        mu = step // 2
        c = step % 2
        u_mu = load_matrix(lambda e: dense[mu, e, c])
        u_t = load_matrix(lambda e: dense[3, e, c])
        edge = mat_mul(u_mu, load_matrix(lambda e: moved[mu, e, c]))
        staple = mat_mul(dagger(edge), u_t)

        def write(e, value):
            rows[mu * 18 + e, pl.ds(c, 1)] = value[3:4]
            rows[mu * 18 + e, pl.ds(2 + c, 1)] = value[7:8]

        store_matrix(staple, write)
        return carry

    lax.fori_loop(0, 6, staple_body, 0)
    for q in range(4):
        up_ref[:, q * 128:q * 128 + 128] = rows[:, q, :].astype(BF16)

    def down_body(e, carry):
        for mu in range(3):
            for c in range(2):
                value = dense[mu, e, c]
                rows[mu * 18 + e, c:c + 1] = value[0:1]
                rows[mu * 18 + e, 2 + c:3 + c] = value[4:5]
        return carry

    lax.fori_loop(0, 18, down_body, 0)
    for q in range(4):
        down_ref[:, q * 128:q * 128 + 128] = rows[:, q, :].astype(BF16)


def block_kernel(widths, links_ref, w1_ref, w2_ref, w3_ref, w4_ref, block_ref, dense, block):
    for e, (part, i, j) in enumerate(ENTRIES):
        dense[e, 0], dense[e, 1] = pack_pair(links_ref[3, part, i, j, 0])
    block[...] = jnp.zeros_like(block)

    def slab_body(c, carry):
        u_t = load_matrix(lambda e: dense[e, c])
        ahead = load_matrix(lambda e: pltpu.roll(dense[e, c], 7, 0))
        two = mat_mul(u_t, ahead)
        later = tuple(
            [[pltpu.roll(part[i][j], 6, 0) for j in range(3)] for i in range(3)] for part in two[:2]
        ) + (two[2],)
        four = mat_mul(two, later)

        def write(e, value):
            if e % 9 < 6:
                row = 4 * (e // 9 * 6 + e % 9)
                block[pl.ds(row + c, 1), :] = value[0:1]
                block[pl.ds(row + 2 + c, 1), :] = value[4:5]

        store_matrix(four, write)
        return carry

    lax.fori_loop(0, 2, slab_body, 0)
    offset = 0
    for ref, width in zip((w2_ref, w3_ref, w1_ref, w4_ref), widths):
        flat = ref[...].astype(F32)
        for r in range(27):
            block[SLABROWS + r:SLABROWS + r + 1, offset:offset + width] = flat[:, width * r:width * r + width]
        offset += width
    block_ref[...] = block[...].astype(BF16)


def gauge_kernel(
    links_ref, cot_ref, up_ref, down_ref, parity_ref, subset_ref,
    fm_ref, fup_ref, fdown_ref, w1_ref, w2_ref,
    dense, cots, moved, staples, sums, halo_up, halo_down, forces, rows,
):
    pack_links(links_ref, dense)
    pack_links(cot_ref, cots)
    for q in range(4):
        halo_up[:, q, :] = up_ref[:, q * 128:q * 128 + 128].astype(F32)
        halo_down[:, q, :] = down_ref[:, q * 128:q * 128 + 128].astype(F32)
    rows[...] = jnp.zeros_like(rows)
    forces[...] = jnp.zeros_like(forces)
    steps = row_iota() % 4
    lanes = lane_iota(8)

    def shift_body(e, carry):
        for nu in range(4):
            pair = [dense[nu, e, 0], dense[nu, e, 1]]
            for mu in range(3):
                if mu != nu:
                    low, high = dense_shift(pair, mu, 1)
                    moved[mu, nu, e, 0] = low
                    moved[mu, nu, e, 1] = high
            if nu < 3:
                halo = halo_pair(halo_down, nu * 18 + e)
                for c in range(2):
                    moved[3, nu, e, c] = jnp.where(steps == 3, halo[c], pltpu.roll(pair[c], 7, 0))
        return carry

    lax.fori_loop(0, 18, shift_body, 0)

    def put_row(channel, c, value):
        for t in range(4):
            rows[t, c, pl.ds(channel, 1), :] = value[t:t + 1]
            rows[t, 2 + c, pl.ds(channel, 1), :] = value[4 + t:5 + t]

    def plane_body(step, carry):
        plane = step // 2
        c = step % 2
        mu = jnp.where(plane < 3, 0, jnp.where(plane < 5, 1, 2))
        nu = jnp.where(plane < 3, plane + 1, jnp.where(plane < 5, plane - 1, 3))
        u_mu = load_matrix(lambda e: dense[mu, e, c])
        u_nu = load_matrix(lambda e: dense[nu, e, c])
        one = mat_mul(u_mu, load_matrix(lambda e: moved[mu, nu, e, c]))
        two = mat_mul(u_nu, load_matrix(lambda e: moved[nu, mu, e, c]))
        loop = mat_mul(one, dagger(two))
        put_row(plane, c, (loop[0][0][0] + loop[0][1][1] + loop[0][2][2]) / 3.0)
        for e, part in enumerate(anti_parts(loop)):
            forces[mu, e, c] += part
            forces[nu, e, c] -= part

        def write_mu(e, value):
            staples[mu, nu, e, c] = value

        def write_nu(e, value):
            staples[nu, mu, e, c] = value

        store_matrix(mat_mul(dagger(one), u_nu), write_mu)
        store_matrix(mat_mul(dagger(two), u_mu), write_nu)
        return carry

    lax.fori_loop(0, 12, plane_body, 0)

    def lower_body(e, carry):
        for mu in range(4):
            acc = [None, None]
            for nu in range(4):
                if nu == mu:
                    continue
                pair = [staples[mu, nu, e, 0], staples[mu, nu, e, 1]]
                if nu < 3:
                    pair = dense_shift(pair, nu, -1)
                else:
                    halo = halo_pair(halo_up, mu * 18 + e)
                    pair = [jnp.where(steps == 0, halo[c], pltpu.roll(pair[c], 1, 0)) for c in range(2)]
                acc = [pair[c] if acc[c] is None else acc[c] + pair[c] for c in range(2)]
            sums[mu, e, 0] = acc[0]
            sums[mu, e, 1] = acc[1]
        return carry

    lax.fori_loop(0, 18, lower_body, 0)

    colour = (lanes // 64 + lanes // 8 % 8 + lanes % 8 + steps) % 2
    parity = jnp.zeros_like(steps)
    subset = jnp.zeros_like(steps)
    for t in range(4):
        parity = jnp.where(steps == t, parity_ref[0, t], parity)
        subset = jnp.where(steps == t, subset_ref[0, t], subset)
    on_site = colour == parity

    def force_body(step, carry):
        mu = step // 2
        c = step % 2
        current = load_matrix(lambda e: dense[mu, e, c])
        omega = mat_mul(current, load_matrix(lambda e: sums[mu, e, c]))
        parts = [part + forces[mu, e, c] for e, part in enumerate(anti_parts(omega))]
        mean = (parts[0] + parts[1] + parts[2]) * (1.0 / 3.0)
        parts = [parts[e] - mean if e < 3 else parts[e] for e in range(9)]
        parts = [part * (1.0 / 12.0) for part in parts]
        applied = anti_mul(parts, current)
        twice = anti_mul(parts, applied)
        gate = jnp.where(jnp.logical_and(on_site, jnp.right_shift(subset, mu) % 2 == 1), 1.0, 0.0)
        slope = jnp.zeros_like(gate)
        curve = jnp.zeros_like(gate)
        for e, (part, i, j) in enumerate(ENTRIES):
            weight = cots[mu, e, c]
            slope = slope + weight * applied[part][i][j]
            curve = curve + weight * twice[part][i][j]
            w1_ref[mu, e, c] = gate * applied[part][i][j]
            w2_ref[mu, e, c] = gate * twice[part][i][j]
        put_row(8 + mu, c, gate * slope)
        put_row(12 + mu, c, gate * curve)
        return carry

    lax.fori_loop(0, 8, force_body, 0)
    for t in range(4):
        for q in range(4):
            value = rows[t, q]
            fm_ref[t, :, q * 128:q * 128 + 128] = value.astype(BF16)
            if t > 0:
                fup_ref[t - 1, :, q * 128:q * 128 + 128] = value[0:8].astype(BF16)
            if t < 3:
                fdown_ref[t, :, q * 128:q * 128 + 128] = value[0:8].astype(BF16)


def selectors():
    row = lax.broadcasted_iota(jnp.int32, (432, 72), 0)
    col = lax.broadcasted_iota(jnp.int32, (432, 72), 1)
    group = row // 12
    spread = (group // 4 * 8 + group % 4 == col).astype(F32).astype(BF16)
    keep = (
        lax.broadcasted_iota(jnp.int32, (432, H), 1) // 4 == lax.broadcasted_iota(jnp.int32, (432, H), 0) % 12
    )
    return spread, keep


def panel_kernel(gathered_ref, weights_ref, loops_ref, p1_ref, p2_ref, p3_ref, p4_ref, b2_ref, b3_ref, b4_ref, weights):
    count = gathered_ref.shape[0]

    def read(d):
        slab = gathered_ref[d, 0:SLABROWS, :].astype(F32)
        real = [[slab[4 * (3 * i + j):4 * (3 * i + j) + 4, :] for j in range(3)] for i in range(2)]
        imag = [[slab[24 + 4 * (3 * i + j):28 + 4 * (3 * i + j), :] for j in range(3)] for i in range(2)]
        real.append([])
        imag.append([])
        for k in range(3):
            i, j = (k + 1) % 3, (k + 2) % 3
            real[2].append(
                (real[0][i] * real[1][j] - imag[0][i] * imag[1][j])
                - (real[0][j] * real[1][i] - imag[0][j] * imag[1][i])
            )
            imag[2].append(
                (real[0][j] * imag[1][i] + imag[0][j] * real[1][i])
                - (real[0][i] * imag[1][j] + imag[0][i] * real[1][j])
            )
        return (real, imag, 1)

    def flat(matrix):
        return tuple(matrix[0][i][j] for i in range(3) for j in range(3)) + tuple(
            imag_of(matrix, i, j) for i in range(3) for j in range(3)
        )

    def chain(d, state):
        return flat(mat_mul(load_matrix(lambda e: state[e]), read(d)))

    state = lax.fori_loop(1, count, chain, flat(read(0)))
    loops_ref[0] = (state[0] + state[4] + state[8]) / 3.0
    loops_ref[1] = (state[9] + state[13] + state[17]) / 3.0

    if weights_ref is None:
        for d in range(count):
            block = gathered_ref[d, SLABROWS:BLOCKROWS, :].astype(F32)
            weights[27 * d:27 * d + 27, :] = block[0:27]
    else:
        weights[...] = weights_ref[...].astype(F32)
    for k in range(TAPS):
        rows = slice(H * k, H * k + H)
        back = slice(H * SWAP[k], H * SWAP[k] + H)
        p2_ref[:, rows] = weights[rows, 0:48].astype(BF16)
        p3_ref[:, rows] = weights[rows, 48:96].astype(BF16)
        p1_ref[:, 8 * k:8 * k + 8] = weights[rows, 96:104].astype(BF16)
        turned = weights[back, :].T
        b2_ref[:, rows] = turned[0:48].astype(BF16)
        b3_ref[:, rows] = turned[48:96].astype(BF16)
    spread, keep = selectors()
    place = (
        lax.broadcasted_iota(jnp.int32, (LANES, H), 0) == 104 + lax.broadcasted_iota(jnp.int32, (LANES, H), 1) % 4
    ).astype(F32).astype(BF16)
    wide = jnp.dot(weights[...].astype(BF16), place, preferred_element_type=F32)
    wide = jnp.where(keep, wide, 0.0).astype(BF16)
    last = lax.dot_general(spread, wide, (((0,), (0,)), ((), ())), preferred_element_type=F32)
    p4_ref[...] = last.astype(BF16)
    for k in range(TAPS):
        b4_ref[:, 8 * k:8 * k + 8] = last[8 * SWAP[k]:8 * SWAP[k] + 8, :].T.astype(BF16)


def panel_kernel_plain(gathered_ref, *rest):
    panel_kernel(gathered_ref, None, *rest)


def chunks_of(value):
    return [value[:, q * 128:q * 128 + 128] for q in range(4)]


def one_shift(chunks, position):
    if position == 0:
        return chunks
    lanes = lane_iota(chunks[0].shape[0])
    sign = 1 if position % 2 == 1 else -1
    if position > 4:
        return [shift_z(chunk, sign, lanes) for chunk in chunks]
    if position > 2:
        return [shift_y(chunk, sign, lanes) for chunk in chunks]
    low = lanes < 64
    rolled = [roll_lanes(chunk, 64) for chunk in chunks]
    if sign > 0:
        return [jnp.where(low, rolled[q], rolled[(q + 1) % 4]) for q in range(4)]
    return [jnp.where(low, rolled[(q + 3) % 4], rolled[q]) for q in range(4)]


def span(slice_index, count=1):
    if isinstance(slice_index, int):
        return slice(slice_index * SITES, (slice_index + count) * SITES)
    return pl.ds(pl.multiple_of(slice_index * SITES, SITES), count * SITES)


def stack_wide(source, target, first, count):
    for s in range(count):
        chunks = chunks_of(source[:, span(first + s)])
        for position in range(7):
            shifted = one_shift(chunks, position)
            for q in range(4):
                lanes = slice(s * SITES + q * 128, s * SITES + q * 128 + 128)
                target[H * position:H * position + H, lanes] = shifted[q]
    width = slice(0, count * SITES)
    target[7 * H:8 * H, width] = source[:, span(first + 1, count)]
    target[8 * H:9 * H, width] = source[:, span(first - 1, count)]


def stack_thin(source, target, first, count):
    for s in range(count):
        chunks = chunks_of(source[:, span(first + s)])
        ahead = chunks_of(source[:, span(first + s + 1)])
        behind = chunks_of(source[:, span(first + s - 1)])
        columns = [one_shift(chunks, position) for position in range(7)] + [ahead, behind]
        for q in range(4):
            lanes = slice(s * SITES + q * 128, s * SITES + q * 128 + 128)
            target[0:72, lanes] = jnp.concatenate([column[q] for column in columns], axis=0).astype(BF16)


def one_minus_square(value):
    value = value.astype(F32)
    return 1.0 - value * value


def conv_kernel(
    split, fm_ref, below_ref, above_ref, fbelow_ref, fabove_ref, loops_ref,
    p1_ref, p2_ref, p3_ref, p4_ref, b2_ref, b3_ref, b4_ref,
    coeff_ref, grads_ref,
    feats, mixed, h1, h2, h3, parts, lasts, g3, g2, wide, thin, packed,
):
    row8 = lax.broadcasted_iota(jnp.int32, (8, SITES), 0)
    loop_re = jnp.concatenate([loops_ref[0, q:q + 1, :] for q in range(4)], axis=1)
    loop_im = jnp.concatenate([loops_ref[1, q:q + 1, :] for q in range(4)], axis=1)
    loops = jnp.where(row8 == 6, loop_re, jnp.where(row8 == 7, loop_im, 0.0))
    loops = loops.astype(BF16).astype(F32)
    for j in range(3):
        feats[:, span(j)] = fbelow_ref[j].astype(F32) + loops
        feats[:, span(15 + j)] = fabove_ref[j].astype(F32) + loops
    for base, ref in ((3, below_ref), (7, fm_ref), (11, above_ref)):
        for j in range(4):
            value = ref[j].astype(F32)
            feats[:, span(base + j)] = value[0:8] + loops
            mixed[:, span(base + j)] = value[8:16]

    def layer_one(step, carry):
        first = 1 + 4 * step
        stack_thin(feats, thin, first, 4)
        out = jnp.dot(p1_ref[...], thin[...], preferred_element_type=F32)
        h1[:, span(first, 4)] = jnp.tanh(out).astype(BF16)
        return carry

    lax.fori_loop(0, 4, layer_one, 0)

    def layer_two(step, carry):
        first = 2 + 2 * step
        stack_wide(h1, wide, first, 2)
        out = jnp.dot(p2_ref[...], wide[:, 0:1024], preferred_element_type=F32)
        h2[:, span(first, 2)] = jnp.tanh(out).astype(BF16)
        return carry

    lax.fori_loop(0, 7, layer_two, 0)

    def layer_three(step, carry):
        first = 3 + 2 * step
        stack_wide(h2, wide, first, 2)
        out = jnp.dot(p3_ref[...], wide[:, 0:1024], preferred_element_type=F32)
        out = jnp.tanh(out).astype(BF16)
        h3[:, span(first, 2)] = out
        taps = jnp.dot(p4_ref[...], out, preferred_element_type=F32)
        for s in range(2):
            acc = None
            for position in range(7):
                shifted = one_shift(
                    chunks_of(taps[8 * position:8 * position + 8, s * SITES:(s + 1) * SITES]), position
                )
                acc = shifted if acc is None else [a + b for a, b in zip(acc, shifted)]
            parts[0, :, span(first + s)] = jnp.concatenate(acc, axis=1)
            parts[1, :, span(first + s)] = taps[56:64, s * SITES:(s + 1) * SITES]
            parts[2, :, span(first + s)] = taps[64:72, s * SITES:(s + 1) * SITES]
        return carry

    lax.fori_loop(0, 6, layer_three, 0)

    def last_layer(step, carry):
        for s in range(2):
            index = 4 + 2 * step + s
            coeff = jnp.tanh(parts[0, :, span(index)] + parts[1, :, span(index + 1)] + parts[2, :, span(index - 1)])
            blend = mixed[:, span(index)]
            value = (blend + coeff * pltpu.roll(blend, 4, 0)) * (1.0 - coeff * coeff)
            lasts[:, span(index)] = jnp.where(row8 < 4, value, 0.0).astype(BF16).astype(F32)
            parts[0, :, span(index)] = coeff
        return carry

    lax.fori_loop(0, 5, last_layer, 0)
    for t in range(4):
        coeff_ref[t] = parts[0, :, span(7 + t)]

    def back_three(first, count):
        stack_thin(lasts, thin, first, count)
        out = jnp.dot(b4_ref[...], thin[:, 0:count * SITES], preferred_element_type=F32)
        g3[:, span(first, count)] = (out * one_minus_square(h3[:, span(first, count)])).astype(BF16)

    back_three(5, 2)
    back_three(11, 2)
    back_three(7, 4)
    own = span(7, 4)
    contract = (((1,), (1,)), ((), ()))
    grad_last = lax.dot_general(thin[...], h3[:, own], contract, preferred_element_type=F32)

    stack_wide(g3, wide, 6, 1)
    out = jnp.dot(b3_ref[...], wide[:, 0:SITES], preferred_element_type=F32)
    g2[:, span(6)] = (out * one_minus_square(h2[:, span(6)])).astype(BF16)
    stack_wide(g3, wide, 11, 1)
    out = jnp.dot(b3_ref[...], wide[:, 0:SITES], preferred_element_type=F32)
    g2[:, span(11)] = (out * one_minus_square(h2[:, span(11)])).astype(BF16)
    stack_wide(g3, wide, 7, 4)
    out = jnp.dot(b3_ref[...], wide[...], preferred_element_type=F32)
    g2[:, own] = (out * one_minus_square(h2[:, own])).astype(BF16)
    grad_third = lax.dot_general(wide[...], h2[:, own], contract, preferred_element_type=F32)

    stack_wide(g2, wide, 7, 4)
    out = jnp.dot(b2_ref[...], wide[...], preferred_element_type=F32)
    g1 = (out * one_minus_square(h1[:, own])).astype(BF16)
    grad_second = lax.dot_general(wide[...], h1[:, own], contract, preferred_element_type=F32)

    stack_thin(feats, thin, 7, 4)
    grad_first = lax.dot_general(g1, thin[...], contract, preferred_element_type=F32)

    spread, keep = selectors()
    ordered = jnp.concatenate([grad_last[8 * SWAP[k]:8 * SWAP[k] + 8] for k in range(TAPS)], axis=0)
    broad = jnp.dot(spread, ordered.astype(BF16), preferred_element_type=F32)
    broad = jnp.where(keep, broad, 0.0).astype(BF16)
    place = (
        lax.broadcasted_iota(jnp.int32, (H, LANES), 1) == 104 + lax.broadcasted_iota(jnp.int32, (H, LANES), 0) % 4
    ).astype(F32).astype(BF16)
    packed[...] = jnp.dot(broad, place, preferred_element_type=F32)
    for k in range(TAPS):
        rows = slice(H * k, H * k + H)
        back = slice(H * SWAP[k], H * SWAP[k] + H)
        packed[rows, 0:48] = grad_second[back]
        packed[rows, 48:96] = grad_third[back]
        packed[rows, 96:104] = grad_first[:, 8 * k:8 * k + 8]
    if split:
        for d in range(16):
            grads_ref[d % 4 * 4 + d // 4] = packed[27 * d:27 * d + 27, :].astype(BF16)
    else:
        grads_ref[...] = packed[...].astype(BF16)


def update_kernel(links_ref, w1_ref, w2_ref, coeff_ref, out_ref, factors):
    for mu in range(4):
        for t in range(4):
            for c in range(2):
                factors[mu, c, t:t + 1, :] = coeff_ref[t, mu:mu + 1, c * 128:c * 128 + 128]
                factors[mu, c, 4 + t:5 + t, :] = coeff_ref[t, mu:mu + 1, 256 + c * 128:384 + c * 128]

    def body(mu, carry):
        factor = [factors[mu, c] for c in range(2)]
        half = [0.5 * value * value for value in factor]
        for e, (part, i, j) in enumerate(ENTRIES):
            pair = pack_pair(links_ref[mu, part, i, j, 0])
            new = [pair[c] + factor[c] * w1_ref[mu, e, c] + half[c] * w2_ref[mu, e, c] for c in range(2)]
            out_ref[mu, part, i, j, 0] = jnp.concatenate(
                [new[0][0:4], new[1][0:4], new[0][4:8], new[1][4:8]], axis=1
            )
        return carry

    lax.fori_loop(0, 4, body, 0)


def half_kernel(inner, parts_ref, out_ref):
    outer = out_ref.shape[0]
    for z in range(outer):
        value = parts_ref[z].astype(F32)
        for c in range(1, inner):
            value = value + parts_ref[c * outer + z].astype(F32)
        out_ref[z] = value.astype(BF16)


def sum_kernel(widths, parts_ref, first_ref, second_ref, third_ref, last_ref):
    value = parts_ref[0].astype(F32)
    for d in range(1, parts_ref.shape[0]):
        value = value + parts_ref[d].astype(F32)
    offset = 0
    for ref, width in zip((second_ref, third_ref, first_ref, last_ref), widths):
        for r in range(27):
            ref[:, width * r:width * r + width] = value[r:r + 1, offset:offset + width]
        offset += width


def call(body, outs, scratch, smem=(), count=0):
    specs = {}
    if smem:
        specs["in_specs"] = [
            pl.BlockSpec(memory_space=pltpu.SMEM if i in smem else pltpu.VMEM) for i in range(count)
        ]
    return pl.pallas_call(
        body,
        out_shape=[jax.ShapeDtypeStruct(shape, dtype) for shape, dtype in outs],
        scratch_shapes=[pltpu.VMEM(shape, dtype) for shape, dtype in scratch],
        compiler_params=pltpu.CompilerParams(vmem_limit_bytes=LIMIT),
        **specs,
    )


def on_device(links, cotangent, parity, link_subset, w_first, w_second, w_third, w_last):
    count = lax.axis_size("tm")

    def send(value, distance):
        return lax.ppermute(value, "tm", [(i, (i + distance) % count) for i in range(count)])

    widths = (768 // count, 768 // count, 128 // count, 64 // count)
    up, down = call(
        face_kernel,
        [((54, SITES), BF16), ((54, SITES), BF16)],
        [((4, 18, 2, 8, LANES), F32), ((3, 18, 2, 8, LANES), F32), ((54, 4, LANES), F32)],
    )(links)
    up = send(up, 1)
    down = send(down, -1)
    (block,) = call(
        functools.partial(block_kernel, widths),
        [((BLOCKROWS, LANES), BF16)],
        [((18, 2, 8, LANES), F32), ((BLOCKROWS, LANES), F32)],
    )(links, w_first[None], w_second[None], w_third[None], w_last[None])
    gathered = lax.all_to_all(
        jnp.broadcast_to(block[None], (count,) + block.shape), "tm", split_axis=0, concat_axis=0, tiled=True
    )
    fm, fup, fdown, applied, twice = call(
        gauge_kernel,
        [
            ((4, 16, SITES), BF16), ((3, 8, SITES), BF16), ((3, 8, SITES), BF16),
            ((4, 18, 2, 8, LANES), F32), ((4, 18, 2, 8, LANES), F32),
        ],
        [
            ((4, 18, 2, 8, LANES), F32), ((4, 18, 2, 8, LANES), F32), ((4, 4, 18, 2, 8, LANES), F32),
            ((4, 4, 18, 2, 8, LANES), F32), ((4, 18, 2, 8, LANES), F32), ((54, 4, LANES), F32), ((54, 4, LANES), F32),
            ((4, 9, 2, 8, LANES), F32), ((4, 4, 16, LANES), F32),
        ],
        smem=(4, 5), count=6,
    )(links, cotangent, up, down, parity, link_subset)
    below = send(fm, 1)
    above = send(fm, -1)
    fbelow = send(fup, 2)
    fabove = send(fdown, -2)

    panel_outs = [
        ((2, 4, LANES), F32), ((H, 72), BF16), ((H, 432), BF16), ((H, 432), BF16), ((72, H), BF16),
        ((H, 432), BF16), ((H, 432), BF16), ((H, 72), BF16),
    ]
    panel_scratch = [((432, LANES), F32)]
    if count == 16:
        loops, p1, p2, p3, p4, b2, b3, b4 = call(panel_kernel_plain, panel_outs, panel_scratch)(gathered)
    else:
        pieces = []
        offset = 0
        for width, full in zip(widths, (48, 48, 8, 4)):
            piece = gathered[:, SLABROWS:SLABROWS + 27, offset:offset + width]
            pieces.append(piece.reshape(432, full))
            offset += width
        pieces.append(jnp.zeros((432, 20), BF16))
        loops, p1, p2, p3, p4, b2, b3, b4 = call(panel_kernel, panel_outs, panel_scratch)(
            gathered, jnp.concatenate(pieces, axis=1)
        )

    window = 18 * SITES
    coeff, grads = call(
        functools.partial(conv_kernel, count == 16),
        [((4, 8, SITES), F32), ((16, 27, LANES) if count == 16 else (432, LANES), BF16)],
        [
            ((8, window), F32), ((8, window), F32), ((H, window), BF16), ((H, window), BF16), ((H, window), BF16),
            ((3, 8, window), F32), ((8, window), F32), ((H, window), BF16), ((H, window), BF16),
            ((432, 4 * SITES), BF16), ((72, 4 * SITES), BF16), ((432, LANES), F32),
        ],
    )(fm, below, above, fbelow, fabove, loops, p1, p2, p3, p4, b2, b3, b4)
    if count != 16:
        offset = 0
        pieces = []
        for width, full in zip(widths, (48, 48, 8, 4)):
            pieces.append(grads[:, offset:offset + full].reshape(count, 27, width))
            offset += full
        grads = jnp.concatenate(pieces, axis=2)
        grads = grads.reshape(count // 4, 4, 27, grads.shape[2]).swapaxes(0, 1)
        grads = grads.reshape(count, 27, grads.shape[3])
    inner = 4
    outer = count // inner
    near = [[inner * z + c for c in range(inner)] for z in range(outer)]
    far = [[inner * z + c for z in range(outer)] for c in range(inner)]
    grads = lax.all_to_all(
        grads, "tm", split_axis=0, concat_axis=0, axis_index_groups=near, tiled=True
    )
    (grads,) = call(
        functools.partial(half_kernel, inner), [((outer,) + grads.shape[1:], BF16)], []
    )(grads)
    grads = lax.all_to_all(
        grads, "tm", split_axis=0, concat_axis=0, axis_index_groups=far, tiled=True
    )
    (new_links,) = call(
        update_kernel, [(links.shape, F32)], [((4, 2, 8, LANES), F32)]
    )(links, applied, twice, coeff)
    grad_first, grad_second, grad_third, grad_last = call(
        functools.partial(sum_kernel, widths),
        [((1, 27 * width), F32) for width in (widths[2], widths[0], widths[1], widths[3])],
        [],
    )(grads)
    return (new_links, grad_first, grad_second, grad_third, grad_last)


def solution(mesh):
    placed = (
        P(None, None, None, None, "groups", "tm", None),
        P(None, None, None, None, "groups", "tm", None),
        P("groups", "tm"),
        P("groups", "tm"),
        P("tm"),
        P("tm"),
        P("tm"),
        P("tm"),
    )
    return jax.shard_map(
        on_device,
        mesh=mesh,
        in_specs=placed,
        out_specs=(
            P(None, None, None, None, "groups", "tm", None),
            P("groups", "tm"),
            P("groups", "tm"),
            P("groups", "tm"),
            P("groups", "tm"),
        ),
        check_vma=False,
    )
```

```python
import functools

import jax
import jax.numpy as jnp
from jax import lax
from jax.experimental import pallas as pl
from jax.experimental.pallas import tpu as pltpu
from jax.sharding import PartitionSpec as P

F32 = jnp.float32
BF16 = jnp.bfloat16
TAPS = 9
H = 48
LANES = 128
SITES = 512
PAIRS = ((0, 1), (0, 2), (0, 3), (1, 2), (1, 3), (2, 3))
SWAP = (0, 2, 1, 4, 3, 6, 5, 8, 7)
ENTRIES = tuple((c, i, j) for c in range(2) for i in range(3) for j in range(3))
SLABROWS = 48
BLOCKROWS = 80
LIMIT = 40 * 1024 * 1024


def lane_iota(rows):
    return lax.broadcasted_iota(jnp.int32, (rows, LANES), 1)


def row_iota():
    return lax.broadcasted_iota(jnp.int32, (8, LANES), 0)


def roll_lanes(value, amount):
    return pltpu.roll(value, amount % LANES, 1)


def shift_z(chunk, sign, lanes):
    z = lanes % 8
    if sign > 0:
        return jnp.where(z == 7, roll_lanes(chunk, 7), roll_lanes(chunk, -1))
    return jnp.where(z == 0, roll_lanes(chunk, -7), roll_lanes(chunk, 1))


def shift_y(chunk, sign, lanes):
    y = lanes // 8 % 8
    if sign > 0:
        return jnp.where(y == 7, roll_lanes(chunk, 56), roll_lanes(chunk, -8))
    return jnp.where(y == 0, roll_lanes(chunk, -56), roll_lanes(chunk, 8))


def dense_shift(pair, axis, sign):
    lanes = lane_iota(8)
    if axis == 2:
        return [shift_z(chunk, sign, lanes) for chunk in pair]
    if axis == 1:
        return [shift_y(chunk, sign, lanes) for chunk in pair]
    low = lanes < 64
    first, second = [roll_lanes(chunk, 64) for chunk in pair]
    if sign > 0:
        return [jnp.where(low, first, second), jnp.where(low, second, pltpu.roll(first, 4, 0))]
    return [jnp.where(low, pltpu.roll(second, 4, 0), first), jnp.where(low, first, second)]


def pack_pair(value):
    return [
        jnp.concatenate([value[:, c * 128:c * 128 + 128], value[:, 256 + c * 128:384 + c * 128]], axis=0)
        for c in range(2)
    ]


def halo_pair(ref, index):
    top = row_iota() < 4
    pair = []
    for c in range(2):
        low = jnp.broadcast_to(ref[index, c:c + 1, :], (8, LANES))
        high = jnp.broadcast_to(ref[index, 2 + c:3 + c, :], (8, LANES))
        pair.append(jnp.where(top, low, high))
    return pair


def load_matrix(read):
    real = [[read(3 * i + j) for j in range(3)] for i in range(3)]
    imag = [[read(9 + 3 * i + j) for j in range(3)] for i in range(3)]
    return (real, imag, 1)


def dagger(matrix):
    real, imag, sign = matrix
    return (
        [[real[j][i] for j in range(3)] for i in range(3)],
        [[imag[j][i] for j in range(3)] for i in range(3)],
        -sign,
    )


def total(terms, signs):
    value = None
    for term, sign in zip(terms, signs):
        if value is None:
            value = term if sign > 0 else -term
        else:
            value = value + term if sign > 0 else value - term
    return value


def mat_mul(left, right):
    lr, li, ls = left
    rr, ri, rs = right
    same = ls == rs
    real = [[None] * 3 for _ in range(3)]
    imag = [[None] * 3 for _ in range(3)]
    for i in range(3):
        for j in range(3):
            real[i][j] = total(
                [lr[i][k] * rr[k][j] for k in range(3)] + [li[i][k] * ri[k][j] for k in range(3)],
                [1, 1, 1] + [-1 if same else 1] * 3,
            )
            imag[i][j] = total(
                [lr[i][k] * ri[k][j] for k in range(3)] + [li[i][k] * rr[k][j] for k in range(3)],
                [1, 1, 1] + [1 if same else -1] * 3,
            )
    return (real, imag, ls if same else rs)


def imag_of(matrix, i, j):
    return matrix[1][i][j] if matrix[2] > 0 else -matrix[1][i][j]


def store_matrix(matrix, write):
    for i in range(3):
        for j in range(3):
            write(3 * i + j, matrix[0][i][j])
            write(9 + 3 * i + j, imag_of(matrix, i, j))


def anti_parts(matrix):
    parts = [2.0 * imag_of(matrix, i, i) for i in range(3)]
    for i, j in ((0, 1), (0, 2), (1, 2)):
        parts.append(matrix[0][i][j] - matrix[0][j][i])
        parts.append(imag_of(matrix, i, j) + imag_of(matrix, j, i))
    return parts


def anti_matrix(parts):
    zero = jnp.zeros_like(parts[0])
    real = [[zero, parts[3], parts[5]], [-parts[3], zero, parts[7]], [-parts[5], -parts[7], zero]]
    imag = [[parts[0], parts[4], parts[6]], [parts[4], parts[1], parts[8]], [parts[6], parts[8], parts[2]]]
    return real, imag


def anti_mul(parts, right):
    real, imag = anti_matrix(parts)
    rr, ri, _ = right
    out_r = [[None] * 3 for _ in range(3)]
    out_i = [[None] * 3 for _ in range(3)]
    for i in range(3):
        for j in range(3):
            value_r = -(imag[i][i] * ri[i][j])
            value_i = imag[i][i] * rr[i][j]
            for k in range(3):
                if k != i:
                    value_r = value_r + real[i][k] * rr[k][j] - imag[i][k] * ri[k][j]
                    value_i = value_i + real[i][k] * ri[k][j] + imag[i][k] * rr[k][j]
            out_r[i][j] = value_r
            out_i[i][j] = value_i
    return (out_r, out_i, 1)


def pack_links(links_ref, dense):
    def body(mu, carry):
        for e, (c, i, j) in enumerate(ENTRIES):
            low, high = pack_pair(links_ref[mu, c, i, j, 0].astype(F32))
            dense[mu, e, 0] = low
            dense[mu, e, 1] = high
        return carry

    lax.fori_loop(0, 4, body, 0)


def face_kernel(links_ref, up_ref, down_ref, dense, moved, rows):
    pack_links(links_ref, dense)

    def shift_body(e, carry):
        pair = [dense[3, e, 0], dense[3, e, 1]]
        for mu in range(3):
            low, high = dense_shift(pair, mu, 1)
            moved[mu, e, 0] = low
            moved[mu, e, 1] = high
        return carry

    lax.fori_loop(0, 18, shift_body, 0)

    def staple_body(step, carry):
        mu = step // 2
        c = step % 2
        u_mu = load_matrix(lambda e: dense[mu, e, c])
        u_t = load_matrix(lambda e: dense[3, e, c])
        edge = mat_mul(u_mu, load_matrix(lambda e: moved[mu, e, c]))
        staple = mat_mul(dagger(edge), u_t)

        def write(e, value):
            rows[mu * 18 + e, pl.ds(c, 1)] = value[3:4]
            rows[mu * 18 + e, pl.ds(2 + c, 1)] = value[7:8]

        store_matrix(staple, write)
        return carry

    lax.fori_loop(0, 6, staple_body, 0)
    for q in range(4):
        up_ref[:, q * 128:q * 128 + 128] = rows[:, q, :].astype(BF16)

    def down_body(e, carry):
        for mu in range(3):
            for c in range(2):
                value = dense[mu, e, c]
                rows[mu * 18 + e, c:c + 1] = value[0:1]
                rows[mu * 18 + e, 2 + c:3 + c] = value[4:5]
        return carry

    lax.fori_loop(0, 18, down_body, 0)
    for q in range(4):
        down_ref[:, q * 128:q * 128 + 128] = rows[:, q, :].astype(BF16)


def block_kernel(widths, dense, w1_ref, w2_ref, w3_ref, w4_ref, block_ref, block):
    block[...] = jnp.zeros_like(block)

    def slab_body(c, carry):
        u_t = load_matrix(lambda e: dense[3, e, c])
        ahead = load_matrix(lambda e: pltpu.roll(dense[3, e, c], 7, 0))
        two = mat_mul(u_t, ahead)
        later = tuple(
            [[pltpu.roll(part[i][j], 6, 0) for j in range(3)] for i in range(3)] for part in two[:2]
        ) + (two[2],)
        four = mat_mul(two, later)

        def write(e, value):
            if e % 9 < 6:
                row = 4 * (e // 9 * 6 + e % 9)
                block[pl.ds(row + c, 1), :] = value[0:1]
                block[pl.ds(row + 2 + c, 1), :] = value[4:5]

        store_matrix(four, write)
        return carry

    lax.fori_loop(0, 2, slab_body, 0)
    offset = 0
    for ref, width in zip((w2_ref, w3_ref, w1_ref, w4_ref), widths):
        flat = ref[...].astype(F32)
        for r in range(27):
            block[SLABROWS + r:SLABROWS + r + 1, offset:offset + width] = flat[:, width * r:width * r + width]
        offset += width
    block_ref[...] = block[...].astype(BF16)


def gauge_kernel(
    dense, cot_ref, up_ref, down_ref, parity_ref, subset_ref,
    fm_ref, fup_ref, fdown_ref, w1_ref, w2_ref,
    cots, moved, staples, sums, halo_up, halo_down, forces, rows,
):
    pack_links(cot_ref, cots)
    for q in range(4):
        halo_up[:, q, :] = up_ref[:, q * 128:q * 128 + 128].astype(F32)
        halo_down[:, q, :] = down_ref[:, q * 128:q * 128 + 128].astype(F32)
    rows[...] = jnp.zeros_like(rows)
    forces[...] = jnp.zeros_like(forces)
    steps = row_iota() % 4
    lanes = lane_iota(8)

    def shift_body(e, carry):
        for nu in range(4):
            pair = [dense[nu, e, 0], dense[nu, e, 1]]
            for mu in range(3):
                if mu != nu:
                    low, high = dense_shift(pair, mu, 1)
                    moved[mu, nu, e, 0] = low
                    moved[mu, nu, e, 1] = high
            if nu < 3:
                halo = halo_pair(halo_down, nu * 18 + e)
                for c in range(2):
                    moved[3, nu, e, c] = jnp.where(steps == 3, halo[c], pltpu.roll(pair[c], 7, 0))
        return carry

    lax.fori_loop(0, 18, shift_body, 0)

    def put_row(channel, c, value):
        for t in range(4):
            rows[t, c, pl.ds(channel, 1), :] = value[t:t + 1]
            rows[t, 2 + c, pl.ds(channel, 1), :] = value[4 + t:5 + t]

    def plane_body(step, carry):
        plane = step // 2
        c = step % 2
        mu = jnp.where(plane < 3, 0, jnp.where(plane < 5, 1, 2))
        nu = jnp.where(plane < 3, plane + 1, jnp.where(plane < 5, plane - 1, 3))
        u_mu = load_matrix(lambda e: dense[mu, e, c])
        u_nu = load_matrix(lambda e: dense[nu, e, c])
        one = mat_mul(u_mu, load_matrix(lambda e: moved[mu, nu, e, c]))
        two = mat_mul(u_nu, load_matrix(lambda e: moved[nu, mu, e, c]))
        loop = mat_mul(one, dagger(two))
        put_row(plane, c, (loop[0][0][0] + loop[0][1][1] + loop[0][2][2]) / 3.0)
        for e, part in enumerate(anti_parts(loop)):
            forces[mu, e, c] += part
            forces[nu, e, c] -= part

        def write_mu(e, value):
            staples[mu, nu, e, c] = value

        def write_nu(e, value):
            staples[nu, mu, e, c] = value

        store_matrix(mat_mul(dagger(one), u_nu), write_mu)
        store_matrix(mat_mul(dagger(two), u_mu), write_nu)
        return carry

    lax.fori_loop(0, 12, plane_body, 0)

    def lower_body(e, carry):
        for mu in range(4):
            acc = [None, None]
            for nu in range(4):
                if nu == mu:
                    continue
                pair = [staples[mu, nu, e, 0], staples[mu, nu, e, 1]]
                if nu < 3:
                    pair = dense_shift(pair, nu, -1)
                else:
                    halo = halo_pair(halo_up, mu * 18 + e)
                    pair = [jnp.where(steps == 0, halo[c], pltpu.roll(pair[c], 1, 0)) for c in range(2)]
                acc = [pair[c] if acc[c] is None else acc[c] + pair[c] for c in range(2)]
            sums[mu, e, 0] = acc[0]
            sums[mu, e, 1] = acc[1]
        return carry

    lax.fori_loop(0, 18, lower_body, 0)

    colour = (lanes // 64 + lanes // 8 % 8 + lanes % 8 + steps) % 2
    parity = jnp.zeros_like(steps)
    subset = jnp.zeros_like(steps)
    for t in range(4):
        parity = jnp.where(steps == t, parity_ref[0, t], parity)
        subset = jnp.where(steps == t, subset_ref[0, t], subset)
    on_site = colour == parity

    def force_body(step, carry):
        mu = step // 2
        c = step % 2
        current = load_matrix(lambda e: dense[mu, e, c])
        omega = mat_mul(current, load_matrix(lambda e: sums[mu, e, c]))
        parts = [part + forces[mu, e, c] for e, part in enumerate(anti_parts(omega))]
        mean = (parts[0] + parts[1] + parts[2]) * (1.0 / 3.0)
        parts = [parts[e] - mean if e < 3 else parts[e] for e in range(9)]
        parts = [part * (1.0 / 12.0) for part in parts]
        applied = anti_mul(parts, current)
        twice = anti_mul(parts, applied)
        gate = jnp.where(jnp.logical_and(on_site, jnp.right_shift(subset, mu) % 2 == 1), 1.0, 0.0)
        slope = jnp.zeros_like(gate)
        curve = jnp.zeros_like(gate)
        for e, (part, i, j) in enumerate(ENTRIES):
            weight = cots[mu, e, c]
            slope = slope + weight * applied[part][i][j]
            curve = curve + weight * twice[part][i][j]
            w1_ref[mu, e, c] = gate * applied[part][i][j]
            w2_ref[mu, e, c] = gate * twice[part][i][j]
        put_row(8 + mu, c, gate * slope)
        put_row(12 + mu, c, gate * curve)
        return carry

    lax.fori_loop(0, 8, force_body, 0)
    for t in range(4):
        for q in range(4):
            value = rows[t, q]
            fm_ref[t, :, q * 128:q * 128 + 128] = value.astype(BF16)
            if t > 0:
                fup_ref[t - 1, :, q * 128:q * 128 + 128] = value[0:8].astype(BF16)
            if t < 3:
                fdown_ref[t, :, q * 128:q * 128 + 128] = value[0:8].astype(BF16)


def selectors():
    row = lax.broadcasted_iota(jnp.int32, (432, 72), 0)
    col = lax.broadcasted_iota(jnp.int32, (432, 72), 1)
    group = row // 12
    spread = (group // 4 * 8 + group % 4 == col).astype(F32).astype(BF16)
    keep = (
        lax.broadcasted_iota(jnp.int32, (432, H), 1) // 4 == lax.broadcasted_iota(jnp.int32, (432, H), 0) % 12
    )
    return spread, keep


def panel_kernel(gathered_ref, weights_ref, loops_ref, p1_ref, p2_ref, p3_ref, p4_ref, b2_ref, b3_ref, b4_ref, weights):
    count = gathered_ref.shape[0]

    def read(d):
        slab = gathered_ref[d, 0:SLABROWS, :].astype(F32)
        real = [[slab[4 * (3 * i + j):4 * (3 * i + j) + 4, :] for j in range(3)] for i in range(2)]
        imag = [[slab[24 + 4 * (3 * i + j):28 + 4 * (3 * i + j), :] for j in range(3)] for i in range(2)]
        real.append([])
        imag.append([])
        for k in range(3):
            i, j = (k + 1) % 3, (k + 2) % 3
            real[2].append(
                (real[0][i] * real[1][j] - imag[0][i] * imag[1][j])
                - (real[0][j] * real[1][i] - imag[0][j] * imag[1][i])
            )
            imag[2].append(
                (real[0][j] * imag[1][i] + imag[0][j] * real[1][i])
                - (real[0][i] * imag[1][j] + imag[0][i] * real[1][j])
            )
        return (real, imag, 1)

    def flat(matrix):
        return tuple(matrix[0][i][j] for i in range(3) for j in range(3)) + tuple(
            imag_of(matrix, i, j) for i in range(3) for j in range(3)
        )

    def chain(d, state):
        return flat(mat_mul(load_matrix(lambda e: state[e]), read(d)))

    state = lax.fori_loop(1, count, chain, flat(read(0)))
    loops_ref[0] = (state[0] + state[4] + state[8]) / 3.0
    loops_ref[1] = (state[9] + state[13] + state[17]) / 3.0

    if weights_ref is None:
        for d in range(count):
            block = gathered_ref[d, SLABROWS:BLOCKROWS, :].astype(F32)
            weights[27 * d:27 * d + 27, :] = block[0:27]
    else:
        weights[...] = weights_ref[...].astype(F32)
    for k in range(TAPS):
        rows = slice(H * k, H * k + H)
        back = slice(H * SWAP[k], H * SWAP[k] + H)
        p2_ref[:, rows] = weights[rows, 0:48].astype(BF16)
        p3_ref[:, rows] = weights[rows, 48:96].astype(BF16)
        p1_ref[:, 8 * k:8 * k + 8] = weights[rows, 96:104].astype(BF16)
        turned = weights[back, :].T
        b2_ref[:, rows] = turned[0:48].astype(BF16)
        b3_ref[:, rows] = turned[48:96].astype(BF16)
    spread, keep = selectors()
    place = (
        lax.broadcasted_iota(jnp.int32, (LANES, H), 0) == 104 + lax.broadcasted_iota(jnp.int32, (LANES, H), 1) % 4
    ).astype(F32).astype(BF16)
    wide = jnp.dot(weights[...].astype(BF16), place, preferred_element_type=F32)
    wide = jnp.where(keep, wide, 0.0).astype(BF16)
    last = lax.dot_general(spread, wide, (((0,), (0,)), ((), ())), preferred_element_type=F32)
    p4_ref[...] = last.astype(BF16)
    for k in range(TAPS):
        b4_ref[:, 8 * k:8 * k + 8] = last[8 * SWAP[k]:8 * SWAP[k] + 8, :].T.astype(BF16)


def panel_kernel_plain(gathered_ref, *rest):
    panel_kernel(gathered_ref, None, *rest)


def chunks_of(value):
    return [value[:, q * 128:q * 128 + 128] for q in range(4)]


def one_shift(chunks, position):
    if position == 0:
        return chunks
    lanes = lane_iota(chunks[0].shape[0])
    sign = 1 if position % 2 == 1 else -1
    if position > 4:
        return [shift_z(chunk, sign, lanes) for chunk in chunks]
    if position > 2:
        return [shift_y(chunk, sign, lanes) for chunk in chunks]
    low = lanes < 64
    rolled = [roll_lanes(chunk, 64) for chunk in chunks]
    if sign > 0:
        return [jnp.where(low, rolled[q], rolled[(q + 1) % 4]) for q in range(4)]
    return [jnp.where(low, rolled[(q + 3) % 4], rolled[q]) for q in range(4)]


def span(slice_index, count=1):
    if isinstance(slice_index, int):
        return slice(slice_index * SITES, (slice_index + count) * SITES)
    return pl.ds(pl.multiple_of(slice_index * SITES, SITES), count * SITES)


def stack_wide(source, target, first, count):
    for s in range(count):
        chunks = chunks_of(source[:, span(first + s)])
        for position in range(7):
            shifted = one_shift(chunks, position)
            for q in range(4):
                lanes = slice(s * SITES + q * 128, s * SITES + q * 128 + 128)
                target[H * position:H * position + H, lanes] = shifted[q]
    width = slice(0, count * SITES)
    target[7 * H:8 * H, width] = source[:, span(first + 1, count)]
    target[8 * H:9 * H, width] = source[:, span(first - 1, count)]


def stack_thin(source, target, first, count):
    for s in range(count):
        chunks = chunks_of(source[:, span(first + s)])
        ahead = chunks_of(source[:, span(first + s + 1)])
        behind = chunks_of(source[:, span(first + s - 1)])
        columns = [one_shift(chunks, position) for position in range(7)] + [ahead, behind]
        for q in range(4):
            lanes = slice(s * SITES + q * 128, s * SITES + q * 128 + 128)
            target[0:72, lanes] = jnp.concatenate([column[q] for column in columns], axis=0).astype(BF16)


def one_minus_square(value):
    value = value.astype(F32)
    return 1.0 - value * value


def conv_kernel(
    split, fm_ref, below_ref, above_ref, fbelow_ref, fabove_ref, loops_ref,
    p1_ref, p2_ref, p3_ref, p4_ref, b2_ref, b3_ref, b4_ref,
    coeff_ref, grads_ref,
    feats, mixed, h1, h2, h3, parts, lasts, g3, g2, wide, thin, packed,
):
    row8 = lax.broadcasted_iota(jnp.int32, (8, SITES), 0)
    loop_re = jnp.concatenate([loops_ref[0, q:q + 1, :] for q in range(4)], axis=1)
    loop_im = jnp.concatenate([loops_ref[1, q:q + 1, :] for q in range(4)], axis=1)
    loops = jnp.where(row8 == 6, loop_re, jnp.where(row8 == 7, loop_im, 0.0))
    loops = loops.astype(BF16).astype(F32)
    for j in range(3):
        feats[:, span(j)] = fbelow_ref[j].astype(F32) + loops
        feats[:, span(15 + j)] = fabove_ref[j].astype(F32) + loops
    for base, ref in ((3, below_ref), (7, fm_ref), (11, above_ref)):
        for j in range(4):
            value = ref[j].astype(F32)
            feats[:, span(base + j)] = value[0:8] + loops
            mixed[:, span(base + j)] = value[8:16]

    def layer_one(step, carry):
        first = 1 + 4 * step
        stack_thin(feats, thin, first, 4)
        out = jnp.dot(p1_ref[...], thin[...], preferred_element_type=F32)
        h1[:, span(first, 4)] = jnp.tanh(out).astype(BF16)
        return carry

    lax.fori_loop(0, 4, layer_one, 0)

    def layer_two(step, carry):
        first = 2 + 2 * step
        stack_wide(h1, wide, first, 2)
        out = jnp.dot(p2_ref[...], wide[:, 0:1024], preferred_element_type=F32)
        h2[:, span(first, 2)] = jnp.tanh(out).astype(BF16)
        return carry

    lax.fori_loop(0, 7, layer_two, 0)

    def layer_three(step, carry):
        first = 3 + 2 * step
        stack_wide(h2, wide, first, 2)
        out = jnp.dot(p3_ref[...], wide[:, 0:1024], preferred_element_type=F32)
        out = jnp.tanh(out).astype(BF16)
        h3[:, span(first, 2)] = out
        taps = jnp.dot(p4_ref[...], out, preferred_element_type=F32)
        for s in range(2):
            acc = None
            for position in range(7):
                shifted = one_shift(
                    chunks_of(taps[8 * position:8 * position + 8, s * SITES:(s + 1) * SITES]), position
                )
                acc = shifted if acc is None else [a + b for a, b in zip(acc, shifted)]
            parts[0, :, span(first + s)] = jnp.concatenate(acc, axis=1)
            parts[1, :, span(first + s)] = taps[56:64, s * SITES:(s + 1) * SITES]
            parts[2, :, span(first + s)] = taps[64:72, s * SITES:(s + 1) * SITES]
        return carry

    lax.fori_loop(0, 6, layer_three, 0)

    def last_layer(step, carry):
        for s in range(2):
            index = 4 + 2 * step + s
            coeff = jnp.tanh(parts[0, :, span(index)] + parts[1, :, span(index + 1)] + parts[2, :, span(index - 1)])
            blend = mixed[:, span(index)]
            value = (blend + coeff * pltpu.roll(blend, 4, 0)) * (1.0 - coeff * coeff)
            lasts[:, span(index)] = jnp.where(row8 < 4, value, 0.0).astype(BF16).astype(F32)
            parts[0, :, span(index)] = coeff
        return carry

    lax.fori_loop(0, 5, last_layer, 0)
    for t in range(4):
        coeff_ref[t] = parts[0, :, span(7 + t)]

    def back_three(first, count):
        stack_thin(lasts, thin, first, count)
        out = jnp.dot(b4_ref[...], thin[:, 0:count * SITES], preferred_element_type=F32)
        g3[:, span(first, count)] = (out * one_minus_square(h3[:, span(first, count)])).astype(BF16)

    back_three(5, 2)
    back_three(11, 2)
    back_three(7, 4)
    own = span(7, 4)
    contract = (((1,), (1,)), ((), ()))
    grad_last = lax.dot_general(thin[...], h3[:, own], contract, preferred_element_type=F32)

    stack_wide(g3, wide, 6, 1)
    out = jnp.dot(b3_ref[...], wide[:, 0:SITES], preferred_element_type=F32)
    g2[:, span(6)] = (out * one_minus_square(h2[:, span(6)])).astype(BF16)
    stack_wide(g3, wide, 11, 1)
    out = jnp.dot(b3_ref[...], wide[:, 0:SITES], preferred_element_type=F32)
    g2[:, span(11)] = (out * one_minus_square(h2[:, span(11)])).astype(BF16)
    stack_wide(g3, wide, 7, 4)
    out = jnp.dot(b3_ref[...], wide[...], preferred_element_type=F32)
    g2[:, own] = (out * one_minus_square(h2[:, own])).astype(BF16)
    grad_third = lax.dot_general(wide[...], h2[:, own], contract, preferred_element_type=F32)

    stack_wide(g2, wide, 7, 4)
    out = jnp.dot(b2_ref[...], wide[...], preferred_element_type=F32)
    g1 = (out * one_minus_square(h1[:, own])).astype(BF16)
    grad_second = lax.dot_general(wide[...], h1[:, own], contract, preferred_element_type=F32)

    stack_thin(feats, thin, 7, 4)
    grad_first = lax.dot_general(g1, thin[...], contract, preferred_element_type=F32)

    spread, keep = selectors()
    ordered = jnp.concatenate([grad_last[8 * SWAP[k]:8 * SWAP[k] + 8] for k in range(TAPS)], axis=0)
    broad = jnp.dot(spread, ordered.astype(BF16), preferred_element_type=F32)
    broad = jnp.where(keep, broad, 0.0).astype(BF16)
    place = (
        lax.broadcasted_iota(jnp.int32, (H, LANES), 1) == 104 + lax.broadcasted_iota(jnp.int32, (H, LANES), 0) % 4
    ).astype(F32).astype(BF16)
    packed[...] = jnp.dot(broad, place, preferred_element_type=F32)
    for k in range(TAPS):
        rows = slice(H * k, H * k + H)
        back = slice(H * SWAP[k], H * SWAP[k] + H)
        packed[rows, 0:48] = grad_second[back]
        packed[rows, 48:96] = grad_third[back]
        packed[rows, 96:104] = grad_first[:, 8 * k:8 * k + 8]
    if split:
        for d in range(16):
            grads_ref[d] = packed[27 * d:27 * d + 27, :].astype(BF16)
    else:
        grads_ref[...] = packed[...].astype(BF16)


def update_kernel(links_ref, w1_ref, w2_ref, coeff_ref, out_ref, factors):
    for mu in range(4):
        for t in range(4):
            for c in range(2):
                factors[mu, c, t:t + 1, :] = coeff_ref[t, mu:mu + 1, c * 128:c * 128 + 128]
                factors[mu, c, 4 + t:5 + t, :] = coeff_ref[t, mu:mu + 1, 256 + c * 128:384 + c * 128]

    def body(mu, carry):
        factor = [factors[mu, c] for c in range(2)]
        half = [0.5 * value * value for value in factor]
        for e, (part, i, j) in enumerate(ENTRIES):
            pair = pack_pair(links_ref[mu, part, i, j, 0])
            new = [pair[c] + factor[c] * w1_ref[mu, e, c] + half[c] * w2_ref[mu, e, c] for c in range(2)]
            out_ref[mu, part, i, j, 0] = jnp.concatenate(
                [new[0][0:4], new[1][0:4], new[0][4:8], new[1][4:8]], axis=1
            )
        return carry

    lax.fori_loop(0, 4, body, 0)


def sum_kernel(widths, parts_ref, first_ref, second_ref, third_ref, last_ref):
    value = parts_ref[0].astype(F32)
    for d in range(1, parts_ref.shape[0]):
        value = value + parts_ref[d].astype(F32)
    offset = 0
    for ref, width in zip((second_ref, third_ref, first_ref, last_ref), widths):
        for r in range(27):
            ref[:, width * r:width * r + width] = value[r:r + 1, offset:offset + width]
        offset += width


def call(body, outs, scratch, smem=(), count=0, cost=None):
    specs = {}
    if smem:
        specs["in_specs"] = [
            pl.BlockSpec(memory_space=pltpu.SMEM if i in smem else pltpu.VMEM) for i in range(count)
        ]
    return pl.pallas_call(
        body,
        out_shape=[jax.ShapeDtypeStruct(shape, dtype) for shape, dtype in outs],
        scratch_shapes=[pltpu.VMEM(shape, dtype) for shape, dtype in scratch],
        compiler_params=pltpu.CompilerParams(vmem_limit_bytes=LIMIT),
        cost_estimate=cost,
        **specs,
    )


def on_device(links, cotangent, parity, link_subset, w_first, w_second, w_third, w_last):
    count = lax.axis_size("tm")

    def send(value, distance):
        return lax.ppermute(value, "tm", [(i, (i + distance) % count) for i in range(count)])

    widths = (768 // count, 768 // count, 128 // count, 64 // count)
    up, down, dense = call(
        face_kernel,
        [((54, SITES), BF16), ((54, SITES), BF16), ((4, 18, 2, 8, LANES), F32)],
        [((3, 18, 2, 8, LANES), F32), ((54, 4, LANES), F32)],
    )(links)
    up = send(up, 1)
    down = send(down, -1)
    (block,) = call(
        functools.partial(block_kernel, widths),
        [((BLOCKROWS, LANES), BF16)],
        [((BLOCKROWS, LANES), F32)],
        cost=pl.CostEstimate(flops=4_000_000_000, bytes_accessed=16_000_000, transcendentals=0),
    )(dense, w_first[None], w_second[None], w_third[None], w_last[None])
    gathered = lax.all_to_all(
        jnp.broadcast_to(block[None], (count,) + block.shape), "tm", split_axis=0, concat_axis=0, tiled=True
    )
    fm, fup, fdown, applied, twice = call(
        gauge_kernel,
        [
            ((4, 16, SITES), BF16), ((3, 8, SITES), BF16), ((3, 8, SITES), BF16),
            ((4, 18, 2, 8, LANES), F32), ((4, 18, 2, 8, LANES), F32),
        ],
        [
            ((4, 18, 2, 8, LANES), F32), ((4, 4, 18, 2, 8, LANES), F32),
            ((4, 4, 18, 2, 8, LANES), F32), ((4, 18, 2, 8, LANES), F32), ((54, 4, LANES), F32), ((54, 4, LANES), F32),
            ((4, 9, 2, 8, LANES), F32), ((4, 4, 16, LANES), F32),
        ],
        smem=(4, 5), count=6,
    )(dense, cotangent, up, down, parity, link_subset)
    below = send(fm, 1)
    above = send(fm, -1)
    fbelow = send(fup, 2)
    fabove = send(fdown, -2)

    panel_outs = [
        ((2, 4, LANES), F32), ((H, 72), BF16), ((H, 432), BF16), ((H, 432), BF16), ((72, H), BF16),
        ((H, 432), BF16), ((H, 432), BF16), ((H, 72), BF16),
    ]
    panel_scratch = [((432, LANES), F32)]
    if count == 16:
        loops, p1, p2, p3, p4, b2, b3, b4 = call(panel_kernel_plain, panel_outs, panel_scratch)(gathered)
    else:
        pieces = []
        offset = 0
        for width, full in zip(widths, (48, 48, 8, 4)):
            piece = gathered[:, SLABROWS:SLABROWS + 27, offset:offset + width]
            pieces.append(piece.reshape(432, full))
            offset += width
        pieces.append(jnp.zeros((432, 20), BF16))
        loops, p1, p2, p3, p4, b2, b3, b4 = call(panel_kernel, panel_outs, panel_scratch)(
            gathered, jnp.concatenate(pieces, axis=1)
        )

    window = 18 * SITES
    coeff, grads = call(
        functools.partial(conv_kernel, count == 16),
        [((4, 8, SITES), F32), ((16, 27, LANES) if count == 16 else (432, LANES), BF16)],
        [
            ((8, window), F32), ((8, window), F32), ((H, window), BF16), ((H, window), BF16), ((H, window), BF16),
            ((3, 8, window), F32), ((8, window), F32), ((H, window), BF16), ((H, window), BF16),
            ((432, 4 * SITES), BF16), ((72, 4 * SITES), BF16), ((432, LANES), F32),
        ],
    )(fm, below, above, fbelow, fabove, loops, p1, p2, p3, p4, b2, b3, b4)
    if count != 16:
        offset = 0
        pieces = []
        for width, full in zip(widths, (48, 48, 8, 4)):
            pieces.append(grads[:, offset:offset + full].reshape(count, 27, width))
            offset += full
        grads = jnp.concatenate(pieces, axis=2)
    grads = lax.all_to_all(grads, "tm", split_axis=0, concat_axis=0, tiled=True)
    (new_links,) = call(
        update_kernel, [(links.shape, F32)], [((4, 2, 8, LANES), F32)]
    )(links, applied, twice, coeff)
    grad_first, grad_second, grad_third, grad_last = call(
        functools.partial(sum_kernel, widths),
        [((1, 27 * width), F32) for width in (widths[2], widths[0], widths[1], widths[3])],
        [],
    )(grads)
    return (new_links, grad_first, grad_second, grad_third, grad_last)


def solution(mesh):
    placed = (
        P(None, None, None, None, "groups", "tm", None),
        P(None, None, None, None, "groups", "tm", None),
        P("groups", "tm"),
        P("groups", "tm"),
        P("tm"),
        P("tm"),
        P("tm"),
        P("tm"),
    )
    return jax.shard_map(
        on_device,
        mesh=mesh,
        in_specs=placed,
        out_specs=(
            P(None, None, None, None, "groups", "tm", None),
            P("groups", "tm"),
            P("groups", "tm"),
            P("groups", "tm"),
            P("groups", "tm"),
        ),
        check_vma=False,
    )
```

```python
import functools

import jax
import jax.numpy as jnp
from jax import lax
from jax.experimental import pallas as pl
from jax.experimental.pallas import tpu as pltpu
from jax.sharding import PartitionSpec as P

F32 = jnp.float32
BF16 = jnp.bfloat16
TAPS = 9
H = 48
LANES = 128
SITES = 512
PAIRS = ((0, 1), (0, 2), (0, 3), (1, 2), (1, 3), (2, 3))
SWAP = (0, 2, 1, 4, 3, 6, 5, 8, 7)
ENTRIES = tuple((c, i, j) for c in range(2) for i in range(3) for j in range(3))
SLABROWS = 24
BLOCKROWS = 64
LIMIT = 40 * 1024 * 1024


def lane_iota(rows):
    return lax.broadcasted_iota(jnp.int32, (rows, LANES), 1)


def row_iota():
    return lax.broadcasted_iota(jnp.int32, (8, LANES), 0)


def roll_lanes(value, amount):
    return pltpu.roll(value, amount % LANES, 1)


def shift_z(chunk, sign, lanes):
    z = lanes % 8
    if sign > 0:
        return jnp.where(z == 7, roll_lanes(chunk, 7), roll_lanes(chunk, -1))
    return jnp.where(z == 0, roll_lanes(chunk, -7), roll_lanes(chunk, 1))


def shift_y(chunk, sign, lanes):
    y = lanes // 8 % 8
    if sign > 0:
        return jnp.where(y == 7, roll_lanes(chunk, 56), roll_lanes(chunk, -8))
    return jnp.where(y == 0, roll_lanes(chunk, -56), roll_lanes(chunk, 8))


def dense_shift(pair, axis, sign):
    lanes = lane_iota(8)
    if axis == 2:
        return [shift_z(chunk, sign, lanes) for chunk in pair]
    if axis == 1:
        return [shift_y(chunk, sign, lanes) for chunk in pair]
    low = lanes < 64
    first, second = [roll_lanes(chunk, 64) for chunk in pair]
    if sign > 0:
        return [jnp.where(low, first, second), jnp.where(low, second, pltpu.roll(first, 4, 0))]
    return [jnp.where(low, pltpu.roll(second, 4, 0), first), jnp.where(low, first, second)]


def pack_pair(value):
    return [
        jnp.concatenate([value[:, c * 128:c * 128 + 128], value[:, 256 + c * 128:384 + c * 128]], axis=0)
        for c in range(2)
    ]


def halo_pair(ref, index):
    top = row_iota() < 4
    pair = []
    for c in range(2):
        low = jnp.broadcast_to(ref[index, c:c + 1, :], (8, LANES))
        high = jnp.broadcast_to(ref[index, 2 + c:3 + c, :], (8, LANES))
        pair.append(jnp.where(top, low, high))
    return pair


def load_matrix(read):
    real = [[read(3 * i + j) for j in range(3)] for i in range(3)]
    imag = [[read(9 + 3 * i + j) for j in range(3)] for i in range(3)]
    return (real, imag, 1)


def dagger(matrix):
    real, imag, sign = matrix
    return (
        [[real[j][i] for j in range(3)] for i in range(3)],
        [[imag[j][i] for j in range(3)] for i in range(3)],
        -sign,
    )


def total(terms, signs):
    value = None
    for term, sign in zip(terms, signs):
        if value is None:
            value = term if sign > 0 else -term
        else:
            value = value + term if sign > 0 else value - term
    return value


def mat_mul(left, right):
    lr, li, ls = left
    rr, ri, rs = right
    same = ls == rs
    height = len(lr)
    real = [[None] * 3 for _ in range(height)]
    imag = [[None] * 3 for _ in range(height)]
    for i in range(height):
        for j in range(3):
            real[i][j] = total(
                [lr[i][k] * rr[k][j] for k in range(3)] + [li[i][k] * ri[k][j] for k in range(3)],
                [1, 1, 1] + [-1 if same else 1] * 3,
            )
            imag[i][j] = total(
                [lr[i][k] * ri[k][j] for k in range(3)] + [li[i][k] * rr[k][j] for k in range(3)],
                [1, 1, 1] + [1 if same else -1] * 3,
            )
    return (real, imag, ls if same else rs)


def imag_of(matrix, i, j):
    return matrix[1][i][j] if matrix[2] > 0 else -matrix[1][i][j]


def store_matrix(matrix, write):
    for i in range(3):
        for j in range(3):
            write(3 * i + j, matrix[0][i][j])
            write(9 + 3 * i + j, imag_of(matrix, i, j))


def two_rows(read):
    real = [[read(3 * i + j) for j in range(3)] for i in range(2)]
    imag = [[read(6 + 3 * i + j) for j in range(3)] for i in range(2)]
    return (real, imag, 1)


def store_rows(matrix, write):
    for i in range(2):
        for j in range(3):
            write(3 * i + j, matrix[0][i][j])
            write(6 + 3 * i + j, imag_of(matrix, i, j))


def special(matrix):
    real, imag, _ = matrix
    last_r, last_i = [], []
    for k in range(3):
        i, j = (k + 1) % 3, (k + 2) % 3
        last_r.append(
            (real[0][i] * real[1][j] - imag[0][i] * imag[1][j])
            - (real[0][j] * real[1][i] - imag[0][j] * imag[1][i])
        )
        last_i.append(
            (real[0][j] * imag[1][i] + imag[0][j] * real[1][i])
            - (real[0][i] * imag[1][j] + imag[0][i] * real[1][j])
        )
    return (real + [last_r], imag + [last_i], 1)


def anti_parts(matrix):
    parts = [2.0 * imag_of(matrix, i, i) for i in range(3)]
    for i, j in ((0, 1), (0, 2), (1, 2)):
        parts.append(matrix[0][i][j] - matrix[0][j][i])
        parts.append(imag_of(matrix, i, j) + imag_of(matrix, j, i))
    return parts


def anti_matrix(parts):
    zero = jnp.zeros_like(parts[0])
    real = [[zero, parts[3], parts[5]], [-parts[3], zero, parts[7]], [-parts[5], -parts[7], zero]]
    imag = [[parts[0], parts[4], parts[6]], [parts[4], parts[1], parts[8]], [parts[6], parts[8], parts[2]]]
    return real, imag


def anti_mul(parts, right):
    real, imag = anti_matrix(parts)
    rr, ri, _ = right
    out_r = [[None] * 3 for _ in range(3)]
    out_i = [[None] * 3 for _ in range(3)]
    for i in range(3):
        for j in range(3):
            value_r = -(imag[i][i] * ri[i][j])
            value_i = imag[i][i] * rr[i][j]
            for k in range(3):
                if k != i:
                    value_r = value_r + real[i][k] * rr[k][j] - imag[i][k] * ri[k][j]
                    value_i = value_i + real[i][k] * ri[k][j] + imag[i][k] * rr[k][j]
            out_r[i][j] = value_r
            out_i[i][j] = value_i
    return (out_r, out_i, 1)


def pack_links(links_ref, dense):
    def body(mu, carry):
        for e, (c, i, j) in enumerate(ENTRIES):
            low, high = pack_pair(links_ref[mu, c, i, j, 0].astype(F32))
            dense[mu, e, 0] = low
            dense[mu, e, 1] = high
        return carry

    lax.fori_loop(0, 4, body, 0)


def face_kernel(links_ref, up_ref, down_ref, dense, edges, staples, slab, moved, rows):
    pack_links(links_ref, dense)

    def shift_body(e, carry):
        pair = [dense[3, e, 0], dense[3, e, 1]]
        for mu in range(3):
            low, high = dense_shift(pair, mu, 1)
            moved[mu, e, 0] = low
            moved[mu, e, 1] = high
        return carry

    lax.fori_loop(0, 18, shift_body, 0)

    def staple_body(step, carry):
        mu = step // 2
        c = step % 2
        u_mu = load_matrix(lambda e: dense[mu, e, c])
        u_t = load_matrix(lambda e: dense[3, e, c])
        edge = mat_mul(u_mu, load_matrix(lambda e: moved[mu, e, c]))

        def write_edge(e, value):
            edges[mu, e, c] = value

        store_matrix(edge, write_edge)

        def write(e, value):
            staples[mu, e, c] = value
            rows[mu * 18 + e, pl.ds(c, 1)] = value[3:4]
            rows[mu * 18 + e, pl.ds(2 + c, 1)] = value[7:8]

        store_matrix(mat_mul(dagger(edge), u_t), write)
        return carry

    lax.fori_loop(0, 6, staple_body, 0)

    def slab_body(c, carry):
        u_t = load_matrix(lambda e: dense[3, e, c])
        ahead = load_matrix(lambda e: pltpu.roll(dense[3, e, c], 7, 0))
        two = mat_mul(u_t, ahead)
        later = tuple(
            [[pltpu.roll(part[i][j], 6, 0) for j in range(3)] for i in range(3)] for part in two[:2]
        ) + (two[2],)
        four = mat_mul((two[0][:2], two[1][:2], two[2]), later)

        def write(e, value):
            slab[e, pl.ds(c, 1)] = value[0:1]
            slab[e, pl.ds(2 + c, 1)] = value[4:5]
            rows[54 + e, pl.ds(c, 1)] = value[0:1]
            rows[54 + e, pl.ds(2 + c, 1)] = value[4:5]

        store_rows(four, write)
        return carry

    lax.fori_loop(0, 2, slab_body, 0)
    for q in range(4):
        up_ref[:, q * 128:q * 128 + 128] = rows[:, q, :].astype(BF16)

    def down_body(e, carry):
        for mu in range(3):
            for c in range(2):
                value = dense[mu, e, c]
                rows[mu * 18 + e, c:c + 1] = value[0:1]
                rows[mu * 18 + e, 2 + c:3 + c] = value[4:5]
        return carry

    lax.fori_loop(0, 18, down_body, 0)
    for q in range(4):
        down_ref[:, q * 128:q * 128 + 128] = rows[:, q, :].astype(BF16)


def block_kernel(
    widths, core_ref, up_ref, down_ref, slab, w1_ref, w2_ref, w3_ref, w4_ref, block_ref, other, block
):
    even = core_ref[0] == 0
    up = up_ref[...].astype(F32)
    down = down_ref[...].astype(F32)
    for q in range(4):
        lanes = slice(q * 128, q * 128 + 128)
        other[:, q, :] = jnp.where(even, down[54:66, lanes], up[54:66, lanes])
    first = two_rows(lambda e: jnp.where(even, slab[e], other[e]))
    second = special(two_rows(lambda e: jnp.where(even, other[e], slab[e])))
    block[...] = jnp.zeros_like(block)

    def write(e, value):
        block[2 * e:2 * e + 2, :] = jnp.where(even, value[0:2], value[2:4])

    store_rows(mat_mul(first, second), write)
    offset = 0
    for ref, width in zip((w2_ref, w3_ref, w1_ref, w4_ref), widths):
        flat = ref[...].astype(F32)
        for r in range(27):
            block[SLABROWS + r:SLABROWS + r + 1, offset:offset + width] = flat[:, width * r:width * r + width]
        offset += width
    value = block[...].astype(BF16)
    for d in range(block_ref.shape[0]):
        block_ref[d] = value


def put_row(rows, channel, c, value):
    for t in range(4):
        rows[t, c, pl.ds(channel, 1), :] = value[t:t + 1]
        rows[t, 2 + c, pl.ds(channel, 1), :] = value[4 + t:5 + t]


def space_kernel(dense, cot_ref, time_staples, cots, rows, forces, sums, moved, staples):
    pack_links(cot_ref, cots)
    rows[...] = jnp.zeros_like(rows)
    forces[...] = jnp.zeros_like(forces)
    steps = row_iota() % 4

    def shift_body(e, carry):
        for nu in range(3):
            pair = [dense[nu, e, 0], dense[nu, e, 1]]
            for mu in range(3):
                if mu != nu:
                    low, high = dense_shift(pair, mu, 1)
                    moved[mu, nu, e, 0] = low
                    moved[mu, nu, e, 1] = high
        return carry

    lax.fori_loop(0, 18, shift_body, 0)

    def plane_body(step, carry):
        plane = step // 2
        c = step % 2
        mu = jnp.where(plane == 2, 1, 0)
        nu = jnp.where(plane == 0, 1, 2)
        u_mu = load_matrix(lambda e: dense[mu, e, c])
        u_nu = load_matrix(lambda e: dense[nu, e, c])
        one = mat_mul(u_mu, load_matrix(lambda e: moved[mu, nu, e, c]))
        two = mat_mul(u_nu, load_matrix(lambda e: moved[nu, mu, e, c]))
        loop = mat_mul(one, dagger(two))
        put_row(rows, jnp.where(plane == 2, 3, plane), c, (loop[0][0][0] + loop[0][1][1] + loop[0][2][2]) / 3.0)
        for e, part in enumerate(anti_parts(loop)):
            forces[mu, e, c] += part
            forces[nu, e, c] -= part

        def write_mu(e, value):
            staples[mu, nu, e, c] = value

        def write_nu(e, value):
            staples[nu, mu, e, c] = value

        store_matrix(mat_mul(dagger(one), u_nu), write_mu)
        store_matrix(mat_mul(dagger(two), u_mu), write_nu)
        return carry

    lax.fori_loop(0, 6, plane_body, 0)

    def lower_body(e, carry):
        for mu in range(3):
            acc = [jnp.where(steps == 0, 0.0, pltpu.roll(time_staples[mu, e, c], 1, 0)) for c in range(2)]
            for nu in range(3):
                if nu != mu:
                    pair = dense_shift([staples[mu, nu, e, 0], staples[mu, nu, e, 1]], nu, -1)
                    acc = [acc[c] + pair[c] for c in range(2)]
            sums[mu, e, 0] = acc[0]
            sums[mu, e, 1] = acc[1]
        return carry

    lax.fori_loop(0, 18, lower_body, 0)


def time_kernel(
    dense, cots, up_ref, down_ref, parity_ref, subset_ref, edges, rows_ref, forces_ref, sums_ref,
    fm_ref, fup_ref, fdown_ref, w1_ref, w2_ref,
    moved, staples, sums, halo_up, halo_down, forces, rows,
):
    for q in range(4):
        halo_up[:, q, :] = up_ref[:, q * 128:q * 128 + 128].astype(F32)
        halo_down[:, q, :] = down_ref[:, q * 128:q * 128 + 128].astype(F32)
    rows[...] = rows_ref[...]
    forces[...] = forces_ref[...]
    steps = row_iota() % 4
    lanes = lane_iota(8)

    def shift_body(e, carry):
        for nu in range(3):
            halo = halo_pair(halo_down, nu * 18 + e)
            below = halo_pair(halo_up, nu * 18 + e)
            for c in range(2):
                moved[nu, e, c] = jnp.where(steps == 3, halo[c], pltpu.roll(dense[nu, e, c], 7, 0))
                sums[nu, e, c] = sums_ref[nu, e, c] + jnp.where(steps == 0, below[c], 0.0)
        return carry

    lax.fori_loop(0, 18, shift_body, 0)

    def plane_body(step, carry):
        mu = step // 2
        c = step % 2
        one = load_matrix(lambda e: edges[mu, e, c])
        two = mat_mul(load_matrix(lambda e: dense[3, e, c]), load_matrix(lambda e: moved[mu, e, c]))
        loop = mat_mul(one, dagger(two))
        put_row(rows, jnp.where(mu == 0, 2, mu + 3), c, (loop[0][0][0] + loop[0][1][1] + loop[0][2][2]) / 3.0)
        for e, part in enumerate(anti_parts(loop)):
            forces[mu, e, c] += part
            forces[3, e, c] -= part

        def write(e, value):
            staples[mu, e, c] = value

        store_matrix(mat_mul(dagger(two), load_matrix(lambda e: dense[mu, e, c])), write)
        return carry

    lax.fori_loop(0, 6, plane_body, 0)

    def lower_body(e, carry):
        acc = None
        for mu in range(3):
            pair = dense_shift([staples[mu, e, 0], staples[mu, e, 1]], mu, -1)
            acc = pair if acc is None else [acc[c] + pair[c] for c in range(2)]
        sums[3, e, 0] = acc[0]
        sums[3, e, 1] = acc[1]
        return carry

    lax.fori_loop(0, 18, lower_body, 0)

    colour = (lanes // 64 + lanes // 8 % 8 + lanes % 8 + steps) % 2
    parity = jnp.zeros_like(steps)
    subset = jnp.zeros_like(steps)
    for t in range(4):
        parity = jnp.where(steps == t, parity_ref[0, t], parity)
        subset = jnp.where(steps == t, subset_ref[0, t], subset)
    on_site = colour == parity

    def force_body(step, carry):
        mu = step // 2
        c = step % 2
        current = load_matrix(lambda e: dense[mu, e, c])
        omega = mat_mul(current, load_matrix(lambda e: sums[mu, e, c]))
        parts = [part + forces[mu, e, c] for e, part in enumerate(anti_parts(omega))]
        mean = (parts[0] + parts[1] + parts[2]) * (1.0 / 3.0)
        parts = [parts[e] - mean if e < 3 else parts[e] for e in range(9)]
        parts = [part * (1.0 / 12.0) for part in parts]
        applied = anti_mul(parts, current)
        twice = anti_mul(parts, applied)
        gate = jnp.where(jnp.logical_and(on_site, jnp.right_shift(subset, mu) % 2 == 1), 1.0, 0.0)
        slope = jnp.zeros_like(gate)
        curve = jnp.zeros_like(gate)
        for e, (part, i, j) in enumerate(ENTRIES):
            weight = cots[mu, e, c]
            slope = slope + weight * applied[part][i][j]
            curve = curve + weight * twice[part][i][j]
            w1_ref[mu, e, c] = gate * applied[part][i][j]
            w2_ref[mu, e, c] = gate * twice[part][i][j]
        put_row(rows, 8 + mu, c, gate * slope)
        put_row(rows, 12 + mu, c, gate * curve)
        return carry

    lax.fori_loop(0, 8, force_body, 0)
    for t in range(4):
        for q in range(4):
            value = rows[t, q]
            fm_ref[t, :, q * 128:q * 128 + 128] = value.astype(BF16)
            if t > 0:
                fup_ref[t - 1, :, q * 128:q * 128 + 128] = value[0:8].astype(BF16)
            if t < 3:
                fdown_ref[t, :, q * 128:q * 128 + 128] = value[0:8].astype(BF16)


def selectors():
    row = lax.broadcasted_iota(jnp.int32, (432, 72), 0)
    col = lax.broadcasted_iota(jnp.int32, (432, 72), 1)
    group = row // 12
    spread = (group // 4 * 8 + group % 4 == col).astype(F32).astype(BF16)
    keep = (
        lax.broadcasted_iota(jnp.int32, (432, H), 1) // 4 == lax.broadcasted_iota(jnp.int32, (432, H), 0) % 12
    )
    return spread, keep


def panel_kernel(gathered_ref, weights_ref, loops_ref, p1_ref, p2_ref, p3_ref, p4_ref, b2_ref, b3_ref, b4_ref, weights):
    count = gathered_ref.shape[0]

    def read(chip):
        low = gathered_ref[2 * chip].astype(F32)
        high = gathered_ref[2 * chip + 1].astype(F32)
        return special(
            two_rows(lambda e: jnp.concatenate([low[2 * e:2 * e + 2], high[2 * e:2 * e + 2]], axis=0))
        )

    def flat(matrix):
        return tuple(matrix[0][i][j] for i in range(3) for j in range(3)) + tuple(
            imag_of(matrix, i, j) for i in range(3) for j in range(3)
        )

    def chain(chip, state):
        return flat(mat_mul(load_matrix(lambda e: state[e]), read(chip)))

    state = lax.fori_loop(1, count // 2, chain, flat(read(0)))
    loops_ref[0] = (state[0] + state[4] + state[8]) / 3.0
    loops_ref[1] = (state[9] + state[13] + state[17]) / 3.0

    if weights_ref is None:
        for d in range(count):
            block = gathered_ref[d].astype(F32)
            weights[27 * d:27 * d + 27, :] = block[SLABROWS:SLABROWS + 27]
    else:
        weights[...] = weights_ref[...].astype(F32)
    for k in range(TAPS):
        rows = slice(H * k, H * k + H)
        back = slice(H * SWAP[k], H * SWAP[k] + H)
        p2_ref[:, rows] = weights[rows, 0:48].astype(BF16)
        p3_ref[:, rows] = weights[rows, 48:96].astype(BF16)
        p1_ref[:, 8 * k:8 * k + 8] = weights[rows, 96:104].astype(BF16)
        turned = weights[back, :].T
        b2_ref[:, rows] = turned[0:48].astype(BF16)
        b3_ref[:, rows] = turned[48:96].astype(BF16)
    spread, keep = selectors()
    place = (
        lax.broadcasted_iota(jnp.int32, (LANES, H), 0) == 104 + lax.broadcasted_iota(jnp.int32, (LANES, H), 1) % 4
    ).astype(F32).astype(BF16)
    wide = jnp.dot(weights[...].astype(BF16), place, preferred_element_type=F32)
    wide = jnp.where(keep, wide, 0.0).astype(BF16)
    last = lax.dot_general(spread, wide, (((0,), (0,)), ((), ())), preferred_element_type=F32)
    p4_ref[...] = last.astype(BF16)
    for k in range(TAPS):
        b4_ref[:, 8 * k:8 * k + 8] = last[8 * SWAP[k]:8 * SWAP[k] + 8, :].T.astype(BF16)


def panel_kernel_plain(gathered_ref, *rest):
    panel_kernel(gathered_ref, None, *rest)


def chunks_of(value):
    return [value[:, q * 128:q * 128 + 128] for q in range(4)]


def one_shift(chunks, position):
    if position == 0:
        return chunks
    lanes = lane_iota(chunks[0].shape[0])
    sign = 1 if position % 2 == 1 else -1
    if position > 4:
        return [shift_z(chunk, sign, lanes) for chunk in chunks]
    if position > 2:
        return [shift_y(chunk, sign, lanes) for chunk in chunks]
    low = lanes < 64
    rolled = [roll_lanes(chunk, 64) for chunk in chunks]
    if sign > 0:
        return [jnp.where(low, rolled[q], rolled[(q + 1) % 4]) for q in range(4)]
    return [jnp.where(low, rolled[(q + 3) % 4], rolled[q]) for q in range(4)]


def span(slice_index, count=1):
    if isinstance(slice_index, int):
        return slice(slice_index * SITES, (slice_index + count) * SITES)
    return pl.ds(pl.multiple_of(slice_index * SITES, SITES), count * SITES)


def stack_wide(source, target, first, count):
    for s in range(count):
        chunks = chunks_of(source[:, span(first + s)])
        for position in range(7):
            shifted = one_shift(chunks, position)
            for q in range(4):
                lanes = slice(s * SITES + q * 128, s * SITES + q * 128 + 128)
                target[H * position:H * position + H, lanes] = shifted[q]
    width = slice(0, count * SITES)
    target[7 * H:8 * H, width] = source[:, span(first + 1, count)]
    target[8 * H:9 * H, width] = source[:, span(first - 1, count)]


def stack_thin(source, target, first, count):
    for s in range(count):
        chunks = chunks_of(source[:, span(first + s)])
        ahead = chunks_of(source[:, span(first + s + 1)])
        behind = chunks_of(source[:, span(first + s - 1)])
        columns = [one_shift(chunks, position) for position in range(7)] + [ahead, behind]
        for q in range(4):
            lanes = slice(s * SITES + q * 128, s * SITES + q * 128 + 128)
            target[0:72, lanes] = jnp.concatenate([column[q] for column in columns], axis=0).astype(BF16)


def one_minus_square(value):
    value = value.astype(F32)
    return 1.0 - value * value


def conv_kernel(
    split, fm_ref, below_ref, above_ref, fbelow_ref, fabove_ref, loops_ref,
    p1_ref, p2_ref, p3_ref, p4_ref, b2_ref, b3_ref, b4_ref,
    coeff_ref, grads_ref,
    feats, mixed, h1, h2, h3, parts, lasts, g3, g2, wide, thin, packed,
):
    row8 = lax.broadcasted_iota(jnp.int32, (8, SITES), 0)
    loop_re = jnp.concatenate([loops_ref[0, q:q + 1, :] for q in range(4)], axis=1)
    loop_im = jnp.concatenate([loops_ref[1, q:q + 1, :] for q in range(4)], axis=1)
    loops = jnp.where(row8 == 6, loop_re, jnp.where(row8 == 7, loop_im, 0.0))
    loops = loops.astype(BF16).astype(F32)
    for j in range(3):
        feats[:, span(j)] = fbelow_ref[j].astype(F32) + loops
        feats[:, span(15 + j)] = fabove_ref[j].astype(F32) + loops
    for base, ref in ((3, below_ref), (7, fm_ref), (11, above_ref)):
        for j in range(4):
            value = ref[j].astype(F32)
            feats[:, span(base + j)] = value[0:8] + loops
            mixed[:, span(base + j)] = value[8:16]

    def layer_one(step, carry):
        first = 1 + 4 * step
        stack_thin(feats, thin, first, 4)
        out = jnp.dot(p1_ref[...], thin[...], preferred_element_type=F32)
        h1[:, span(first, 4)] = jnp.tanh(out).astype(BF16)
        return carry

    lax.fori_loop(0, 4, layer_one, 0)

    def layer_two(step, carry):
        first = 2 + 2 * step
        stack_wide(h1, wide, first, 2)
        out = jnp.dot(p2_ref[...], wide[:, 0:1024], preferred_element_type=F32)
        h2[:, span(first, 2)] = jnp.tanh(out).astype(BF16)
        return carry

    lax.fori_loop(0, 7, layer_two, 0)

    def layer_three(step, carry):
        first = 3 + 2 * step
        stack_wide(h2, wide, first, 2)
        out = jnp.dot(p3_ref[...], wide[:, 0:1024], preferred_element_type=F32)
        out = jnp.tanh(out).astype(BF16)
        h3[:, span(first, 2)] = out
        taps = jnp.dot(p4_ref[...], out, preferred_element_type=F32)
        for s in range(2):
            acc = None
            for position in range(7):
                shifted = one_shift(
                    chunks_of(taps[8 * position:8 * position + 8, s * SITES:(s + 1) * SITES]), position
                )
                acc = shifted if acc is None else [a + b for a, b in zip(acc, shifted)]
            parts[0, :, span(first + s)] = jnp.concatenate(acc, axis=1)
            parts[1, :, span(first + s)] = taps[56:64, s * SITES:(s + 1) * SITES]
            parts[2, :, span(first + s)] = taps[64:72, s * SITES:(s + 1) * SITES]
        return carry

    lax.fori_loop(0, 6, layer_three, 0)

    def last_layer(step, carry):
        for s in range(2):
            index = 4 + 2 * step + s
            coeff = jnp.tanh(parts[0, :, span(index)] + parts[1, :, span(index + 1)] + parts[2, :, span(index - 1)])
            blend = mixed[:, span(index)]
            value = (blend + coeff * pltpu.roll(blend, 4, 0)) * (1.0 - coeff * coeff)
            lasts[:, span(index)] = jnp.where(row8 < 4, value, 0.0).astype(BF16).astype(F32)
            parts[0, :, span(index)] = coeff
        return carry

    lax.fori_loop(0, 5, last_layer, 0)
    for t in range(4):
        coeff_ref[t] = parts[0, :, span(7 + t)]

    def back_three(first, count):
        stack_thin(lasts, thin, first, count)
        out = jnp.dot(b4_ref[...], thin[:, 0:count * SITES], preferred_element_type=F32)
        g3[:, span(first, count)] = (out * one_minus_square(h3[:, span(first, count)])).astype(BF16)

    back_three(5, 2)
    back_three(11, 2)
    back_three(7, 4)
    own = span(7, 4)
    contract = (((1,), (1,)), ((), ()))
    grad_last = lax.dot_general(thin[...], h3[:, own], contract, preferred_element_type=F32)

    stack_wide(g3, wide, 6, 1)
    out = jnp.dot(b3_ref[...], wide[:, 0:SITES], preferred_element_type=F32)
    g2[:, span(6)] = (out * one_minus_square(h2[:, span(6)])).astype(BF16)
    stack_wide(g3, wide, 11, 1)
    out = jnp.dot(b3_ref[...], wide[:, 0:SITES], preferred_element_type=F32)
    g2[:, span(11)] = (out * one_minus_square(h2[:, span(11)])).astype(BF16)
    stack_wide(g3, wide, 7, 4)
    out = jnp.dot(b3_ref[...], wide[...], preferred_element_type=F32)
    g2[:, own] = (out * one_minus_square(h2[:, own])).astype(BF16)
    grad_third = lax.dot_general(wide[...], h2[:, own], contract, preferred_element_type=F32)

    stack_wide(g2, wide, 7, 4)
    out = jnp.dot(b2_ref[...], wide[...], preferred_element_type=F32)
    g1 = (out * one_minus_square(h1[:, own])).astype(BF16)
    grad_second = lax.dot_general(wide[...], h1[:, own], contract, preferred_element_type=F32)

    stack_thin(feats, thin, 7, 4)
    grad_first = lax.dot_general(g1, thin[...], contract, preferred_element_type=F32)

    spread, keep = selectors()
    ordered = jnp.concatenate([grad_last[8 * SWAP[k]:8 * SWAP[k] + 8] for k in range(TAPS)], axis=0)
    broad = jnp.dot(spread, ordered.astype(BF16), preferred_element_type=F32)
    broad = jnp.where(keep, broad, 0.0).astype(BF16)
    place = (
        lax.broadcasted_iota(jnp.int32, (H, LANES), 1) == 104 + lax.broadcasted_iota(jnp.int32, (H, LANES), 0) % 4
    ).astype(F32).astype(BF16)
    packed[...] = jnp.dot(broad, place, preferred_element_type=F32)
    for k in range(TAPS):
        rows = slice(H * k, H * k + H)
        back = slice(H * SWAP[k], H * SWAP[k] + H)
        packed[rows, 0:48] = grad_second[back]
        packed[rows, 48:96] = grad_third[back]
        packed[rows, 96:104] = grad_first[:, 8 * k:8 * k + 8]
    if split:
        for d in range(16):
            grads_ref[d] = packed[27 * d:27 * d + 27, :].astype(BF16)
    else:
        grads_ref[...] = packed[...].astype(BF16)


def update_kernel(links_ref, w1_ref, w2_ref, coeff_ref, out_ref, factors):
    for mu in range(4):
        for t in range(4):
            for c in range(2):
                factors[mu, c, t:t + 1, :] = coeff_ref[t, mu:mu + 1, c * 128:c * 128 + 128]
                factors[mu, c, 4 + t:5 + t, :] = coeff_ref[t, mu:mu + 1, 256 + c * 128:384 + c * 128]

    def body(mu, carry):
        factor = [factors[mu, c] for c in range(2)]
        half = [0.5 * value * value for value in factor]
        for e, (part, i, j) in enumerate(ENTRIES):
            pair = pack_pair(links_ref[mu, part, i, j, 0])
            new = [pair[c] + factor[c] * w1_ref[mu, e, c] + half[c] * w2_ref[mu, e, c] for c in range(2)]
            out_ref[mu, part, i, j, 0] = jnp.concatenate(
                [new[0][0:4], new[1][0:4], new[0][4:8], new[1][4:8]], axis=1
            )
        return carry

    lax.fori_loop(0, 4, body, 0)


def sum_kernel(widths, parts_ref, first_ref, second_ref, third_ref, last_ref):
    value = parts_ref[0].astype(F32)
    for d in range(1, parts_ref.shape[0]):
        value = value + parts_ref[d].astype(F32)
    offset = 0
    for ref, width in zip((second_ref, third_ref, first_ref, last_ref), widths):
        for r in range(27):
            ref[:, width * r:width * r + width] = value[r:r + 1, offset:offset + width]
        offset += width


def call(body, outs, scratch, smem=(), count=0, cost=None):
    specs = {}
    if smem:
        specs["in_specs"] = [
            pl.BlockSpec(memory_space=pltpu.SMEM if i in smem else pltpu.VMEM) for i in range(count)
        ]
    return pl.pallas_call(
        body,
        out_shape=[jax.ShapeDtypeStruct(shape, dtype) for shape, dtype in outs],
        scratch_shapes=[pltpu.VMEM(shape, dtype) for shape, dtype in scratch],
        compiler_params=pltpu.CompilerParams(vmem_limit_bytes=LIMIT),
        cost_estimate=cost,
        **specs,
    )


def on_device(links, cotangent, parity, link_subset, w_first, w_second, w_third, w_last):
    count = lax.axis_size("tm")

    def send(value, distance):
        return lax.ppermute(value, "tm", [(i, (i + distance) % count) for i in range(count)])

    widths = (768 // count, 768 // count, 128 // count, 64 // count)
    field = ((4, 18, 2, 8, LANES), F32)
    space = ((3, 18, 2, 8, LANES), F32)
    edge_rows = ((66, SITES), BF16)
    up, down, dense, edges, staples, slab = call(
        face_kernel,
        [edge_rows, edge_rows, field, space, space, ((12, 4, LANES), F32)],
        [space, ((66, 4, LANES), F32)],
    )(links)
    up = send(up, 1)
    down = send(down, -1)
    cots, rows, forces, sums = call(
        space_kernel,
        [field, ((4, 4, 16, LANES), F32), ((4, 9, 2, 8, LANES), F32), space],
        [((3, 3, 18, 2, 8, LANES), F32), ((3, 3, 18, 2, 8, LANES), F32)],
        cost=pl.CostEstimate(flops=4_000_000_000, bytes_accessed=16_000_000, transcendentals=0),
    )(dense, cotangent, staples)
    core = (lax.axis_index("tm") % 2).astype(jnp.int32)[None]
    (block,) = call(
        functools.partial(block_kernel, widths),
        [((count, BLOCKROWS, LANES), BF16)],
        [((12, 4, LANES), F32), ((BLOCKROWS, LANES), F32)],
        smem=(0,), count=8,
    )(core, up, down, slab, w_first[None], w_second[None], w_third[None], w_last[None])
    gathered = lax.all_to_all(block, "tm", split_axis=0, concat_axis=0, tiled=True)
    fm, fup, fdown, applied, twice = call(
        time_kernel,
        [((4, 16, SITES), BF16), ((3, 8, SITES), BF16), ((3, 8, SITES), BF16), field, field],
        [
            space, space, field, ((66, 4, LANES), F32), ((66, 4, LANES), F32),
            ((4, 9, 2, 8, LANES), F32), ((4, 4, 16, LANES), F32),
        ],
        smem=(4, 5), count=10,
    )(dense, cots, up, down, parity, link_subset, edges, rows, forces, sums)
    below = send(fm, 1)
    above = send(fm, -1)
    fbelow = send(fup, 2)
    fabove = send(fdown, -2)

    panel_outs = [
        ((2, 4, LANES), F32), ((H, 72), BF16), ((H, 432), BF16), ((H, 432), BF16), ((72, H), BF16),
        ((H, 432), BF16), ((H, 432), BF16), ((H, 72), BF16),
    ]
    panel_scratch = [((432, LANES), F32)]
    if count == 16:
        loops, p1, p2, p3, p4, b2, b3, b4 = call(panel_kernel_plain, panel_outs, panel_scratch)(gathered)
    else:
        pieces = []
        offset = 0
        for width, full in zip(widths, (48, 48, 8, 4)):
            piece = gathered[:, SLABROWS:SLABROWS + 27, offset:offset + width]
            pieces.append(piece.reshape(432, full))
            offset += width
        pieces.append(jnp.zeros((432, 20), BF16))
        loops, p1, p2, p3, p4, b2, b3, b4 = call(panel_kernel, panel_outs, panel_scratch)(
            gathered, jnp.concatenate(pieces, axis=1)
        )

    window = 18 * SITES
    coeff, grads = call(
        functools.partial(conv_kernel, count == 16),
        [((4, 8, SITES), F32), ((16, 27, LANES) if count == 16 else (432, LANES), BF16)],
        [
            ((8, window), F32), ((8, window), F32), ((H, window), BF16), ((H, window), BF16), ((H, window), BF16),
            ((3, 8, window), F32), ((8, window), F32), ((H, window), BF16), ((H, window), BF16),
            ((432, 4 * SITES), BF16), ((72, 4 * SITES), BF16), ((432, LANES), F32),
        ],
    )(fm, below, above, fbelow, fabove, loops, p1, p2, p3, p4, b2, b3, b4)
    if count != 16:
        offset = 0
        pieces = []
        for width, full in zip(widths, (48, 48, 8, 4)):
            pieces.append(grads[:, offset:offset + full].reshape(count, 27, width))
            offset += full
        grads = jnp.concatenate(pieces, axis=2)
    grads = lax.all_to_all(grads, "tm", split_axis=0, concat_axis=0, tiled=True)
    (new_links,) = call(
        update_kernel, [(links.shape, F32)], [((4, 2, 8, LANES), F32)]
    )(links, applied, twice, coeff)
    grad_first, grad_second, grad_third, grad_last = call(
        functools.partial(sum_kernel, widths),
        [((1, 27 * width), F32) for width in (widths[2], widths[0], widths[1], widths[3])],
        [],
    )(grads)
    return (new_links, grad_first, grad_second, grad_third, grad_last)


def solution(mesh):
    placed = (
        P(None, None, None, None, "groups", "tm", None),
        P(None, None, None, None, "groups", "tm", None),
        P("groups", "tm"),
        P("groups", "tm"),
        P("tm"),
        P("tm"),
        P("tm"),
        P("tm"),
    )
    return jax.shard_map(
        on_device,
        mesh=mesh,
        in_specs=placed,
        out_specs=(
            P(None, None, None, None, "groups", "tm", None),
            P("groups", "tm"),
            P("groups", "tm"),
            P("groups", "tm"),
            P("groups", "tm"),
        ),
        check_vma=False,
    )
```

```python
import functools

import jax
import jax.numpy as jnp
from jax import lax
from jax.experimental import pallas as pl
from jax.experimental.pallas import tpu as pltpu
from jax.sharding import PartitionSpec as P

F32 = jnp.float32
BF16 = jnp.bfloat16
TAPS = 9
H = 48
LANES = 128
SITES = 512
PAIRS = ((0, 1), (0, 2), (0, 3), (1, 2), (1, 3), (2, 3))
SWAP = (0, 2, 1, 4, 3, 6, 5, 8, 7)
ENTRIES = tuple((c, i, j) for c in range(2) for i in range(3) for j in range(3))
SLABROWS = 24
BLOCKROWS = 64
LIMIT = 40 * 1024 * 1024


def lane_iota(rows):
    return lax.broadcasted_iota(jnp.int32, (rows, LANES), 1)


def row_iota():
    return lax.broadcasted_iota(jnp.int32, (8, LANES), 0)


def roll_lanes(value, amount):
    return pltpu.roll(value, amount % LANES, 1)


def shift_z(chunk, sign, lanes):
    z = lanes % 8
    if sign > 0:
        return jnp.where(z == 7, roll_lanes(chunk, 7), roll_lanes(chunk, -1))
    return jnp.where(z == 0, roll_lanes(chunk, -7), roll_lanes(chunk, 1))


def shift_y(chunk, sign, lanes):
    y = lanes // 8 % 8
    if sign > 0:
        return jnp.where(y == 7, roll_lanes(chunk, 56), roll_lanes(chunk, -8))
    return jnp.where(y == 0, roll_lanes(chunk, -56), roll_lanes(chunk, 8))


def dense_shift(pair, axis, sign):
    lanes = lane_iota(8)
    if axis == 2:
        return [shift_z(chunk, sign, lanes) for chunk in pair]
    if axis == 1:
        return [shift_y(chunk, sign, lanes) for chunk in pair]
    low = lanes < 64
    first, second = [roll_lanes(chunk, 64) for chunk in pair]
    if sign > 0:
        return [jnp.where(low, first, second), jnp.where(low, second, pltpu.roll(first, 4, 0))]
    return [jnp.where(low, pltpu.roll(second, 4, 0), first), jnp.where(low, first, second)]


def pack_pair(value):
    return [
        jnp.concatenate([value[:, c * 128:c * 128 + 128], value[:, 256 + c * 128:384 + c * 128]], axis=0)
        for c in range(2)
    ]


def halo_pair(ref, index):
    top = row_iota() < 4
    pair = []
    for c in range(2):
        low = jnp.broadcast_to(ref[index, c:c + 1, :], (8, LANES))
        high = jnp.broadcast_to(ref[index, 2 + c:3 + c, :], (8, LANES))
        pair.append(jnp.where(top, low, high))
    return pair


def load_matrix(read):
    real = [[read(3 * i + j) for j in range(3)] for i in range(3)]
    imag = [[read(9 + 3 * i + j) for j in range(3)] for i in range(3)]
    return (real, imag, 1)


def dagger(matrix):
    real, imag, sign = matrix
    return (
        [[real[j][i] for j in range(3)] for i in range(3)],
        [[imag[j][i] for j in range(3)] for i in range(3)],
        -sign,
    )


def total(terms, signs):
    value = None
    for term, sign in zip(terms, signs):
        if value is None:
            value = term if sign > 0 else -term
        else:
            value = value + term if sign > 0 else value - term
    return value


def mat_mul(left, right):
    lr, li, ls = left
    rr, ri, rs = right
    same = ls == rs
    height = len(lr)
    real = [[None] * 3 for _ in range(height)]
    imag = [[None] * 3 for _ in range(height)]
    for i in range(height):
        for j in range(3):
            real[i][j] = total(
                [lr[i][k] * rr[k][j] for k in range(3)] + [li[i][k] * ri[k][j] for k in range(3)],
                [1, 1, 1] + [-1 if same else 1] * 3,
            )
            imag[i][j] = total(
                [lr[i][k] * ri[k][j] for k in range(3)] + [li[i][k] * rr[k][j] for k in range(3)],
                [1, 1, 1] + [1 if same else -1] * 3,
            )
    return (real, imag, ls if same else rs)


def imag_of(matrix, i, j):
    return matrix[1][i][j] if matrix[2] > 0 else -matrix[1][i][j]


def store_matrix(matrix, write):
    for i in range(3):
        for j in range(3):
            write(3 * i + j, matrix[0][i][j])
            write(9 + 3 * i + j, imag_of(matrix, i, j))


def two_rows(read):
    real = [[read(3 * i + j) for j in range(3)] for i in range(2)]
    imag = [[read(6 + 3 * i + j) for j in range(3)] for i in range(2)]
    return (real, imag, 1)


def store_rows(matrix, write):
    for i in range(2):
        for j in range(3):
            write(3 * i + j, matrix[0][i][j])
            write(6 + 3 * i + j, imag_of(matrix, i, j))


def special(matrix):
    real, imag, _ = matrix
    last_r, last_i = [], []
    for k in range(3):
        i, j = (k + 1) % 3, (k + 2) % 3
        last_r.append(
            (real[0][i] * real[1][j] - imag[0][i] * imag[1][j])
            - (real[0][j] * real[1][i] - imag[0][j] * imag[1][i])
        )
        last_i.append(
            (real[0][j] * imag[1][i] + imag[0][j] * real[1][i])
            - (real[0][i] * imag[1][j] + imag[0][i] * real[1][j])
        )
    return (real + [last_r], imag + [last_i], 1)


def anti_parts(matrix):
    parts = [2.0 * imag_of(matrix, i, i) for i in range(3)]
    for i, j in ((0, 1), (0, 2), (1, 2)):
        parts.append(matrix[0][i][j] - matrix[0][j][i])
        parts.append(imag_of(matrix, i, j) + imag_of(matrix, j, i))
    return parts


def anti_matrix(parts):
    zero = jnp.zeros_like(parts[0])
    real = [[zero, parts[3], parts[5]], [-parts[3], zero, parts[7]], [-parts[5], -parts[7], zero]]
    imag = [[parts[0], parts[4], parts[6]], [parts[4], parts[1], parts[8]], [parts[6], parts[8], parts[2]]]
    return real, imag


def anti_mul(parts, right):
    real, imag = anti_matrix(parts)
    rr, ri, _ = right
    out_r = [[None] * 3 for _ in range(3)]
    out_i = [[None] * 3 for _ in range(3)]
    for i in range(3):
        for j in range(3):
            value_r = -(imag[i][i] * ri[i][j])
            value_i = imag[i][i] * rr[i][j]
            for k in range(3):
                if k != i:
                    value_r = value_r + real[i][k] * rr[k][j] - imag[i][k] * ri[k][j]
                    value_i = value_i + real[i][k] * ri[k][j] + imag[i][k] * rr[k][j]
            out_r[i][j] = value_r
            out_i[i][j] = value_i
    return (out_r, out_i, 1)


def pack_links(links_ref, dense):
    def body(mu, carry):
        for e, (c, i, j) in enumerate(ENTRIES):
            low, high = pack_pair(links_ref[mu, c, i, j, 0].astype(F32))
            dense[mu, e, 0] = low
            dense[mu, e, 1] = high
        return carry

    lax.fori_loop(0, 4, body, 0)


def face_kernel(links_ref, up_ref, down_ref, dense, edges, staples, slab, moved, rows):
    pack_links(links_ref, dense)

    def shift_body(e, carry):
        pair = [dense[3, e, 0], dense[3, e, 1]]
        for mu in range(3):
            low, high = dense_shift(pair, mu, 1)
            moved[mu, e, 0] = low
            moved[mu, e, 1] = high
        return carry

    lax.fori_loop(0, 18, shift_body, 0)

    def staple_body(step, carry):
        mu = step // 2
        c = step % 2
        u_mu = load_matrix(lambda e: dense[mu, e, c])
        u_t = load_matrix(lambda e: dense[3, e, c])
        edge = mat_mul(u_mu, load_matrix(lambda e: moved[mu, e, c]))

        def write_edge(e, value):
            edges[mu, e, c] = value

        store_matrix(edge, write_edge)

        def write(e, value):
            staples[mu, e, c] = value
            rows[mu * 18 + e, pl.ds(c, 1)] = value[3:4]
            rows[mu * 18 + e, pl.ds(2 + c, 1)] = value[7:8]

        store_matrix(mat_mul(dagger(edge), u_t), write)
        return carry

    lax.fori_loop(0, 6, staple_body, 0)

    def slab_body(c, carry):
        u_t = load_matrix(lambda e: dense[3, e, c])
        ahead = load_matrix(lambda e: pltpu.roll(dense[3, e, c], 7, 0))
        two = mat_mul(u_t, ahead)
        later = tuple(
            [[pltpu.roll(part[i][j], 6, 0) for j in range(3)] for i in range(3)] for part in two[:2]
        ) + (two[2],)
        four = mat_mul((two[0][:2], two[1][:2], two[2]), later)

        def write(e, value):
            slab[e, pl.ds(c, 1)] = value[0:1]
            slab[e, pl.ds(2 + c, 1)] = value[4:5]
            rows[54 + e, pl.ds(c, 1)] = value[0:1]
            rows[54 + e, pl.ds(2 + c, 1)] = value[4:5]

        store_rows(four, write)
        return carry

    lax.fori_loop(0, 2, slab_body, 0)
    for q in range(4):
        up_ref[:, q * 128:q * 128 + 128] = rows[:, q, :].astype(BF16)

    def down_body(e, carry):
        for mu in range(3):
            for c in range(2):
                value = dense[mu, e, c]
                rows[mu * 18 + e, c:c + 1] = value[0:1]
                rows[mu * 18 + e, 2 + c:3 + c] = value[4:5]
        return carry

    lax.fori_loop(0, 18, down_body, 0)
    for q in range(4):
        down_ref[:, q * 128:q * 128 + 128] = rows[:, q, :].astype(BF16)


def block_kernel(
    widths, core_ref, up_ref, down_ref, slab, w1_ref, w2_ref, w3_ref, w4_ref, block_ref, other, block
):
    even = core_ref[0] == 0
    up = up_ref[...].astype(F32)
    down = down_ref[...].astype(F32)
    for q in range(4):
        lanes = slice(q * 128, q * 128 + 128)
        other[:, q, :] = jnp.where(even, down[54:66, lanes], up[54:66, lanes])
    first = two_rows(lambda e: jnp.where(even, slab[e], other[e]))
    second = special(two_rows(lambda e: jnp.where(even, other[e], slab[e])))
    block[...] = jnp.zeros_like(block)

    def write(e, value):
        block[2 * e:2 * e + 2, :] = jnp.where(even, value[0:2], value[2:4])

    store_rows(mat_mul(first, second), write)
    offset = 0
    for ref, width in zip((w2_ref, w3_ref, w1_ref, w4_ref), widths):
        flat = ref[...].astype(F32)
        for r in range(27):
            block[SLABROWS + r:SLABROWS + r + 1, offset:offset + width] = flat[:, width * r:width * r + width]
        offset += width
    value = block[...].astype(BF16)
    for d in range(block_ref.shape[0]):
        block_ref[d] = value


def put_row(rows, channel, c, value):
    for t in range(4):
        rows[t, c, pl.ds(channel, 1), :] = value[t:t + 1]
        rows[t, 2 + c, pl.ds(channel, 1), :] = value[4 + t:5 + t]


def space_kernel(dense, cot_ref, time_staples, cots, rows, forces, sums, moved, staples):
    pack_links(cot_ref, cots)
    rows[...] = jnp.zeros_like(rows)
    forces[...] = jnp.zeros_like(forces)
    steps = row_iota() % 4

    def shift_body(e, carry):
        for nu in range(3):
            pair = [dense[nu, e, 0], dense[nu, e, 1]]
            for mu in range(3):
                if mu != nu:
                    low, high = dense_shift(pair, mu, 1)
                    moved[mu, nu, e, 0] = low
                    moved[mu, nu, e, 1] = high
        return carry

    lax.fori_loop(0, 18, shift_body, 0)

    def plane_body(step, carry):
        plane = step // 2
        c = step % 2
        mu = jnp.where(plane == 2, 1, 0)
        nu = jnp.where(plane == 0, 1, 2)
        u_mu = load_matrix(lambda e: dense[mu, e, c])
        u_nu = load_matrix(lambda e: dense[nu, e, c])
        one = mat_mul(u_mu, load_matrix(lambda e: moved[mu, nu, e, c]))
        two = mat_mul(u_nu, load_matrix(lambda e: moved[nu, mu, e, c]))
        loop = mat_mul(one, dagger(two))
        put_row(rows, jnp.where(plane == 2, 3, plane), c, (loop[0][0][0] + loop[0][1][1] + loop[0][2][2]) / 3.0)
        for e, part in enumerate(anti_parts(loop)):
            forces[mu, e, c] += part
            forces[nu, e, c] -= part

        def write_mu(e, value):
            staples[mu, nu, e, c] = value

        def write_nu(e, value):
            staples[nu, mu, e, c] = value

        store_matrix(mat_mul(dagger(one), u_nu), write_mu)
        store_matrix(mat_mul(dagger(two), u_mu), write_nu)
        return carry

    lax.fori_loop(0, 6, plane_body, 0)

    def lower_body(e, carry):
        for mu in range(3):
            acc = [jnp.where(steps == 0, 0.0, pltpu.roll(time_staples[mu, e, c], 1, 0)) for c in range(2)]
            for nu in range(3):
                if nu != mu:
                    pair = dense_shift([staples[mu, nu, e, 0], staples[mu, nu, e, 1]], nu, -1)
                    acc = [acc[c] + pair[c] for c in range(2)]
            sums[mu, e, 0] = acc[0]
            sums[mu, e, 1] = acc[1]
        return carry

    lax.fori_loop(0, 18, lower_body, 0)


def time_kernel(
    dense, cots, up_ref, down_ref, parity_ref, subset_ref, edges, rows_ref, forces_ref, sums_ref,
    fm_ref, fup_ref, fdown_ref, w1_ref, w2_ref,
    moved, staples, sums, halo_up, halo_down, forces, rows,
):
    for q in range(4):
        halo_up[:, q, :] = up_ref[:, q * 128:q * 128 + 128].astype(F32)
        halo_down[:, q, :] = down_ref[:, q * 128:q * 128 + 128].astype(F32)
    rows[...] = rows_ref[...]
    forces[...] = forces_ref[...]
    steps = row_iota() % 4
    lanes = lane_iota(8)

    def shift_body(e, carry):
        for nu in range(3):
            halo = halo_pair(halo_down, nu * 18 + e)
            below = halo_pair(halo_up, nu * 18 + e)
            for c in range(2):
                moved[nu, e, c] = jnp.where(steps == 3, halo[c], pltpu.roll(dense[nu, e, c], 7, 0))
                sums[nu, e, c] = sums_ref[nu, e, c] + jnp.where(steps == 0, below[c], 0.0)
        return carry

    lax.fori_loop(0, 18, shift_body, 0)

    def plane_body(step, carry):
        mu = step // 2
        c = step % 2
        one = load_matrix(lambda e: edges[mu, e, c])
        two = mat_mul(load_matrix(lambda e: dense[3, e, c]), load_matrix(lambda e: moved[mu, e, c]))
        loop = mat_mul(one, dagger(two))
        put_row(rows, jnp.where(mu == 0, 2, mu + 3), c, (loop[0][0][0] + loop[0][1][1] + loop[0][2][2]) / 3.0)
        for e, part in enumerate(anti_parts(loop)):
            forces[mu, e, c] += part
            forces[3, e, c] -= part

        def write(e, value):
            staples[mu, e, c] = value

        store_matrix(mat_mul(dagger(two), load_matrix(lambda e: dense[mu, e, c])), write)
        return carry

    lax.fori_loop(0, 6, plane_body, 0)

    def lower_body(e, carry):
        acc = None
        for mu in range(3):
            pair = dense_shift([staples[mu, e, 0], staples[mu, e, 1]], mu, -1)
            acc = pair if acc is None else [acc[c] + pair[c] for c in range(2)]
        sums[3, e, 0] = acc[0]
        sums[3, e, 1] = acc[1]
        return carry

    lax.fori_loop(0, 18, lower_body, 0)

    colour = (lanes // 64 + lanes // 8 % 8 + lanes % 8 + steps) % 2
    parity = jnp.zeros_like(steps)
    subset = jnp.zeros_like(steps)
    for t in range(4):
        parity = jnp.where(steps == t, parity_ref[0, t], parity)
        subset = jnp.where(steps == t, subset_ref[0, t], subset)
    on_site = colour == parity

    def force_body(step, carry):
        mu = step // 2
        c = step % 2
        current = load_matrix(lambda e: dense[mu, e, c])
        omega = mat_mul(current, load_matrix(lambda e: sums[mu, e, c]))
        parts = [part + forces[mu, e, c] for e, part in enumerate(anti_parts(omega))]
        mean = (parts[0] + parts[1] + parts[2]) * (1.0 / 3.0)
        parts = [parts[e] - mean if e < 3 else parts[e] for e in range(9)]
        parts = [part * (1.0 / 12.0) for part in parts]
        applied = anti_mul(parts, current)
        twice = anti_mul(parts, applied)
        gate = jnp.where(jnp.logical_and(on_site, jnp.right_shift(subset, mu) % 2 == 1), 1.0, 0.0)
        slope = jnp.zeros_like(gate)
        curve = jnp.zeros_like(gate)
        for e, (part, i, j) in enumerate(ENTRIES):
            weight = cots[mu, e, c]
            slope = slope + weight * applied[part][i][j]
            curve = curve + weight * twice[part][i][j]
            w1_ref[mu, e, c] = gate * applied[part][i][j]
            w2_ref[mu, e, c] = gate * twice[part][i][j]
        put_row(rows, 8 + mu, c, gate * slope)
        put_row(rows, 12 + mu, c, gate * curve)
        return carry

    lax.fori_loop(0, 8, force_body, 0)
    for t in range(4):
        for q in range(4):
            value = rows[t, q]
            fm_ref[t, :, q * 128:q * 128 + 128] = value.astype(BF16)
            if t > 0:
                fup_ref[t - 1, :, q * 128:q * 128 + 128] = value[0:8].astype(BF16)
            if t < 3:
                fdown_ref[t, :, q * 128:q * 128 + 128] = value[0:8].astype(BF16)


def selectors():
    row = lax.broadcasted_iota(jnp.int32, (432, 72), 0)
    col = lax.broadcasted_iota(jnp.int32, (432, 72), 1)
    group = row // 12
    spread = (group // 4 * 8 + group % 4 == col).astype(F32).astype(BF16)
    keep = (
        lax.broadcasted_iota(jnp.int32, (432, H), 1) // 4 == lax.broadcasted_iota(jnp.int32, (432, H), 0) % 12
    )
    return spread, keep


def panel_kernel(gathered_ref, weights_ref, loops_ref, p1_ref, p2_ref, p3_ref, p4_ref, b2_ref, b3_ref, b4_ref, weights):
    count = gathered_ref.shape[0]

    def read(chip):
        low = gathered_ref[2 * chip].astype(F32)
        high = gathered_ref[2 * chip + 1].astype(F32)
        return special(
            two_rows(lambda e: jnp.concatenate([low[2 * e:2 * e + 2], high[2 * e:2 * e + 2]], axis=0))
        )

    def flat(matrix):
        return tuple(matrix[0][i][j] for i in range(3) for j in range(3)) + tuple(
            imag_of(matrix, i, j) for i in range(3) for j in range(3)
        )

    def chain(chip, state):
        return flat(mat_mul(load_matrix(lambda e: state[e]), read(chip)))

    state = lax.fori_loop(1, count // 2, chain, flat(read(0)))
    loops_ref[0] = (state[0] + state[4] + state[8]) / 3.0
    loops_ref[1] = (state[9] + state[13] + state[17]) / 3.0

    if weights_ref is None:
        for d in range(count):
            block = gathered_ref[d].astype(F32)
            weights[27 * d:27 * d + 27, :] = block[SLABROWS:SLABROWS + 27]
    else:
        weights[...] = weights_ref[...].astype(F32)
    for k in range(TAPS):
        rows = slice(H * k, H * k + H)
        back = slice(H * SWAP[k], H * SWAP[k] + H)
        p2_ref[:, rows] = weights[rows, 0:48].astype(BF16)
        p3_ref[:, rows] = weights[rows, 48:96].astype(BF16)
        p1_ref[:, 8 * k:8 * k + 8] = weights[rows, 96:104].astype(BF16)
        turned = weights[back, :].T
        b2_ref[:, rows] = turned[0:48].astype(BF16)
        b3_ref[:, rows] = turned[48:96].astype(BF16)
    spread, keep = selectors()
    place = (
        lax.broadcasted_iota(jnp.int32, (LANES, H), 0) == 104 + lax.broadcasted_iota(jnp.int32, (LANES, H), 1) % 4
    ).astype(F32).astype(BF16)
    wide = jnp.dot(weights[...].astype(BF16), place, preferred_element_type=F32)
    wide = jnp.where(keep, wide, 0.0).astype(BF16)
    last = lax.dot_general(spread, wide, (((0,), (0,)), ((), ())), preferred_element_type=F32)
    p4_ref[...] = last.astype(BF16)
    for k in range(TAPS):
        b4_ref[:, 8 * k:8 * k + 8] = last[8 * SWAP[k]:8 * SWAP[k] + 8, :].T.astype(BF16)


def panel_kernel_plain(gathered_ref, *rest):
    panel_kernel(gathered_ref, None, *rest)


def chunks_of(value):
    return [value[:, q * 128:q * 128 + 128] for q in range(4)]


def one_shift(chunks, position):
    if position == 0:
        return chunks
    lanes = lane_iota(chunks[0].shape[0])
    sign = 1 if position % 2 == 1 else -1
    if position > 4:
        return [shift_z(chunk, sign, lanes) for chunk in chunks]
    if position > 2:
        return [shift_y(chunk, sign, lanes) for chunk in chunks]
    low = lanes < 64
    rolled = [roll_lanes(chunk, 64) for chunk in chunks]
    if sign > 0:
        return [jnp.where(low, rolled[q], rolled[(q + 1) % 4]) for q in range(4)]
    return [jnp.where(low, rolled[(q + 3) % 4], rolled[q]) for q in range(4)]


def span(slice_index, count=1):
    if isinstance(slice_index, int):
        return slice(slice_index * SITES, (slice_index + count) * SITES)
    return pl.ds(pl.multiple_of(slice_index * SITES, SITES), count * SITES)


def slot_of(slot):
    return slice(slot * SITES, (slot + 1) * SITES)


def stack_wide(source, target, index, slot):
    chunks = chunks_of(source[:, span(index)])
    for position in range(7):
        shifted = one_shift(chunks, position)
        for q in range(4):
            lanes = slice(slot * SITES + q * 128, slot * SITES + q * 128 + 128)
            target[H * position:H * position + H, lanes] = shifted[q]
    target[7 * H:8 * H, slot_of(slot)] = source[:, span(index + 1)]
    target[8 * H:9 * H, slot_of(slot)] = source[:, span(index - 1)]


def stack_thin(source, target, index, slot):
    chunks = chunks_of(source[:, span(index)])
    ahead = chunks_of(source[:, span(index + 1)])
    behind = chunks_of(source[:, span(index - 1)])
    columns = [one_shift(chunks, position) for position in range(7)] + [ahead, behind]
    for q in range(4):
        lanes = slice(slot * SITES + q * 128, slot * SITES + q * 128 + 128)
        target[0:72, lanes] = jnp.concatenate([column[q] for column in columns], axis=0).astype(BF16)


def one_minus_square(value):
    value = value.astype(F32)
    return 1.0 - value * value


def conv_kernel(
    split, fm_ref, below_ref, above_ref, fbelow_ref, fabove_ref, loops_ref,
    p1_ref, p2_ref, p3_ref, p4_ref, b2_ref, b3_ref, b4_ref,
    coeff_ref, grads_ref,
    feats, mixed, h1, h2, h3, parts, lasts, g3, g2, g1, wide, thin, packed,
):
    row8 = lax.broadcasted_iota(jnp.int32, (8, SITES), 0)
    loop_re = jnp.concatenate([loops_ref[0, q:q + 1, :] for q in range(4)], axis=1)
    loop_im = jnp.concatenate([loops_ref[1, q:q + 1, :] for q in range(4)], axis=1)
    loops = jnp.where(row8 == 6, loop_re, jnp.where(row8 == 7, loop_im, 0.0))
    loops = loops.astype(BF16).astype(F32)
    for j in range(3):
        feats[:, span(j)] = fbelow_ref[j].astype(F32) + loops
        feats[:, span(15 + j)] = fabove_ref[j].astype(F32) + loops
    for base, ref in ((3, below_ref), (7, fm_ref), (11, above_ref)):
        for j in range(4):
            value = ref[j].astype(F32)
            feats[:, span(base + j)] = value[0:8] + loops
            mixed[:, span(base + j)] = value[8:16]

    def wide_dot(source, weights, index, slot):
        stack_wide(source, wide, index, slot)
        return jnp.dot(weights[...], wide[:, slot_of(slot)], preferred_element_type=F32)

    def thin_dot(source, weights, index, slot):
        stack_thin(source, thin, index, slot)
        return jnp.dot(weights[...], thin[:, slot_of(slot)], preferred_element_type=F32)

    for index in range(1, 17):
        h1[:, span(index)] = jnp.tanh(thin_dot(feats, p1_ref, index, index % 4)).astype(BF16)
    for index in range(2, 16):
        h2[:, span(index)] = jnp.tanh(wide_dot(h1, p2_ref, index, index % 4)).astype(BF16)
    for index in range(3, 15):
        out = jnp.tanh(wide_dot(h2, p3_ref, index, index % 4)).astype(BF16)
        h3[:, span(index)] = out
        taps = jnp.dot(p4_ref[...], out, preferred_element_type=F32)
        acc = None
        for position in range(7):
            shifted = one_shift(chunks_of(taps[8 * position:8 * position + 8]), position)
            acc = shifted if acc is None else [a + b for a, b in zip(acc, shifted)]
        parts[0, :, span(index)] = jnp.concatenate(acc, axis=1)
        parts[1, :, span(index)] = taps[56:64]
        parts[2, :, span(index)] = taps[64:72]

    for index in range(4, 14):
        coeff = jnp.tanh(parts[0, :, span(index)] + parts[1, :, span(index + 1)] + parts[2, :, span(index - 1)])
        blend = mixed[:, span(index)]
        value = (blend + coeff * pltpu.roll(blend, 4, 0)) * (1.0 - coeff * coeff)
        lasts[:, span(index)] = jnp.where(row8 < 4, value, 0.0).astype(BF16).astype(F32)
        if 7 <= index < 11:
            coeff_ref[index - 7] = coeff

    own = span(7, 4)
    contract = (((1,), (1,)), ((), ()))
    for index in (5, 6, 11, 12, 7, 8, 9, 10):
        out = thin_dot(lasts, b4_ref, index, (index + 1) % 4)
        g3[:, span(index)] = (out * one_minus_square(h3[:, span(index)])).astype(BF16)
    grad_last = lax.dot_general(thin[...], h3[:, own], contract, preferred_element_type=F32)
    for index in (6, 11, 7, 8, 9, 10):
        out = wide_dot(g3, b3_ref, index, (index + 1) % 4)
        g2[:, span(index)] = (out * one_minus_square(h2[:, span(index)])).astype(BF16)
    grad_third = lax.dot_general(wide[...], h2[:, own], contract, preferred_element_type=F32)
    for index in (7, 8, 9, 10):
        out = wide_dot(g2, b2_ref, index, (index + 1) % 4)
        g1[:, slot_of(index - 7)] = (out * one_minus_square(h1[:, span(index)])).astype(BF16)
    grad_second = lax.dot_general(wide[...], h1[:, own], contract, preferred_element_type=F32)
    for index in (7, 8, 9, 10):
        stack_thin(feats, thin, index, index - 7)
    grad_first = lax.dot_general(g1[...], thin[...], contract, preferred_element_type=F32)

    spread, keep = selectors()
    ordered = jnp.concatenate([grad_last[8 * SWAP[k]:8 * SWAP[k] + 8] for k in range(TAPS)], axis=0)
    broad = jnp.dot(spread, ordered.astype(BF16), preferred_element_type=F32)
    broad = jnp.where(keep, broad, 0.0).astype(BF16)
    place = (
        lax.broadcasted_iota(jnp.int32, (H, LANES), 1) == 104 + lax.broadcasted_iota(jnp.int32, (H, LANES), 0) % 4
    ).astype(F32).astype(BF16)
    packed[...] = jnp.dot(broad, place, preferred_element_type=F32)
    for k in range(TAPS):
        rows = slice(H * k, H * k + H)
        back = slice(H * SWAP[k], H * SWAP[k] + H)
        packed[rows, 0:48] = grad_second[back]
        packed[rows, 48:96] = grad_third[back]
        packed[rows, 96:104] = grad_first[:, 8 * k:8 * k + 8]
    if split:
        for d in range(16):
            grads_ref[d] = packed[27 * d:27 * d + 27, :].astype(BF16)
    else:
        grads_ref[...] = packed[...].astype(BF16)


def update_kernel(links_ref, w1_ref, w2_ref, coeff_ref, out_ref, factors):
    for mu in range(4):
        for t in range(4):
            for c in range(2):
                factors[mu, c, t:t + 1, :] = coeff_ref[t, mu:mu + 1, c * 128:c * 128 + 128]
                factors[mu, c, 4 + t:5 + t, :] = coeff_ref[t, mu:mu + 1, 256 + c * 128:384 + c * 128]

    def body(mu, carry):
        factor = [factors[mu, c] for c in range(2)]
        half = [0.5 * value * value for value in factor]
        for e, (part, i, j) in enumerate(ENTRIES):
            pair = pack_pair(links_ref[mu, part, i, j, 0])
            new = [pair[c] + factor[c] * w1_ref[mu, e, c] + half[c] * w2_ref[mu, e, c] for c in range(2)]
            out_ref[mu, part, i, j, 0] = jnp.concatenate(
                [new[0][0:4], new[1][0:4], new[0][4:8], new[1][4:8]], axis=1
            )
        return carry

    lax.fori_loop(0, 4, body, 0)


def sum_kernel(widths, parts_ref, first_ref, second_ref, third_ref, last_ref):
    value = parts_ref[0].astype(F32)
    for d in range(1, parts_ref.shape[0]):
        value = value + parts_ref[d].astype(F32)
    offset = 0
    for ref, width in zip((second_ref, third_ref, first_ref, last_ref), widths):
        for r in range(27):
            ref[:, width * r:width * r + width] = value[r:r + 1, offset:offset + width]
        offset += width


def call(body, outs, scratch, smem=(), count=0, cost=None):
    specs = {}
    if smem:
        specs["in_specs"] = [
            pl.BlockSpec(memory_space=pltpu.SMEM if i in smem else pltpu.VMEM) for i in range(count)
        ]
    return pl.pallas_call(
        body,
        out_shape=[jax.ShapeDtypeStruct(shape, dtype) for shape, dtype in outs],
        scratch_shapes=[pltpu.VMEM(shape, dtype) for shape, dtype in scratch],
        compiler_params=pltpu.CompilerParams(vmem_limit_bytes=LIMIT),
        cost_estimate=cost,
        **specs,
    )


def on_device(links, cotangent, parity, link_subset, w_first, w_second, w_third, w_last):
    count = lax.axis_size("tm")

    def send(value, distance):
        return lax.ppermute(value, "tm", [(i, (i + distance) % count) for i in range(count)])

    widths = (768 // count, 768 // count, 128 // count, 64 // count)
    field = ((4, 18, 2, 8, LANES), F32)
    space = ((3, 18, 2, 8, LANES), F32)
    edge_rows = ((66, SITES), BF16)
    up, down, dense, edges, staples, slab = call(
        face_kernel,
        [edge_rows, edge_rows, field, space, space, ((12, 4, LANES), F32)],
        [space, ((66, 4, LANES), F32)],
    )(links)
    up = send(up, 1)
    down = send(down, -1)
    cots, rows, forces, sums = call(
        space_kernel,
        [field, ((4, 4, 16, LANES), F32), ((4, 9, 2, 8, LANES), F32), space],
        [((3, 3, 18, 2, 8, LANES), F32), ((3, 3, 18, 2, 8, LANES), F32)],
        cost=pl.CostEstimate(flops=4_000_000_000, bytes_accessed=16_000_000, transcendentals=0),
    )(dense, cotangent, staples)
    core = (lax.axis_index("tm") % 2).astype(jnp.int32)[None]
    (block,) = call(
        functools.partial(block_kernel, widths),
        [((count, BLOCKROWS, LANES), BF16)],
        [((12, 4, LANES), F32), ((BLOCKROWS, LANES), F32)],
        smem=(0,), count=8,
    )(core, up, down, slab, w_first[None], w_second[None], w_third[None], w_last[None])
    gathered = lax.all_to_all(block, "tm", split_axis=0, concat_axis=0, tiled=True)
    fm, fup, fdown, applied, twice = call(
        time_kernel,
        [((4, 16, SITES), BF16), ((3, 8, SITES), BF16), ((3, 8, SITES), BF16), field, field],
        [
            space, space, field, ((66, 4, LANES), F32), ((66, 4, LANES), F32),
            ((4, 9, 2, 8, LANES), F32), ((4, 4, 16, LANES), F32),
        ],
        smem=(4, 5), count=10,
    )(dense, cots, up, down, parity, link_subset, edges, rows, forces, sums)
    below = send(fm, 1)
    above = send(fm, -1)
    fbelow = send(fup, 2)
    fabove = send(fdown, -2)

    panel_outs = [
        ((2, 4, LANES), F32), ((H, 72), BF16), ((H, 432), BF16), ((H, 432), BF16), ((72, H), BF16),
        ((H, 432), BF16), ((H, 432), BF16), ((H, 72), BF16),
    ]
    panel_scratch = [((432, LANES), F32)]
    if count == 16:
        loops, p1, p2, p3, p4, b2, b3, b4 = call(panel_kernel_plain, panel_outs, panel_scratch)(gathered)
    else:
        pieces = []
        offset = 0
        for width, full in zip(widths, (48, 48, 8, 4)):
            piece = gathered[:, SLABROWS:SLABROWS + 27, offset:offset + width]
            pieces.append(piece.reshape(432, full))
            offset += width
        pieces.append(jnp.zeros((432, 20), BF16))
        loops, p1, p2, p3, p4, b2, b3, b4 = call(panel_kernel, panel_outs, panel_scratch)(
            gathered, jnp.concatenate(pieces, axis=1)
        )

    window = 18 * SITES
    coeff, grads = call(
        functools.partial(conv_kernel, count == 16),
        [((4, 8, SITES), F32), ((16, 27, LANES) if count == 16 else (432, LANES), BF16)],
        [
            ((8, window), F32), ((8, window), F32), ((H, window), BF16), ((H, window), BF16), ((H, window), BF16),
            ((3, 8, window), F32), ((8, window), F32), ((H, window), BF16), ((H, window), BF16), ((H, 4 * SITES), BF16),
            ((432, 4 * SITES), BF16), ((72, 4 * SITES), BF16), ((432, LANES), F32),
        ],
    )(fm, below, above, fbelow, fabove, loops, p1, p2, p3, p4, b2, b3, b4)
    if count != 16:
        offset = 0
        pieces = []
        for width, full in zip(widths, (48, 48, 8, 4)):
            pieces.append(grads[:, offset:offset + full].reshape(count, 27, width))
            offset += full
        grads = jnp.concatenate(pieces, axis=2)
    grads = lax.all_to_all(grads, "tm", split_axis=0, concat_axis=0, tiled=True)
    (new_links,) = call(
        update_kernel, [(links.shape, F32)], [((4, 2, 8, LANES), F32)]
    )(links, applied, twice, coeff)
    grad_first, grad_second, grad_third, grad_last = call(
        functools.partial(sum_kernel, widths),
        [((1, 27 * width), F32) for width in (widths[2], widths[0], widths[1], widths[3])],
        [],
    )(grads)
    return (new_links, grad_first, grad_second, grad_third, grad_last)


def solution(mesh):
    placed = (
        P(None, None, None, None, "groups", "tm", None),
        P(None, None, None, None, "groups", "tm", None),
        P("groups", "tm"),
        P("groups", "tm"),
        P("tm"),
        P("tm"),
        P("tm"),
        P("tm"),
    )
    return jax.shard_map(
        on_device,
        mesh=mesh,
        in_specs=placed,
        out_specs=(
            P(None, None, None, None, "groups", "tm", None),
            P("groups", "tm"),
            P("groups", "tm"),
            P("groups", "tm"),
            P("groups", "tm"),
        ),
        check_vma=False,
    )
```

```python
import functools

import jax
import jax.numpy as jnp
from jax import lax
from jax.experimental import pallas as pl
from jax.experimental.pallas import tpu as pltpu
from jax.sharding import PartitionSpec as P

F32 = jnp.float32
BF16 = jnp.bfloat16
TAPS = 9
H = 48
LANES = 128
SITES = 512
PAIRS = ((0, 1), (0, 2), (0, 3), (1, 2), (1, 3), (2, 3))
SWAP = (0, 2, 1, 4, 3, 6, 5, 8, 7)
ENTRIES = tuple((c, i, j) for c in range(2) for i in range(3) for j in range(3))
SLABROWS = 24
BLOCKROWS = 64
LIMIT = 40 * 1024 * 1024


def lane_iota(rows):
    return lax.broadcasted_iota(jnp.int32, (rows, LANES), 1)


def row_iota():
    return lax.broadcasted_iota(jnp.int32, (8, LANES), 0)


def roll_lanes(value, amount):
    return pltpu.roll(value, amount % LANES, 1)


def shift_z(chunk, sign, lanes):
    z = lanes % 8
    if sign > 0:
        return jnp.where(z == 7, roll_lanes(chunk, 7), roll_lanes(chunk, -1))
    return jnp.where(z == 0, roll_lanes(chunk, -7), roll_lanes(chunk, 1))


def shift_y(chunk, sign, lanes):
    y = lanes // 8 % 8
    if sign > 0:
        return jnp.where(y == 7, roll_lanes(chunk, 56), roll_lanes(chunk, -8))
    return jnp.where(y == 0, roll_lanes(chunk, -56), roll_lanes(chunk, 8))


def dense_shift(pair, axis, sign):
    lanes = lane_iota(8)
    if axis == 2:
        return [shift_z(chunk, sign, lanes) for chunk in pair]
    if axis == 1:
        return [shift_y(chunk, sign, lanes) for chunk in pair]
    low = lanes < 64
    first, second = [roll_lanes(chunk, 64) for chunk in pair]
    if sign > 0:
        return [jnp.where(low, first, second), jnp.where(low, second, pltpu.roll(first, 4, 0))]
    return [jnp.where(low, pltpu.roll(second, 4, 0), first), jnp.where(low, first, second)]


def pack_pair(value):
    return [
        jnp.concatenate([value[:, c * 128:c * 128 + 128], value[:, 256 + c * 128:384 + c * 128]], axis=0)
        for c in range(2)
    ]


def halo_pair(ref, index):
    top = row_iota() < 4
    pair = []
    for c in range(2):
        low = jnp.broadcast_to(ref[index, c:c + 1, :], (8, LANES))
        high = jnp.broadcast_to(ref[index, 2 + c:3 + c, :], (8, LANES))
        pair.append(jnp.where(top, low, high))
    return pair


def load_matrix(read):
    real = [[read(3 * i + j) for j in range(3)] for i in range(3)]
    imag = [[read(9 + 3 * i + j) for j in range(3)] for i in range(3)]
    return (real, imag, 1)


def dagger(matrix):
    real, imag, sign = matrix
    return (
        [[real[j][i] for j in range(3)] for i in range(3)],
        [[imag[j][i] for j in range(3)] for i in range(3)],
        -sign,
    )


def total(terms, signs):
    value = None
    for term, sign in zip(terms, signs):
        if value is None:
            value = term if sign > 0 else -term
        else:
            value = value + term if sign > 0 else value - term
    return value


def mat_mul(left, right):
    lr, li, ls = left
    rr, ri, rs = right
    same = ls == rs
    height = len(lr)
    real = [[None] * 3 for _ in range(height)]
    imag = [[None] * 3 for _ in range(height)]
    for i in range(height):
        for j in range(3):
            real[i][j] = total(
                [lr[i][k] * rr[k][j] for k in range(3)] + [li[i][k] * ri[k][j] for k in range(3)],
                [1, 1, 1] + [-1 if same else 1] * 3,
            )
            imag[i][j] = total(
                [lr[i][k] * ri[k][j] for k in range(3)] + [li[i][k] * rr[k][j] for k in range(3)],
                [1, 1, 1] + [1 if same else -1] * 3,
            )
    return (real, imag, ls if same else rs)


def imag_of(matrix, i, j):
    return matrix[1][i][j] if matrix[2] > 0 else -matrix[1][i][j]


def store_matrix(matrix, write):
    for i in range(3):
        for j in range(3):
            write(3 * i + j, matrix[0][i][j])
            write(9 + 3 * i + j, imag_of(matrix, i, j))


def two_rows(read):
    real = [[read(3 * i + j) for j in range(3)] for i in range(2)]
    imag = [[read(6 + 3 * i + j) for j in range(3)] for i in range(2)]
    return (real, imag, 1)


def store_rows(matrix, write):
    for i in range(2):
        for j in range(3):
            write(3 * i + j, matrix[0][i][j])
            write(6 + 3 * i + j, imag_of(matrix, i, j))


def special(matrix):
    real, imag, _ = matrix
    last_r, last_i = [], []
    for k in range(3):
        i, j = (k + 1) % 3, (k + 2) % 3
        last_r.append(
            (real[0][i] * real[1][j] - imag[0][i] * imag[1][j])
            - (real[0][j] * real[1][i] - imag[0][j] * imag[1][i])
        )
        last_i.append(
            (real[0][j] * imag[1][i] + imag[0][j] * real[1][i])
            - (real[0][i] * imag[1][j] + imag[0][i] * real[1][j])
        )
    return (real + [last_r], imag + [last_i], 1)


def anti_parts(matrix):
    parts = [2.0 * imag_of(matrix, i, i) for i in range(3)]
    for i, j in ((0, 1), (0, 2), (1, 2)):
        parts.append(matrix[0][i][j] - matrix[0][j][i])
        parts.append(imag_of(matrix, i, j) + imag_of(matrix, j, i))
    return parts


def anti_matrix(parts):
    zero = jnp.zeros_like(parts[0])
    real = [[zero, parts[3], parts[5]], [-parts[3], zero, parts[7]], [-parts[5], -parts[7], zero]]
    imag = [[parts[0], parts[4], parts[6]], [parts[4], parts[1], parts[8]], [parts[6], parts[8], parts[2]]]
    return real, imag


def anti_mul(parts, right):
    real, imag = anti_matrix(parts)
    rr, ri, _ = right
    out_r = [[None] * 3 for _ in range(3)]
    out_i = [[None] * 3 for _ in range(3)]
    for i in range(3):
        for j in range(3):
            value_r = -(imag[i][i] * ri[i][j])
            value_i = imag[i][i] * rr[i][j]
            for k in range(3):
                if k != i:
                    value_r = value_r + real[i][k] * rr[k][j] - imag[i][k] * ri[k][j]
                    value_i = value_i + real[i][k] * ri[k][j] + imag[i][k] * rr[k][j]
            out_r[i][j] = value_r
            out_i[i][j] = value_i
    return (out_r, out_i, 1)


def pack_links(links_ref, dense):
    def body(mu, carry):
        for e, (c, i, j) in enumerate(ENTRIES):
            low, high = pack_pair(links_ref[mu, c, i, j, 0].astype(F32))
            dense[mu, e, 0] = low
            dense[mu, e, 1] = high
        return carry

    lax.fori_loop(0, 4, body, 0)


def face_kernel(links_ref, up_ref, down_ref, dense, edges, staples, slab, moved, rows):
    pack_links(links_ref, dense)

    def shift_body(e, carry):
        pair = [dense[3, e, 0], dense[3, e, 1]]
        for mu in range(3):
            low, high = dense_shift(pair, mu, 1)
            moved[mu, e, 0] = low
            moved[mu, e, 1] = high
        return carry

    lax.fori_loop(0, 18, shift_body, 0)

    def staple_body(step, carry):
        mu = step // 2
        c = step % 2
        u_mu = load_matrix(lambda e: dense[mu, e, c])
        u_t = load_matrix(lambda e: dense[3, e, c])
        edge = mat_mul(u_mu, load_matrix(lambda e: moved[mu, e, c]))

        def write_edge(e, value):
            edges[mu, e, c] = value

        store_matrix(edge, write_edge)

        def write(e, value):
            staples[mu, e, c] = value
            rows[16 + mu * 18 + e, pl.ds(c, 1)] = value[3:4]
            rows[16 + mu * 18 + e, pl.ds(2 + c, 1)] = value[7:8]

        store_matrix(mat_mul(dagger(edge), u_t), write)
        return carry

    lax.fori_loop(0, 6, staple_body, 0)

    def slab_body(c, carry):
        u_t = load_matrix(lambda e: dense[3, e, c])
        ahead = load_matrix(lambda e: pltpu.roll(dense[3, e, c], 7, 0))
        two = mat_mul(u_t, ahead)
        later = tuple(
            [[pltpu.roll(part[i][j], 6, 0) for j in range(3)] for i in range(3)] for part in two[:2]
        ) + (two[2],)
        four = mat_mul((two[0][:2], two[1][:2], two[2]), later)

        def write(e, value):
            slab[e, pl.ds(c, 1)] = value[0:1]
            slab[e, pl.ds(2 + c, 1)] = value[4:5]
            rows[e, pl.ds(c, 1)] = value[0:1]
            rows[e, pl.ds(2 + c, 1)] = value[4:5]

        store_rows(four, write)
        return carry

    lax.fori_loop(0, 2, slab_body, 0)
    for q in range(4):
        up_ref[:, q * 128:q * 128 + 128] = rows[:, q, :].astype(BF16)

    def down_body(e, carry):
        for mu in range(3):
            for c in range(2):
                value = dense[mu, e, c]
                rows[16 + mu * 18 + e, c:c + 1] = value[0:1]
                rows[16 + mu * 18 + e, 2 + c:3 + c] = value[4:5]
        return carry

    lax.fori_loop(0, 18, down_body, 0)
    for q in range(4):
        down_ref[:, q * 128:q * 128 + 128] = rows[:, q, :].astype(BF16)


def block_kernel(
    widths, core_ref, up_ref, down_ref, slab, w1_ref, w2_ref, w3_ref, w4_ref, rows_ref, block_ref, other, block
):
    even = core_ref[0] == 0
    up = up_ref[0:16].astype(F32)
    down = down_ref[0:16].astype(F32)
    for q in range(4):
        lanes = slice(q * 128, q * 128 + 128)
        other[:, q, :] = jnp.where(even, down[0:12, lanes], up[0:12, lanes])
    first = two_rows(lambda e: jnp.where(even, slab[e], other[e]))
    second = special(two_rows(lambda e: jnp.where(even, other[e], slab[e])))

    def write(e, value):
        block[2 * e:2 * e + 2, :] = jnp.where(even, value[0:2], value[2:4])

    store_rows(mat_mul(first, second), write)
    block[SLABROWS:BLOCKROWS] = jnp.zeros((BLOCKROWS - SLABROWS, LANES), F32)
    offset = 0
    for ref, width in zip((w2_ref, w3_ref, w1_ref, w4_ref), widths):
        flat = ref[...].astype(F32)
        for r in range(27):
            block[SLABROWS + r:SLABROWS + r + 1, offset:offset + width] = (
                flat[width * r:width * r + width].reshape(1, width)
            )
        offset += width
    value = block[...].astype(BF16)
    for d in range(block_ref.shape[0]):
        block_ref[d] = value


def put_row(rows, channel, c, value):
    for t in range(4):
        rows[t, c, pl.ds(channel, 1), :] = value[t:t + 1]
        rows[t, 2 + c, pl.ds(channel, 1), :] = value[4 + t:5 + t]


def space_kernel(
    parity_ref, subset_ref, dense, cot_ref, time_staples, cots, rows, forces, sums, gates, moved, staples
):
    pack_links(cot_ref, cots)
    rows[...] = jnp.zeros_like(rows)
    forces[...] = jnp.zeros_like(forces)
    steps = row_iota() % 4
    lanes = lane_iota(8)
    colour = (lanes // 64 + lanes // 8 % 8 + lanes % 8 + steps) % 2
    parity = jnp.zeros_like(steps)
    subset = jnp.zeros_like(steps)
    for t in range(4):
        parity = jnp.where(steps == t, parity_ref[0, t], parity)
        subset = jnp.where(steps == t, subset_ref[0, t], subset)
    for mu in range(4):
        active = jnp.logical_and(colour == parity, jnp.right_shift(subset, mu) % 2 == 1)
        gates[mu] = jnp.where(active, 1.0, 0.0)

    def shift_body(e, carry):
        for nu in range(3):
            pair = [dense[nu, e, 0], dense[nu, e, 1]]
            for mu in range(3):
                if mu != nu:
                    low, high = dense_shift(pair, mu, 1)
                    moved[mu, nu, e, 0] = low
                    moved[mu, nu, e, 1] = high
        return carry

    lax.fori_loop(0, 18, shift_body, 0)

    def plane_body(step, carry):
        plane = step // 2
        c = step % 2
        mu = jnp.where(plane == 2, 1, 0)
        nu = jnp.where(plane == 0, 1, 2)
        u_mu = load_matrix(lambda e: dense[mu, e, c])
        u_nu = load_matrix(lambda e: dense[nu, e, c])
        one = mat_mul(u_mu, load_matrix(lambda e: moved[mu, nu, e, c]))
        two = mat_mul(u_nu, load_matrix(lambda e: moved[nu, mu, e, c]))
        loop = mat_mul(one, dagger(two))
        put_row(rows, jnp.where(plane == 2, 3, plane), c, (loop[0][0][0] + loop[0][1][1] + loop[0][2][2]) / 3.0)
        for e, part in enumerate(anti_parts(loop)):
            forces[mu, e, c] += part
            forces[nu, e, c] -= part

        def write_mu(e, value):
            staples[mu, nu, e, c] = value

        def write_nu(e, value):
            staples[nu, mu, e, c] = value

        store_matrix(mat_mul(dagger(one), u_nu), write_mu)
        store_matrix(mat_mul(dagger(two), u_mu), write_nu)
        return carry

    lax.fori_loop(0, 6, plane_body, 0)

    def lower_body(e, carry):
        for mu in range(3):
            acc = [jnp.where(steps == 0, 0.0, pltpu.roll(time_staples[mu, e, c], 1, 0)) for c in range(2)]
            for nu in range(3):
                if nu != mu:
                    pair = dense_shift([staples[mu, nu, e, 0], staples[mu, nu, e, 1]], nu, -1)
                    acc = [acc[c] + pair[c] for c in range(2)]
            sums[mu, e, 0] = acc[0]
            sums[mu, e, 1] = acc[1]
        return carry

    lax.fori_loop(0, 18, lower_body, 0)


def time_kernel(
    dense, cots, up_ref, down_ref, gates, edges, rows_ref, forces_ref, sums_ref,
    fm_ref, fup_ref, fdown_ref, w1_ref, w2_ref,
    moved, staples, sums, halo_up, halo_down, forces, rows,
):
    for q in range(4):
        halo_up[:, q, :] = up_ref[:, q * 128:q * 128 + 128].astype(F32)
        halo_down[:, q, :] = down_ref[:, q * 128:q * 128 + 128].astype(F32)
    rows[...] = rows_ref[...]
    forces[...] = forces_ref[...]
    steps = row_iota() % 4

    def shift_body(e, carry):
        for nu in range(3):
            halo = halo_pair(halo_down, 16 + nu * 18 + e)
            below = halo_pair(halo_up, 16 + nu * 18 + e)
            for c in range(2):
                moved[nu, e, c] = jnp.where(steps == 3, halo[c], pltpu.roll(dense[nu, e, c], 7, 0))
                sums[nu, e, c] = sums_ref[nu, e, c] + jnp.where(steps == 0, below[c], 0.0)
        return carry

    lax.fori_loop(0, 18, shift_body, 0)

    def plane_body(step, carry):
        mu = step // 2
        c = step % 2
        one = load_matrix(lambda e: edges[mu, e, c])
        two = mat_mul(load_matrix(lambda e: dense[3, e, c]), load_matrix(lambda e: moved[mu, e, c]))
        loop = mat_mul(one, dagger(two))
        put_row(rows, jnp.where(mu == 0, 2, mu + 3), c, (loop[0][0][0] + loop[0][1][1] + loop[0][2][2]) / 3.0)
        for e, part in enumerate(anti_parts(loop)):
            forces[mu, e, c] += part
            forces[3, e, c] -= part

        def write(e, value):
            staples[mu, e, c] = value

        store_matrix(mat_mul(dagger(two), load_matrix(lambda e: dense[mu, e, c])), write)
        return carry

    lax.fori_loop(0, 6, plane_body, 0)

    def lower_body(e, carry):
        acc = None
        for mu in range(3):
            pair = dense_shift([staples[mu, e, 0], staples[mu, e, 1]], mu, -1)
            acc = pair if acc is None else [acc[c] + pair[c] for c in range(2)]
        sums[3, e, 0] = acc[0]
        sums[3, e, 1] = acc[1]
        return carry

    lax.fori_loop(0, 18, lower_body, 0)

    def force_body(step, carry):
        mu = step // 2
        c = step % 2
        current = load_matrix(lambda e: dense[mu, e, c])
        omega = mat_mul(current, load_matrix(lambda e: sums[mu, e, c]))
        parts = [part + forces[mu, e, c] for e, part in enumerate(anti_parts(omega))]
        mean = (parts[0] + parts[1] + parts[2]) * (1.0 / 3.0)
        parts = [parts[e] - mean if e < 3 else parts[e] for e in range(9)]
        parts = [part * (1.0 / 12.0) for part in parts]
        applied = anti_mul(parts, current)
        twice = anti_mul(parts, applied)
        gate = gates[mu]
        slope = jnp.zeros_like(gate)
        curve = jnp.zeros_like(gate)
        for e, (part, i, j) in enumerate(ENTRIES):
            weight = cots[mu, e, c]
            slope = slope + weight * applied[part][i][j]
            curve = curve + weight * twice[part][i][j]
            w1_ref[mu, e, c] = gate * applied[part][i][j]
            w2_ref[mu, e, c] = gate * twice[part][i][j]
        put_row(rows, 8 + mu, c, gate * slope)
        put_row(rows, 12 + mu, c, gate * curve)
        return carry

    lax.fori_loop(0, 8, force_body, 0)
    for t in range(4):
        for q in range(4):
            value = rows[t, q]
            fm_ref[t, :, q * 128:q * 128 + 128] = value.astype(BF16)
            if t > 0:
                fup_ref[t - 1, :, q * 128:q * 128 + 128] = value[0:8].astype(BF16)
            if t < 3:
                fdown_ref[t, :, q * 128:q * 128 + 128] = value[0:8].astype(BF16)


def selectors():
    row = lax.broadcasted_iota(jnp.int32, (432, 72), 0)
    col = lax.broadcasted_iota(jnp.int32, (432, 72), 1)
    group = row // 12
    spread = (group // 4 * 8 + group % 4 == col).astype(F32).astype(BF16)
    keep = (
        lax.broadcasted_iota(jnp.int32, (432, H), 1) // 4 == lax.broadcasted_iota(jnp.int32, (432, H), 0) % 12
    )
    return spread, keep


def panel_kernel(gathered_ref, weights_ref, loops_ref, p1_ref, p2_ref, p3_ref, p4_ref, b2_ref, b3_ref, b4_ref, weights):
    count = gathered_ref.shape[0]

    def read(chip):
        low = gathered_ref[2 * chip].astype(F32)
        high = gathered_ref[2 * chip + 1].astype(F32)
        return special(
            two_rows(lambda e: jnp.concatenate([low[2 * e:2 * e + 2], high[2 * e:2 * e + 2]], axis=0))
        )

    def flat(matrix):
        return tuple(matrix[0][i][j] for i in range(3) for j in range(3)) + tuple(
            imag_of(matrix, i, j) for i in range(3) for j in range(3)
        )

    def chain(chip, state):
        return flat(mat_mul(load_matrix(lambda e: state[e]), read(chip)))

    state = lax.fori_loop(1, count // 2, chain, flat(read(0)))
    loops_ref[0] = (state[0] + state[4] + state[8]) / 3.0
    loops_ref[1] = (state[9] + state[13] + state[17]) / 3.0

    if weights_ref is None:
        for d in range(count):
            block = gathered_ref[d].astype(F32)
            weights[27 * d:27 * d + 27, :] = block[SLABROWS:SLABROWS + 27]
    else:
        weights[...] = weights_ref[...].astype(F32)
    for k in range(TAPS):
        rows = slice(H * k, H * k + H)
        back = slice(H * SWAP[k], H * SWAP[k] + H)
        p2_ref[:, rows] = weights[rows, 0:48].astype(BF16)
        p3_ref[:, rows] = weights[rows, 48:96].astype(BF16)
        p1_ref[:, 8 * k:8 * k + 8] = weights[rows, 96:104].astype(BF16)
        turned = weights[back, :].T
        b2_ref[:, rows] = turned[0:48].astype(BF16)
        b3_ref[:, rows] = turned[48:96].astype(BF16)
    spread, keep = selectors()
    place = (
        lax.broadcasted_iota(jnp.int32, (LANES, H), 0) == 104 + lax.broadcasted_iota(jnp.int32, (LANES, H), 1) % 4
    ).astype(F32).astype(BF16)
    wide = jnp.dot(weights[...].astype(BF16), place, preferred_element_type=F32)
    wide = jnp.where(keep, wide, 0.0).astype(BF16)
    last = lax.dot_general(spread, wide, (((0,), (0,)), ((), ())), preferred_element_type=F32)
    p4_ref[...] = last.astype(BF16)
    for k in range(TAPS):
        b4_ref[:, 8 * k:8 * k + 8] = last[8 * SWAP[k]:8 * SWAP[k] + 8, :].T.astype(BF16)


def panel_kernel_plain(gathered_ref, *rest):
    panel_kernel(gathered_ref, None, *rest)


def chunks_of(value):
    return [value[:, q * 128:q * 128 + 128] for q in range(4)]


def one_shift(chunks, position):
    if position == 0:
        return chunks
    lanes = lane_iota(chunks[0].shape[0])
    sign = 1 if position % 2 == 1 else -1
    if position > 4:
        return [shift_z(chunk, sign, lanes) for chunk in chunks]
    if position > 2:
        return [shift_y(chunk, sign, lanes) for chunk in chunks]
    low = lanes < 64
    rolled = [roll_lanes(chunk, 64) for chunk in chunks]
    if sign > 0:
        return [jnp.where(low, rolled[q], rolled[(q + 1) % 4]) for q in range(4)]
    return [jnp.where(low, rolled[(q + 3) % 4], rolled[q]) for q in range(4)]


def span(slice_index, count=1):
    if isinstance(slice_index, int):
        return slice(slice_index * SITES, (slice_index + count) * SITES)
    return pl.ds(pl.multiple_of(slice_index * SITES, SITES), count * SITES)


def slot_of(slot):
    return slice(slot * SITES, (slot + 1) * SITES)


def stack_wide(source, target, index, slot):
    chunks = chunks_of(source[:, span(index)])
    for position in range(7):
        shifted = one_shift(chunks, position)
        for q in range(4):
            lanes = slice(slot * SITES + q * 128, slot * SITES + q * 128 + 128)
            target[H * position:H * position + H, lanes] = shifted[q]
    target[7 * H:8 * H, slot_of(slot)] = source[:, span(index + 1)]
    target[8 * H:9 * H, slot_of(slot)] = source[:, span(index - 1)]


def stack_thin(source, target, index, slot):
    chunks = chunks_of(source[:, span(index)])
    ahead = chunks_of(source[:, span(index + 1)])
    behind = chunks_of(source[:, span(index - 1)])
    columns = [one_shift(chunks, position) for position in range(7)] + [ahead, behind]
    for q in range(4):
        lanes = slice(slot * SITES + q * 128, slot * SITES + q * 128 + 128)
        target[0:72, lanes] = jnp.concatenate([column[q] for column in columns], axis=0).astype(BF16)


def one_minus_square(value):
    value = value.astype(F32)
    return 1.0 - value * value


def conv_kernel(
    split, fm_ref, below_ref, above_ref, fbelow_ref, fabove_ref, loops_ref,
    p1_ref, p2_ref, p3_ref, p4_ref, b2_ref, b3_ref, b4_ref,
    coeff_ref, grads_ref,
    feats, mixed, h1, h2, h3, parts, lasts, g3, g2, g1, wide, thin, packed,
):
    row8 = lax.broadcasted_iota(jnp.int32, (8, SITES), 0)
    loop_re = jnp.concatenate([loops_ref[0, q:q + 1, :] for q in range(4)], axis=1)
    loop_im = jnp.concatenate([loops_ref[1, q:q + 1, :] for q in range(4)], axis=1)
    loops = jnp.where(row8 == 6, loop_re, jnp.where(row8 == 7, loop_im, 0.0))
    loops = loops.astype(BF16).astype(F32)
    for j in range(3):
        feats[:, span(j)] = fbelow_ref[j].astype(F32) + loops
        feats[:, span(15 + j)] = fabove_ref[j].astype(F32) + loops
    for base, ref in ((3, below_ref), (7, fm_ref), (11, above_ref)):
        for j in range(4):
            value = ref[j].astype(F32)
            feats[:, span(base + j)] = value[0:8] + loops
            mixed[:, span(base + j)] = value[8:16]

    def wide_dot(source, weights, index, slot):
        stack_wide(source, wide, index, slot)
        return jnp.dot(weights[...], wide[:, slot_of(slot)], preferred_element_type=F32)

    def thin_dot(source, weights, index, slot):
        stack_thin(source, thin, index, slot)
        return jnp.dot(weights[...], thin[:, slot_of(slot)], preferred_element_type=F32)

    for index in range(1, 17):
        h1[:, span(index)] = jnp.tanh(thin_dot(feats, p1_ref, index, index % 4)).astype(BF16)
    for index in range(2, 16):
        h2[:, span(index)] = jnp.tanh(wide_dot(h1, p2_ref, index, index % 4)).astype(BF16)
    for index in range(3, 15):
        out = jnp.tanh(wide_dot(h2, p3_ref, index, index % 4)).astype(BF16)
        h3[:, span(index)] = out
        taps = jnp.dot(p4_ref[...], out, preferred_element_type=F32)
        acc = None
        for position in range(7):
            shifted = one_shift(chunks_of(taps[8 * position:8 * position + 8]), position)
            acc = shifted if acc is None else [a + b for a, b in zip(acc, shifted)]
        parts[0, :, span(index)] = jnp.concatenate(acc, axis=1)
        parts[1, :, span(index)] = taps[56:64]
        parts[2, :, span(index)] = taps[64:72]

    for index in range(4, 14):
        coeff = jnp.tanh(parts[0, :, span(index)] + parts[1, :, span(index + 1)] + parts[2, :, span(index - 1)])
        blend = mixed[:, span(index)]
        value = (blend + coeff * pltpu.roll(blend, 4, 0)) * (1.0 - coeff * coeff)
        lasts[:, span(index)] = jnp.where(row8 < 4, value, 0.0).astype(BF16).astype(F32)
        if 7 <= index < 11:
            coeff_ref[index - 7] = coeff

    own = span(7, 4)
    contract = (((1,), (1,)), ((), ()))
    for index in (5, 6, 11, 12, 7, 8, 9, 10):
        out = thin_dot(lasts, b4_ref, index, (index + 1) % 4)
        g3[:, span(index)] = (out * one_minus_square(h3[:, span(index)])).astype(BF16)
    grad_last = lax.dot_general(thin[...], h3[:, own], contract, preferred_element_type=F32)
    for index in (6, 11, 7, 8, 9, 10):
        out = wide_dot(g3, b3_ref, index, (index + 1) % 4)
        g2[:, span(index)] = (out * one_minus_square(h2[:, span(index)])).astype(BF16)
    grad_third = lax.dot_general(wide[...], h2[:, own], contract, preferred_element_type=F32)
    for index in (7, 8, 9, 10):
        out = wide_dot(g2, b2_ref, index, (index + 1) % 4)
        g1[:, slot_of(index - 7)] = (out * one_minus_square(h1[:, span(index)])).astype(BF16)
    grad_second = lax.dot_general(wide[...], h1[:, own], contract, preferred_element_type=F32)
    for index in (7, 8, 9, 10):
        stack_thin(feats, thin, index, index - 7)
    grad_first = lax.dot_general(g1[...], thin[...], contract, preferred_element_type=F32)

    spread, keep = selectors()
    ordered = jnp.concatenate([grad_last[8 * SWAP[k]:8 * SWAP[k] + 8] for k in range(TAPS)], axis=0)
    broad = jnp.dot(spread, ordered.astype(BF16), preferred_element_type=F32)
    broad = jnp.where(keep, broad, 0.0).astype(BF16)
    place = (
        lax.broadcasted_iota(jnp.int32, (H, LANES), 1) == 104 + lax.broadcasted_iota(jnp.int32, (H, LANES), 0) % 4
    ).astype(F32).astype(BF16)
    packed[...] = jnp.dot(broad, place, preferred_element_type=F32)
    for k in range(TAPS):
        rows = slice(H * k, H * k + H)
        back = slice(H * SWAP[k], H * SWAP[k] + H)
        packed[rows, 0:48] = grad_second[back]
        packed[rows, 48:96] = grad_third[back]
        packed[rows, 96:104] = grad_first[:, 8 * k:8 * k + 8]
    if split:
        for d in range(16):
            grads_ref[d] = packed[27 * d:27 * d + 27, :].astype(BF16)
    else:
        grads_ref[...] = packed[...].astype(BF16)


def update_kernel(dense, w1_ref, w2_ref, coeff_ref, out_ref, factors):
    for mu in range(4):
        for t in range(4):
            for c in range(2):
                factors[mu, c, t:t + 1, :] = coeff_ref[t, mu:mu + 1, c * 128:c * 128 + 128]
                factors[mu, c, 4 + t:5 + t, :] = coeff_ref[t, mu:mu + 1, 256 + c * 128:384 + c * 128]

    def body(mu, carry):
        factor = [factors[mu, c] for c in range(2)]
        half = [0.5 * value * value for value in factor]
        for e, (part, i, j) in enumerate(ENTRIES):
            new = [dense[mu, e, c] + factor[c] * w1_ref[mu, e, c] + half[c] * w2_ref[mu, e, c] for c in range(2)]
            out_ref[mu, part, i, j, 0] = jnp.concatenate(
                [new[0][0:4], new[1][0:4], new[0][4:8], new[1][4:8]], axis=1
            )
        return carry

    lax.fori_loop(0, 4, body, 0)


def sum_kernel(widths, parts_ref, first_ref, second_ref, third_ref, last_ref):
    value = parts_ref[0].astype(F32)
    for d in range(1, parts_ref.shape[0]):
        value = value + parts_ref[d].astype(F32)
    offset = 0
    for ref, width in zip((second_ref, third_ref, first_ref, last_ref), widths):
        for r in range(27):
            ref[:, width * r:width * r + width] = value[r:r + 1, offset:offset + width]
        offset += width


def call(body, outs, scratch, places=None, cost=None):
    specs = {}
    if places is not None:
        specs["in_specs"] = [pl.BlockSpec(memory_space=place) for place in places]
    return pl.pallas_call(
        body,
        out_shape=[jax.ShapeDtypeStruct(shape, dtype) for shape, dtype in outs],
        scratch_shapes=[pltpu.VMEM(*item) if isinstance(item, tuple) else item for item in scratch],
        compiler_params=pltpu.CompilerParams(vmem_limit_bytes=LIMIT),
        cost_estimate=cost,
        **specs,
    )


def on_device(links, cotangent, parity, link_subset, w_first, w_second, w_third, w_last):
    count = lax.axis_size("tm")

    def send(value, distance):
        return lax.ppermute(value, "tm", [(i, (i + distance) % count) for i in range(count)])

    widths = (768 // count, 768 // count, 128 // count, 64 // count)
    field = ((4, 18, 2, 8, LANES), F32)
    space = ((3, 18, 2, 8, LANES), F32)
    edge_rows = ((70, SITES), BF16)
    vmem, smem = pltpu.VMEM, pltpu.SMEM
    up, down, dense, edges, staples, slab = call(
        face_kernel,
        [edge_rows, edge_rows, field, space, space, ((12, 4, LANES), F32)],
        [space, ((70, 4, LANES), F32)],
    )(links)
    up = send(up, 1)
    down = send(down, -1)
    cots, rows, forces, sums, gates = call(
        space_kernel,
        [field, ((4, 4, 16, LANES), F32), ((4, 9, 2, 8, LANES), F32), space, ((4, 8, LANES), F32)],
        [((3, 3, 18, 2, 8, LANES), F32), ((3, 3, 18, 2, 8, LANES), F32)],
        places=(smem, smem, vmem, vmem, vmem),
        cost=pl.CostEstimate(flops=4_000_000_000, bytes_accessed=16_000_000, transcendentals=0),
    )(parity, link_subset, dense, cotangent, staples)
    core = (lax.axis_index("tm") % 2).astype(jnp.int32)[None]
    (block,) = call(
        functools.partial(block_kernel, widths),
        [((count, BLOCKROWS, LANES), BF16)],
        [((12, 4, LANES), F32), ((BLOCKROWS, LANES), F32)],
        places=(smem,) + (vmem,) * 8,
    )(core, up, down, slab, w_first, w_second, w_third, w_last, rows)
    gathered = lax.all_to_all(block, "tm", split_axis=0, concat_axis=0, tiled=True)
    fm, fup, fdown, applied, twice = call(
        time_kernel,
        [((4, 16, SITES), BF16), ((3, 8, SITES), BF16), ((3, 8, SITES), BF16), field, field],
        [
            space, space, field, ((70, 4, LANES), F32), ((70, 4, LANES), F32),
            ((4, 9, 2, 8, LANES), F32), ((4, 4, 16, LANES), F32),
        ],
    )(dense, cots, up, down, gates, edges, rows, forces, sums)
    below = send(fm, 1)
    above = send(fm, -1)
    fbelow = send(fup, 2)
    fabove = send(fdown, -2)

    panel_outs = [
        ((2, 4, LANES), F32), ((H, 72), BF16), ((H, 432), BF16), ((H, 432), BF16), ((72, H), BF16),
        ((H, 432), BF16), ((H, 432), BF16), ((H, 72), BF16),
    ]
    panel_scratch = [((432, LANES), F32)]
    if count == 16:
        loops, p1, p2, p3, p4, b2, b3, b4 = call(panel_kernel_plain, panel_outs, panel_scratch)(gathered)
    else:
        pieces = []
        offset = 0
        for width, full in zip(widths, (48, 48, 8, 4)):
            piece = gathered[:, SLABROWS:SLABROWS + 27, offset:offset + width]
            pieces.append(piece.reshape(432, full))
            offset += width
        pieces.append(jnp.zeros((432, 20), BF16))
        loops, p1, p2, p3, p4, b2, b3, b4 = call(panel_kernel, panel_outs, panel_scratch)(
            gathered, jnp.concatenate(pieces, axis=1)
        )

    window = 18 * SITES
    coeff, grads = call(
        functools.partial(conv_kernel, count == 16),
        [((4, 8, SITES), F32), ((16, 27, LANES) if count == 16 else (432, LANES), BF16)],
        [
            ((8, window), F32), ((8, window), F32), ((H, window), BF16), ((H, window), BF16), ((H, window), BF16),
            ((3, 8, window), F32), ((8, window), F32), ((H, window), BF16), ((H, window), BF16), ((H, 4 * SITES), BF16),
            ((432, 4 * SITES), BF16), ((72, 4 * SITES), BF16), ((432, LANES), F32),
        ],
    )(fm, below, above, fbelow, fabove, loops, p1, p2, p3, p4, b2, b3, b4)
    if count != 16:
        offset = 0
        pieces = []
        for width, full in zip(widths, (48, 48, 8, 4)):
            pieces.append(grads[:, offset:offset + full].reshape(count, 27, width))
            offset += full
        grads = jnp.concatenate(pieces, axis=2)
    grads = lax.all_to_all(grads, "tm", split_axis=0, concat_axis=0, tiled=True)
    (new_links,) = call(
        update_kernel, [(links.shape, F32)], [((4, 2, 8, LANES), F32)]
    )(dense, applied, twice, coeff)
    grad_first, grad_second, grad_third, grad_last = call(
        functools.partial(sum_kernel, widths),
        [((1, 27 * width), F32) for width in (widths[2], widths[0], widths[1], widths[3])],
        [],
    )(grads)
    return (new_links, grad_first, grad_second, grad_third, grad_last)


def solution(mesh):
    placed = (
        P(None, None, None, None, "groups", "tm", None),
        P(None, None, None, None, "groups", "tm", None),
        P("groups", "tm"),
        P("groups", "tm"),
        P("tm"),
        P("tm"),
        P("tm"),
        P("tm"),
    )
    return jax.shard_map(
        on_device,
        mesh=mesh,
        in_specs=placed,
        out_specs=(
            P(None, None, None, None, "groups", "tm", None),
            P("groups", "tm"),
            P("groups", "tm"),
            P("groups", "tm"),
            P("groups", "tm"),
        ),
        check_vma=False,
    )
```

```python
import functools

import jax
import jax.numpy as jnp
from jax import lax
from jax.experimental import pallas as pl
from jax.experimental.pallas import tpu as pltpu
from jax.sharding import PartitionSpec as P

F32 = jnp.float32
BF16 = jnp.bfloat16
TAPS = 9
H = 48
LANES = 128
SITES = 512
PAIRS = ((0, 1), (0, 2), (0, 3), (1, 2), (1, 3), (2, 3))
SWAP = (0, 2, 1, 4, 3, 6, 5, 8, 7)
ENTRIES = tuple((c, i, j) for c in range(2) for i in range(3) for j in range(3))
SLABROWS = 24
BLOCKROWS = 64
LIMIT = 8 * 1024 * 1024


def lane_iota(rows):
    return lax.broadcasted_iota(jnp.int32, (rows, LANES), 1)


def row_iota():
    return lax.broadcasted_iota(jnp.int32, (8, LANES), 0)


def roll_lanes(value, amount):
    return pltpu.roll(value, amount % LANES, 1)


def shift_z(chunk, sign, lanes):
    z = lanes % 8
    if sign > 0:
        return jnp.where(z == 7, roll_lanes(chunk, 7), roll_lanes(chunk, -1))
    return jnp.where(z == 0, roll_lanes(chunk, -7), roll_lanes(chunk, 1))


def shift_y(chunk, sign, lanes):
    y = lanes // 8 % 8
    if sign > 0:
        return jnp.where(y == 7, roll_lanes(chunk, 56), roll_lanes(chunk, -8))
    return jnp.where(y == 0, roll_lanes(chunk, -56), roll_lanes(chunk, 8))


def dense_shift(pair, axis, sign):
    lanes = lane_iota(8)
    if axis == 2:
        return [shift_z(chunk, sign, lanes) for chunk in pair]
    if axis == 1:
        return [shift_y(chunk, sign, lanes) for chunk in pair]
    low = lanes < 64
    first, second = [roll_lanes(chunk, 64) for chunk in pair]
    if sign > 0:
        return [jnp.where(low, first, second), jnp.where(low, second, pltpu.roll(first, 4, 0))]
    return [jnp.where(low, pltpu.roll(second, 4, 0), first), jnp.where(low, first, second)]


def pack_pair(value):
    return [
        jnp.concatenate([value[:, c * 128:c * 128 + 128], value[:, 256 + c * 128:384 + c * 128]], axis=0)
        for c in range(2)
    ]


def halo_pair(ref, index):
    top = row_iota() < 4
    pair = []
    for c in range(2):
        low = jnp.broadcast_to(ref[index, c:c + 1, :], (8, LANES))
        high = jnp.broadcast_to(ref[index, 2 + c:3 + c, :], (8, LANES))
        pair.append(jnp.where(top, low, high))
    return pair


def load_matrix(read):
    real = [[read(3 * i + j) for j in range(3)] for i in range(3)]
    imag = [[read(9 + 3 * i + j) for j in range(3)] for i in range(3)]
    return (real, imag, 1)


def dagger(matrix):
    real, imag, sign = matrix
    return (
        [[real[j][i] for j in range(3)] for i in range(3)],
        [[imag[j][i] for j in range(3)] for i in range(3)],
        -sign,
    )


def total(terms, signs):
    value = None
    for term, sign in zip(terms, signs):
        if value is None:
            value = term if sign > 0 else -term
        else:
            value = value + term if sign > 0 else value - term
    return value


def mat_mul(left, right):
    lr, li, ls = left
    rr, ri, rs = right
    same = ls == rs
    height = len(lr)
    real = [[None] * 3 for _ in range(height)]
    imag = [[None] * 3 for _ in range(height)]
    for i in range(height):
        for j in range(3):
            real[i][j] = total(
                [lr[i][k] * rr[k][j] for k in range(3)] + [li[i][k] * ri[k][j] for k in range(3)],
                [1, 1, 1] + [-1 if same else 1] * 3,
            )
            imag[i][j] = total(
                [lr[i][k] * ri[k][j] for k in range(3)] + [li[i][k] * rr[k][j] for k in range(3)],
                [1, 1, 1] + [1 if same else -1] * 3,
            )
    return (real, imag, ls if same else rs)


def imag_of(matrix, i, j):
    return matrix[1][i][j] if matrix[2] > 0 else -matrix[1][i][j]


def store_matrix(matrix, write):
    for i in range(3):
        for j in range(3):
            write(3 * i + j, matrix[0][i][j])
            write(9 + 3 * i + j, imag_of(matrix, i, j))


def two_rows(read):
    real = [[read(3 * i + j) for j in range(3)] for i in range(2)]
    imag = [[read(6 + 3 * i + j) for j in range(3)] for i in range(2)]
    return (real, imag, 1)


def store_rows(matrix, write):
    for i in range(2):
        for j in range(3):
            write(3 * i + j, matrix[0][i][j])
            write(6 + 3 * i + j, imag_of(matrix, i, j))


def special(matrix):
    real, imag, _ = matrix
    last_r, last_i = [], []
    for k in range(3):
        i, j = (k + 1) % 3, (k + 2) % 3
        last_r.append(
            (real[0][i] * real[1][j] - imag[0][i] * imag[1][j])
            - (real[0][j] * real[1][i] - imag[0][j] * imag[1][i])
        )
        last_i.append(
            (real[0][j] * imag[1][i] + imag[0][j] * real[1][i])
            - (real[0][i] * imag[1][j] + imag[0][i] * real[1][j])
        )
    return (real + [last_r], imag + [last_i], 1)


def anti_parts(matrix):
    parts = [2.0 * imag_of(matrix, i, i) for i in range(3)]
    for i, j in ((0, 1), (0, 2), (1, 2)):
        parts.append(matrix[0][i][j] - matrix[0][j][i])
        parts.append(imag_of(matrix, i, j) + imag_of(matrix, j, i))
    return parts


def anti_matrix(parts):
    zero = jnp.zeros_like(parts[0])
    real = [[zero, parts[3], parts[5]], [-parts[3], zero, parts[7]], [-parts[5], -parts[7], zero]]
    imag = [[parts[0], parts[4], parts[6]], [parts[4], parts[1], parts[8]], [parts[6], parts[8], parts[2]]]
    return real, imag


def anti_mul(parts, right):
    real, imag = anti_matrix(parts)
    rr, ri, _ = right
    out_r = [[None] * 3 for _ in range(3)]
    out_i = [[None] * 3 for _ in range(3)]
    for i in range(3):
        for j in range(3):
            value_r = -(imag[i][i] * ri[i][j])
            value_i = imag[i][i] * rr[i][j]
            for k in range(3):
                if k != i:
                    value_r = value_r + real[i][k] * rr[k][j] - imag[i][k] * ri[k][j]
                    value_i = value_i + real[i][k] * ri[k][j] + imag[i][k] * rr[k][j]
            out_r[i][j] = value_r
            out_i[i][j] = value_i
    return (out_r, out_i, 1)


def pack_links(links_ref, dense):
    def body(mu, carry):
        for e, (c, i, j) in enumerate(ENTRIES):
            low, high = pack_pair(links_ref[mu, c, i, j, 0].astype(F32))
            dense[mu, e, 0] = low
            dense[mu, e, 1] = high
        return carry

    lax.fori_loop(0, 4, body, 0)


def face_kernel(links_ref, up_ref, down_ref, dense, edges, staples, slab, moved, rows):
    pack_links(links_ref, dense)

    def shift_body(e, carry):
        pair = [dense[3, e, 0], dense[3, e, 1]]
        for mu in range(3):
            low, high = dense_shift(pair, mu, 1)
            moved[mu, e, 0] = low
            moved[mu, e, 1] = high
        return carry

    lax.fori_loop(0, 18, shift_body, 0)

    def staple_body(step, carry):
        mu = step // 2
        c = step % 2
        u_mu = load_matrix(lambda e: dense[mu, e, c])
        u_t = load_matrix(lambda e: dense[3, e, c])
        edge = mat_mul(u_mu, load_matrix(lambda e: moved[mu, e, c]))

        def write_edge(e, value):
            edges[mu, e, c] = value

        store_matrix(edge, write_edge)

        def write(e, value):
            staples[mu, e, c] = value
            rows[16 + mu * 18 + e, pl.ds(c, 1)] = value[3:4]
            rows[16 + mu * 18 + e, pl.ds(2 + c, 1)] = value[7:8]

        store_matrix(mat_mul(dagger(edge), u_t), write)
        return carry

    lax.fori_loop(0, 6, staple_body, 0)

    def slab_body(c, carry):
        u_t = load_matrix(lambda e: dense[3, e, c])
        ahead = load_matrix(lambda e: pltpu.roll(dense[3, e, c], 7, 0))
        two = mat_mul(u_t, ahead)
        later = tuple(
            [[pltpu.roll(part[i][j], 6, 0) for j in range(3)] for i in range(3)] for part in two[:2]
        ) + (two[2],)
        four = mat_mul((two[0][:2], two[1][:2], two[2]), later)

        def write(e, value):
            slab[e, pl.ds(c, 1)] = value[0:1]
            slab[e, pl.ds(2 + c, 1)] = value[4:5]
            rows[e, pl.ds(c, 1)] = value[0:1]
            rows[e, pl.ds(2 + c, 1)] = value[4:5]

        store_rows(four, write)
        return carry

    lax.fori_loop(0, 2, slab_body, 0)
    for q in range(4):
        up_ref[:, q * 128:q * 128 + 128] = rows[:, q, :].astype(BF16)

    def down_body(e, carry):
        for mu in range(3):
            for c in range(2):
                value = dense[mu, e, c]
                rows[16 + mu * 18 + e, c:c + 1] = value[0:1]
                rows[16 + mu * 18 + e, 2 + c:3 + c] = value[4:5]
        return carry

    lax.fori_loop(0, 18, down_body, 0)
    for q in range(4):
        down_ref[:, q * 128:q * 128 + 128] = rows[:, q, :].astype(BF16)


def block_kernel(
    widths, core_ref, up_ref, down_ref, slab, w1_ref, w2_ref, w3_ref, w4_ref, rows_ref, block_ref, other, block
):
    even = core_ref[0] == 0
    up = up_ref[0:16].astype(F32)
    down = down_ref[0:16].astype(F32)
    for q in range(4):
        lanes = slice(q * 128, q * 128 + 128)
        other[:, q, :] = jnp.where(even, down[0:12, lanes], up[0:12, lanes])
    first = two_rows(lambda e: jnp.where(even, slab[e], other[e]))
    second = special(two_rows(lambda e: jnp.where(even, other[e], slab[e])))

    def write(e, value):
        block[2 * e:2 * e + 2, :] = jnp.where(even, value[0:2], value[2:4])

    store_rows(mat_mul(first, second), write)
    block[SLABROWS:BLOCKROWS] = jnp.zeros((BLOCKROWS - SLABROWS, LANES), F32)
    offset = 0
    for ref, width in zip((w2_ref, w3_ref, w1_ref, w4_ref), widths):
        flat = ref[...].astype(F32)
        for r in range(27):
            block[SLABROWS + r:SLABROWS + r + 1, offset:offset + width] = (
                flat[width * r:width * r + width].reshape(1, width)
            )
        offset += width
    value = block[...].astype(BF16)
    for d in range(block_ref.shape[0]):
        block_ref[d] = value


def put_row(rows, channel, c, value):
    for t in range(4):
        rows[t, c, pl.ds(channel, 1), :] = value[t:t + 1]
        rows[t, 2 + c, pl.ds(channel, 1), :] = value[4 + t:5 + t]


def space_kernel(
    parity_ref, subset_ref, dense, cot_ref, time_staples, cots, rows, forces, sums, gates, moved, staples
):
    pack_links(cot_ref, cots)
    rows[...] = jnp.zeros_like(rows)
    forces[...] = jnp.zeros_like(forces)
    steps = row_iota() % 4
    lanes = lane_iota(8)
    colour = (lanes // 64 + lanes // 8 % 8 + lanes % 8 + steps) % 2
    parity = jnp.zeros_like(steps)
    subset = jnp.zeros_like(steps)
    for t in range(4):
        parity = jnp.where(steps == t, parity_ref[0, t], parity)
        subset = jnp.where(steps == t, subset_ref[0, t], subset)
    for mu in range(4):
        active = jnp.logical_and(colour == parity, jnp.right_shift(subset, mu) % 2 == 1)
        gates[mu] = jnp.where(active, 1.0, 0.0)

    def shift_body(e, carry):
        for nu in range(3):
            pair = [dense[nu, e, 0], dense[nu, e, 1]]
            for mu in range(3):
                if mu != nu:
                    low, high = dense_shift(pair, mu, 1)
                    moved[mu, nu, e, 0] = low
                    moved[mu, nu, e, 1] = high
        return carry

    lax.fori_loop(0, 18, shift_body, 0)

    def plane_body(step, carry):
        plane = step // 2
        c = step % 2
        mu = jnp.where(plane == 2, 1, 0)
        nu = jnp.where(plane == 0, 1, 2)
        u_mu = load_matrix(lambda e: dense[mu, e, c])
        u_nu = load_matrix(lambda e: dense[nu, e, c])
        one = mat_mul(u_mu, load_matrix(lambda e: moved[mu, nu, e, c]))
        two = mat_mul(u_nu, load_matrix(lambda e: moved[nu, mu, e, c]))
        loop = mat_mul(one, dagger(two))
        put_row(rows, jnp.where(plane == 2, 3, plane), c, (loop[0][0][0] + loop[0][1][1] + loop[0][2][2]) / 3.0)
        for e, part in enumerate(anti_parts(loop)):
            forces[mu, e, c] += part
            forces[nu, e, c] -= part

        def write_mu(e, value):
            staples[mu, nu, e, c] = value

        def write_nu(e, value):
            staples[nu, mu, e, c] = value

        store_matrix(mat_mul(dagger(one), u_nu), write_mu)
        store_matrix(mat_mul(dagger(two), u_mu), write_nu)
        return carry

    lax.fori_loop(0, 6, plane_body, 0)

    def lower_body(e, carry):
        for mu in range(3):
            acc = [jnp.where(steps == 0, 0.0, pltpu.roll(time_staples[mu, e, c], 1, 0)) for c in range(2)]
            for nu in range(3):
                if nu != mu:
                    pair = dense_shift([staples[mu, nu, e, 0], staples[mu, nu, e, 1]], nu, -1)
                    acc = [acc[c] + pair[c] for c in range(2)]
            sums[mu, e, 0] = acc[0]
            sums[mu, e, 1] = acc[1]
        return carry

    lax.fori_loop(0, 18, lower_body, 0)


def time_kernel(
    dense, cots, up_ref, down_ref, gates, edges, rows_ref, forces_ref, sums_ref,
    fm_ref, fup_ref, fdown_ref, w1_ref, w2_ref,
    moved, staples, sums, halo_up, halo_down, forces, rows,
):
    for q in range(4):
        halo_up[:, q, :] = up_ref[:, q * 128:q * 128 + 128].astype(F32)
        halo_down[:, q, :] = down_ref[:, q * 128:q * 128 + 128].astype(F32)
    rows[...] = rows_ref[...]
    forces[...] = forces_ref[...]
    steps = row_iota() % 4

    def shift_body(e, carry):
        for nu in range(3):
            halo = halo_pair(halo_down, 16 + nu * 18 + e)
            below = halo_pair(halo_up, 16 + nu * 18 + e)
            for c in range(2):
                moved[nu, e, c] = jnp.where(steps == 3, halo[c], pltpu.roll(dense[nu, e, c], 7, 0))
                sums[nu, e, c] = sums_ref[nu, e, c] + jnp.where(steps == 0, below[c], 0.0)
        return carry

    lax.fori_loop(0, 18, shift_body, 0)

    def plane_body(step, carry):
        mu = step // 2
        c = step % 2
        one = load_matrix(lambda e: edges[mu, e, c])
        two = mat_mul(load_matrix(lambda e: dense[3, e, c]), load_matrix(lambda e: moved[mu, e, c]))
        loop = mat_mul(one, dagger(two))
        put_row(rows, jnp.where(mu == 0, 2, mu + 3), c, (loop[0][0][0] + loop[0][1][1] + loop[0][2][2]) / 3.0)
        for e, part in enumerate(anti_parts(loop)):
            forces[mu, e, c] += part
            forces[3, e, c] -= part

        def write(e, value):
            staples[mu, e, c] = value

        store_matrix(mat_mul(dagger(two), load_matrix(lambda e: dense[mu, e, c])), write)
        return carry

    lax.fori_loop(0, 6, plane_body, 0)

    def lower_body(e, carry):
        acc = None
        for mu in range(3):
            pair = dense_shift([staples[mu, e, 0], staples[mu, e, 1]], mu, -1)
            acc = pair if acc is None else [acc[c] + pair[c] for c in range(2)]
        sums[3, e, 0] = acc[0]
        sums[3, e, 1] = acc[1]
        return carry

    lax.fori_loop(0, 18, lower_body, 0)

    def force_body(step, carry):
        mu = step // 2
        c = step % 2
        current = load_matrix(lambda e: dense[mu, e, c])
        omega = mat_mul(current, load_matrix(lambda e: sums[mu, e, c]))
        parts = [part + forces[mu, e, c] for e, part in enumerate(anti_parts(omega))]
        mean = (parts[0] + parts[1] + parts[2]) * (1.0 / 3.0)
        parts = [parts[e] - mean if e < 3 else parts[e] for e in range(9)]
        parts = [part * (1.0 / 12.0) for part in parts]
        applied = anti_mul(parts, current)
        twice = anti_mul(parts, applied)
        gate = gates[mu]
        slope = jnp.zeros_like(gate)
        curve = jnp.zeros_like(gate)
        for e, (part, i, j) in enumerate(ENTRIES):
            weight = cots[mu, e, c]
            slope = slope + weight * applied[part][i][j]
            curve = curve + weight * twice[part][i][j]
            w1_ref[mu, e, c] = gate * applied[part][i][j]
            w2_ref[mu, e, c] = gate * twice[part][i][j]
        put_row(rows, 8 + mu, c, gate * slope)
        put_row(rows, 12 + mu, c, gate * curve)
        return carry

    lax.fori_loop(0, 8, force_body, 0)
    for t in range(4):
        for q in range(4):
            value = rows[t, q]
            fm_ref[t, :, q * 128:q * 128 + 128] = value.astype(BF16)
            if t > 0:
                fup_ref[t - 1, :, q * 128:q * 128 + 128] = value[0:8].astype(BF16)
            if t < 3:
                fdown_ref[t, :, q * 128:q * 128 + 128] = value[0:8].astype(BF16)


def selectors():
    row = lax.broadcasted_iota(jnp.int32, (432, 72), 0)
    col = lax.broadcasted_iota(jnp.int32, (432, 72), 1)
    group = row // 12
    spread = (group // 4 * 8 + group % 4 == col).astype(F32).astype(BF16)
    keep = (
        lax.broadcasted_iota(jnp.int32, (432, H), 1) // 4 == lax.broadcasted_iota(jnp.int32, (432, H), 0) % 12
    )
    return spread, keep


def panel_kernel(gathered_ref, weights_ref, loops_ref, p1_ref, p2_ref, p3_ref, p4_ref, b2_ref, b3_ref, b4_ref, weights):
    count = gathered_ref.shape[0]

    def read(chip):
        low = gathered_ref[2 * chip].astype(F32)
        high = gathered_ref[2 * chip + 1].astype(F32)
        return special(
            two_rows(lambda e: jnp.concatenate([low[2 * e:2 * e + 2], high[2 * e:2 * e + 2]], axis=0))
        )

    def flat(matrix):
        return tuple(matrix[0][i][j] for i in range(3) for j in range(3)) + tuple(
            imag_of(matrix, i, j) for i in range(3) for j in range(3)
        )

    def chain(chip, state):
        return flat(mat_mul(load_matrix(lambda e: state[e]), read(chip)))

    state = lax.fori_loop(1, count // 2, chain, flat(read(0)))
    loops_ref[0] = (state[0] + state[4] + state[8]) / 3.0
    loops_ref[1] = (state[9] + state[13] + state[17]) / 3.0

    if weights_ref is None:
        for d in range(count):
            block = gathered_ref[d].astype(F32)
            weights[27 * d:27 * d + 27, :] = block[SLABROWS:SLABROWS + 27]
    else:
        weights[...] = weights_ref[...].astype(F32)
    for k in range(TAPS):
        rows = slice(H * k, H * k + H)
        back = slice(H * SWAP[k], H * SWAP[k] + H)
        p2_ref[:, rows] = weights[rows, 0:48].astype(BF16)
        p3_ref[:, rows] = weights[rows, 48:96].astype(BF16)
        p1_ref[:, 8 * k:8 * k + 8] = weights[rows, 96:104].astype(BF16)
        turned = weights[back, :].T
        b2_ref[:, rows] = turned[0:48].astype(BF16)
        b3_ref[:, rows] = turned[48:96].astype(BF16)
    spread, keep = selectors()
    place = (
        lax.broadcasted_iota(jnp.int32, (LANES, H), 0) == 104 + lax.broadcasted_iota(jnp.int32, (LANES, H), 1) % 4
    ).astype(F32).astype(BF16)
    wide = jnp.dot(weights[...].astype(BF16), place, preferred_element_type=F32)
    wide = jnp.where(keep, wide, 0.0).astype(BF16)
    last = lax.dot_general(spread, wide, (((0,), (0,)), ((), ())), preferred_element_type=F32)
    p4_ref[...] = last.astype(BF16)
    for k in range(TAPS):
        b4_ref[:, 8 * k:8 * k + 8] = last[8 * SWAP[k]:8 * SWAP[k] + 8, :].T.astype(BF16)


def panel_kernel_plain(gathered_ref, *rest):
    panel_kernel(gathered_ref, None, *rest)


def chunks_of(value):
    return [value[:, q * 128:q * 128 + 128] for q in range(4)]


def one_shift(chunks, position):
    if position == 0:
        return chunks
    lanes = lane_iota(chunks[0].shape[0])
    sign = 1 if position % 2 == 1 else -1
    if position > 4:
        return [shift_z(chunk, sign, lanes) for chunk in chunks]
    if position > 2:
        return [shift_y(chunk, sign, lanes) for chunk in chunks]
    low = lanes < 64
    rolled = [roll_lanes(chunk, 64) for chunk in chunks]
    if sign > 0:
        return [jnp.where(low, rolled[q], rolled[(q + 1) % 4]) for q in range(4)]
    return [jnp.where(low, rolled[(q + 3) % 4], rolled[q]) for q in range(4)]


def span(slice_index, count=1):
    if isinstance(slice_index, int):
        return slice(slice_index * SITES, (slice_index + count) * SITES)
    return pl.ds(pl.multiple_of(slice_index * SITES, SITES), count * SITES)


def slot_of(slot):
    return slice(slot * SITES, (slot + 1) * SITES)


def stack_wide(source, target, index, slot):
    chunks = chunks_of(source[:, span(index)])
    for position in range(7):
        shifted = one_shift(chunks, position)
        for q in range(4):
            lanes = slice(slot * SITES + q * 128, slot * SITES + q * 128 + 128)
            target[H * position:H * position + H, lanes] = shifted[q]
    target[7 * H:8 * H, slot_of(slot)] = source[:, span(index + 1)]
    target[8 * H:9 * H, slot_of(slot)] = source[:, span(index - 1)]


def stack_thin(source, target, index, slot):
    chunks = chunks_of(source[:, span(index)])
    ahead = chunks_of(source[:, span(index + 1)])
    behind = chunks_of(source[:, span(index - 1)])
    columns = [one_shift(chunks, position) for position in range(7)] + [ahead, behind]
    for q in range(4):
        lanes = slice(slot * SITES + q * 128, slot * SITES + q * 128 + 128)
        target[0:72, lanes] = jnp.concatenate([column[q] for column in columns], axis=0).astype(BF16)


def one_minus_square(value):
    value = value.astype(F32)
    return 1.0 - value * value


def conv_kernel(
    split, fm_ref, below_ref, above_ref, fbelow_ref, fabove_ref, loops_ref,
    p1_ref, p2_ref, p3_ref, p4_ref, b2_ref, b3_ref, b4_ref,
    coeff_ref, grads_ref,
    feats, mixed, h1, h2, h3, parts, lasts, g3, g2, g1, wide, thin, packed,
):
    row8 = lax.broadcasted_iota(jnp.int32, (8, SITES), 0)
    loop_re = jnp.concatenate([loops_ref[0, q:q + 1, :] for q in range(4)], axis=1)
    loop_im = jnp.concatenate([loops_ref[1, q:q + 1, :] for q in range(4)], axis=1)
    loops = jnp.where(row8 == 6, loop_re, jnp.where(row8 == 7, loop_im, 0.0))
    loops = loops.astype(BF16).astype(F32)
    for j in range(3):
        feats[:, span(j)] = fbelow_ref[j].astype(F32) + loops
        feats[:, span(15 + j)] = fabove_ref[j].astype(F32) + loops
    for base, ref in ((3, below_ref), (7, fm_ref), (11, above_ref)):
        for j in range(4):
            value = ref[j].astype(F32)
            feats[:, span(base + j)] = value[0:8] + loops
            mixed[:, span(base + j)] = value[8:16]

    def wide_dot(source, weights, index, slot):
        stack_wide(source, wide, index, slot)
        return jnp.dot(weights[...], wide[:, slot_of(slot)], preferred_element_type=F32)

    def thin_dot(source, weights, index, slot):
        stack_thin(source, thin, index, slot)
        return jnp.dot(weights[...], thin[:, slot_of(slot)], preferred_element_type=F32)

    for index in range(1, 17):
        h1[:, span(index)] = jnp.tanh(thin_dot(feats, p1_ref, index, index % 4)).astype(BF16)
    for index in range(2, 16):
        h2[:, span(index)] = jnp.tanh(wide_dot(h1, p2_ref, index, index % 4)).astype(BF16)
    for index in range(3, 15):
        out = jnp.tanh(wide_dot(h2, p3_ref, index, index % 4)).astype(BF16)
        h3[:, span(index)] = out
        taps = jnp.dot(p4_ref[...], out, preferred_element_type=F32)
        acc = None
        for position in range(7):
            shifted = one_shift(chunks_of(taps[8 * position:8 * position + 8]), position)
            acc = shifted if acc is None else [a + b for a, b in zip(acc, shifted)]
        parts[0, :, span(index)] = jnp.concatenate(acc, axis=1)
        parts[1, :, span(index)] = taps[56:64]
        parts[2, :, span(index)] = taps[64:72]

    for index in range(4, 14):
        coeff = jnp.tanh(parts[0, :, span(index)] + parts[1, :, span(index + 1)] + parts[2, :, span(index - 1)])
        blend = mixed[:, span(index)]
        value = (blend + coeff * pltpu.roll(blend, 4, 0)) * (1.0 - coeff * coeff)
        lasts[:, span(index)] = jnp.where(row8 < 4, value, 0.0).astype(BF16).astype(F32)
        if 7 <= index < 11:
            coeff_ref[index - 7] = coeff

    own = span(7, 4)
    contract = (((1,), (1,)), ((), ()))
    for index in (5, 6, 11, 12, 7, 8, 9, 10):
        out = thin_dot(lasts, b4_ref, index, (index + 1) % 4)
        g3[:, span(index)] = (out * one_minus_square(h3[:, span(index)])).astype(BF16)
    grad_last = lax.dot_general(thin[...], h3[:, own], contract, preferred_element_type=F32)
    for index in (6, 11, 7, 8, 9, 10):
        out = wide_dot(g3, b3_ref, index, (index + 1) % 4)
        g2[:, span(index)] = (out * one_minus_square(h2[:, span(index)])).astype(BF16)
    grad_third = lax.dot_general(wide[...], h2[:, own], contract, preferred_element_type=F32)
    for index in (7, 8, 9, 10):
        out = wide_dot(g2, b2_ref, index, (index + 1) % 4)
        g1[:, slot_of(index - 7)] = (out * one_minus_square(h1[:, span(index)])).astype(BF16)
    grad_second = lax.dot_general(wide[...], h1[:, own], contract, preferred_element_type=F32)
    for index in (7, 8, 9, 10):
        stack_thin(feats, thin, index, index - 7)
    grad_first = lax.dot_general(g1[...], thin[...], contract, preferred_element_type=F32)

    spread, keep = selectors()
    ordered = jnp.concatenate([grad_last[8 * SWAP[k]:8 * SWAP[k] + 8] for k in range(TAPS)], axis=0)
    broad = jnp.dot(spread, ordered.astype(BF16), preferred_element_type=F32)
    broad = jnp.where(keep, broad, 0.0).astype(BF16)
    place = (
        lax.broadcasted_iota(jnp.int32, (H, LANES), 1) == 104 + lax.broadcasted_iota(jnp.int32, (H, LANES), 0) % 4
    ).astype(F32).astype(BF16)
    packed[...] = jnp.dot(broad, place, preferred_element_type=F32)
    for k in range(TAPS):
        rows = slice(H * k, H * k + H)
        back = slice(H * SWAP[k], H * SWAP[k] + H)
        packed[rows, 0:48] = grad_second[back]
        packed[rows, 48:96] = grad_third[back]
        packed[rows, 96:104] = grad_first[:, 8 * k:8 * k + 8]
    if split:
        for d in range(16):
            grads_ref[d] = packed[27 * d:27 * d + 27, :].astype(BF16)
    else:
        grads_ref[...] = packed[...].astype(BF16)


def update_kernel(dense, w1_ref, w2_ref, coeff_ref, out_ref, factors):
    for mu in range(4):
        for t in range(4):
            for c in range(2):
                factors[mu, c, t:t + 1, :] = coeff_ref[t, mu:mu + 1, c * 128:c * 128 + 128]
                factors[mu, c, 4 + t:5 + t, :] = coeff_ref[t, mu:mu + 1, 256 + c * 128:384 + c * 128]

    def body(mu, carry):
        factor = [factors[mu, c] for c in range(2)]
        half = [0.5 * value * value for value in factor]
        for e, (part, i, j) in enumerate(ENTRIES):
            new = [dense[mu, e, c] + factor[c] * w1_ref[mu, e, c] + half[c] * w2_ref[mu, e, c] for c in range(2)]
            out_ref[mu, part, i, j, 0] = jnp.concatenate(
                [new[0][0:4], new[1][0:4], new[0][4:8], new[1][4:8]], axis=1
            )
        return carry

    lax.fori_loop(0, 4, body, 0)


def sum_kernel(widths, parts_ref, first_ref, second_ref, third_ref, last_ref):
    value = parts_ref[0].astype(F32)
    for d in range(1, parts_ref.shape[0]):
        value = value + parts_ref[d].astype(F32)
    offset = 0
    for ref, width in zip((second_ref, third_ref, first_ref, last_ref), widths):
        for r in range(27):
            ref[:, width * r:width * r + width] = value[r:r + 1, offset:offset + width]
        offset += width


def call(body, outs, scratch, places=None, cost=None, limit=LIMIT):
    specs = {}
    if places is not None:
        specs["in_specs"] = [pl.BlockSpec(memory_space=place) for place in places]
    return pl.pallas_call(
        body,
        out_shape=[jax.ShapeDtypeStruct(shape, dtype) for shape, dtype in outs],
        scratch_shapes=[pltpu.VMEM(*item) if isinstance(item, tuple) else item for item in scratch],
        compiler_params=pltpu.CompilerParams(vmem_limit_bytes=limit),
        cost_estimate=cost,
        **specs,
    )


def on_device(links, cotangent, parity, link_subset, w_first, w_second, w_third, w_last):
    count = lax.axis_size("tm")

    def send(value, distance):
        return lax.ppermute(value, "tm", [(i, (i + distance) % count) for i in range(count)])

    widths = (768 // count, 768 // count, 128 // count, 64 // count)
    field = ((4, 18, 2, 8, LANES), F32)
    space = ((3, 18, 2, 8, LANES), F32)
    edge_rows = ((70, SITES), BF16)
    vmem, smem = pltpu.VMEM, pltpu.SMEM
    up, down, dense, edges, staples, slab = call(
        face_kernel,
        [edge_rows, edge_rows, field, space, space, ((12, 4, LANES), F32)],
        [space, ((70, 4, LANES), F32)],
    )(links)
    up = send(up, 1)
    down = send(down, -1)
    cots, rows, forces, sums, gates = call(
        space_kernel,
        [field, ((4, 4, 16, LANES), F32), ((4, 9, 2, 8, LANES), F32), space, ((4, 8, LANES), F32)],
        [((3, 3, 18, 2, 8, LANES), F32), ((3, 3, 18, 2, 8, LANES), F32)],
        places=(smem, smem, vmem, vmem, vmem),
        cost=pl.CostEstimate(flops=4_000_000_000, bytes_accessed=16_000_000, transcendentals=0),
    )(parity, link_subset, dense, cotangent, staples)
    core = (lax.axis_index("tm") % 2).astype(jnp.int32)[None]
    (block,) = call(
        functools.partial(block_kernel, widths),
        [((count, BLOCKROWS, LANES), BF16)],
        [((12, 4, LANES), F32), ((BLOCKROWS, LANES), F32)],
        places=(smem,) + (vmem,) * 8,
    )(core, up, down, slab, w_first, w_second, w_third, w_last, rows)
    gathered = lax.all_to_all(block, "tm", split_axis=0, concat_axis=0, tiled=True)
    fm, fup, fdown, applied, twice = call(
        time_kernel,
        [((4, 16, SITES), BF16), ((3, 8, SITES), BF16), ((3, 8, SITES), BF16), field, field],
        [
            space, space, field, ((70, 4, LANES), F32), ((70, 4, LANES), F32),
            ((4, 9, 2, 8, LANES), F32), ((4, 4, 16, LANES), F32),
        ],
    )(dense, cots, up, down, gates, edges, rows, forces, sums)
    below = send(fm, 1)
    above = send(fm, -1)
    fbelow = send(fup, 2)
    fabove = send(fdown, -2)

    panel_outs = [
        ((2, 4, LANES), F32), ((H, 72), BF16), ((H, 432), BF16), ((H, 432), BF16), ((72, H), BF16),
        ((H, 432), BF16), ((H, 432), BF16), ((H, 72), BF16),
    ]
    panel_scratch = [((432, LANES), F32)]
    if count == 16:
        loops, p1, p2, p3, p4, b2, b3, b4 = call(panel_kernel_plain, panel_outs, panel_scratch)(gathered)
    else:
        pieces = []
        offset = 0
        for width, full in zip(widths, (48, 48, 8, 4)):
            piece = gathered[:, SLABROWS:SLABROWS + 27, offset:offset + width]
            pieces.append(piece.reshape(432, full))
            offset += width
        pieces.append(jnp.zeros((432, 20), BF16))
        loops, p1, p2, p3, p4, b2, b3, b4 = call(panel_kernel, panel_outs, panel_scratch)(
            gathered, jnp.concatenate(pieces, axis=1)
        )

    window = 18 * SITES
    coeff, grads = call(
        functools.partial(conv_kernel, count == 16),
        [((4, 8, SITES), F32), ((16, 27, LANES) if count == 16 else (432, LANES), BF16)],
        [
            ((8, window), F32), ((8, window), F32), ((H, window), BF16), ((H, window), BF16), ((H, window), BF16),
            ((3, 8, window), F32), ((8, window), F32), ((H, window), BF16), ((H, window), BF16), ((H, 4 * SITES), BF16),
            ((432, 4 * SITES), BF16), ((72, 4 * SITES), BF16), ((432, LANES), F32),
        ],
        limit=20 * 1024 * 1024,
    )(fm, below, above, fbelow, fabove, loops, p1, p2, p3, p4, b2, b3, b4)
    if count != 16:
        offset = 0
        pieces = []
        for width, full in zip(widths, (48, 48, 8, 4)):
            pieces.append(grads[:, offset:offset + full].reshape(count, 27, width))
            offset += full
        grads = jnp.concatenate(pieces, axis=2)
    grads = lax.all_to_all(grads, "tm", split_axis=0, concat_axis=0, tiled=True)
    (new_links,) = call(
        update_kernel, [(links.shape, F32)], [((4, 2, 8, LANES), F32)]
    )(dense, applied, twice, coeff)
    grad_first, grad_second, grad_third, grad_last = call(
        functools.partial(sum_kernel, widths),
        [((1, 27 * width), F32) for width in (widths[2], widths[0], widths[1], widths[3])],
        [],
    )(grads)
    return (new_links, grad_first, grad_second, grad_third, grad_last)


def solution(mesh):
    placed = (
        P(None, None, None, None, "groups", "tm", None),
        P(None, None, None, None, "groups", "tm", None),
        P("groups", "tm"),
        P("groups", "tm"),
        P("tm"),
        P("tm"),
        P("tm"),
        P("tm"),
    )
    return jax.shard_map(
        on_device,
        mesh=mesh,
        in_specs=placed,
        out_specs=(
            P(None, None, None, None, "groups", "tm", None),
            P("groups", "tm"),
            P("groups", "tm"),
            P("groups", "tm"),
            P("groups", "tm"),
        ),
        check_vma=False,
    )
```

```python
import functools

import jax
import jax.numpy as jnp
from jax import lax
from jax.experimental import pallas as pl
from jax.experimental.pallas import tpu as pltpu
from jax.sharding import PartitionSpec as P

F32 = jnp.float32
BF16 = jnp.bfloat16
TAPS = 9
H = 48
LANES = 128
SITES = 512
PAIRS = ((0, 1), (0, 2), (0, 3), (1, 2), (1, 3), (2, 3))
SWAP = (0, 2, 1, 4, 3, 6, 5, 8, 7)
ENTRIES = tuple((c, i, j) for c in range(2) for i in range(3) for j in range(3))
SLABROWS = 24
BLOCKROWS = 64
LIMIT = 8 * 1024 * 1024


def lane_iota(rows):
    return lax.broadcasted_iota(jnp.int32, (rows, LANES), 1)


def row_iota():
    return lax.broadcasted_iota(jnp.int32, (8, LANES), 0)


def roll_lanes(value, amount):
    return pltpu.roll(value, amount % LANES, 1)


def shift_z(chunk, sign, lanes):
    z = lanes % 8
    if sign > 0:
        return jnp.where(z == 7, roll_lanes(chunk, 7), roll_lanes(chunk, -1))
    return jnp.where(z == 0, roll_lanes(chunk, -7), roll_lanes(chunk, 1))


def shift_y(chunk, sign, lanes):
    y = lanes // 8 % 8
    if sign > 0:
        return jnp.where(y == 7, roll_lanes(chunk, 56), roll_lanes(chunk, -8))
    return jnp.where(y == 0, roll_lanes(chunk, -56), roll_lanes(chunk, 8))


def dense_shift(pair, axis, sign):
    lanes = lane_iota(8)
    if axis == 2:
        return [shift_z(chunk, sign, lanes) for chunk in pair]
    if axis == 1:
        return [shift_y(chunk, sign, lanes) for chunk in pair]
    low = lanes < 64
    first, second = [roll_lanes(chunk, 64) for chunk in pair]
    if sign > 0:
        return [jnp.where(low, first, second), jnp.where(low, second, pltpu.roll(first, 4, 0))]
    return [jnp.where(low, pltpu.roll(second, 4, 0), first), jnp.where(low, first, second)]


def pack_pair(value):
    return [
        jnp.concatenate([value[:, c * 128:c * 128 + 128], value[:, 256 + c * 128:384 + c * 128]], axis=0)
        for c in range(2)
    ]


def halo_pair(ref, index):
    top = row_iota() < 4
    pair = []
    for c in range(2):
        low = jnp.broadcast_to(ref[index, c:c + 1, :], (8, LANES))
        high = jnp.broadcast_to(ref[index, 2 + c:3 + c, :], (8, LANES))
        pair.append(jnp.where(top, low, high))
    return pair


def load_matrix(read):
    real = [[read(3 * i + j) for j in range(3)] for i in range(3)]
    imag = [[read(9 + 3 * i + j) for j in range(3)] for i in range(3)]
    return (real, imag, 1)


def dagger(matrix):
    real, imag, sign = matrix
    return (
        [[real[j][i] for j in range(3)] for i in range(3)],
        [[imag[j][i] for j in range(3)] for i in range(3)],
        -sign,
    )


def total(terms, signs):
    value = None
    for term, sign in zip(terms, signs):
        if value is None:
            value = term if sign > 0 else -term
        else:
            value = value + term if sign > 0 else value - term
    return value


def mat_mul(left, right):
    lr, li, ls = left
    rr, ri, rs = right
    same = ls == rs
    height = len(lr)
    real = [[None] * 3 for _ in range(height)]
    imag = [[None] * 3 for _ in range(height)]
    for i in range(height):
        for j in range(3):
            real[i][j] = total(
                [lr[i][k] * rr[k][j] for k in range(3)] + [li[i][k] * ri[k][j] for k in range(3)],
                [1, 1, 1] + [-1 if same else 1] * 3,
            )
            imag[i][j] = total(
                [lr[i][k] * ri[k][j] for k in range(3)] + [li[i][k] * rr[k][j] for k in range(3)],
                [1, 1, 1] + [1 if same else -1] * 3,
            )
    return (real, imag, ls if same else rs)


def imag_of(matrix, i, j):
    return matrix[1][i][j] if matrix[2] > 0 else -matrix[1][i][j]


def store_matrix(matrix, write):
    for i in range(3):
        for j in range(3):
            write(3 * i + j, matrix[0][i][j])
            write(9 + 3 * i + j, imag_of(matrix, i, j))


def two_rows(read):
    real = [[read(3 * i + j) for j in range(3)] for i in range(2)]
    imag = [[read(6 + 3 * i + j) for j in range(3)] for i in range(2)]
    return (real, imag, 1)


def store_rows(matrix, write):
    for i in range(2):
        for j in range(3):
            write(3 * i + j, matrix[0][i][j])
            write(6 + 3 * i + j, imag_of(matrix, i, j))


def special(matrix):
    real, imag, _ = matrix
    last_r, last_i = [], []
    for k in range(3):
        i, j = (k + 1) % 3, (k + 2) % 3
        last_r.append(
            (real[0][i] * real[1][j] - imag[0][i] * imag[1][j])
            - (real[0][j] * real[1][i] - imag[0][j] * imag[1][i])
        )
        last_i.append(
            (real[0][j] * imag[1][i] + imag[0][j] * real[1][i])
            - (real[0][i] * imag[1][j] + imag[0][i] * real[1][j])
        )
    return (real + [last_r], imag + [last_i], 1)


def anti_parts(matrix):
    parts = [2.0 * imag_of(matrix, i, i) for i in range(3)]
    for i, j in ((0, 1), (0, 2), (1, 2)):
        parts.append(matrix[0][i][j] - matrix[0][j][i])
        parts.append(imag_of(matrix, i, j) + imag_of(matrix, j, i))
    return parts


def anti_matrix(parts):
    zero = jnp.zeros_like(parts[0])
    real = [[zero, parts[3], parts[5]], [-parts[3], zero, parts[7]], [-parts[5], -parts[7], zero]]
    imag = [[parts[0], parts[4], parts[6]], [parts[4], parts[1], parts[8]], [parts[6], parts[8], parts[2]]]
    return real, imag


def anti_mul(parts, right):
    real, imag = anti_matrix(parts)
    rr, ri, _ = right
    out_r = [[None] * 3 for _ in range(3)]
    out_i = [[None] * 3 for _ in range(3)]
    for i in range(3):
        for j in range(3):
            value_r = -(imag[i][i] * ri[i][j])
            value_i = imag[i][i] * rr[i][j]
            for k in range(3):
                if k != i:
                    value_r = value_r + real[i][k] * rr[k][j] - imag[i][k] * ri[k][j]
                    value_i = value_i + real[i][k] * ri[k][j] + imag[i][k] * rr[k][j]
            out_r[i][j] = value_r
            out_i[i][j] = value_i
    return (out_r, out_i, 1)


def pack_links(links_ref, dense):
    def body(mu, carry):
        for e, (c, i, j) in enumerate(ENTRIES):
            low, high = pack_pair(links_ref[mu, c, i, j, 0].astype(F32))
            dense[mu, e, 0] = low
            dense[mu, e, 1] = high
        return carry

    lax.fori_loop(0, 4, body, 0)


def face_kernel(links_ref, up_ref, down_ref, dense, edges, staples, slab, moved, rows):
    pack_links(links_ref, dense)

    def shift_body(e, carry):
        pair = [dense[3, e, 0], dense[3, e, 1]]
        for mu in range(3):
            low, high = dense_shift(pair, mu, 1)
            moved[mu, e, 0] = low
            moved[mu, e, 1] = high
        return carry

    lax.fori_loop(0, 18, shift_body, 0)

    def staple_body(step, carry):
        mu = step // 2
        c = step % 2
        u_mu = load_matrix(lambda e: dense[mu, e, c])
        u_t = load_matrix(lambda e: dense[3, e, c])
        edge = mat_mul(u_mu, load_matrix(lambda e: moved[mu, e, c]))

        def write_edge(e, value):
            edges[mu, e, c] = value

        store_matrix(edge, write_edge)

        def write(e, value):
            staples[mu, e, c] = value
            rows[16 + mu * 18 + e, pl.ds(c, 1)] = value[3:4]
            rows[16 + mu * 18 + e, pl.ds(2 + c, 1)] = value[7:8]

        store_matrix(mat_mul(dagger(edge), u_t), write)
        return carry

    lax.fori_loop(0, 6, staple_body, 0)

    def slab_body(c, carry):
        u_t = load_matrix(lambda e: dense[3, e, c])
        ahead = load_matrix(lambda e: pltpu.roll(dense[3, e, c], 7, 0))
        two = mat_mul(u_t, ahead)
        later = tuple(
            [[pltpu.roll(part[i][j], 6, 0) for j in range(3)] for i in range(3)] for part in two[:2]
        ) + (two[2],)
        four = mat_mul((two[0][:2], two[1][:2], two[2]), later)

        def write(e, value):
            slab[e, pl.ds(c, 1)] = value[0:1]
            slab[e, pl.ds(2 + c, 1)] = value[4:5]
            rows[e, pl.ds(c, 1)] = value[0:1]
            rows[e, pl.ds(2 + c, 1)] = value[4:5]

        store_rows(four, write)
        return carry

    lax.fori_loop(0, 2, slab_body, 0)
    for q in range(4):
        up_ref[:, q * 128:q * 128 + 128] = rows[:, q, :].astype(BF16)

    def down_body(e, carry):
        for mu in range(3):
            for c in range(2):
                value = dense[mu, e, c]
                rows[16 + mu * 18 + e, c:c + 1] = value[0:1]
                rows[16 + mu * 18 + e, 2 + c:3 + c] = value[4:5]
        return carry

    lax.fori_loop(0, 18, down_body, 0)
    for q in range(4):
        down_ref[:, q * 128:q * 128 + 128] = rows[:, q, :].astype(BF16)


def block_kernel(
    widths, core_ref, up_ref, down_ref, slab, w1_ref, w2_ref, w3_ref, w4_ref, after_ref, block_ref, other, block
):
    even = core_ref[0] == 0
    up = up_ref[0:16].astype(F32)
    down = down_ref[0:16].astype(F32)
    for q in range(4):
        lanes = slice(q * 128, q * 128 + 128)
        other[:, q, :] = jnp.where(even, down[0:12, lanes], up[0:12, lanes])
    first = two_rows(lambda e: jnp.where(even, slab[e], other[e]))
    second = special(two_rows(lambda e: jnp.where(even, other[e], slab[e])))

    def write(e, value):
        block[2 * e:2 * e + 2, :] = jnp.where(even, value[0:2], value[2:4])

    store_rows(mat_mul(first, second), write)
    block[SLABROWS:BLOCKROWS] = jnp.zeros((BLOCKROWS - SLABROWS, LANES), F32)
    offset = 0
    for ref, width in zip((w2_ref, w3_ref, w1_ref, w4_ref), widths):
        flat = ref[...].astype(F32)
        for r in range(27):
            block[SLABROWS + r:SLABROWS + r + 1, offset:offset + width] = (
                flat[width * r:width * r + width].reshape(1, width)
            )
        offset += width
    value = block[...].astype(BF16)
    for d in range(block_ref.shape[0]):
        block_ref[d] = value


def put_row(rows, channel, c, value):
    for t in range(4):
        rows[t, c, pl.ds(channel, 1), :] = value[t:t + 1]
        rows[t, 2 + c, pl.ds(channel, 1), :] = value[4 + t:5 + t]


def space_kernel(
    parity_ref, subset_ref, dense, cot_ref, time_staples, cots, rows, forces, sums, gates, moved, staples
):
    pack_links(cot_ref, cots)
    rows[...] = jnp.zeros_like(rows)
    forces[...] = jnp.zeros_like(forces)
    steps = row_iota() % 4
    lanes = lane_iota(8)
    colour = (lanes // 64 + lanes // 8 % 8 + lanes % 8 + steps) % 2
    parity = jnp.zeros_like(steps)
    subset = jnp.zeros_like(steps)
    for t in range(4):
        parity = jnp.where(steps == t, parity_ref[0, t], parity)
        subset = jnp.where(steps == t, subset_ref[0, t], subset)
    for mu in range(4):
        active = jnp.logical_and(colour == parity, jnp.right_shift(subset, mu) % 2 == 1)
        gates[mu] = jnp.where(active, 1.0, 0.0)

    def shift_body(e, carry):
        for nu in range(3):
            pair = [dense[nu, e, 0], dense[nu, e, 1]]
            for mu in range(3):
                if mu != nu:
                    low, high = dense_shift(pair, mu, 1)
                    moved[mu, nu, e, 0] = low
                    moved[mu, nu, e, 1] = high
        return carry

    lax.fori_loop(0, 18, shift_body, 0)

    def plane_body(step, carry):
        plane = step // 2
        c = step % 2
        mu = jnp.where(plane == 2, 1, 0)
        nu = jnp.where(plane == 0, 1, 2)
        u_mu = load_matrix(lambda e: dense[mu, e, c])
        u_nu = load_matrix(lambda e: dense[nu, e, c])
        one = mat_mul(u_mu, load_matrix(lambda e: moved[mu, nu, e, c]))
        two = mat_mul(u_nu, load_matrix(lambda e: moved[nu, mu, e, c]))
        loop = mat_mul(one, dagger(two))
        put_row(rows, jnp.where(plane == 2, 3, plane), c, (loop[0][0][0] + loop[0][1][1] + loop[0][2][2]) / 3.0)
        for e, part in enumerate(anti_parts(loop)):
            forces[mu, e, c] += part
            forces[nu, e, c] -= part

        def write_mu(e, value):
            staples[mu, nu, e, c] = value

        def write_nu(e, value):
            staples[nu, mu, e, c] = value

        store_matrix(mat_mul(dagger(one), u_nu), write_mu)
        store_matrix(mat_mul(dagger(two), u_mu), write_nu)
        return carry

    lax.fori_loop(0, 6, plane_body, 0)

    def lower_body(e, carry):
        for mu in range(3):
            acc = [jnp.where(steps == 0, 0.0, pltpu.roll(time_staples[mu, e, c], 1, 0)) for c in range(2)]
            for nu in range(3):
                if nu != mu:
                    pair = dense_shift([staples[mu, nu, e, 0], staples[mu, nu, e, 1]], nu, -1)
                    acc = [acc[c] + pair[c] for c in range(2)]
            sums[mu, e, 0] = acc[0]
            sums[mu, e, 1] = acc[1]
        return carry

    lax.fori_loop(0, 18, lower_body, 0)


def time_kernel(
    dense, cots, up_ref, down_ref, gates, edges, rows_ref, forces_ref, sums_ref,
    fm_ref, fup_ref, fdown_ref, w1_ref, w2_ref,
    moved, staples, sums, halo_up, halo_down, forces, rows,
):
    for q in range(4):
        halo_up[:, q, :] = up_ref[:, q * 128:q * 128 + 128].astype(F32)
        halo_down[:, q, :] = down_ref[:, q * 128:q * 128 + 128].astype(F32)
    rows[...] = rows_ref[...]
    forces[...] = forces_ref[...]
    steps = row_iota() % 4

    def shift_body(e, carry):
        for nu in range(3):
            halo = halo_pair(halo_down, 16 + nu * 18 + e)
            below = halo_pair(halo_up, 16 + nu * 18 + e)
            for c in range(2):
                moved[nu, e, c] = jnp.where(steps == 3, halo[c], pltpu.roll(dense[nu, e, c], 7, 0))
                sums[nu, e, c] = sums_ref[nu, e, c] + jnp.where(steps == 0, below[c], 0.0)
        return carry

    lax.fori_loop(0, 18, shift_body, 0)

    def plane_body(step, carry):
        mu = step // 2
        c = step % 2
        one = load_matrix(lambda e: edges[mu, e, c])
        two = mat_mul(load_matrix(lambda e: dense[3, e, c]), load_matrix(lambda e: moved[mu, e, c]))
        loop = mat_mul(one, dagger(two))
        put_row(rows, jnp.where(mu == 0, 2, mu + 3), c, (loop[0][0][0] + loop[0][1][1] + loop[0][2][2]) / 3.0)
        for e, part in enumerate(anti_parts(loop)):
            forces[mu, e, c] += part
            forces[3, e, c] -= part

        def write(e, value):
            staples[mu, e, c] = value

        store_matrix(mat_mul(dagger(two), load_matrix(lambda e: dense[mu, e, c])), write)
        return carry

    lax.fori_loop(0, 6, plane_body, 0)

    def lower_body(e, carry):
        acc = None
        for mu in range(3):
            pair = dense_shift([staples[mu, e, 0], staples[mu, e, 1]], mu, -1)
            acc = pair if acc is None else [acc[c] + pair[c] for c in range(2)]
        sums[3, e, 0] = acc[0]
        sums[3, e, 1] = acc[1]
        return carry

    lax.fori_loop(0, 18, lower_body, 0)

    def force_body(step, carry):
        mu = step // 2
        c = step % 2
        current = load_matrix(lambda e: dense[mu, e, c])
        omega = mat_mul(current, load_matrix(lambda e: sums[mu, e, c]))
        parts = [part + forces[mu, e, c] for e, part in enumerate(anti_parts(omega))]
        mean = (parts[0] + parts[1] + parts[2]) * (1.0 / 3.0)
        parts = [parts[e] - mean if e < 3 else parts[e] for e in range(9)]
        parts = [part * (1.0 / 12.0) for part in parts]
        applied = anti_mul(parts, current)
        twice = anti_mul(parts, applied)
        gate = gates[mu]
        slope = jnp.zeros_like(gate)
        curve = jnp.zeros_like(gate)
        for e, (part, i, j) in enumerate(ENTRIES):
            weight = cots[mu, e, c]
            slope = slope + weight * applied[part][i][j]
            curve = curve + weight * twice[part][i][j]
            w1_ref[mu, e, c] = gate * applied[part][i][j]
            w2_ref[mu, e, c] = gate * twice[part][i][j]
        put_row(rows, 8 + mu, c, gate * slope)
        put_row(rows, 12 + mu, c, gate * curve)
        return carry

    lax.fori_loop(0, 8, force_body, 0)
    for t in range(4):
        for q in range(4):
            value = rows[t, q]
            fm_ref[t, :, q * 128:q * 128 + 128] = value.astype(BF16)
            if t > 0:
                fup_ref[t - 1, :, q * 128:q * 128 + 128] = value[0:8].astype(BF16)
            if t < 3:
                fdown_ref[t, :, q * 128:q * 128 + 128] = value[0:8].astype(BF16)


def selectors():
    row = lax.broadcasted_iota(jnp.int32, (432, 72), 0)
    col = lax.broadcasted_iota(jnp.int32, (432, 72), 1)
    group = row // 12
    spread = (group // 4 * 8 + group % 4 == col).astype(F32).astype(BF16)
    keep = (
        lax.broadcasted_iota(jnp.int32, (432, H), 1) // 4 == lax.broadcasted_iota(jnp.int32, (432, H), 0) % 12
    )
    return spread, keep


def panel_kernel(gathered_ref, weights_ref, loops_ref, p1_ref, p2_ref, p3_ref, p4_ref, b2_ref, b3_ref, b4_ref, weights):
    count = gathered_ref.shape[0]

    def read(chip):
        low = gathered_ref[2 * chip].astype(F32)
        high = gathered_ref[2 * chip + 1].astype(F32)
        return special(
            two_rows(lambda e: jnp.concatenate([low[2 * e:2 * e + 2], high[2 * e:2 * e + 2]], axis=0))
        )

    def flat(matrix):
        return tuple(matrix[0][i][j] for i in range(3) for j in range(3)) + tuple(
            imag_of(matrix, i, j) for i in range(3) for j in range(3)
        )

    def chain(chip, state):
        return flat(mat_mul(load_matrix(lambda e: state[e]), read(chip)))

    state = lax.fori_loop(1, count // 2, chain, flat(read(0)))
    loops_ref[0] = (state[0] + state[4] + state[8]) / 3.0
    loops_ref[1] = (state[9] + state[13] + state[17]) / 3.0

    if weights_ref is None:
        for d in range(count):
            block = gathered_ref[d].astype(F32)
            weights[27 * d:27 * d + 27, :] = block[SLABROWS:SLABROWS + 27]
    else:
        weights[...] = weights_ref[...].astype(F32)
    for k in range(TAPS):
        rows = slice(H * k, H * k + H)
        back = slice(H * SWAP[k], H * SWAP[k] + H)
        p2_ref[:, rows] = weights[rows, 0:48].astype(BF16)
        p3_ref[:, rows] = weights[rows, 48:96].astype(BF16)
        p1_ref[:, 8 * k:8 * k + 8] = weights[rows, 96:104].astype(BF16)
        turned = weights[back, :].T
        b2_ref[:, rows] = turned[0:48].astype(BF16)
        b3_ref[:, rows] = turned[48:96].astype(BF16)
    spread, keep = selectors()
    place = (
        lax.broadcasted_iota(jnp.int32, (LANES, H), 0) == 104 + lax.broadcasted_iota(jnp.int32, (LANES, H), 1) % 4
    ).astype(F32).astype(BF16)
    wide = jnp.dot(weights[...].astype(BF16), place, preferred_element_type=F32)
    wide = jnp.where(keep, wide, 0.0).astype(BF16)
    last = lax.dot_general(spread, wide, (((0,), (0,)), ((), ())), preferred_element_type=F32)
    p4_ref[...] = last.astype(BF16)
    for k in range(TAPS):
        b4_ref[:, 8 * k:8 * k + 8] = last[8 * SWAP[k]:8 * SWAP[k] + 8, :].T.astype(BF16)


def panel_kernel_plain(gathered_ref, *rest):
    panel_kernel(gathered_ref, None, *rest)


def chunks_of(value):
    return [value[:, q * 128:q * 128 + 128] for q in range(4)]


def one_shift(chunks, position):
    if position == 0:
        return chunks
    lanes = lane_iota(chunks[0].shape[0])
    sign = 1 if position % 2 == 1 else -1
    if position > 4:
        return [shift_z(chunk, sign, lanes) for chunk in chunks]
    if position > 2:
        return [shift_y(chunk, sign, lanes) for chunk in chunks]
    low = lanes < 64
    rolled = [roll_lanes(chunk, 64) for chunk in chunks]
    if sign > 0:
        return [jnp.where(low, rolled[q], rolled[(q + 1) % 4]) for q in range(4)]
    return [jnp.where(low, rolled[(q + 3) % 4], rolled[q]) for q in range(4)]


def span(slice_index, count=1):
    if isinstance(slice_index, int):
        return slice(slice_index * SITES, (slice_index + count) * SITES)
    return pl.ds(pl.multiple_of(slice_index * SITES, SITES), count * SITES)


def slot_of(slot):
    return slice(slot * SITES, (slot + 1) * SITES)


def stack_wide(source, target, index, slot):
    chunks = chunks_of(source[:, span(index)])
    for position in range(7):
        shifted = one_shift(chunks, position)
        for q in range(4):
            lanes = slice(slot * SITES + q * 128, slot * SITES + q * 128 + 128)
            target[H * position:H * position + H, lanes] = shifted[q]
    target[7 * H:8 * H, slot_of(slot)] = source[:, span(index + 1)]
    target[8 * H:9 * H, slot_of(slot)] = source[:, span(index - 1)]


def stack_thin(source, target, index, slot):
    chunks = chunks_of(source[:, span(index)])
    ahead = chunks_of(source[:, span(index + 1)])
    behind = chunks_of(source[:, span(index - 1)])
    columns = [one_shift(chunks, position) for position in range(7)] + [ahead, behind]
    for q in range(4):
        lanes = slice(slot * SITES + q * 128, slot * SITES + q * 128 + 128)
        target[0:72, lanes] = jnp.concatenate([column[q] for column in columns], axis=0).astype(BF16)


def one_minus_square(value):
    value = value.astype(F32)
    return 1.0 - value * value


def conv_kernel(
    split, fm_ref, below_ref, above_ref, fbelow_ref, fabove_ref, loops_ref,
    p1_ref, p2_ref, p3_ref, p4_ref, b2_ref, b3_ref, b4_ref,
    coeff_ref, grads_ref,
    feats, mixed, h1, h2, h3, parts, lasts, g3, g2, g1, wide, thin, packed,
):
    row8 = lax.broadcasted_iota(jnp.int32, (8, SITES), 0)
    loop_re = jnp.concatenate([loops_ref[0, q:q + 1, :] for q in range(4)], axis=1)
    loop_im = jnp.concatenate([loops_ref[1, q:q + 1, :] for q in range(4)], axis=1)
    loops = jnp.where(row8 == 6, loop_re, jnp.where(row8 == 7, loop_im, 0.0))
    loops = loops.astype(BF16).astype(F32)
    for j in range(3):
        feats[:, span(j)] = fbelow_ref[j].astype(F32) + loops
        feats[:, span(15 + j)] = fabove_ref[j].astype(F32) + loops
    for base, ref in ((3, below_ref), (7, fm_ref), (11, above_ref)):
        for j in range(4):
            value = ref[j].astype(F32)
            feats[:, span(base + j)] = value[0:8] + loops
            mixed[:, span(base + j)] = value[8:16]

    def wide_dot(source, weights, index, slot):
        stack_wide(source, wide, index, slot)
        return jnp.dot(weights[...], wide[:, slot_of(slot)], preferred_element_type=F32)

    def thin_dot(source, weights, index, slot):
        stack_thin(source, thin, index, slot)
        return jnp.dot(weights[...], thin[:, slot_of(slot)], preferred_element_type=F32)

    for index in range(1, 17):
        h1[:, span(index)] = jnp.tanh(thin_dot(feats, p1_ref, index, index % 4)).astype(BF16)
    for index in range(2, 16):
        h2[:, span(index)] = jnp.tanh(wide_dot(h1, p2_ref, index, index % 4)).astype(BF16)
    for index in range(3, 15):
        out = jnp.tanh(wide_dot(h2, p3_ref, index, index % 4)).astype(BF16)
        h3[:, span(index)] = out
        taps = jnp.dot(p4_ref[...], out, preferred_element_type=F32)
        acc = None
        for position in range(7):
            shifted = one_shift(chunks_of(taps[8 * position:8 * position + 8]), position)
            acc = shifted if acc is None else [a + b for a, b in zip(acc, shifted)]
        parts[0, :, span(index)] = jnp.concatenate(acc, axis=1)
        parts[1, :, span(index)] = taps[56:64]
        parts[2, :, span(index)] = taps[64:72]

    for index in range(4, 14):
        coeff = jnp.tanh(parts[0, :, span(index)] + parts[1, :, span(index + 1)] + parts[2, :, span(index - 1)])
        blend = mixed[:, span(index)]
        value = (blend + coeff * pltpu.roll(blend, 4, 0)) * (1.0 - coeff * coeff)
        lasts[:, span(index)] = jnp.where(row8 < 4, value, 0.0).astype(BF16).astype(F32)
        if 7 <= index < 11:
            coeff_ref[index - 7] = coeff

    own = span(7, 4)
    contract = (((1,), (1,)), ((), ()))
    for index in (5, 6, 11, 12, 7, 8, 9, 10):
        out = thin_dot(lasts, b4_ref, index, (index + 1) % 4)
        g3[:, span(index)] = (out * one_minus_square(h3[:, span(index)])).astype(BF16)
    grad_last = lax.dot_general(thin[...], h3[:, own], contract, preferred_element_type=F32)
    for index in (6, 11, 7, 8, 9, 10):
        out = wide_dot(g3, b3_ref, index, (index + 1) % 4)
        g2[:, span(index)] = (out * one_minus_square(h2[:, span(index)])).astype(BF16)
    grad_third = lax.dot_general(wide[...], h2[:, own], contract, preferred_element_type=F32)
    for index in (7, 8, 9, 10):
        out = wide_dot(g2, b2_ref, index, (index + 1) % 4)
        g1[:, slot_of(index - 7)] = (out * one_minus_square(h1[:, span(index)])).astype(BF16)
    grad_second = lax.dot_general(wide[...], h1[:, own], contract, preferred_element_type=F32)
    for index in (7, 8, 9, 10):
        stack_thin(feats, thin, index, index - 7)
    grad_first = lax.dot_general(g1[...], thin[...], contract, preferred_element_type=F32)

    spread, keep = selectors()
    ordered = jnp.concatenate([grad_last[8 * SWAP[k]:8 * SWAP[k] + 8] for k in range(TAPS)], axis=0)
    broad = jnp.dot(spread, ordered.astype(BF16), preferred_element_type=F32)
    broad = jnp.where(keep, broad, 0.0).astype(BF16)
    place = (
        lax.broadcasted_iota(jnp.int32, (H, LANES), 1) == 104 + lax.broadcasted_iota(jnp.int32, (H, LANES), 0) % 4
    ).astype(F32).astype(BF16)
    packed[...] = jnp.dot(broad, place, preferred_element_type=F32)
    for k in range(TAPS):
        rows = slice(H * k, H * k + H)
        back = slice(H * SWAP[k], H * SWAP[k] + H)
        packed[rows, 0:48] = grad_second[back]
        packed[rows, 48:96] = grad_third[back]
        packed[rows, 96:104] = grad_first[:, 8 * k:8 * k + 8]
    if split:
        for d in range(16):
            grads_ref[d] = packed[27 * d:27 * d + 27, :].astype(BF16)
    else:
        grads_ref[...] = packed[...].astype(BF16)


def update_kernel(dense, w1_ref, w2_ref, coeff_ref, out_ref, factors):
    for mu in range(4):
        for t in range(4):
            for c in range(2):
                factors[mu, c, t:t + 1, :] = coeff_ref[t, mu:mu + 1, c * 128:c * 128 + 128]
                factors[mu, c, 4 + t:5 + t, :] = coeff_ref[t, mu:mu + 1, 256 + c * 128:384 + c * 128]

    def body(mu, carry):
        factor = [factors[mu, c] for c in range(2)]
        half = [0.5 * value * value for value in factor]
        for e, (part, i, j) in enumerate(ENTRIES):
            new = [dense[mu, e, c] + factor[c] * w1_ref[mu, e, c] + half[c] * w2_ref[mu, e, c] for c in range(2)]
            out_ref[mu, part, i, j, 0] = jnp.concatenate(
                [new[0][0:4], new[1][0:4], new[0][4:8], new[1][4:8]], axis=1
            )
        return carry

    lax.fori_loop(0, 4, body, 0)


def sum_kernel(widths, parts_ref, first_ref, second_ref, third_ref, last_ref):
    value = parts_ref[0].astype(F32)
    for d in range(1, parts_ref.shape[0]):
        value = value + parts_ref[d].astype(F32)
    offset = 0
    for ref, width in zip((second_ref, third_ref, first_ref, last_ref), widths):
        for r in range(27):
            ref[:, width * r:width * r + width] = value[r:r + 1, offset:offset + width]
        offset += width


def call(body, outs, scratch, places=None, cost=None, limit=LIMIT):
    specs = {}
    if places is not None:
        specs["in_specs"] = [pl.BlockSpec(memory_space=place) for place in places]
    return pl.pallas_call(
        body,
        out_shape=[jax.ShapeDtypeStruct(shape, dtype) for shape, dtype in outs],
        scratch_shapes=[pltpu.VMEM(*item) if isinstance(item, tuple) else item for item in scratch],
        compiler_params=pltpu.CompilerParams(vmem_limit_bytes=limit),
        cost_estimate=cost,
        **specs,
    )


def on_device(links, cotangent, parity, link_subset, w_first, w_second, w_third, w_last):
    count = lax.axis_size("tm")

    def send(value, distance):
        return lax.ppermute(value, "tm", [(i, (i + distance) % count) for i in range(count)])

    widths = (768 // count, 768 // count, 128 // count, 64 // count)
    field = ((4, 18, 2, 8, LANES), F32)
    space = ((3, 18, 2, 8, LANES), F32)
    edge_rows = ((70, SITES), BF16)
    vmem, smem = pltpu.VMEM, pltpu.SMEM
    up, down, dense, edges, staples, slab = call(
        face_kernel,
        [edge_rows, edge_rows, field, space, space, ((12, 4, LANES), F32)],
        [space, ((70, 4, LANES), F32)],
    )(links)
    up = send(up, 1)
    down = send(down, -1)
    cots, rows, forces, sums, gates = call(
        space_kernel,
        [field, ((4, 4, 16, LANES), F32), ((4, 9, 2, 8, LANES), F32), space, ((4, 8, LANES), F32)],
        [((3, 3, 18, 2, 8, LANES), F32), ((3, 3, 18, 2, 8, LANES), F32)],
        places=(smem, smem, vmem, vmem, vmem),
        cost=pl.CostEstimate(flops=4_000_000_000, bytes_accessed=16_000_000, transcendentals=0),
    )(parity, link_subset, dense, cotangent, staples)
    fm, fup, fdown, applied, twice = call(
        time_kernel,
        [((4, 16, SITES), BF16), ((3, 8, SITES), BF16), ((3, 8, SITES), BF16), field, field],
        [
            space, space, field, ((70, 4, LANES), F32), ((70, 4, LANES), F32),
            ((4, 9, 2, 8, LANES), F32), ((4, 4, 16, LANES), F32),
        ],
    )(dense, cots, up, down, gates, edges, rows, forces, sums)
    core = (lax.axis_index("tm") % 2).astype(jnp.int32)[None]
    (block,) = call(
        functools.partial(block_kernel, widths),
        [((count, BLOCKROWS, LANES), BF16)],
        [((12, 4, LANES), F32), ((BLOCKROWS, LANES), F32)],
        places=(smem,) + (vmem,) * 8,
    )(core, up, down, slab, w_first, w_second, w_third, w_last, fdown)
    gathered = lax.all_to_all(block, "tm", split_axis=0, concat_axis=0, tiled=True)
    below = send(fm, 1)
    above = send(fm, -1)
    fbelow = send(fup, 2)
    fabove = send(fdown, -2)

    panel_outs = [
        ((2, 4, LANES), F32), ((H, 72), BF16), ((H, 432), BF16), ((H, 432), BF16), ((72, H), BF16),
        ((H, 432), BF16), ((H, 432), BF16), ((H, 72), BF16),
    ]
    panel_scratch = [((432, LANES), F32)]
    if count == 16:
        loops, p1, p2, p3, p4, b2, b3, b4 = call(panel_kernel_plain, panel_outs, panel_scratch)(gathered)
    else:
        pieces = []
        offset = 0
        for width, full in zip(widths, (48, 48, 8, 4)):
            piece = gathered[:, SLABROWS:SLABROWS + 27, offset:offset + width]
            pieces.append(piece.reshape(432, full))
            offset += width
        pieces.append(jnp.zeros((432, 20), BF16))
        loops, p1, p2, p3, p4, b2, b3, b4 = call(panel_kernel, panel_outs, panel_scratch)(
            gathered, jnp.concatenate(pieces, axis=1)
        )

    window = 18 * SITES
    coeff, grads = call(
        functools.partial(conv_kernel, count == 16),
        [((4, 8, SITES), F32), ((16, 27, LANES) if count == 16 else (432, LANES), BF16)],
        [
            ((8, window), F32), ((8, window), F32), ((H, window), BF16), ((H, window), BF16), ((H, window), BF16),
            ((3, 8, window), F32), ((8, window), F32), ((H, window), BF16), ((H, window), BF16), ((H, 4 * SITES), BF16),
            ((432, 4 * SITES), BF16), ((72, 4 * SITES), BF16), ((432, LANES), F32),
        ],
        limit=20 * 1024 * 1024,
    )(fm, below, above, fbelow, fabove, loops, p1, p2, p3, p4, b2, b3, b4)
    if count != 16:
        offset = 0
        pieces = []
        for width, full in zip(widths, (48, 48, 8, 4)):
            pieces.append(grads[:, offset:offset + full].reshape(count, 27, width))
            offset += full
        grads = jnp.concatenate(pieces, axis=2)
    grads = lax.all_to_all(grads, "tm", split_axis=0, concat_axis=0, tiled=True)
    (new_links,) = call(
        update_kernel, [(links.shape, F32)], [((4, 2, 8, LANES), F32)]
    )(dense, applied, twice, coeff)
    grad_first, grad_second, grad_third, grad_last = call(
        functools.partial(sum_kernel, widths),
        [((1, 27 * width), F32) for width in (widths[2], widths[0], widths[1], widths[3])],
        [],
    )(grads)
    return (new_links, grad_first, grad_second, grad_third, grad_last)


def solution(mesh):
    placed = (
        P(None, None, None, None, "groups", "tm", None),
        P(None, None, None, None, "groups", "tm", None),
        P("groups", "tm"),
        P("groups", "tm"),
        P("tm"),
        P("tm"),
        P("tm"),
        P("tm"),
    )
    return jax.shard_map(
        on_device,
        mesh=mesh,
        in_specs=placed,
        out_specs=(
            P(None, None, None, None, "groups", "tm", None),
            P("groups", "tm"),
            P("groups", "tm"),
            P("groups", "tm"),
            P("groups", "tm"),
        ),
        check_vma=False,
    )
```

```python
import functools

import jax
import jax.numpy as jnp
from jax import lax
from jax.experimental import pallas as pl
from jax.experimental.pallas import tpu as pltpu
from jax.sharding import PartitionSpec as P

F32 = jnp.float32
BF16 = jnp.bfloat16
TAPS = 9
H = 48
LANES = 128
SITES = 512
PAIRS = ((0, 1), (0, 2), (0, 3), (1, 2), (1, 3), (2, 3))
SWAP = (0, 2, 1, 4, 3, 6, 5, 8, 7)
ENTRIES = tuple((c, i, j) for c in range(2) for i in range(3) for j in range(3))
EDGE = 4
STAPLE = 7
PLANE = 180
GATE = 186
SLABROWS = 24
BLOCKROWS = 64
LIMIT = 8 * 1024 * 1024


def lane_iota(rows):
    return lax.broadcasted_iota(jnp.int32, (rows, LANES), 1)


def row_iota():
    return lax.broadcasted_iota(jnp.int32, (8, LANES), 0)


def roll_lanes(value, amount):
    return pltpu.roll(value, amount % LANES, 1)


def shift_z(chunk, sign, lanes):
    z = lanes % 8
    if sign > 0:
        return jnp.where(z == 7, roll_lanes(chunk, 7), roll_lanes(chunk, -1))
    return jnp.where(z == 0, roll_lanes(chunk, -7), roll_lanes(chunk, 1))


def shift_y(chunk, sign, lanes):
    y = lanes // 8 % 8
    if sign > 0:
        return jnp.where(y == 7, roll_lanes(chunk, 56), roll_lanes(chunk, -8))
    return jnp.where(y == 0, roll_lanes(chunk, -56), roll_lanes(chunk, 8))


def dense_shift(pair, axis, sign):
    lanes = lane_iota(8)
    if axis == 2:
        return [shift_z(chunk, sign, lanes) for chunk in pair]
    if axis == 1:
        return [shift_y(chunk, sign, lanes) for chunk in pair]
    low = lanes < 64
    first, second = [roll_lanes(chunk, 64) for chunk in pair]
    if sign > 0:
        return [jnp.where(low, first, second), jnp.where(low, second, pltpu.roll(first, 4, 0))]
    return [jnp.where(low, pltpu.roll(second, 4, 0), first), jnp.where(low, first, second)]


def pack_pair(value):
    return [
        jnp.concatenate([value[:, c * 128:c * 128 + 128], value[:, 256 + c * 128:384 + c * 128]], axis=0)
        for c in range(2)
    ]


def halo_pair(ref, index):
    top = row_iota() < 4
    pair = []
    for c in range(2):
        low = jnp.broadcast_to(ref[index, c:c + 1, :], (8, LANES))
        high = jnp.broadcast_to(ref[index, 2 + c:3 + c, :], (8, LANES))
        pair.append(jnp.where(top, low, high))
    return pair


def load_matrix(read):
    real = [[read(3 * i + j) for j in range(3)] for i in range(3)]
    imag = [[read(9 + 3 * i + j) for j in range(3)] for i in range(3)]
    return (real, imag, 1)


def dagger(matrix):
    real, imag, sign = matrix
    return (
        [[real[j][i] for j in range(3)] for i in range(3)],
        [[imag[j][i] for j in range(3)] for i in range(3)],
        -sign,
    )


def total(terms, signs):
    value = None
    for term, sign in zip(terms, signs):
        if value is None:
            value = term if sign > 0 else -term
        else:
            value = value + term if sign > 0 else value - term
    return value


def mat_mul(left, right):
    lr, li, ls = left
    rr, ri, rs = right
    same = ls == rs
    height = len(lr)
    real = [[None] * 3 for _ in range(height)]
    imag = [[None] * 3 for _ in range(height)]
    for i in range(height):
        for j in range(3):
            real[i][j] = total(
                [lr[i][k] * rr[k][j] for k in range(3)] + [li[i][k] * ri[k][j] for k in range(3)],
                [1, 1, 1] + [-1 if same else 1] * 3,
            )
            imag[i][j] = total(
                [lr[i][k] * ri[k][j] for k in range(3)] + [li[i][k] * rr[k][j] for k in range(3)],
                [1, 1, 1] + [1 if same else -1] * 3,
            )
    return (real, imag, ls if same else rs)


def imag_of(matrix, i, j):
    return matrix[1][i][j] if matrix[2] > 0 else -matrix[1][i][j]


def store_matrix(matrix, write):
    for i in range(3):
        for j in range(3):
            write(3 * i + j, matrix[0][i][j])
            write(9 + 3 * i + j, imag_of(matrix, i, j))


def two_rows(read):
    real = [[read(3 * i + j) for j in range(3)] for i in range(2)]
    imag = [[read(6 + 3 * i + j) for j in range(3)] for i in range(2)]
    return (real, imag, 1)


def store_rows(matrix, write):
    for i in range(2):
        for j in range(3):
            write(3 * i + j, matrix[0][i][j])
            write(6 + 3 * i + j, imag_of(matrix, i, j))


def special(matrix):
    real, imag, _ = matrix
    last_r, last_i = [], []
    for k in range(3):
        i, j = (k + 1) % 3, (k + 2) % 3
        last_r.append(
            (real[0][i] * real[1][j] - imag[0][i] * imag[1][j])
            - (real[0][j] * real[1][i] - imag[0][j] * imag[1][i])
        )
        last_i.append(
            (real[0][j] * imag[1][i] + imag[0][j] * real[1][i])
            - (real[0][i] * imag[1][j] + imag[0][i] * real[1][j])
        )
    return (real + [last_r], imag + [last_i], 1)


def anti_parts(matrix):
    parts = [2.0 * imag_of(matrix, i, i) for i in range(3)]
    for i, j in ((0, 1), (0, 2), (1, 2)):
        parts.append(matrix[0][i][j] - matrix[0][j][i])
        parts.append(imag_of(matrix, i, j) + imag_of(matrix, j, i))
    return parts


def anti_matrix(parts):
    zero = jnp.zeros_like(parts[0])
    real = [[zero, parts[3], parts[5]], [-parts[3], zero, parts[7]], [-parts[5], -parts[7], zero]]
    imag = [[parts[0], parts[4], parts[6]], [parts[4], parts[1], parts[8]], [parts[6], parts[8], parts[2]]]
    return real, imag


def anti_mul(parts, right):
    real, imag = anti_matrix(parts)
    rr, ri, _ = right
    out_r = [[None] * 3 for _ in range(3)]
    out_i = [[None] * 3 for _ in range(3)]
    for i in range(3):
        for j in range(3):
            value_r = -(imag[i][i] * ri[i][j])
            value_i = imag[i][i] * rr[i][j]
            for k in range(3):
                if k != i:
                    value_r = value_r + real[i][k] * rr[k][j] - imag[i][k] * ri[k][j]
                    value_i = value_i + real[i][k] * ri[k][j] + imag[i][k] * rr[k][j]
            out_r[i][j] = value_r
            out_i[i][j] = value_i
    return (out_r, out_i, 1)


def pack_links(links_ref, dense):
    def body(mu, carry):
        for e, (c, i, j) in enumerate(ENTRIES):
            low, high = pack_pair(links_ref[mu, c, i, j, 0].astype(F32))
            dense[mu, e, 0] = low
            dense[mu, e, 1] = high
        return carry

    lax.fori_loop(0, 4, body, 0)


def face_kernel(links_ref, up_ref, down_ref, dense, slab, moved, rows):
    pack_links(links_ref, dense)

    def shift_body(e, carry):
        pair = [dense[3, e, 0], dense[3, e, 1]]
        for mu in range(3):
            low, high = dense_shift(pair, mu, 1)
            moved[mu, e, 0] = low
            moved[mu, e, 1] = high
        return carry

    lax.fori_loop(0, 18, shift_body, 0)

    def staple_body(step, carry):
        mu = step // 2
        c = step % 2
        u_mu = load_matrix(lambda e: dense[mu, e, c])
        u_t = load_matrix(lambda e: dense[3, e, c])
        edge = mat_mul(u_mu, load_matrix(lambda e: moved[mu, e, c]))

        def write_edge(e, value):
            dense[EDGE + mu, e, c] = value

        store_matrix(edge, write_edge)

        def write(e, value):
            dense[STAPLE + mu, e, c] = value
            rows[16 + mu * 18 + e, pl.ds(c, 1)] = value[3:4]
            rows[16 + mu * 18 + e, pl.ds(2 + c, 1)] = value[7:8]

        store_matrix(mat_mul(dagger(edge), u_t), write)
        return carry

    lax.fori_loop(0, 6, staple_body, 0)

    def slab_body(c, carry):
        u_t = load_matrix(lambda e: dense[3, e, c])
        ahead = load_matrix(lambda e: pltpu.roll(dense[3, e, c], 7, 0))
        two = mat_mul(u_t, ahead)
        later = tuple(
            [[pltpu.roll(part[i][j], 6, 0) for j in range(3)] for i in range(3)] for part in two[:2]
        ) + (two[2],)
        four = mat_mul((two[0][:2], two[1][:2], two[2]), later)

        def write(e, value):
            slab[e, pl.ds(c, 1)] = value[0:1]
            slab[e, pl.ds(2 + c, 1)] = value[4:5]
            rows[e, pl.ds(c, 1)] = value[0:1]
            rows[e, pl.ds(2 + c, 1)] = value[4:5]

        store_rows(four, write)
        return carry

    lax.fori_loop(0, 2, slab_body, 0)
    for q in range(4):
        up_ref[:, q * 128:q * 128 + 128] = rows[:, q, :].astype(BF16)

    def down_body(e, carry):
        for mu in range(3):
            for c in range(2):
                value = dense[mu, e, c]
                rows[16 + mu * 18 + e, c:c + 1] = value[0:1]
                rows[16 + mu * 18 + e, 2 + c:3 + c] = value[4:5]
        return carry

    lax.fori_loop(0, 18, down_body, 0)
    for q in range(4):
        down_ref[:, q * 128:q * 128 + 128] = rows[:, q, :].astype(BF16)


def block_kernel(
    widths, core_ref, up_ref, down_ref, slab, w1_ref, w2_ref, w3_ref, w4_ref, after_ref, block_ref, other, block
):
    even = core_ref[0] == 0
    up = up_ref[0:16].astype(F32)
    down = down_ref[0:16].astype(F32)
    for q in range(4):
        lanes = slice(q * 128, q * 128 + 128)
        other[:, q, :] = jnp.where(even, down[0:12, lanes], up[0:12, lanes])
    first = two_rows(lambda e: jnp.where(even, slab[e], other[e]))
    second = special(two_rows(lambda e: jnp.where(even, other[e], slab[e])))

    def write(e, value):
        block[2 * e:2 * e + 2, :] = jnp.where(even, value[0:2], value[2:4])

    store_rows(mat_mul(first, second), write)
    block[SLABROWS:BLOCKROWS] = jnp.zeros((BLOCKROWS - SLABROWS, LANES), F32)
    offset = 0
    for ref, width in zip((w2_ref, w3_ref, w1_ref, w4_ref), widths):
        flat = ref[...].astype(F32)
        for r in range(27):
            block[SLABROWS + r:SLABROWS + r + 1, offset:offset + width] = (
                flat[width * r:width * r + width].reshape(1, width)
            )
        offset += width
    value = block[...].astype(BF16)
    for d in range(block_ref.shape[0]):
        block_ref[d] = value


def put_row(rows, channel, c, value):
    for t in range(4):
        rows[t, c, pl.ds(channel, 1), :] = value[t:t + 1]
        rows[t, 2 + c, pl.ds(channel, 1), :] = value[4 + t:5 + t]


def sum_at(mu, e, c):
    return (mu * 18 + e) * 2 + c


def force_at(mu, e, c):
    return 108 + (mu * 9 + e) * 2 + c


def cot_at(mu, e, c):
    return 190 + (mu * 18 + e) * 2 + c


def space_kernel(parity_ref, subset_ref, dense, cot_ref, state, moved, staples):
    def cot_body(mu, carry):
        for e, (part, i, j) in enumerate(ENTRIES):
            low, high = pack_pair(cot_ref[mu, part, i, j, 0].astype(F32))
            state[cot_at(mu, e, 0)] = low
            state[cot_at(mu, e, 1)] = high
        return carry

    lax.fori_loop(0, 4, cot_body, 0)
    state[108:180] = jnp.zeros((72, 8, LANES), F32)
    steps = row_iota() % 4
    lanes = lane_iota(8)
    colour = (lanes // 64 + lanes // 8 % 8 + lanes % 8 + steps) % 2
    parity = jnp.zeros_like(steps)
    subset = jnp.zeros_like(steps)
    for t in range(4):
        parity = jnp.where(steps == t, parity_ref[0, t], parity)
        subset = jnp.where(steps == t, subset_ref[0, t], subset)
    for mu in range(4):
        active = jnp.logical_and(colour == parity, jnp.right_shift(subset, mu) % 2 == 1)
        state[GATE + mu] = jnp.where(active, 1.0, 0.0)

    def shift_body(e, carry):
        for nu in range(3):
            pair = [dense[nu, e, 0], dense[nu, e, 1]]
            for mu in range(3):
                if mu != nu:
                    low, high = dense_shift(pair, mu, 1)
                    moved[mu, nu, e, 0] = low
                    moved[mu, nu, e, 1] = high
        return carry

    lax.fori_loop(0, 18, shift_body, 0)

    def plane_body(step, carry):
        plane = step // 2
        c = step % 2
        mu = jnp.where(plane == 2, 1, 0)
        nu = jnp.where(plane == 0, 1, 2)
        u_mu = load_matrix(lambda e: dense[mu, e, c])
        u_nu = load_matrix(lambda e: dense[nu, e, c])
        one = mat_mul(u_mu, load_matrix(lambda e: moved[mu, nu, e, c]))
        two = mat_mul(u_nu, load_matrix(lambda e: moved[nu, mu, e, c]))
        loop = mat_mul(one, dagger(two))
        state[PLANE + step] = (loop[0][0][0] + loop[0][1][1] + loop[0][2][2]) / 3.0
        for e, part in enumerate(anti_parts(loop)):
            state[force_at(mu, e, c)] += part
            state[force_at(nu, e, c)] -= part

        def write_mu(e, value):
            staples[mu, nu, e, c] = value

        def write_nu(e, value):
            staples[nu, mu, e, c] = value

        store_matrix(mat_mul(dagger(one), u_nu), write_mu)
        store_matrix(mat_mul(dagger(two), u_mu), write_nu)
        return carry

    lax.fori_loop(0, 6, plane_body, 0)

    def lower_body(e, carry):
        for mu in range(3):
            acc = [jnp.where(steps == 0, 0.0, pltpu.roll(dense[STAPLE + mu, e, c], 1, 0)) for c in range(2)]
            for nu in range(3):
                if nu != mu:
                    pair = dense_shift([staples[mu, nu, e, 0], staples[mu, nu, e, 1]], nu, -1)
                    acc = [acc[c] + pair[c] for c in range(2)]
            state[sum_at(mu, e, 0)] = acc[0]
            state[sum_at(mu, e, 1)] = acc[1]
        return carry

    lax.fori_loop(0, 18, lower_body, 0)


def time_kernel(
    dense, state, up_ref, down_ref,
    fm_ref, fup_ref, fdown_ref, w1_ref, w2_ref,
    moved, staples, sums, halo_up, halo_down, forces, rows,
):
    for q in range(4):
        halo_up[:, q, :] = up_ref[:, q * 128:q * 128 + 128].astype(F32)
        halo_down[:, q, :] = down_ref[:, q * 128:q * 128 + 128].astype(F32)
    rows[...] = jnp.zeros_like(rows)
    for channel, plane in ((0, 0), (1, 1), (3, 2)):
        for c in range(2):
            put_row(rows, channel, c, state[PLANE + 2 * plane + c])
    for mu in range(4):
        for e in range(9):
            for c in range(2):
                forces[mu, e, c] = state[force_at(mu, e, c)]
    steps = row_iota() % 4

    def shift_body(e, carry):
        for nu in range(3):
            halo = halo_pair(halo_down, 16 + nu * 18 + e)
            below = halo_pair(halo_up, 16 + nu * 18 + e)
            for c in range(2):
                moved[nu, e, c] = jnp.where(steps == 3, halo[c], pltpu.roll(dense[nu, e, c], 7, 0))
                sums[nu, e, c] = state[sum_at(nu, e, c)] + jnp.where(steps == 0, below[c], 0.0)
        return carry

    lax.fori_loop(0, 18, shift_body, 0)

    def plane_body(step, carry):
        mu = step // 2
        c = step % 2
        one = load_matrix(lambda e: dense[EDGE + mu, e, c])
        two = mat_mul(load_matrix(lambda e: dense[3, e, c]), load_matrix(lambda e: moved[mu, e, c]))
        loop = mat_mul(one, dagger(two))
        put_row(rows, jnp.where(mu == 0, 2, mu + 3), c, (loop[0][0][0] + loop[0][1][1] + loop[0][2][2]) / 3.0)
        for e, part in enumerate(anti_parts(loop)):
            forces[mu, e, c] += part
            forces[3, e, c] -= part

        def write(e, value):
            staples[mu, e, c] = value

        store_matrix(mat_mul(dagger(two), load_matrix(lambda e: dense[mu, e, c])), write)
        return carry

    lax.fori_loop(0, 6, plane_body, 0)

    def lower_body(e, carry):
        acc = None
        for mu in range(3):
            pair = dense_shift([staples[mu, e, 0], staples[mu, e, 1]], mu, -1)
            acc = pair if acc is None else [acc[c] + pair[c] for c in range(2)]
        sums[3, e, 0] = acc[0]
        sums[3, e, 1] = acc[1]
        return carry

    lax.fori_loop(0, 18, lower_body, 0)

    def force_body(step, carry):
        mu = step // 2
        c = step % 2
        current = load_matrix(lambda e: dense[mu, e, c])
        omega = mat_mul(current, load_matrix(lambda e: sums[mu, e, c]))
        parts = [part + forces[mu, e, c] for e, part in enumerate(anti_parts(omega))]
        mean = (parts[0] + parts[1] + parts[2]) * (1.0 / 3.0)
        parts = [parts[e] - mean if e < 3 else parts[e] for e in range(9)]
        parts = [part * (1.0 / 12.0) for part in parts]
        applied = anti_mul(parts, current)
        twice = anti_mul(parts, applied)
        gate = state[GATE + mu]
        slope = jnp.zeros_like(gate)
        curve = jnp.zeros_like(gate)
        for e, (part, i, j) in enumerate(ENTRIES):
            weight = state[cot_at(mu, e, c)]
            slope = slope + weight * applied[part][i][j]
            curve = curve + weight * twice[part][i][j]
            w1_ref[mu, e, c] = gate * applied[part][i][j]
            w2_ref[mu, e, c] = gate * twice[part][i][j]
        put_row(rows, 8 + mu, c, gate * slope)
        put_row(rows, 12 + mu, c, gate * curve)
        return carry

    lax.fori_loop(0, 8, force_body, 0)
    for t in range(4):
        for q in range(4):
            value = rows[t, q]
            fm_ref[t, :, q * 128:q * 128 + 128] = value.astype(BF16)
            if t > 0:
                fup_ref[t - 1, :, q * 128:q * 128 + 128] = value[0:8].astype(BF16)
            if t < 3:
                fdown_ref[t, :, q * 128:q * 128 + 128] = value[0:8].astype(BF16)


def selectors():
    row = lax.broadcasted_iota(jnp.int32, (432, 72), 0)
    col = lax.broadcasted_iota(jnp.int32, (432, 72), 1)
    group = row // 12
    spread = (group // 4 * 8 + group % 4 == col).astype(F32).astype(BF16)
    keep = (
        lax.broadcasted_iota(jnp.int32, (432, H), 1) // 4 == lax.broadcasted_iota(jnp.int32, (432, H), 0) % 12
    )
    return spread, keep


def panel_kernel(gathered_ref, weights_ref, loops_ref, p1_ref, p2_ref, p3_ref, p4_ref, b2_ref, b3_ref, b4_ref, weights):
    count = gathered_ref.shape[0]

    def read(chip):
        low = gathered_ref[2 * chip].astype(F32)
        high = gathered_ref[2 * chip + 1].astype(F32)
        return special(
            two_rows(lambda e: jnp.concatenate([low[2 * e:2 * e + 2], high[2 * e:2 * e + 2]], axis=0))
        )

    def flat(matrix):
        return tuple(matrix[0][i][j] for i in range(3) for j in range(3)) + tuple(
            imag_of(matrix, i, j) for i in range(3) for j in range(3)
        )

    def chain(chip, state):
        return flat(mat_mul(load_matrix(lambda e: state[e]), read(chip)))

    state = lax.fori_loop(1, count // 2, chain, flat(read(0)))
    loops_ref[0] = (state[0] + state[4] + state[8]) / 3.0
    loops_ref[1] = (state[9] + state[13] + state[17]) / 3.0

    if weights_ref is None:
        for d in range(count):
            block = gathered_ref[d].astype(F32)
            weights[27 * d:27 * d + 27, :] = block[SLABROWS:SLABROWS + 27]
    else:
        weights[...] = weights_ref[...].astype(F32)
    for k in range(TAPS):
        rows = slice(H * k, H * k + H)
        back = slice(H * SWAP[k], H * SWAP[k] + H)
        p2_ref[:, rows] = weights[rows, 0:48].astype(BF16)
        p3_ref[:, rows] = weights[rows, 48:96].astype(BF16)
        p1_ref[:, 8 * k:8 * k + 8] = weights[rows, 96:104].astype(BF16)
        turned = weights[back, :].T
        b2_ref[:, rows] = turned[0:48].astype(BF16)
        b3_ref[:, rows] = turned[48:96].astype(BF16)
    spread, keep = selectors()
    place = (
        lax.broadcasted_iota(jnp.int32, (LANES, H), 0) == 104 + lax.broadcasted_iota(jnp.int32, (LANES, H), 1) % 4
    ).astype(F32).astype(BF16)
    wide = jnp.dot(weights[...].astype(BF16), place, preferred_element_type=F32)
    wide = jnp.where(keep, wide, 0.0).astype(BF16)
    last = lax.dot_general(spread, wide, (((0,), (0,)), ((), ())), preferred_element_type=F32)
    p4_ref[...] = last.astype(BF16)
    for k in range(TAPS):
        b4_ref[:, 8 * k:8 * k + 8] = last[8 * SWAP[k]:8 * SWAP[k] + 8, :].T.astype(BF16)


def panel_kernel_plain(gathered_ref, *rest):
    panel_kernel(gathered_ref, None, *rest)


def chunks_of(value):
    return [value[:, q * 128:q * 128 + 128] for q in range(4)]


def one_shift(chunks, position):
    if position == 0:
        return chunks
    lanes = lane_iota(chunks[0].shape[0])
    sign = 1 if position % 2 == 1 else -1
    if position > 4:
        return [shift_z(chunk, sign, lanes) for chunk in chunks]
    if position > 2:
        return [shift_y(chunk, sign, lanes) for chunk in chunks]
    low = lanes < 64
    rolled = [roll_lanes(chunk, 64) for chunk in chunks]
    if sign > 0:
        return [jnp.where(low, rolled[q], rolled[(q + 1) % 4]) for q in range(4)]
    return [jnp.where(low, rolled[(q + 3) % 4], rolled[q]) for q in range(4)]


def span(slice_index, count=1):
    if isinstance(slice_index, int):
        return slice(slice_index * SITES, (slice_index + count) * SITES)
    return pl.ds(pl.multiple_of(slice_index * SITES, SITES), count * SITES)


def slot_of(slot):
    return slice(slot * SITES, (slot + 1) * SITES)


def stack_wide(source, target, index, slot):
    chunks = chunks_of(source[:, span(index)])
    for position in range(7):
        shifted = one_shift(chunks, position)
        for q in range(4):
            lanes = slice(slot * SITES + q * 128, slot * SITES + q * 128 + 128)
            target[H * position:H * position + H, lanes] = shifted[q]
    target[7 * H:8 * H, slot_of(slot)] = source[:, span(index + 1)]
    target[8 * H:9 * H, slot_of(slot)] = source[:, span(index - 1)]


def stack_thin(source, target, index, slot):
    chunks = chunks_of(source[:, span(index)])
    ahead = chunks_of(source[:, span(index + 1)])
    behind = chunks_of(source[:, span(index - 1)])
    columns = [one_shift(chunks, position) for position in range(7)] + [ahead, behind]
    for q in range(4):
        lanes = slice(slot * SITES + q * 128, slot * SITES + q * 128 + 128)
        target[0:72, lanes] = jnp.concatenate([column[q] for column in columns], axis=0).astype(BF16)


def one_minus_square(value):
    value = value.astype(F32)
    return 1.0 - value * value


def conv_kernel(
    split, fm_ref, below_ref, above_ref, fbelow_ref, fabove_ref, loops_ref,
    p1_ref, p2_ref, p3_ref, p4_ref, b2_ref, b3_ref, b4_ref,
    coeff_ref, grads_ref,
    feats, mixed, h1, h2, h3, parts, lasts, g3, g2, g1, wide, thin, packed,
):
    row8 = lax.broadcasted_iota(jnp.int32, (8, SITES), 0)
    loop_re = jnp.concatenate([loops_ref[0, q:q + 1, :] for q in range(4)], axis=1)
    loop_im = jnp.concatenate([loops_ref[1, q:q + 1, :] for q in range(4)], axis=1)
    loops = jnp.where(row8 == 6, loop_re, jnp.where(row8 == 7, loop_im, 0.0))
    loops = loops.astype(BF16).astype(F32)
    for j in range(3):
        feats[:, span(j)] = fbelow_ref[j].astype(F32) + loops
        feats[:, span(15 + j)] = fabove_ref[j].astype(F32) + loops
    for base, ref in ((3, below_ref), (7, fm_ref), (11, above_ref)):
        for j in range(4):
            value = ref[j].astype(F32)
            feats[:, span(base + j)] = value[0:8] + loops
            mixed[:, span(base + j)] = value[8:16]

    def wide_dot(source, weights, index, slot):
        stack_wide(source, wide, index, slot)
        return jnp.dot(weights[...], wide[:, slot_of(slot)], preferred_element_type=F32)

    def thin_dot(source, weights, index, slot):
        stack_thin(source, thin, index, slot)
        return jnp.dot(weights[...], thin[:, slot_of(slot)], preferred_element_type=F32)

    for index in range(1, 17):
        h1[:, span(index)] = jnp.tanh(thin_dot(feats, p1_ref, index, index % 4)).astype(BF16)
    for index in range(2, 16):
        h2[:, span(index)] = jnp.tanh(wide_dot(h1, p2_ref, index, index % 4)).astype(BF16)
    for index in range(3, 15):
        out = jnp.tanh(wide_dot(h2, p3_ref, index, index % 4)).astype(BF16)
        h3[:, span(index)] = out
        taps = jnp.dot(p4_ref[...], out, preferred_element_type=F32)
        acc = None
        for position in range(7):
            shifted = one_shift(chunks_of(taps[8 * position:8 * position + 8]), position)
            acc = shifted if acc is None else [a + b for a, b in zip(acc, shifted)]
        parts[0, :, span(index)] = jnp.concatenate(acc, axis=1)
        parts[1, :, span(index)] = taps[56:64]
        parts[2, :, span(index)] = taps[64:72]

    for index in range(4, 14):
        coeff = jnp.tanh(parts[0, :, span(index)] + parts[1, :, span(index + 1)] + parts[2, :, span(index - 1)])
        blend = mixed[:, span(index)]
        value = (blend + coeff * pltpu.roll(blend, 4, 0)) * (1.0 - coeff * coeff)
        lasts[:, span(index)] = jnp.where(row8 < 4, value, 0.0).astype(BF16).astype(F32)
        if 7 <= index < 11:
            coeff_ref[index - 7] = coeff

    own = span(7, 4)
    contract = (((1,), (1,)), ((), ()))
    for index in (5, 6, 11, 12, 7, 8, 9, 10):
        out = thin_dot(lasts, b4_ref, index, (index + 1) % 4)
        g3[:, span(index)] = (out * one_minus_square(h3[:, span(index)])).astype(BF16)
    grad_last = lax.dot_general(thin[...], h3[:, own], contract, preferred_element_type=F32)
    for index in (6, 11, 7, 8, 9, 10):
        out = wide_dot(g3, b3_ref, index, (index + 1) % 4)
        g2[:, span(index)] = (out * one_minus_square(h2[:, span(index)])).astype(BF16)
    grad_third = lax.dot_general(wide[...], h2[:, own], contract, preferred_element_type=F32)
    for index in (7, 8, 9, 10):
        out = wide_dot(g2, b2_ref, index, (index + 1) % 4)
        g1[:, slot_of(index - 7)] = (out * one_minus_square(h1[:, span(index)])).astype(BF16)
    grad_second = lax.dot_general(wide[...], h1[:, own], contract, preferred_element_type=F32)
    for index in (7, 8, 9, 10):
        stack_thin(feats, thin, index, index - 7)
    grad_first = lax.dot_general(g1[...], thin[...], contract, preferred_element_type=F32)

    spread, keep = selectors()
    ordered = jnp.concatenate([grad_last[8 * SWAP[k]:8 * SWAP[k] + 8] for k in range(TAPS)], axis=0)
    broad = jnp.dot(spread, ordered.astype(BF16), preferred_element_type=F32)
    broad = jnp.where(keep, broad, 0.0).astype(BF16)
    place = (
        lax.broadcasted_iota(jnp.int32, (H, LANES), 1) == 104 + lax.broadcasted_iota(jnp.int32, (H, LANES), 0) % 4
    ).astype(F32).astype(BF16)
    packed[...] = jnp.dot(broad, place, preferred_element_type=F32)
    for k in range(TAPS):
        rows = slice(H * k, H * k + H)
        back = slice(H * SWAP[k], H * SWAP[k] + H)
        packed[rows, 0:48] = grad_second[back]
        packed[rows, 48:96] = grad_third[back]
        packed[rows, 96:104] = grad_first[:, 8 * k:8 * k + 8]
    if split:
        for d in range(16):
            grads_ref[d] = packed[27 * d:27 * d + 27, :].astype(BF16)
    else:
        grads_ref[...] = packed[...].astype(BF16)


def update_kernel(dense, w1_ref, w2_ref, coeff_ref, out_ref, factors):
    for mu in range(4):
        for t in range(4):
            for c in range(2):
                factors[mu, c, t:t + 1, :] = coeff_ref[t, mu:mu + 1, c * 128:c * 128 + 128]
                factors[mu, c, 4 + t:5 + t, :] = coeff_ref[t, mu:mu + 1, 256 + c * 128:384 + c * 128]

    def body(mu, carry):
        factor = [factors[mu, c] for c in range(2)]
        half = [0.5 * value * value for value in factor]
        for e, (part, i, j) in enumerate(ENTRIES):
            new = [dense[mu, e, c] + factor[c] * w1_ref[mu, e, c] + half[c] * w2_ref[mu, e, c] for c in range(2)]
            out_ref[mu, part, i, j, 0] = jnp.concatenate(
                [new[0][0:4], new[1][0:4], new[0][4:8], new[1][4:8]], axis=1
            )
        return carry

    lax.fori_loop(0, 4, body, 0)


def sum_kernel(widths, parts_ref, first_ref, second_ref, third_ref, last_ref):
    value = parts_ref[0].astype(F32)
    for d in range(1, parts_ref.shape[0]):
        value = value + parts_ref[d].astype(F32)
    offset = 0
    for ref, width in zip((second_ref, third_ref, first_ref, last_ref), widths):
        for r in range(27):
            ref[:, width * r:width * r + width] = value[r:r + 1, offset:offset + width]
        offset += width


def call(body, outs, scratch, places=None, cost=None, limit=LIMIT):
    specs = {}
    if places is not None:
        specs["in_specs"] = [pl.BlockSpec(memory_space=place) for place in places]
    return pl.pallas_call(
        body,
        out_shape=[jax.ShapeDtypeStruct(shape, dtype) for shape, dtype in outs],
        scratch_shapes=[pltpu.VMEM(*item) if isinstance(item, tuple) else item for item in scratch],
        compiler_params=pltpu.CompilerParams(vmem_limit_bytes=limit),
        cost_estimate=cost,
        **specs,
    )


def on_device(links, cotangent, parity, link_subset, w_first, w_second, w_third, w_last):
    count = lax.axis_size("tm")

    def send(value, distance):
        return lax.ppermute(value, "tm", [(i, (i + distance) % count) for i in range(count)])

    widths = (768 // count, 768 // count, 128 // count, 64 // count)
    vmem, smem = pltpu.VMEM, pltpu.SMEM
    field = ((4, 18, 2, 8, LANES), F32)
    space = ((3, 18, 2, 8, LANES), F32)
    edge_rows = ((70, SITES), BF16)
    up, down, dense, slab = call(
        face_kernel,
        [edge_rows, edge_rows, ((10, 18, 2, 8, LANES), F32), ((12, 4, LANES), F32)],
        [space, ((70, 4, LANES), F32)],
    )(links)
    up = send(up, 1)
    down = send(down, -1)
    (state,) = call(
        space_kernel,
        [((334, 8, LANES), F32)],
        [((3, 3, 18, 2, 8, LANES), F32), ((3, 3, 18, 2, 8, LANES), F32)],
        places=(smem, smem, vmem, vmem),
        cost=pl.CostEstimate(flops=4_000_000_000, bytes_accessed=16_000_000, transcendentals=0),
    )(parity, link_subset, dense, cotangent)
    core = (lax.axis_index("tm") % 2).astype(jnp.int32)[None]
    (block,) = call(
        functools.partial(block_kernel, widths),
        [((count, BLOCKROWS, LANES), BF16)],
        [((12, 4, LANES), F32), ((BLOCKROWS, LANES), F32)],
        places=(smem,) + (vmem,) * 7 + (pl.ANY,),
    )(core, up, down, slab, w_first, w_second, w_third, w_last, state)
    gathered = lax.all_to_all(block, "tm", split_axis=0, concat_axis=0, tiled=True)
    fm, fup, fdown, applied, twice = call(
        time_kernel,
        [((4, 16, SITES), BF16), ((3, 8, SITES), BF16), ((3, 8, SITES), BF16), field, field],
        [
            space, space, field, ((70, 4, LANES), F32), ((70, 4, LANES), F32),
            ((4, 9, 2, 8, LANES), F32), ((4, 4, 16, LANES), F32),
        ],
    )(dense, state, up, down)
    below = send(fm, 1)
    above = send(fm, -1)
    fbelow = send(fup, 2)
    fabove = send(fdown, -2)

    panel_outs = [
        ((2, 4, LANES), F32), ((H, 72), BF16), ((H, 432), BF16), ((H, 432), BF16), ((72, H), BF16),
        ((H, 432), BF16), ((H, 432), BF16), ((H, 72), BF16),
    ]
    panel_scratch = [((432, LANES), F32)]
    if count == 16:
        loops, p1, p2, p3, p4, b2, b3, b4 = call(panel_kernel_plain, panel_outs, panel_scratch)(gathered)
    else:
        pieces = []
        offset = 0
        for width, full in zip(widths, (48, 48, 8, 4)):
            piece = gathered[:, SLABROWS:SLABROWS + 27, offset:offset + width]
            pieces.append(piece.reshape(432, full))
            offset += width
        pieces.append(jnp.zeros((432, 20), BF16))
        loops, p1, p2, p3, p4, b2, b3, b4 = call(panel_kernel, panel_outs, panel_scratch)(
            gathered, jnp.concatenate(pieces, axis=1)
        )

    window = 18 * SITES
    coeff, grads = call(
        functools.partial(conv_kernel, count == 16),
        [((4, 8, SITES), F32), ((16, 27, LANES) if count == 16 else (432, LANES), BF16)],
        [
            ((8, window), F32), ((8, window), F32), ((H, window), BF16), ((H, window), BF16), ((H, window), BF16),
            ((3, 8, window), F32), ((8, window), F32), ((H, window), BF16), ((H, window), BF16), ((H, 4 * SITES), BF16),
            ((432, 4 * SITES), BF16), ((72, 4 * SITES), BF16), ((432, LANES), F32),
        ],
        limit=20 * 1024 * 1024,
    )(fm, below, above, fbelow, fabove, loops, p1, p2, p3, p4, b2, b3, b4)
    if count != 16:
        offset = 0
        pieces = []
        for width, full in zip(widths, (48, 48, 8, 4)):
            pieces.append(grads[:, offset:offset + full].reshape(count, 27, width))
            offset += full
        grads = jnp.concatenate(pieces, axis=2)
    grads = lax.all_to_all(grads, "tm", split_axis=0, concat_axis=0, tiled=True)
    (new_links,) = call(
        update_kernel, [(links.shape, F32)], [((4, 2, 8, LANES), F32)]
    )(dense, applied, twice, coeff)
    grad_first, grad_second, grad_third, grad_last = call(
        functools.partial(sum_kernel, widths),
        [((1, 27 * width), F32) for width in (widths[2], widths[0], widths[1], widths[3])],
        [],
    )(grads)
    return (new_links, grad_first, grad_second, grad_third, grad_last)


def solution(mesh):
    placed = (
        P(None, None, None, None, "groups", "tm", None),
        P(None, None, None, None, "groups", "tm", None),
        P("groups", "tm"),
        P("groups", "tm"),
        P("tm"),
        P("tm"),
        P("tm"),
        P("tm"),
    )
    return jax.shard_map(
        on_device,
        mesh=mesh,
        in_specs=placed,
        out_specs=(
            P(None, None, None, None, "groups", "tm", None),
            P("groups", "tm"),
            P("groups", "tm"),
            P("groups", "tm"),
            P("groups", "tm"),
        ),
        check_vma=False,
    )
```

```python
import functools

import jax
import jax.numpy as jnp
from jax import lax
from jax.experimental import pallas as pl
from jax.experimental.pallas import tpu as pltpu
from jax.sharding import PartitionSpec as P

F32 = jnp.float32
BF16 = jnp.bfloat16
TAPS = 9
H = 48
LANES = 128
SITES = 512
PAIRS = ((0, 1), (0, 2), (0, 3), (1, 2), (1, 3), (2, 3))
SWAP = (0, 2, 1, 4, 3, 6, 5, 8, 7)
ENTRIES = tuple((c, i, j) for c in range(2) for i in range(3) for j in range(3))
EDGE = 4
STAPLE = 7
PLANE = 180
GATE = 186
SLABROWS = 24
BLOCKROWS = 64
LIMIT = 8 * 1024 * 1024


def lane_iota(rows):
    return lax.broadcasted_iota(jnp.int32, (rows, LANES), 1)


def row_iota():
    return lax.broadcasted_iota(jnp.int32, (8, LANES), 0)


def roll_lanes(value, amount):
    return pltpu.roll(value, amount % LANES, 1)


def shift_z(chunk, sign, lanes):
    z = lanes % 8
    if sign > 0:
        return jnp.where(z == 7, roll_lanes(chunk, 7), roll_lanes(chunk, -1))
    return jnp.where(z == 0, roll_lanes(chunk, -7), roll_lanes(chunk, 1))


def shift_y(chunk, sign, lanes):
    y = lanes // 8 % 8
    if sign > 0:
        return jnp.where(y == 7, roll_lanes(chunk, 56), roll_lanes(chunk, -8))
    return jnp.where(y == 0, roll_lanes(chunk, -56), roll_lanes(chunk, 8))


def dense_shift(pair, axis, sign):
    lanes = lane_iota(8)
    if axis == 2:
        return [shift_z(chunk, sign, lanes) for chunk in pair]
    if axis == 1:
        return [shift_y(chunk, sign, lanes) for chunk in pair]
    low = lanes < 64
    first, second = [roll_lanes(chunk, 64) for chunk in pair]
    if sign > 0:
        return [jnp.where(low, first, second), jnp.where(low, second, pltpu.roll(first, 4, 0))]
    return [jnp.where(low, pltpu.roll(second, 4, 0), first), jnp.where(low, first, second)]


def pack_pair(value):
    return [
        jnp.concatenate([value[:, c * 128:c * 128 + 128], value[:, 256 + c * 128:384 + c * 128]], axis=0)
        for c in range(2)
    ]


def halo_pair(ref, index):
    top = row_iota() < 4
    pair = []
    for c in range(2):
        low = jnp.broadcast_to(ref[index, c:c + 1, :], (8, LANES))
        high = jnp.broadcast_to(ref[index, 2 + c:3 + c, :], (8, LANES))
        pair.append(jnp.where(top, low, high))
    return pair


def load_matrix(read):
    real = [[read(3 * i + j) for j in range(3)] for i in range(3)]
    imag = [[read(9 + 3 * i + j) for j in range(3)] for i in range(3)]
    return (real, imag, 1)


def dagger(matrix):
    real, imag, sign = matrix
    return (
        [[real[j][i] for j in range(3)] for i in range(3)],
        [[imag[j][i] for j in range(3)] for i in range(3)],
        -sign,
    )


def total(terms, signs):
    value = None
    for term, sign in zip(terms, signs):
        if value is None:
            value = term if sign > 0 else -term
        else:
            value = value + term if sign > 0 else value - term
    return value


def mat_mul(left, right):
    lr, li, ls = left
    rr, ri, rs = right
    same = ls == rs
    height = len(lr)
    real = [[None] * 3 for _ in range(height)]
    imag = [[None] * 3 for _ in range(height)]
    for i in range(height):
        for j in range(3):
            real[i][j] = total(
                [lr[i][k] * rr[k][j] for k in range(3)] + [li[i][k] * ri[k][j] for k in range(3)],
                [1, 1, 1] + [-1 if same else 1] * 3,
            )
            imag[i][j] = total(
                [lr[i][k] * ri[k][j] for k in range(3)] + [li[i][k] * rr[k][j] for k in range(3)],
                [1, 1, 1] + [1 if same else -1] * 3,
            )
    return (real, imag, ls if same else rs)


def imag_of(matrix, i, j):
    return matrix[1][i][j] if matrix[2] > 0 else -matrix[1][i][j]


def store_matrix(matrix, write):
    for i in range(3):
        for j in range(3):
            write(3 * i + j, matrix[0][i][j])
            write(9 + 3 * i + j, imag_of(matrix, i, j))


def two_rows(read):
    real = [[read(3 * i + j) for j in range(3)] for i in range(2)]
    imag = [[read(6 + 3 * i + j) for j in range(3)] for i in range(2)]
    return (real, imag, 1)


def store_rows(matrix, write):
    for i in range(2):
        for j in range(3):
            write(3 * i + j, matrix[0][i][j])
            write(6 + 3 * i + j, imag_of(matrix, i, j))


def special(matrix):
    real, imag, _ = matrix
    last_r, last_i = [], []
    for k in range(3):
        i, j = (k + 1) % 3, (k + 2) % 3
        last_r.append(
            (real[0][i] * real[1][j] - imag[0][i] * imag[1][j])
            - (real[0][j] * real[1][i] - imag[0][j] * imag[1][i])
        )
        last_i.append(
            (real[0][j] * imag[1][i] + imag[0][j] * real[1][i])
            - (real[0][i] * imag[1][j] + imag[0][i] * real[1][j])
        )
    return (real + [last_r], imag + [last_i], 1)


def anti_parts(matrix):
    parts = [2.0 * imag_of(matrix, i, i) for i in range(3)]
    for i, j in ((0, 1), (0, 2), (1, 2)):
        parts.append(matrix[0][i][j] - matrix[0][j][i])
        parts.append(imag_of(matrix, i, j) + imag_of(matrix, j, i))
    return parts


def anti_matrix(parts):
    zero = jnp.zeros_like(parts[0])
    real = [[zero, parts[3], parts[5]], [-parts[3], zero, parts[7]], [-parts[5], -parts[7], zero]]
    imag = [[parts[0], parts[4], parts[6]], [parts[4], parts[1], parts[8]], [parts[6], parts[8], parts[2]]]
    return real, imag


def anti_mul(parts, right):
    real, imag = anti_matrix(parts)
    rr, ri, _ = right
    out_r = [[None] * 3 for _ in range(3)]
    out_i = [[None] * 3 for _ in range(3)]
    for i in range(3):
        for j in range(3):
            value_r = -(imag[i][i] * ri[i][j])
            value_i = imag[i][i] * rr[i][j]
            for k in range(3):
                if k != i:
                    value_r = value_r + real[i][k] * rr[k][j] - imag[i][k] * ri[k][j]
                    value_i = value_i + real[i][k] * ri[k][j] + imag[i][k] * rr[k][j]
            out_r[i][j] = value_r
            out_i[i][j] = value_i
    return (out_r, out_i, 1)


def pack_links(links_ref, dense):
    def body(mu, carry):
        for e, (c, i, j) in enumerate(ENTRIES):
            low, high = pack_pair(links_ref[mu, c, i, j, 0].astype(F32))
            dense[mu, e, 0] = low
            dense[mu, e, 1] = high
        return carry

    lax.fori_loop(0, 4, body, 0)


def face_kernel(links_ref, up_ref, down_ref, dense, slab, moved, rows):
    pack_links(links_ref, dense)

    def shift_body(e, carry):
        pair = [dense[3, e, 0], dense[3, e, 1]]
        for mu in range(3):
            low, high = dense_shift(pair, mu, 1)
            moved[mu, e, 0] = low
            moved[mu, e, 1] = high
        return carry

    lax.fori_loop(0, 18, shift_body, 0)

    def staple_body(step, carry):
        mu = step // 2
        c = step % 2
        u_mu = load_matrix(lambda e: dense[mu, e, c])
        u_t = load_matrix(lambda e: dense[3, e, c])
        edge = mat_mul(u_mu, load_matrix(lambda e: moved[mu, e, c]))

        def write_edge(e, value):
            dense[EDGE + mu, e, c] = value

        store_matrix(edge, write_edge)

        def write(e, value):
            dense[STAPLE + mu, e, c] = value
            rows[16 + mu * 18 + e, pl.ds(c, 1)] = value[3:4]
            rows[16 + mu * 18 + e, pl.ds(2 + c, 1)] = value[7:8]

        store_matrix(mat_mul(dagger(edge), u_t), write)
        return carry

    lax.fori_loop(0, 6, staple_body, 0)

    def slab_body(c, carry):
        u_t = load_matrix(lambda e: dense[3, e, c])
        ahead = load_matrix(lambda e: pltpu.roll(dense[3, e, c], 7, 0))
        two = mat_mul(u_t, ahead)
        later = tuple(
            [[pltpu.roll(part[i][j], 6, 0) for j in range(3)] for i in range(3)] for part in two[:2]
        ) + (two[2],)
        four = mat_mul((two[0][:2], two[1][:2], two[2]), later)

        def write(e, value):
            slab[e, pl.ds(c, 1)] = value[0:1]
            slab[e, pl.ds(2 + c, 1)] = value[4:5]
            rows[e, pl.ds(c, 1)] = value[0:1]
            rows[e, pl.ds(2 + c, 1)] = value[4:5]

        store_rows(four, write)
        return carry

    lax.fori_loop(0, 2, slab_body, 0)
    for q in range(4):
        up_ref[:, q * 128:q * 128 + 128] = rows[:, q, :].astype(BF16)

    def down_body(e, carry):
        for mu in range(3):
            for c in range(2):
                value = dense[mu, e, c]
                rows[16 + mu * 18 + e, c:c + 1] = value[0:1]
                rows[16 + mu * 18 + e, 2 + c:3 + c] = value[4:5]
        return carry

    lax.fori_loop(0, 18, down_body, 0)
    for q in range(4):
        down_ref[:, q * 128:q * 128 + 128] = rows[:, q, :].astype(BF16)


def block_kernel(
    widths, core_ref, up_ref, down_ref, slab, w1_ref, w2_ref, w3_ref, w4_ref, after_ref, block_ref, other, block
):
    even = core_ref[0] == 0
    up = up_ref[0:16].astype(F32)
    down = down_ref[0:16].astype(F32)
    for q in range(4):
        lanes = slice(q * 128, q * 128 + 128)
        other[:, q, :] = jnp.where(even, down[0:12, lanes], up[0:12, lanes])
    first = two_rows(lambda e: jnp.where(even, slab[e], other[e]))
    second = special(two_rows(lambda e: jnp.where(even, other[e], slab[e])))

    def write(e, value):
        block[2 * e:2 * e + 2, :] = jnp.where(even, value[0:2], value[2:4])

    store_rows(mat_mul(first, second), write)
    block[SLABROWS:BLOCKROWS] = jnp.zeros((BLOCKROWS - SLABROWS, LANES), F32)
    offset = 0
    for ref, width in zip((w2_ref, w3_ref, w1_ref, w4_ref), widths):
        flat = ref[...].astype(F32)
        for r in range(27):
            block[SLABROWS + r:SLABROWS + r + 1, offset:offset + width] = (
                flat[width * r:width * r + width].reshape(1, width)
            )
        offset += width
    value = block[...].astype(BF16)
    for d in range(block_ref.shape[0]):
        block_ref[d] = value


def put_row(rows, channel, c, value):
    for t in range(4):
        rows[t, c, pl.ds(channel, 1), :] = value[t:t + 1]
        rows[t, 2 + c, pl.ds(channel, 1), :] = value[4 + t:5 + t]


def sum_at(mu, e, c):
    return (mu * 18 + e) * 2 + c


def force_at(mu, e, c):
    return 108 + (mu * 9 + e) * 2 + c


def cot_at(mu, e, c):
    return 190 + (mu * 18 + e) * 2 + c


def space_kernel(code_ref, dense, cot_ref, state, moved, staples):
    def cot_body(mu, carry):
        for e, (part, i, j) in enumerate(ENTRIES):
            low, high = pack_pair(cot_ref[mu, part, i, j, 0].astype(F32))
            state[cot_at(mu, e, 0)] = low
            state[cot_at(mu, e, 1)] = high
        return carry

    lax.fori_loop(0, 4, cot_body, 0)
    state[108:180] = jnp.zeros((72, 8, LANES), F32)
    steps = row_iota() % 4
    lanes = lane_iota(8)
    colour = (lanes // 64 + lanes // 8 % 8 + lanes % 8 + steps) % 2
    code = jnp.zeros_like(steps)
    for t in range(4):
        code = jnp.where(steps == t, code_ref[0, t], code)
    for mu in range(4):
        active = jnp.logical_and(colour == code % 2, jnp.right_shift(code, mu + 1) % 2 == 1)
        state[GATE + mu] = jnp.where(active, 1.0, 0.0)

    def shift_body(e, carry):
        for nu in range(3):
            pair = [dense[nu, e, 0], dense[nu, e, 1]]
            for mu in range(3):
                if mu != nu:
                    low, high = dense_shift(pair, mu, 1)
                    moved[mu, nu, e, 0] = low
                    moved[mu, nu, e, 1] = high
        return carry

    lax.fori_loop(0, 18, shift_body, 0)

    def plane_body(step, carry):
        plane = step // 2
        c = step % 2
        mu = jnp.where(plane == 2, 1, 0)
        nu = jnp.where(plane == 0, 1, 2)
        u_mu = load_matrix(lambda e: dense[mu, e, c])
        u_nu = load_matrix(lambda e: dense[nu, e, c])
        one = mat_mul(u_mu, load_matrix(lambda e: moved[mu, nu, e, c]))
        two = mat_mul(u_nu, load_matrix(lambda e: moved[nu, mu, e, c]))
        loop = mat_mul(one, dagger(two))
        state[PLANE + step] = (loop[0][0][0] + loop[0][1][1] + loop[0][2][2]) / 3.0
        for e, part in enumerate(anti_parts(loop)):
            state[force_at(mu, e, c)] += part
            state[force_at(nu, e, c)] -= part

        def write_mu(e, value):
            staples[mu, nu, e, c] = value

        def write_nu(e, value):
            staples[nu, mu, e, c] = value

        store_matrix(mat_mul(dagger(one), u_nu), write_mu)
        store_matrix(mat_mul(dagger(two), u_mu), write_nu)
        return carry

    lax.fori_loop(0, 6, plane_body, 0)

    def lower_body(e, carry):
        for mu in range(3):
            acc = [jnp.where(steps == 0, 0.0, pltpu.roll(dense[STAPLE + mu, e, c], 1, 0)) for c in range(2)]
            for nu in range(3):
                if nu != mu:
                    pair = dense_shift([staples[mu, nu, e, 0], staples[mu, nu, e, 1]], nu, -1)
                    acc = [acc[c] + pair[c] for c in range(2)]
            state[sum_at(mu, e, 0)] = acc[0]
            state[sum_at(mu, e, 1)] = acc[1]
        return carry

    lax.fori_loop(0, 18, lower_body, 0)


def time_kernel(
    dense, state, up_ref, down_ref,
    fm_ref, fup_ref, fdown_ref, w1_ref, w2_ref,
    moved, staples, sums, halo_up, halo_down, forces, rows,
):
    for q in range(4):
        halo_up[:, q, :] = up_ref[:, q * 128:q * 128 + 128].astype(F32)
        halo_down[:, q, :] = down_ref[:, q * 128:q * 128 + 128].astype(F32)
    rows[...] = jnp.zeros_like(rows)
    for channel, plane in ((0, 0), (1, 1), (3, 2)):
        for c in range(2):
            put_row(rows, channel, c, state[PLANE + 2 * plane + c])
    for mu in range(4):
        for e in range(9):
            for c in range(2):
                forces[mu, e, c] = state[force_at(mu, e, c)]
    steps = row_iota() % 4

    def shift_body(e, carry):
        for nu in range(3):
            halo = halo_pair(halo_down, 16 + nu * 18 + e)
            below = halo_pair(halo_up, 16 + nu * 18 + e)
            for c in range(2):
                moved[nu, e, c] = jnp.where(steps == 3, halo[c], pltpu.roll(dense[nu, e, c], 7, 0))
                sums[nu, e, c] = state[sum_at(nu, e, c)] + jnp.where(steps == 0, below[c], 0.0)
        return carry

    lax.fori_loop(0, 18, shift_body, 0)

    def plane_body(step, carry):
        mu = step // 2
        c = step % 2
        one = load_matrix(lambda e: dense[EDGE + mu, e, c])
        two = mat_mul(load_matrix(lambda e: dense[3, e, c]), load_matrix(lambda e: moved[mu, e, c]))
        loop = mat_mul(one, dagger(two))
        put_row(rows, jnp.where(mu == 0, 2, mu + 3), c, (loop[0][0][0] + loop[0][1][1] + loop[0][2][2]) / 3.0)
        for e, part in enumerate(anti_parts(loop)):
            forces[mu, e, c] += part
            forces[3, e, c] -= part

        def write(e, value):
            staples[mu, e, c] = value

        store_matrix(mat_mul(dagger(two), load_matrix(lambda e: dense[mu, e, c])), write)
        return carry

    lax.fori_loop(0, 6, plane_body, 0)

    def lower_body(e, carry):
        acc = None
        for mu in range(3):
            pair = dense_shift([staples[mu, e, 0], staples[mu, e, 1]], mu, -1)
            acc = pair if acc is None else [acc[c] + pair[c] for c in range(2)]
        sums[3, e, 0] = acc[0]
        sums[3, e, 1] = acc[1]
        return carry

    lax.fori_loop(0, 18, lower_body, 0)

    def force_body(step, carry):
        mu = step // 2
        c = step % 2
        current = load_matrix(lambda e: dense[mu, e, c])
        omega = mat_mul(current, load_matrix(lambda e: sums[mu, e, c]))
        parts = [part + forces[mu, e, c] for e, part in enumerate(anti_parts(omega))]
        mean = (parts[0] + parts[1] + parts[2]) * (1.0 / 3.0)
        parts = [parts[e] - mean if e < 3 else parts[e] for e in range(9)]
        parts = [part * (1.0 / 12.0) for part in parts]
        applied = anti_mul(parts, current)
        twice = anti_mul(parts, applied)
        gate = state[GATE + mu]
        slope = jnp.zeros_like(gate)
        curve = jnp.zeros_like(gate)
        for e, (part, i, j) in enumerate(ENTRIES):
            weight = state[cot_at(mu, e, c)]
            slope = slope + weight * applied[part][i][j]
            curve = curve + weight * twice[part][i][j]
            w1_ref[mu, e, c] = gate * applied[part][i][j]
            w2_ref[mu, e, c] = gate * twice[part][i][j]
        put_row(rows, 8 + mu, c, gate * slope)
        put_row(rows, 12 + mu, c, gate * curve)
        return carry

    lax.fori_loop(0, 8, force_body, 0)
    for t in range(4):
        for q in range(4):
            value = rows[t, q]
            fm_ref[t, :, q * 128:q * 128 + 128] = value.astype(BF16)
            if t > 0:
                fup_ref[t - 1, :, q * 128:q * 128 + 128] = value[0:8].astype(BF16)
            if t < 3:
                fdown_ref[t, :, q * 128:q * 128 + 128] = value[0:8].astype(BF16)


def selectors():
    row = lax.broadcasted_iota(jnp.int32, (432, 72), 0)
    col = lax.broadcasted_iota(jnp.int32, (432, 72), 1)
    group = row // 12
    spread = (group // 4 * 8 + group % 4 == col).astype(F32).astype(BF16)
    keep = (
        lax.broadcasted_iota(jnp.int32, (432, H), 1) // 4 == lax.broadcasted_iota(jnp.int32, (432, H), 0) % 12
    )
    return spread, keep


def panel_kernel(gathered_ref, weights_ref, loops_ref, p1_ref, p2_ref, p3_ref, p4_ref, b2_ref, b3_ref, b4_ref, weights):
    count = gathered_ref.shape[0]

    def read(chip):
        low = gathered_ref[2 * chip].astype(F32)
        high = gathered_ref[2 * chip + 1].astype(F32)
        return special(
            two_rows(lambda e: jnp.concatenate([low[2 * e:2 * e + 2], high[2 * e:2 * e + 2]], axis=0))
        )

    def flat(matrix):
        return tuple(matrix[0][i][j] for i in range(3) for j in range(3)) + tuple(
            imag_of(matrix, i, j) for i in range(3) for j in range(3)
        )

    def chain(chip, state):
        return flat(mat_mul(load_matrix(lambda e: state[e]), read(chip)))

    state = lax.fori_loop(1, count // 2, chain, flat(read(0)))
    loops_ref[0] = (state[0] + state[4] + state[8]) / 3.0
    loops_ref[1] = (state[9] + state[13] + state[17]) / 3.0

    if weights_ref is None:
        for d in range(count):
            block = gathered_ref[d].astype(F32)
            weights[27 * d:27 * d + 27, :] = block[SLABROWS:SLABROWS + 27]
    else:
        weights[...] = weights_ref[...].astype(F32)
    for k in range(TAPS):
        rows = slice(H * k, H * k + H)
        back = slice(H * SWAP[k], H * SWAP[k] + H)
        p2_ref[:, rows] = weights[rows, 0:48].astype(BF16)
        p3_ref[:, rows] = weights[rows, 48:96].astype(BF16)
        p1_ref[:, 8 * k:8 * k + 8] = weights[rows, 96:104].astype(BF16)
        turned = weights[back, :].T
        b2_ref[:, rows] = turned[0:48].astype(BF16)
        b3_ref[:, rows] = turned[48:96].astype(BF16)
    spread, keep = selectors()
    place = (
        lax.broadcasted_iota(jnp.int32, (LANES, H), 0) == 104 + lax.broadcasted_iota(jnp.int32, (LANES, H), 1) % 4
    ).astype(F32).astype(BF16)
    wide = jnp.dot(weights[...].astype(BF16), place, preferred_element_type=F32)
    wide = jnp.where(keep, wide, 0.0).astype(BF16)
    last = lax.dot_general(spread, wide, (((0,), (0,)), ((), ())), preferred_element_type=F32)
    p4_ref[...] = last.astype(BF16)
    for k in range(TAPS):
        b4_ref[:, 8 * k:8 * k + 8] = last[8 * SWAP[k]:8 * SWAP[k] + 8, :].T.astype(BF16)


def panel_kernel_plain(gathered_ref, *rest):
    panel_kernel(gathered_ref, None, *rest)


def chunks_of(value):
    return [value[:, q * 128:q * 128 + 128] for q in range(4)]


def one_shift(chunks, position):
    if position == 0:
        return chunks
    lanes = lane_iota(chunks[0].shape[0])
    sign = 1 if position % 2 == 1 else -1
    if position > 4:
        return [shift_z(chunk, sign, lanes) for chunk in chunks]
    if position > 2:
        return [shift_y(chunk, sign, lanes) for chunk in chunks]
    low = lanes < 64
    rolled = [roll_lanes(chunk, 64) for chunk in chunks]
    if sign > 0:
        return [jnp.where(low, rolled[q], rolled[(q + 1) % 4]) for q in range(4)]
    return [jnp.where(low, rolled[(q + 3) % 4], rolled[q]) for q in range(4)]


def all_shifts(chunks):
    lanes = lane_iota(chunks[0].shape[0])
    y = lanes // 8 % 8
    z = lanes % 8
    low = lanes < 64
    half = [roll_lanes(chunk, 64) for chunk in chunks]
    return [
        chunks,
        [jnp.where(low, half[q], half[(q + 1) % 4]) for q in range(4)],
        [jnp.where(low, half[(q + 3) % 4], half[q]) for q in range(4)],
        [roll_lanes(jnp.where(y == 0, half[q], chunks[q]), -8) for q in range(4)],
        [roll_lanes(jnp.where(y == 7, half[q], chunks[q]), 8) for q in range(4)],
        [roll_lanes(jnp.where(z == 0, roll_lanes(chunk, 8), chunk), -1) for chunk in chunks],
        [roll_lanes(jnp.where(z == 7, roll_lanes(chunk, -8), chunk), 1) for chunk in chunks],
    ]


def span(slice_index, count=1):
    if isinstance(slice_index, int):
        return slice(slice_index * SITES, (slice_index + count) * SITES)
    return pl.ds(pl.multiple_of(slice_index * SITES, SITES), count * SITES)


def slot_of(slot):
    return slice(slot * SITES, (slot + 1) * SITES)


def stack_wide(source, target, index, slot):
    chunks = chunks_of(source[:, span(index)])
    for position, shifted in enumerate(all_shifts(chunks)):
        for q in range(4):
            lanes = slice(slot * SITES + q * 128, slot * SITES + q * 128 + 128)
            target[H * position:H * position + H, lanes] = shifted[q]
    target[7 * H:8 * H, slot_of(slot)] = source[:, span(index + 1)]
    target[8 * H:9 * H, slot_of(slot)] = source[:, span(index - 1)]


def stack_thin(source, target, index, slot):
    chunks = chunks_of(source[:, span(index)])
    ahead = chunks_of(source[:, span(index + 1)])
    behind = chunks_of(source[:, span(index - 1)])
    columns = all_shifts(chunks) + [ahead, behind]
    for q in range(4):
        lanes = slice(slot * SITES + q * 128, slot * SITES + q * 128 + 128)
        target[0:72, lanes] = jnp.concatenate([column[q] for column in columns], axis=0).astype(BF16)


def one_minus_square(value):
    value = value.astype(F32)
    return 1.0 - value * value


def conv_kernel(
    split, fm_ref, below_ref, above_ref, fbelow_ref, fabove_ref, loops_ref,
    p1_ref, p2_ref, p3_ref, p4_ref, b2_ref, b3_ref, b4_ref,
    coeff_ref, grads_ref,
    feats, mixed, h1, h2, h3, parts, lasts, g3, g2, g1, wide, thin, packed,
):
    row8 = lax.broadcasted_iota(jnp.int32, (8, SITES), 0)
    loop_re = jnp.concatenate([loops_ref[0, q:q + 1, :] for q in range(4)], axis=1)
    loop_im = jnp.concatenate([loops_ref[1, q:q + 1, :] for q in range(4)], axis=1)
    loops = jnp.where(row8 == 6, loop_re, jnp.where(row8 == 7, loop_im, 0.0))
    loops = loops.astype(BF16).astype(F32)
    for j in range(3):
        feats[:, span(j)] = fbelow_ref[j].astype(F32) + loops
        feats[:, span(15 + j)] = fabove_ref[j].astype(F32) + loops
    for base, ref in ((3, below_ref), (7, fm_ref), (11, above_ref)):
        for j in range(4):
            value = ref[j].astype(F32)
            feats[:, span(base + j)] = value[0:8] + loops
            mixed[:, span(base + j)] = value[8:16]

    def wide_dot(source, weights, index, slot):
        stack_wide(source, wide, index, slot)
        return jnp.dot(weights[...], wide[:, slot_of(slot)], preferred_element_type=F32)

    def thin_dot(source, weights, index, slot):
        stack_thin(source, thin, index, slot)
        return jnp.dot(weights[...], thin[:, slot_of(slot)], preferred_element_type=F32)

    for index in range(1, 17):
        h1[:, span(index)] = jnp.tanh(thin_dot(feats, p1_ref, index, index % 4)).astype(BF16)
    for index in range(2, 16):
        h2[:, span(index)] = jnp.tanh(wide_dot(h1, p2_ref, index, index % 4)).astype(BF16)
    for index in range(3, 15):
        out = jnp.tanh(wide_dot(h2, p3_ref, index, index % 4)).astype(BF16)
        h3[:, span(index)] = out
        taps = jnp.dot(p4_ref[...], out, preferred_element_type=F32)
        acc = None
        for position in range(7):
            shifted = one_shift(chunks_of(taps[8 * position:8 * position + 8]), position)
            acc = shifted if acc is None else [a + b for a, b in zip(acc, shifted)]
        parts[0, :, span(index)] = jnp.concatenate(acc, axis=1)
        parts[1, :, span(index)] = taps[56:64]
        parts[2, :, span(index)] = taps[64:72]

    for index in range(4, 14):
        coeff = jnp.tanh(parts[0, :, span(index)] + parts[1, :, span(index + 1)] + parts[2, :, span(index - 1)])
        blend = mixed[:, span(index)]
        value = (blend + coeff * pltpu.roll(blend, 4, 0)) * (1.0 - coeff * coeff)
        lasts[:, span(index)] = jnp.where(row8 < 4, value, 0.0).astype(BF16).astype(F32)
        if 7 <= index < 11:
            coeff_ref[index - 7] = coeff

    own = span(7, 4)
    contract = (((1,), (1,)), ((), ()))
    for index in (5, 6, 11, 12, 7, 8, 9, 10):
        out = thin_dot(lasts, b4_ref, index, (index + 1) % 4)
        g3[:, span(index)] = (out * one_minus_square(h3[:, span(index)])).astype(BF16)
    grad_last = lax.dot_general(thin[...], h3[:, own], contract, preferred_element_type=F32)
    for index in (6, 11, 7, 8, 9, 10):
        out = wide_dot(g3, b3_ref, index, (index + 1) % 4)
        g2[:, span(index)] = (out * one_minus_square(h2[:, span(index)])).astype(BF16)
    grad_third = lax.dot_general(wide[...], h2[:, own], contract, preferred_element_type=F32)
    for index in (7, 8, 9, 10):
        out = wide_dot(g2, b2_ref, index, (index + 1) % 4)
        g1[:, slot_of(index - 7)] = (out * one_minus_square(h1[:, span(index)])).astype(BF16)
    grad_second = lax.dot_general(wide[...], h1[:, own], contract, preferred_element_type=F32)
    for index in (7, 8, 9, 10):
        stack_thin(feats, thin, index, index - 7)
    grad_first = lax.dot_general(g1[...], thin[...], contract, preferred_element_type=F32)

    spread, keep = selectors()
    ordered = jnp.concatenate([grad_last[8 * SWAP[k]:8 * SWAP[k] + 8] for k in range(TAPS)], axis=0)
    broad = jnp.dot(spread, ordered.astype(BF16), preferred_element_type=F32)
    broad = jnp.where(keep, broad, 0.0).astype(BF16)
    place = (
        lax.broadcasted_iota(jnp.int32, (H, LANES), 1) == 104 + lax.broadcasted_iota(jnp.int32, (H, LANES), 0) % 4
    ).astype(F32).astype(BF16)
    packed[...] = jnp.dot(broad, place, preferred_element_type=F32)
    for k in range(TAPS):
        rows = slice(H * k, H * k + H)
        back = slice(H * SWAP[k], H * SWAP[k] + H)
        packed[rows, 0:48] = grad_second[back]
        packed[rows, 48:96] = grad_third[back]
        packed[rows, 96:104] = grad_first[:, 8 * k:8 * k + 8]
    if split:
        for d in range(16):
            grads_ref[d] = packed[27 * d:27 * d + 27, :].astype(BF16)
    else:
        grads_ref[...] = packed[...].astype(BF16)


def update_kernel(links_ref, w1_ref, w2_ref, coeff_ref, out_ref, factors):
    for mu in range(4):
        for t in range(4):
            for c in range(2):
                factors[mu, c, t:t + 1, :] = coeff_ref[t, mu:mu + 1, c * 128:c * 128 + 128]
                factors[mu, c, 4 + t:5 + t, :] = coeff_ref[t, mu:mu + 1, 256 + c * 128:384 + c * 128]

    def body(mu, carry):
        factor = [factors[mu, c] for c in range(2)]
        half = [0.5 * value * value for value in factor]
        for e, (part, i, j) in enumerate(ENTRIES):
            pair = pack_pair(links_ref[mu, part, i, j, 0])
            new = [pair[c] + factor[c] * w1_ref[mu, e, c] + half[c] * w2_ref[mu, e, c] for c in range(2)]
            out_ref[mu, part, i, j, 0] = jnp.concatenate(
                [new[0][0:4], new[1][0:4], new[0][4:8], new[1][4:8]], axis=1
            )
        return carry

    lax.fori_loop(0, 4, body, 0)


def sum_kernel(widths, parts_ref, first_ref, second_ref, third_ref, last_ref):
    value = parts_ref[0].astype(F32)
    for d in range(1, parts_ref.shape[0]):
        value = value + parts_ref[d].astype(F32)
    offset = 0
    for ref, width in zip((second_ref, third_ref, first_ref, last_ref), widths):
        for r in range(27):
            ref[:, width * r:width * r + width] = value[r:r + 1, offset:offset + width]
        offset += width


def call(body, outs, scratch, places=None, cost=None, limit=LIMIT):
    specs = {}
    if places is not None:
        specs["in_specs"] = [pl.BlockSpec(memory_space=place) for place in places]
    return pl.pallas_call(
        body,
        out_shape=[jax.ShapeDtypeStruct(shape, dtype) for shape, dtype in outs],
        scratch_shapes=[pltpu.VMEM(*item) if isinstance(item, tuple) else item for item in scratch],
        compiler_params=pltpu.CompilerParams(vmem_limit_bytes=limit),
        cost_estimate=cost,
        **specs,
    )


def on_device(links, cotangent, parity, link_subset, w_first, w_second, w_third, w_last):
    count = lax.axis_size("tm")

    def send(value, distance):
        return lax.ppermute(value, "tm", [(i, (i + distance) % count) for i in range(count)])

    widths = (768 // count, 768 // count, 128 // count, 64 // count)
    vmem, smem = pltpu.VMEM, pltpu.SMEM
    field = ((4, 18, 2, 8, LANES), F32)
    space = ((3, 18, 2, 8, LANES), F32)
    edge_rows = ((70, SITES), BF16)
    up, down, dense, slab = call(
        face_kernel,
        [edge_rows, edge_rows, ((10, 18, 2, 8, LANES), F32), ((12, 4, LANES), F32)],
        [space, ((70, 4, LANES), F32)],
    )(links)
    up = send(up, 1)
    down = send(down, -1)
    (state,) = call(
        space_kernel,
        [((334, 8, LANES), F32)],
        [((3, 3, 18, 2, 8, LANES), F32), ((3, 3, 18, 2, 8, LANES), F32)],
        places=(smem, vmem, vmem),
        cost=pl.CostEstimate(flops=4_000_000_000, bytes_accessed=16_000_000, transcendentals=0),
    )(parity + 2 * link_subset, dense, cotangent)
    core = (lax.axis_index("tm") % 2).astype(jnp.int32)[None]
    (block,) = call(
        functools.partial(block_kernel, widths),
        [((count, BLOCKROWS, LANES), BF16)],
        [((12, 4, LANES), F32), ((BLOCKROWS, LANES), F32)],
        places=(smem,) + (vmem,) * 7 + (pl.ANY,),
    )(core, up, down, slab, w_first, w_second, w_third, w_last, state)
    gathered = lax.all_to_all(block, "tm", split_axis=0, concat_axis=0, tiled=True)
    fm, fup, fdown, applied, twice = call(
        time_kernel,
        [((4, 16, SITES), BF16), ((3, 8, SITES), BF16), ((3, 8, SITES), BF16), field, field],
        [
            space, space, field, ((70, 4, LANES), F32), ((70, 4, LANES), F32),
            ((4, 9, 2, 8, LANES), F32), ((4, 4, 16, LANES), F32),
        ],
    )(dense, state, up, down)
    below = send(fm, 1)
    above = send(fm, -1)
    fbelow = send(fup, 2)
    fabove = send(fdown, -2)

    panel_outs = [
        ((2, 4, LANES), F32), ((H, 72), BF16), ((H, 432), BF16), ((H, 432), BF16), ((72, H), BF16),
        ((H, 432), BF16), ((H, 432), BF16), ((H, 72), BF16),
    ]
    panel_scratch = [((432, LANES), F32)]
    if count == 16:
        loops, p1, p2, p3, p4, b2, b3, b4 = call(panel_kernel_plain, panel_outs, panel_scratch)(gathered)
    else:
        pieces = []
        offset = 0
        for width, full in zip(widths, (48, 48, 8, 4)):
            piece = gathered[:, SLABROWS:SLABROWS + 27, offset:offset + width]
            pieces.append(piece.reshape(432, full))
            offset += width
        pieces.append(jnp.zeros((432, 20), BF16))
        loops, p1, p2, p3, p4, b2, b3, b4 = call(panel_kernel, panel_outs, panel_scratch)(
            gathered, jnp.concatenate(pieces, axis=1)
        )

    window = 18 * SITES
    coeff, grads = call(
        functools.partial(conv_kernel, count == 16),
        [((4, 8, SITES), F32), ((16, 27, LANES) if count == 16 else (432, LANES), BF16)],
        [
            ((8, window), F32), ((8, window), F32), ((H, window), BF16), ((H, window), BF16), ((H, window), BF16),
            ((3, 8, window), F32), ((8, window), F32), ((H, window), BF16), ((H, window), BF16), ((H, 4 * SITES), BF16),
            ((432, 4 * SITES), BF16), ((72, 4 * SITES), BF16), ((432, LANES), F32),
        ],
        limit=LIMIT,
    )(fm, below, above, fbelow, fabove, loops, p1, p2, p3, p4, b2, b3, b4)
    if count != 16:
        offset = 0
        pieces = []
        for width, full in zip(widths, (48, 48, 8, 4)):
            pieces.append(grads[:, offset:offset + full].reshape(count, 27, width))
            offset += full
        grads = jnp.concatenate(pieces, axis=2)
    grads = lax.all_to_all(grads, "tm", split_axis=0, concat_axis=0, tiled=True)
    (new_links,) = call(
        update_kernel, [(links.shape, F32)], [((4, 2, 8, LANES), F32)]
    )(links, applied, twice, coeff)
    grad_first, grad_second, grad_third, grad_last = call(
        functools.partial(sum_kernel, widths),
        [((1, 27 * width), F32) for width in (widths[2], widths[0], widths[1], widths[3])],
        [],
    )(grads)
    return (new_links, grad_first, grad_second, grad_third, grad_last)


def solution(mesh):
    placed = (
        P(None, None, None, None, "groups", "tm", None),
        P(None, None, None, None, "groups", "tm", None),
        P("groups", "tm"),
        P("groups", "tm"),
        P("tm"),
        P("tm"),
        P("tm"),
        P("tm"),
    )
    return jax.shard_map(
        on_device,
        mesh=mesh,
        in_specs=placed,
        out_specs=(
            P(None, None, None, None, "groups", "tm", None),
            P("groups", "tm"),
            P("groups", "tm"),
            P("groups", "tm"),
            P("groups", "tm"),
        ),
        check_vma=False,
    )
```

```python
import functools

import jax
import jax.numpy as jnp
from jax import lax
from jax.experimental import pallas as pl
from jax.experimental.pallas import tpu as pltpu
from jax.sharding import PartitionSpec as P

F32 = jnp.float32
BF16 = jnp.bfloat16
TAPS = 9
H = 48
LANES = 128
SITES = 512
PAIRS = ((0, 1), (0, 2), (0, 3), (1, 2), (1, 3), (2, 3))
SWAP = (0, 2, 1, 4, 3, 6, 5, 8, 7)
ENTRIES = tuple((c, i, j) for c in range(2) for i in range(3) for j in range(3))
EDGE = 4
STAPLE = 7
PLANE = 180
GATE = 186
SLABROWS = 24
BLOCKROWS = 64
LIMIT = 8 * 1024 * 1024


def lane_iota(rows):
    return lax.broadcasted_iota(jnp.int32, (rows, LANES), 1)


def row_iota():
    return lax.broadcasted_iota(jnp.int32, (8, LANES), 0)


def roll_lanes(value, amount):
    return pltpu.roll(value, amount % LANES, 1)


def shift_z(chunk, sign, lanes):
    z = lanes % 8
    if sign > 0:
        return jnp.where(z == 7, roll_lanes(chunk, 7), roll_lanes(chunk, -1))
    return jnp.where(z == 0, roll_lanes(chunk, -7), roll_lanes(chunk, 1))


def shift_y(chunk, sign, lanes):
    y = lanes // 8 % 8
    if sign > 0:
        return jnp.where(y == 7, roll_lanes(chunk, 56), roll_lanes(chunk, -8))
    return jnp.where(y == 0, roll_lanes(chunk, -56), roll_lanes(chunk, 8))


def dense_shift(pair, axis, sign):
    lanes = lane_iota(8)
    if axis == 2:
        return [shift_z(chunk, sign, lanes) for chunk in pair]
    if axis == 1:
        return [shift_y(chunk, sign, lanes) for chunk in pair]
    low = lanes < 64
    first, second = [roll_lanes(chunk, 64) for chunk in pair]
    if sign > 0:
        return [jnp.where(low, first, second), jnp.where(low, second, pltpu.roll(first, 4, 0))]
    return [jnp.where(low, pltpu.roll(second, 4, 0), first), jnp.where(low, first, second)]


def pack_pair(value):
    return [
        jnp.concatenate([value[:, c * 128:c * 128 + 128], value[:, 256 + c * 128:384 + c * 128]], axis=0)
        for c in range(2)
    ]


def halo_pair(ref, index):
    top = row_iota() < 4
    pair = []
    for c in range(2):
        low = jnp.broadcast_to(ref[index, c:c + 1, :], (8, LANES))
        high = jnp.broadcast_to(ref[index, 2 + c:3 + c, :], (8, LANES))
        pair.append(jnp.where(top, low, high))
    return pair


def load_matrix(read):
    real = [[read(3 * i + j) for j in range(3)] for i in range(3)]
    imag = [[read(9 + 3 * i + j) for j in range(3)] for i in range(3)]
    return (real, imag, 1)


def dagger(matrix):
    real, imag, sign = matrix
    return (
        [[real[j][i] for j in range(3)] for i in range(3)],
        [[imag[j][i] for j in range(3)] for i in range(3)],
        -sign,
    )


def total(terms, signs):
    value = None
    for term, sign in zip(terms, signs):
        if value is None:
            value = term if sign > 0 else -term
        else:
            value = value + term if sign > 0 else value - term
    return value


def mat_mul(left, right):
    lr, li, ls = left
    rr, ri, rs = right
    same = ls == rs
    height = len(lr)
    real = [[None] * 3 for _ in range(height)]
    imag = [[None] * 3 for _ in range(height)]
    for i in range(height):
        for j in range(3):
            real[i][j] = total(
                [lr[i][k] * rr[k][j] for k in range(3)] + [li[i][k] * ri[k][j] for k in range(3)],
                [1, 1, 1] + [-1 if same else 1] * 3,
            )
            imag[i][j] = total(
                [lr[i][k] * ri[k][j] for k in range(3)] + [li[i][k] * rr[k][j] for k in range(3)],
                [1, 1, 1] + [1 if same else -1] * 3,
            )
    return (real, imag, ls if same else rs)


def imag_of(matrix, i, j):
    return matrix[1][i][j] if matrix[2] > 0 else -matrix[1][i][j]


def store_matrix(matrix, write):
    for i in range(3):
        for j in range(3):
            write(3 * i + j, matrix[0][i][j])
            write(9 + 3 * i + j, imag_of(matrix, i, j))


def two_rows(read):
    real = [[read(3 * i + j) for j in range(3)] for i in range(2)]
    imag = [[read(6 + 3 * i + j) for j in range(3)] for i in range(2)]
    return (real, imag, 1)


def store_rows(matrix, write):
    for i in range(2):
        for j in range(3):
            write(3 * i + j, matrix[0][i][j])
            write(6 + 3 * i + j, imag_of(matrix, i, j))


def special(matrix):
    real, imag, _ = matrix
    last_r, last_i = [], []
    for k in range(3):
        i, j = (k + 1) % 3, (k + 2) % 3
        last_r.append(
            (real[0][i] * real[1][j] - imag[0][i] * imag[1][j])
            - (real[0][j] * real[1][i] - imag[0][j] * imag[1][i])
        )
        last_i.append(
            (real[0][j] * imag[1][i] + imag[0][j] * real[1][i])
            - (real[0][i] * imag[1][j] + imag[0][i] * real[1][j])
        )
    return (real + [last_r], imag + [last_i], 1)


def anti_parts(matrix):
    parts = [2.0 * imag_of(matrix, i, i) for i in range(3)]
    for i, j in ((0, 1), (0, 2), (1, 2)):
        parts.append(matrix[0][i][j] - matrix[0][j][i])
        parts.append(imag_of(matrix, i, j) + imag_of(matrix, j, i))
    return parts


def anti_matrix(parts):
    zero = jnp.zeros_like(parts[0])
    real = [[zero, parts[3], parts[5]], [-parts[3], zero, parts[7]], [-parts[5], -parts[7], zero]]
    imag = [[parts[0], parts[4], parts[6]], [parts[4], parts[1], parts[8]], [parts[6], parts[8], parts[2]]]
    return real, imag


def anti_mul(parts, right):
    real, imag = anti_matrix(parts)
    rr, ri, _ = right
    out_r = [[None] * 3 for _ in range(3)]
    out_i = [[None] * 3 for _ in range(3)]
    for i in range(3):
        for j in range(3):
            value_r = -(imag[i][i] * ri[i][j])
            value_i = imag[i][i] * rr[i][j]
            for k in range(3):
                if k != i:
                    value_r = value_r + real[i][k] * rr[k][j] - imag[i][k] * ri[k][j]
                    value_i = value_i + real[i][k] * ri[k][j] + imag[i][k] * rr[k][j]
            out_r[i][j] = value_r
            out_i[i][j] = value_i
    return (out_r, out_i, 1)


def pack_links(links_ref, dense):
    def body(mu, carry):
        for e, (c, i, j) in enumerate(ENTRIES):
            low, high = pack_pair(links_ref[mu, c, i, j, 0].astype(F32))
            dense[mu, e, 0] = low
            dense[mu, e, 1] = high
        return carry

    lax.fori_loop(0, 4, body, 0)


def face_kernel(links_ref, up_ref, down_ref, dense, slab, moved, rows):
    pack_links(links_ref, dense)

    def shift_body(e, carry):
        pair = [dense[3, e, 0], dense[3, e, 1]]
        for mu in range(3):
            low, high = dense_shift(pair, mu, 1)
            moved[mu, e, 0] = low
            moved[mu, e, 1] = high
        return carry

    lax.fori_loop(0, 18, shift_body, 0)

    def staple_body(step, carry):
        mu = step // 2
        c = step % 2
        u_mu = load_matrix(lambda e: dense[mu, e, c])
        u_t = load_matrix(lambda e: dense[3, e, c])
        edge = mat_mul(u_mu, load_matrix(lambda e: moved[mu, e, c]))

        def write_edge(e, value):
            dense[EDGE + mu, e, c] = value

        store_matrix(edge, write_edge)

        def write(e, value):
            dense[STAPLE + mu, e, c] = value
            rows[16 + mu * 18 + e, pl.ds(c, 1)] = value[3:4]
            rows[16 + mu * 18 + e, pl.ds(2 + c, 1)] = value[7:8]

        store_matrix(mat_mul(dagger(edge), u_t), write)
        return carry

    lax.fori_loop(0, 6, staple_body, 0)

    def slab_body(c, carry):
        u_t = load_matrix(lambda e: dense[3, e, c])
        ahead = load_matrix(lambda e: pltpu.roll(dense[3, e, c], 7, 0))
        two = mat_mul(u_t, ahead)
        later = tuple(
            [[pltpu.roll(part[i][j], 6, 0) for j in range(3)] for i in range(3)] for part in two[:2]
        ) + (two[2],)
        four = mat_mul((two[0][:2], two[1][:2], two[2]), later)

        def write(e, value):
            slab[e, pl.ds(c, 1)] = value[0:1]
            slab[e, pl.ds(2 + c, 1)] = value[4:5]
            rows[e, pl.ds(c, 1)] = value[0:1]
            rows[e, pl.ds(2 + c, 1)] = value[4:5]

        store_rows(four, write)
        return carry

    lax.fori_loop(0, 2, slab_body, 0)
    for q in range(4):
        up_ref[:, q * 128:q * 128 + 128] = rows[:, q, :].astype(BF16)

    def down_body(e, carry):
        for mu in range(3):
            for c in range(2):
                value = dense[mu, e, c]
                rows[16 + mu * 18 + e, c:c + 1] = value[0:1]
                rows[16 + mu * 18 + e, 2 + c:3 + c] = value[4:5]
        return carry

    lax.fori_loop(0, 18, down_body, 0)
    for q in range(4):
        down_ref[:, q * 128:q * 128 + 128] = rows[:, q, :].astype(BF16)


def block_kernel(
    widths, core_ref, up_ref, down_ref, slab, w1_ref, w2_ref, w3_ref, w4_ref, after_ref, block_ref, other, block
):
    even = core_ref[0] == 0
    up = up_ref[0:16].astype(F32)
    down = down_ref[0:16].astype(F32)
    for q in range(4):
        lanes = slice(q * 128, q * 128 + 128)
        other[:, q, :] = jnp.where(even, down[0:12, lanes], up[0:12, lanes])
    first = two_rows(lambda e: jnp.where(even, slab[e], other[e]))
    second = special(two_rows(lambda e: jnp.where(even, other[e], slab[e])))

    def write(e, value):
        block[2 * e:2 * e + 2, :] = jnp.where(even, value[0:2], value[2:4])

    store_rows(mat_mul(first, second), write)
    block[SLABROWS:BLOCKROWS] = jnp.zeros((BLOCKROWS - SLABROWS, LANES), F32)
    offset = 0
    for ref, width in zip((w2_ref, w3_ref, w1_ref, w4_ref), widths):
        flat = ref[...].astype(F32)
        for r in range(27):
            block[SLABROWS + r:SLABROWS + r + 1, offset:offset + width] = (
                flat[width * r:width * r + width].reshape(1, width)
            )
        offset += width
    value = block[...].astype(BF16)
    for d in range(block_ref.shape[0]):
        block_ref[d] = value


def put_row(rows, channel, c, value):
    for t in range(4):
        rows[t, c, pl.ds(channel, 1), :] = value[t:t + 1]
        rows[t, 2 + c, pl.ds(channel, 1), :] = value[4 + t:5 + t]


def sum_at(mu, e, c):
    return (mu * 18 + e) * 2 + c


def force_at(mu, e, c):
    return 108 + (mu * 9 + e) * 2 + c


def cot_at(mu, e, c):
    return 190 + (mu * 18 + e) * 2 + c


def space_kernel(code_ref, dense, cot_ref, state, moved, staples):
    def cot_body(mu, carry):
        for e, (part, i, j) in enumerate(ENTRIES):
            low, high = pack_pair(cot_ref[mu, part, i, j, 0].astype(F32))
            state[cot_at(mu, e, 0)] = low
            state[cot_at(mu, e, 1)] = high
        return carry

    lax.fori_loop(0, 4, cot_body, 0)
    state[108:180] = jnp.zeros((72, 8, LANES), F32)
    steps = row_iota() % 4
    lanes = lane_iota(8)
    colour = (lanes // 64 + lanes // 8 % 8 + lanes % 8 + steps) % 2
    code = jnp.zeros_like(steps)
    for t in range(4):
        code = jnp.where(steps == t, code_ref[0, t], code)
    for mu in range(4):
        active = jnp.logical_and(colour == code % 2, jnp.right_shift(code, mu + 1) % 2 == 1)
        state[GATE + mu] = jnp.where(active, 1.0, 0.0)

    def shift_body(e, carry):
        for nu in range(3):
            pair = [dense[nu, e, 0], dense[nu, e, 1]]
            for mu in range(3):
                if mu != nu:
                    low, high = dense_shift(pair, mu, 1)
                    moved[mu, nu, e, 0] = low
                    moved[mu, nu, e, 1] = high
        return carry

    lax.fori_loop(0, 18, shift_body, 0)

    def plane_body(step, carry):
        plane = step // 2
        c = step % 2
        mu = jnp.where(plane == 2, 1, 0)
        nu = jnp.where(plane == 0, 1, 2)
        u_mu = load_matrix(lambda e: dense[mu, e, c])
        u_nu = load_matrix(lambda e: dense[nu, e, c])
        one = mat_mul(u_mu, load_matrix(lambda e: moved[mu, nu, e, c]))
        two = mat_mul(u_nu, load_matrix(lambda e: moved[nu, mu, e, c]))
        loop = mat_mul(one, dagger(two))
        state[PLANE + step] = (loop[0][0][0] + loop[0][1][1] + loop[0][2][2]) / 3.0
        for e, part in enumerate(anti_parts(loop)):
            state[force_at(mu, e, c)] += part
            state[force_at(nu, e, c)] -= part

        def write_mu(e, value):
            staples[mu, nu, e, c] = value

        def write_nu(e, value):
            staples[nu, mu, e, c] = value

        store_matrix(mat_mul(dagger(one), u_nu), write_mu)
        store_matrix(mat_mul(dagger(two), u_mu), write_nu)
        return carry

    lax.fori_loop(0, 6, plane_body, 0)

    def lower_body(e, carry):
        for mu in range(3):
            acc = [jnp.where(steps == 0, 0.0, pltpu.roll(dense[STAPLE + mu, e, c], 1, 0)) for c in range(2)]
            for nu in range(3):
                if nu != mu:
                    pair = dense_shift([staples[mu, nu, e, 0], staples[mu, nu, e, 1]], nu, -1)
                    acc = [acc[c] + pair[c] for c in range(2)]
            state[sum_at(mu, e, 0)] = acc[0]
            state[sum_at(mu, e, 1)] = acc[1]
        return carry

    lax.fori_loop(0, 18, lower_body, 0)


def time_kernel(
    dense, state, up_ref, down_ref,
    fm_ref, fup_ref, fdown_ref, w1_ref, w2_ref,
    moved, staples, sums, halo_up, halo_down, forces, rows,
):
    for q in range(4):
        halo_up[:, q, :] = up_ref[:, q * 128:q * 128 + 128].astype(F32)
        halo_down[:, q, :] = down_ref[:, q * 128:q * 128 + 128].astype(F32)
    rows[...] = jnp.zeros_like(rows)
    for channel, plane in ((0, 0), (1, 1), (3, 2)):
        for c in range(2):
            put_row(rows, channel, c, state[PLANE + 2 * plane + c])
    for mu in range(4):
        for e in range(9):
            for c in range(2):
                forces[mu, e, c] = state[force_at(mu, e, c)]
    steps = row_iota() % 4

    def shift_body(e, carry):
        for nu in range(3):
            halo = halo_pair(halo_down, 16 + nu * 18 + e)
            below = halo_pair(halo_up, 16 + nu * 18 + e)
            for c in range(2):
                moved[nu, e, c] = jnp.where(steps == 3, halo[c], pltpu.roll(dense[nu, e, c], 7, 0))
                sums[nu, e, c] = state[sum_at(nu, e, c)] + jnp.where(steps == 0, below[c], 0.0)
        return carry

    lax.fori_loop(0, 18, shift_body, 0)

    def plane_body(step, carry):
        mu = step // 2
        c = step % 2
        one = load_matrix(lambda e: dense[EDGE + mu, e, c])
        two = mat_mul(load_matrix(lambda e: dense[3, e, c]), load_matrix(lambda e: moved[mu, e, c]))
        loop = mat_mul(one, dagger(two))
        put_row(rows, jnp.where(mu == 0, 2, mu + 3), c, (loop[0][0][0] + loop[0][1][1] + loop[0][2][2]) / 3.0)
        for e, part in enumerate(anti_parts(loop)):
            forces[mu, e, c] += part
            forces[3, e, c] -= part

        def write(e, value):
            staples[mu, e, c] = value

        store_matrix(mat_mul(dagger(two), load_matrix(lambda e: dense[mu, e, c])), write)
        return carry

    lax.fori_loop(0, 6, plane_body, 0)

    def lower_body(e, carry):
        acc = None
        for mu in range(3):
            pair = dense_shift([staples[mu, e, 0], staples[mu, e, 1]], mu, -1)
            acc = pair if acc is None else [acc[c] + pair[c] for c in range(2)]
        sums[3, e, 0] = acc[0]
        sums[3, e, 1] = acc[1]
        return carry

    lax.fori_loop(0, 18, lower_body, 0)

    def force_body(step, carry):
        mu = step // 2
        c = step % 2
        current = load_matrix(lambda e: dense[mu, e, c])
        omega = mat_mul(current, load_matrix(lambda e: sums[mu, e, c]))
        parts = [part + forces[mu, e, c] for e, part in enumerate(anti_parts(omega))]
        mean = (parts[0] + parts[1] + parts[2]) * (1.0 / 3.0)
        parts = [parts[e] - mean if e < 3 else parts[e] for e in range(9)]
        parts = [part * (1.0 / 12.0) for part in parts]
        applied = anti_mul(parts, current)
        twice = anti_mul(parts, applied)
        gate = state[GATE + mu]
        slope = jnp.zeros_like(gate)
        curve = jnp.zeros_like(gate)
        for e, (part, i, j) in enumerate(ENTRIES):
            weight = state[cot_at(mu, e, c)]
            slope = slope + weight * applied[part][i][j]
            curve = curve + weight * twice[part][i][j]
            w1_ref[mu, e, c] = gate * applied[part][i][j]
            w2_ref[mu, e, c] = gate * twice[part][i][j]
        put_row(rows, 8 + mu, c, gate * slope)
        put_row(rows, 12 + mu, c, gate * curve)
        return carry

    lax.fori_loop(0, 8, force_body, 0)
    for t in range(4):
        for q in range(4):
            value = rows[t, q]
            fm_ref[t, :, q * 128:q * 128 + 128] = value.astype(BF16)
            if t > 0:
                fup_ref[t - 1, :, q * 128:q * 128 + 128] = value[0:8].astype(BF16)
            if t < 3:
                fdown_ref[t, :, q * 128:q * 128 + 128] = value[0:8].astype(BF16)


def selectors():
    row = lax.broadcasted_iota(jnp.int32, (432, 72), 0)
    col = lax.broadcasted_iota(jnp.int32, (432, 72), 1)
    group = row // 12
    spread = (group // 4 * 8 + group % 4 == col).astype(F32).astype(BF16)
    keep = (
        lax.broadcasted_iota(jnp.int32, (432, H), 1) // 4 == lax.broadcasted_iota(jnp.int32, (432, H), 0) % 12
    )
    return spread, keep


def panel_kernel(gathered_ref, weights_ref, loops_ref, p1_ref, p2_ref, p3_ref, p4_ref, b2_ref, b3_ref, b4_ref, weights):
    count = gathered_ref.shape[0]

    def read(chip):
        low = gathered_ref[2 * chip].astype(F32)
        high = gathered_ref[2 * chip + 1].astype(F32)
        return special(
            two_rows(lambda e: jnp.concatenate([low[2 * e:2 * e + 2], high[2 * e:2 * e + 2]], axis=0))
        )

    def flat(matrix):
        return tuple(matrix[0][i][j] for i in range(3) for j in range(3)) + tuple(
            imag_of(matrix, i, j) for i in range(3) for j in range(3)
        )

    def chain(chip, state):
        return flat(mat_mul(load_matrix(lambda e: state[e]), read(chip)))

    state = lax.fori_loop(1, count // 2, chain, flat(read(0)))
    loops_ref[0] = (state[0] + state[4] + state[8]) / 3.0
    loops_ref[1] = (state[9] + state[13] + state[17]) / 3.0

    if weights_ref is None:
        for d in range(count):
            block = gathered_ref[d].astype(F32)
            weights[27 * d:27 * d + 27, :] = block[SLABROWS:SLABROWS + 27]
    else:
        weights[...] = weights_ref[...].astype(F32)
    for k in range(TAPS):
        rows = slice(H * k, H * k + H)
        back = slice(H * SWAP[k], H * SWAP[k] + H)
        p2_ref[:, rows] = weights[rows, 0:48].astype(BF16)
        p3_ref[:, rows] = weights[rows, 48:96].astype(BF16)
        p1_ref[:, 8 * k:8 * k + 8] = weights[rows, 96:104].astype(BF16)
        turned = weights[back, :].T
        b2_ref[:, rows] = turned[0:48].astype(BF16)
        b3_ref[:, rows] = turned[48:96].astype(BF16)
    spread, keep = selectors()
    place = (
        lax.broadcasted_iota(jnp.int32, (LANES, H), 0) == 104 + lax.broadcasted_iota(jnp.int32, (LANES, H), 1) % 4
    ).astype(F32).astype(BF16)
    wide = jnp.dot(weights[...].astype(BF16), place, preferred_element_type=F32)
    wide = jnp.where(keep, wide, 0.0).astype(BF16)
    last = lax.dot_general(spread, wide, (((0,), (0,)), ((), ())), preferred_element_type=F32)
    p4_ref[...] = last.astype(BF16)
    for k in range(TAPS):
        b4_ref[:, 8 * k:8 * k + 8] = last[8 * SWAP[k]:8 * SWAP[k] + 8, :].T.astype(BF16)


def panel_kernel_plain(gathered_ref, *rest):
    panel_kernel(gathered_ref, None, *rest)


def chunks_of(value):
    return [value[:, q * 128:q * 128 + 128] for q in range(4)]


def one_shift(chunks, position):
    if position == 0:
        return chunks
    lanes = lane_iota(chunks[0].shape[0])
    sign = 1 if position % 2 == 1 else -1
    if position > 4:
        return [shift_z(chunk, sign, lanes) for chunk in chunks]
    if position > 2:
        return [shift_y(chunk, sign, lanes) for chunk in chunks]
    low = lanes < 64
    rolled = [roll_lanes(chunk, 64) for chunk in chunks]
    if sign > 0:
        return [jnp.where(low, rolled[q], rolled[(q + 1) % 4]) for q in range(4)]
    return [jnp.where(low, rolled[(q + 3) % 4], rolled[q]) for q in range(4)]


def all_shifts(chunks):
    lanes = lane_iota(chunks[0].shape[0])
    y = lanes // 8 % 8
    z = lanes % 8
    low = lanes < 64
    half = [roll_lanes(chunk, 64) for chunk in chunks]
    return [
        chunks,
        [jnp.where(low, half[q], half[(q + 1) % 4]) for q in range(4)],
        [jnp.where(low, half[(q + 3) % 4], half[q]) for q in range(4)],
        [roll_lanes(jnp.where(y == 0, half[q], chunks[q]), -8) for q in range(4)],
        [roll_lanes(jnp.where(y == 7, half[q], chunks[q]), 8) for q in range(4)],
        [roll_lanes(jnp.where(z == 0, roll_lanes(chunk, 8), chunk), -1) for chunk in chunks],
        [roll_lanes(jnp.where(z == 7, roll_lanes(chunk, -8), chunk), 1) for chunk in chunks],
    ]


def span(slice_index, count=1):
    if isinstance(slice_index, int):
        return slice(slice_index * SITES, (slice_index + count) * SITES)
    return pl.ds(pl.multiple_of(slice_index * SITES, SITES), count * SITES)


def slot_of(slot):
    return slice(slot * SITES, (slot + 1) * SITES)


def stack_wide(source, target, index, slot):
    chunks = chunks_of(source[:, span(index)])
    for position, shifted in enumerate(all_shifts(chunks)):
        for q in range(4):
            lanes = slice(slot * SITES + q * 128, slot * SITES + q * 128 + 128)
            target[H * position:H * position + H, lanes] = shifted[q]
    target[7 * H:8 * H, slot_of(slot)] = source[:, span(index + 1)]
    target[8 * H:9 * H, slot_of(slot)] = source[:, span(index - 1)]


def stack_thin(source, target, index, slot):
    chunks = chunks_of(source[:, span(index)])
    ahead = chunks_of(source[:, span(index + 1)])
    behind = chunks_of(source[:, span(index - 1)])
    columns = all_shifts(chunks) + [ahead, behind]
    for q in range(4):
        lanes = slice(slot * SITES + q * 128, slot * SITES + q * 128 + 128)
        target[0:72, lanes] = jnp.concatenate([column[q] for column in columns], axis=0).astype(BF16)


def one_minus_square(value):
    value = value.astype(F32)
    return 1.0 - value * value


def conv_kernel(
    split, fm_ref, below_ref, above_ref, fbelow_ref, fabove_ref, loops_ref,
    p1_ref, p2_ref, p3_ref, p4_ref, b2_ref, b3_ref, b4_ref,
    coeff_ref, grads_ref,
    feats, mixed, h1, h2, h3, parts, lasts, g3, g2, g1, wide, thin, packed,
):
    row8 = lax.broadcasted_iota(jnp.int32, (8, SITES), 0)
    loop_re = jnp.concatenate([loops_ref[0, q:q + 1, :] for q in range(4)], axis=1)
    loop_im = jnp.concatenate([loops_ref[1, q:q + 1, :] for q in range(4)], axis=1)
    loops = jnp.where(row8 == 6, loop_re, jnp.where(row8 == 7, loop_im, 0.0))
    loops = loops.astype(BF16).astype(F32)
    for j in range(3):
        feats[:, span(j)] = fbelow_ref[j].astype(F32) + loops
        feats[:, span(15 + j)] = fabove_ref[j].astype(F32) + loops
    for base, ref in ((3, below_ref), (7, fm_ref), (11, above_ref)):
        for j in range(4):
            value = ref[j].astype(F32)
            feats[:, span(base + j)] = value[0:8] + loops
            mixed[:, span(base + j)] = value[8:16]

    def wide_dot(source, weights, index, slot):
        stack_wide(source, wide, index, slot)
        return jnp.dot(weights[...], wide[:, slot_of(slot)], preferred_element_type=F32)

    def thin_dot(source, weights, index, slot):
        stack_thin(source, thin, index, slot)
        return jnp.dot(weights[...], thin[:, slot_of(slot)], preferred_element_type=F32)

    for index in range(1, 17):
        h1[:, span(index)] = jnp.tanh(thin_dot(feats, p1_ref, index, index % 4)).astype(BF16)
    for index in range(2, 16):
        h2[:, span(index)] = jnp.tanh(wide_dot(h1, p2_ref, index, index % 4)).astype(BF16)
    for index in range(3, 15):
        out = jnp.tanh(wide_dot(h2, p3_ref, index, index % 4)).astype(BF16)
        h3[:, span(index)] = out
        taps = jnp.dot(p4_ref[...], out, preferred_element_type=F32)
        acc = None
        for position in range(7):
            shifted = one_shift(chunks_of(taps[8 * position:8 * position + 8]), position)
            acc = shifted if acc is None else [a + b for a, b in zip(acc, shifted)]
        parts[0, :, span(index)] = jnp.concatenate(acc, axis=1)
        parts[1, :, span(index)] = taps[56:64]
        parts[2, :, span(index)] = taps[64:72]

    for index in range(4, 14):
        coeff = jnp.tanh(parts[0, :, span(index)] + parts[1, :, span(index + 1)] + parts[2, :, span(index - 1)])
        blend = mixed[:, span(index)]
        value = (blend + coeff * pltpu.roll(blend, 4, 0)) * (1.0 - coeff * coeff)
        lasts[:, span(index)] = jnp.where(row8 < 4, value, 0.0).astype(BF16).astype(F32)
        if 7 <= index < 11:
            coeff_ref[index - 7] = coeff

    own = span(7, 4)
    contract = (((1,), (1,)), ((), ()))
    for index in (5, 6, 11, 12, 7, 8, 9, 10):
        out = thin_dot(lasts, b4_ref, index, (index + 1) % 4)
        g3[:, span(index)] = (out * one_minus_square(h3[:, span(index)])).astype(BF16)
    grad_last = lax.dot_general(thin[...], h3[:, own], contract, preferred_element_type=F32)
    for index in (6, 11, 7, 8, 9, 10):
        out = wide_dot(g3, b3_ref, index, (index + 1) % 4)
        g2[:, span(index)] = (out * one_minus_square(h2[:, span(index)])).astype(BF16)
    grad_third = lax.dot_general(wide[...], h2[:, own], contract, preferred_element_type=F32)
    for index in (7, 8, 9, 10):
        out = wide_dot(g2, b2_ref, index, (index + 1) % 4)
        g1[:, slot_of(index - 7)] = (out * one_minus_square(h1[:, span(index)])).astype(BF16)
    grad_second = lax.dot_general(wide[...], h1[:, own], contract, preferred_element_type=F32)
    for index in (7, 8, 9, 10):
        stack_thin(feats, thin, index, index - 7)
    grad_first = lax.dot_general(g1[...], thin[...], contract, preferred_element_type=F32)

    spread, keep = selectors()
    ordered = jnp.concatenate([grad_last[8 * SWAP[k]:8 * SWAP[k] + 8] for k in range(TAPS)], axis=0)
    broad = jnp.dot(spread, ordered.astype(BF16), preferred_element_type=F32)
    broad = jnp.where(keep, broad, 0.0).astype(BF16)
    place = (
        lax.broadcasted_iota(jnp.int32, (H, LANES), 1) == 104 + lax.broadcasted_iota(jnp.int32, (H, LANES), 0) % 4
    ).astype(F32).astype(BF16)
    packed[...] = jnp.dot(broad, place, preferred_element_type=F32)
    for k in range(TAPS):
        rows = slice(H * k, H * k + H)
        back = slice(H * SWAP[k], H * SWAP[k] + H)
        packed[rows, 0:48] = grad_second[back]
        packed[rows, 48:96] = grad_third[back]
        packed[rows, 96:104] = grad_first[:, 8 * k:8 * k + 8]
    if split:
        for d in range(16):
            grads_ref[d] = packed[27 * d:27 * d + 27, :].astype(BF16)
    else:
        grads_ref[...] = packed[...].astype(BF16)


def update_kernel(dense, w1_ref, w2_ref, coeff_ref, out_ref, factors):
    for mu in range(4):
        for t in range(4):
            for c in range(2):
                factors[mu, c, t:t + 1, :] = coeff_ref[t, mu:mu + 1, c * 128:c * 128 + 128]
                factors[mu, c, 4 + t:5 + t, :] = coeff_ref[t, mu:mu + 1, 256 + c * 128:384 + c * 128]

    def body(mu, carry):
        factor = [factors[mu, c] for c in range(2)]
        half = [0.5 * value * value for value in factor]
        for e, (part, i, j) in enumerate(ENTRIES):
            new = [dense[mu, e, c] + factor[c] * w1_ref[mu, e, c] + half[c] * w2_ref[mu, e, c] for c in range(2)]
            out_ref[mu, part, i, j, 0] = jnp.concatenate(
                [new[0][0:4], new[1][0:4], new[0][4:8], new[1][4:8]], axis=1
            )
        return carry

    lax.fori_loop(0, 4, body, 0)


def sum_kernel(widths, parts_ref, first_ref, second_ref, third_ref, last_ref):
    value = parts_ref[0].astype(F32)
    for d in range(1, parts_ref.shape[0]):
        value = value + parts_ref[d].astype(F32)
    offset = 0
    for ref, width in zip((second_ref, third_ref, first_ref, last_ref), widths):
        for r in range(27):
            ref[:, width * r:width * r + width] = value[r:r + 1, offset:offset + width]
        offset += width


def call(body, outs, scratch, places=None, cost=None, limit=LIMIT):
    specs = {}
    if places is not None:
        specs["in_specs"] = [pl.BlockSpec(memory_space=place) for place in places]
    return pl.pallas_call(
        body,
        out_shape=[jax.ShapeDtypeStruct(shape, dtype) for shape, dtype in outs],
        scratch_shapes=[pltpu.VMEM(*item) if isinstance(item, tuple) else item for item in scratch],
        compiler_params=pltpu.CompilerParams(vmem_limit_bytes=limit),
        cost_estimate=cost,
        **specs,
    )


def on_device(links, cotangent, parity, link_subset, w_first, w_second, w_third, w_last):
    count = lax.axis_size("tm")

    def send(value, distance):
        return lax.ppermute(value, "tm", [(i, (i + distance) % count) for i in range(count)])

    widths = (768 // count, 768 // count, 128 // count, 64 // count)
    vmem, smem = pltpu.VMEM, pltpu.SMEM
    field = ((4, 18, 2, 8, LANES), F32)
    space = ((3, 18, 2, 8, LANES), F32)
    edge_rows = ((70, SITES), BF16)
    up, down, dense, slab = call(
        face_kernel,
        [edge_rows, edge_rows, ((10, 18, 2, 8, LANES), F32), ((12, 4, LANES), F32)],
        [space, ((70, 4, LANES), F32)],
    )(links)
    up = send(up, 1)
    down = send(down, -1)
    (state,) = call(
        space_kernel,
        [((334, 8, LANES), F32)],
        [((3, 3, 18, 2, 8, LANES), F32), ((3, 3, 18, 2, 8, LANES), F32)],
        places=(smem, vmem, vmem),
        cost=pl.CostEstimate(flops=4_000_000_000, bytes_accessed=16_000_000, transcendentals=0),
    )(parity + 2 * link_subset, dense, cotangent)
    core = (lax.axis_index("tm") % 2).astype(jnp.int32)[None]
    (block,) = call(
        functools.partial(block_kernel, widths),
        [((count, BLOCKROWS, LANES), BF16)],
        [((12, 4, LANES), F32), ((BLOCKROWS, LANES), F32)],
        places=(smem,) + (vmem,) * 7 + (pl.ANY,),
    )(core, up, down, slab, w_first, w_second, w_third, w_last, state)
    gathered = lax.all_to_all(block, "tm", split_axis=0, concat_axis=0, tiled=True)
    fm, fup, fdown, applied, twice = call(
        time_kernel,
        [((4, 16, SITES), BF16), ((3, 8, SITES), BF16), ((3, 8, SITES), BF16), field, field],
        [
            space, space, field, ((70, 4, LANES), F32), ((70, 4, LANES), F32),
            ((4, 9, 2, 8, LANES), F32), ((4, 4, 16, LANES), F32),
        ],
    )(dense, state, up, down)
    below = send(fm, 1)
    above = send(fm, -1)
    fbelow = send(fup, 2)
    fabove = send(fdown, -2)

    panel_outs = [
        ((2, 4, LANES), F32), ((H, 72), BF16), ((H, 432), BF16), ((H, 432), BF16), ((72, H), BF16),
        ((H, 432), BF16), ((H, 432), BF16), ((H, 72), BF16),
    ]
    panel_scratch = [((432, LANES), F32)]
    if count == 16:
        loops, p1, p2, p3, p4, b2, b3, b4 = call(panel_kernel_plain, panel_outs, panel_scratch)(gathered)
    else:
        pieces = []
        offset = 0
        for width, full in zip(widths, (48, 48, 8, 4)):
            piece = gathered[:, SLABROWS:SLABROWS + 27, offset:offset + width]
            pieces.append(piece.reshape(432, full))
            offset += width
        pieces.append(jnp.zeros((432, 20), BF16))
        loops, p1, p2, p3, p4, b2, b3, b4 = call(panel_kernel, panel_outs, panel_scratch)(
            gathered, jnp.concatenate(pieces, axis=1)
        )

    window = 18 * SITES
    coeff, grads = call(
        functools.partial(conv_kernel, count == 16),
        [((4, 8, SITES), F32), ((16, 27, LANES) if count == 16 else (432, LANES), BF16)],
        [
            ((8, window), F32), ((8, window), F32), ((H, window), BF16), ((H, window), BF16), ((H, window), BF16),
            ((3, 8, window), F32), ((8, window), F32), ((H, window), BF16), ((H, window), BF16), ((H, 4 * SITES), BF16),
            ((432, 4 * SITES), BF16), ((72, 4 * SITES), BF16), ((432, LANES), F32),
        ],
        limit=20 * 1024 * 1024,
    )(fm, below, above, fbelow, fabove, loops, p1, p2, p3, p4, b2, b3, b4)
    if count != 16:
        offset = 0
        pieces = []
        for width, full in zip(widths, (48, 48, 8, 4)):
            pieces.append(grads[:, offset:offset + full].reshape(count, 27, width))
            offset += full
        grads = jnp.concatenate(pieces, axis=2)
    grads = lax.all_to_all(grads, "tm", split_axis=0, concat_axis=0, tiled=True)
    (new_links,) = call(
        update_kernel, [(links.shape, F32)], [((4, 2, 8, LANES), F32)]
    )(dense, applied, twice, coeff)
    grad_first, grad_second, grad_third, grad_last = call(
        functools.partial(sum_kernel, widths),
        [((1, 27 * width), F32) for width in (widths[2], widths[0], widths[1], widths[3])],
        [],
    )(grads)
    return (new_links, grad_first, grad_second, grad_third, grad_last)


def solution(mesh):
    placed = (
        P(None, None, None, None, "groups", "tm", None),
        P(None, None, None, None, "groups", "tm", None),
        P("groups", "tm"),
        P("groups", "tm"),
        P("tm"),
        P("tm"),
        P("tm"),
        P("tm"),
    )
    return jax.shard_map(
        on_device,
        mesh=mesh,
        in_specs=placed,
        out_specs=(
            P(None, None, None, None, "groups", "tm", None),
            P("groups", "tm"),
            P("groups", "tm"),
            P("groups", "tm"),
            P("groups", "tm"),
        ),
        check_vma=False,
    )
```

```python
import functools

import jax
import jax.numpy as jnp
from jax import lax
from jax.experimental import pallas as pl
from jax.experimental.pallas import tpu as pltpu
from jax.sharding import PartitionSpec as P

F32 = jnp.float32
BF16 = jnp.bfloat16
TAPS = 9
H = 48
LANES = 128
SITES = 512
PAIRS = ((0, 1), (0, 2), (0, 3), (1, 2), (1, 3), (2, 3))
SWAP = (0, 2, 1, 4, 3, 6, 5, 8, 7)
ENTRIES = tuple((c, i, j) for c in range(2) for i in range(3) for j in range(3))
PLANE = 180
SLABROWS = 24
BLOCKROWS = 64
LIMIT = 8 * 1024 * 1024


def lane_iota(rows):
    return lax.broadcasted_iota(jnp.int32, (rows, LANES), 1)


def row_iota():
    return lax.broadcasted_iota(jnp.int32, (8, LANES), 0)


def roll_lanes(value, amount):
    return pltpu.roll(value, amount % LANES, 1)


def shift_z(chunk, sign, lanes):
    z = lanes % 8
    if sign > 0:
        return jnp.where(z == 7, roll_lanes(chunk, 7), roll_lanes(chunk, -1))
    return jnp.where(z == 0, roll_lanes(chunk, -7), roll_lanes(chunk, 1))


def shift_y(chunk, sign, lanes):
    y = lanes // 8 % 8
    if sign > 0:
        return jnp.where(y == 7, roll_lanes(chunk, 56), roll_lanes(chunk, -8))
    return jnp.where(y == 0, roll_lanes(chunk, -56), roll_lanes(chunk, 8))


def dense_shift(pair, axis, sign):
    lanes = lane_iota(8)
    if axis == 2:
        return [shift_z(chunk, sign, lanes) for chunk in pair]
    if axis == 1:
        return [shift_y(chunk, sign, lanes) for chunk in pair]
    low = lanes < 64
    first, second = [roll_lanes(chunk, 64) for chunk in pair]
    if sign > 0:
        return [jnp.where(low, first, second), jnp.where(low, second, pltpu.roll(first, 4, 0))]
    return [jnp.where(low, pltpu.roll(second, 4, 0), first), jnp.where(low, first, second)]


def pack_pair(value):
    return [
        jnp.concatenate([value[:, c * 128:c * 128 + 128], value[:, 256 + c * 128:384 + c * 128]], axis=0)
        for c in range(2)
    ]


def halo_pair(ref, index):
    top = row_iota() < 4
    pair = []
    for c in range(2):
        low = jnp.broadcast_to(ref[index, c:c + 1, :], (8, LANES))
        high = jnp.broadcast_to(ref[index, 2 + c:3 + c, :], (8, LANES))
        pair.append(jnp.where(top, low, high))
    return pair


def load_matrix(read):
    real = [[read(3 * i + j) for j in range(3)] for i in range(3)]
    imag = [[read(9 + 3 * i + j) for j in range(3)] for i in range(3)]
    return (real, imag, 1)


def dagger(matrix):
    real, imag, sign = matrix
    return (
        [[real[j][i] for j in range(3)] for i in range(3)],
        [[imag[j][i] for j in range(3)] for i in range(3)],
        -sign,
    )


def total(terms, signs):
    value = None
    for term, sign in zip(terms, signs):
        if value is None:
            value = term if sign > 0 else -term
        else:
            value = value + term if sign > 0 else value - term
    return value


def mat_mul(left, right):
    lr, li, ls = left
    rr, ri, rs = right
    same = ls == rs
    height = len(lr)
    real = [[None] * 3 for _ in range(height)]
    imag = [[None] * 3 for _ in range(height)]
    for i in range(height):
        for j in range(3):
            real[i][j] = total(
                [lr[i][k] * rr[k][j] for k in range(3)] + [li[i][k] * ri[k][j] for k in range(3)],
                [1, 1, 1] + [-1 if same else 1] * 3,
            )
            imag[i][j] = total(
                [lr[i][k] * ri[k][j] for k in range(3)] + [li[i][k] * rr[k][j] for k in range(3)],
                [1, 1, 1] + [1 if same else -1] * 3,
            )
    return (real, imag, ls if same else rs)


def imag_of(matrix, i, j):
    return matrix[1][i][j] if matrix[2] > 0 else -matrix[1][i][j]


def store_matrix(matrix, write):
    for i in range(3):
        for j in range(3):
            write(3 * i + j, matrix[0][i][j])
            write(9 + 3 * i + j, imag_of(matrix, i, j))


def two_rows(read):
    real = [[read(3 * i + j) for j in range(3)] for i in range(2)]
    imag = [[read(6 + 3 * i + j) for j in range(3)] for i in range(2)]
    return (real, imag, 1)


def store_rows(matrix, write):
    for i in range(2):
        for j in range(3):
            write(3 * i + j, matrix[0][i][j])
            write(6 + 3 * i + j, imag_of(matrix, i, j))


def special(matrix):
    real, imag, _ = matrix
    last_r, last_i = [], []
    for k in range(3):
        i, j = (k + 1) % 3, (k + 2) % 3
        last_r.append(
            (real[0][i] * real[1][j] - imag[0][i] * imag[1][j])
            - (real[0][j] * real[1][i] - imag[0][j] * imag[1][i])
        )
        last_i.append(
            (real[0][j] * imag[1][i] + imag[0][j] * real[1][i])
            - (real[0][i] * imag[1][j] + imag[0][i] * real[1][j])
        )
    return (real + [last_r], imag + [last_i], 1)


def anti_parts(matrix):
    parts = [2.0 * imag_of(matrix, i, i) for i in range(3)]
    for i, j in ((0, 1), (0, 2), (1, 2)):
        parts.append(matrix[0][i][j] - matrix[0][j][i])
        parts.append(imag_of(matrix, i, j) + imag_of(matrix, j, i))
    return parts


def anti_matrix(parts):
    zero = jnp.zeros_like(parts[0])
    real = [[zero, parts[3], parts[5]], [-parts[3], zero, parts[7]], [-parts[5], -parts[7], zero]]
    imag = [[parts[0], parts[4], parts[6]], [parts[4], parts[1], parts[8]], [parts[6], parts[8], parts[2]]]
    return real, imag


def anti_mul(parts, right):
    real, imag = anti_matrix(parts)
    rr, ri, _ = right
    out_r = [[None] * 3 for _ in range(3)]
    out_i = [[None] * 3 for _ in range(3)]
    for i in range(3):
        for j in range(3):
            value_r = -(imag[i][i] * ri[i][j])
            value_i = imag[i][i] * rr[i][j]
            for k in range(3):
                if k != i:
                    value_r = value_r + real[i][k] * rr[k][j] - imag[i][k] * ri[k][j]
                    value_i = value_i + real[i][k] * ri[k][j] + imag[i][k] * rr[k][j]
            out_r[i][j] = value_r
            out_i[i][j] = value_i
    return (out_r, out_i, 1)


def pack_links(links_ref, dense):
    def body(mu, carry):
        for e, (c, i, j) in enumerate(ENTRIES):
            low, high = pack_pair(links_ref[mu, c, i, j, 0].astype(F32))
            dense[mu, e, 0] = low
            dense[mu, e, 1] = high
        return carry

    lax.fori_loop(0, 4, body, 0)


def face_kernel(links_ref, up_ref, down_ref, dense, edges, staples, slab, moved, rows):
    pack_links(links_ref, dense)

    def shift_body(e, carry):
        pair = [dense[3, e, 0], dense[3, e, 1]]
        for mu in range(3):
            low, high = dense_shift(pair, mu, 1)
            moved[mu, e, 0] = low
            moved[mu, e, 1] = high
        return carry

    lax.fori_loop(0, 18, shift_body, 0, unroll=3)

    def staple_body(step, carry):
        mu = step // 2
        c = step % 2
        u_mu = load_matrix(lambda e: dense[mu, e, c])
        u_t = load_matrix(lambda e: dense[3, e, c])
        edge = mat_mul(u_mu, load_matrix(lambda e: moved[mu, e, c]))

        def write_edge(e, value):
            edges[mu, e, c] = value

        store_matrix(edge, write_edge)

        def write(e, value):
            staples[mu, e, c] = value
            rows[16 + mu * 18 + e, pl.ds(c, 1)] = value[3:4]
            rows[16 + mu * 18 + e, pl.ds(2 + c, 1)] = value[7:8]

        store_matrix(mat_mul(dagger(edge), u_t), write)
        return carry

    lax.fori_loop(0, 6, staple_body, 0)

    def slab_body(c, carry):
        u_t = load_matrix(lambda e: dense[3, e, c])
        ahead = load_matrix(lambda e: pltpu.roll(dense[3, e, c], 7, 0))
        two = mat_mul(u_t, ahead)
        later = tuple(
            [[pltpu.roll(part[i][j], 6, 0) for j in range(3)] for i in range(3)] for part in two[:2]
        ) + (two[2],)
        four = mat_mul((two[0][:2], two[1][:2], two[2]), later)

        def write(e, value):
            slab[e, pl.ds(c, 1)] = value[0:1]
            slab[e, pl.ds(2 + c, 1)] = value[4:5]
            rows[e, pl.ds(c, 1)] = value[0:1]
            rows[e, pl.ds(2 + c, 1)] = value[4:5]

        store_rows(four, write)
        return carry

    lax.fori_loop(0, 2, slab_body, 0)
    for q in range(4):
        up_ref[:, q * 128:q * 128 + 128] = rows[:, q, :].astype(BF16)

    def down_body(e, carry):
        for mu in range(3):
            for c in range(2):
                value = dense[mu, e, c]
                rows[16 + mu * 18 + e, c:c + 1] = value[0:1]
                rows[16 + mu * 18 + e, 2 + c:3 + c] = value[4:5]
        return carry

    lax.fori_loop(0, 18, down_body, 0, unroll=3)
    for q in range(4):
        down_ref[:, q * 128:q * 128 + 128] = rows[:, q, :].astype(BF16)


def block_kernel(
    widths, core_ref, up_ref, down_ref, slab, w1_ref, w2_ref, w3_ref, w4_ref, after_ref, block_ref, other, block
):
    even = core_ref[0] == 0
    up = up_ref[0:16].astype(F32)
    down = down_ref[0:16].astype(F32)
    for q in range(4):
        lanes = slice(q * 128, q * 128 + 128)
        other[:, q, :] = jnp.where(even, down[0:12, lanes], up[0:12, lanes])
    first = two_rows(lambda e: jnp.where(even, slab[e], other[e]))
    second = special(two_rows(lambda e: jnp.where(even, other[e], slab[e])))

    def write(e, value):
        block[2 * e:2 * e + 2, :] = jnp.where(even, value[0:2], value[2:4])

    store_rows(mat_mul(first, second), write)
    block[SLABROWS:BLOCKROWS] = jnp.zeros((BLOCKROWS - SLABROWS, LANES), F32)
    offset = 0
    for ref, width in zip((w2_ref, w3_ref, w1_ref, w4_ref), widths):
        flat = ref[...].astype(F32)
        for r in range(27):
            block[SLABROWS + r:SLABROWS + r + 1, offset:offset + width] = (
                flat[width * r:width * r + width].reshape(1, width)
            )
        offset += width
    value = block[...].astype(BF16)
    for d in range(block_ref.shape[0]):
        block_ref[d] = value


def put_row(rows, channel, c, value):
    for t in range(4):
        rows[t, c, pl.ds(channel, 1), :] = value[t:t + 1]
        rows[t, 2 + c, pl.ds(channel, 1), :] = value[4 + t:5 + t]


def sum_at(mu, e, c):
    return (mu * 18 + e) * 2 + c


def force_at(mu, e, c):
    return 108 + (mu * 9 + e) * 2 + c


def space_kernel(dense, time_staples, state, moved, staples):
    state[108:180] = jnp.zeros((72, 8, LANES), F32)
    steps = row_iota() % 4

    def shift_body(e, carry):
        for nu in range(3):
            pair = [dense[nu, e, 0], dense[nu, e, 1]]
            for mu in range(3):
                if mu != nu:
                    low, high = dense_shift(pair, mu, 1)
                    moved[mu, nu, e, 0] = low
                    moved[mu, nu, e, 1] = high
        return carry

    lax.fori_loop(0, 18, shift_body, 0, unroll=3)

    def plane_body(step, carry):
        plane = step // 2
        c = step % 2
        mu = jnp.where(plane == 2, 1, 0)
        nu = jnp.where(plane == 0, 1, 2)
        u_mu = load_matrix(lambda e: dense[mu, e, c])
        u_nu = load_matrix(lambda e: dense[nu, e, c])
        one = mat_mul(u_mu, load_matrix(lambda e: moved[mu, nu, e, c]))
        two = mat_mul(u_nu, load_matrix(lambda e: moved[nu, mu, e, c]))
        loop = mat_mul(one, dagger(two))
        state[PLANE + step] = (loop[0][0][0] + loop[0][1][1] + loop[0][2][2]) / 3.0
        for e, part in enumerate(anti_parts(loop)):
            state[force_at(mu, e, c)] += part
            state[force_at(nu, e, c)] -= part

        def write_mu(e, value):
            staples[mu, nu, e, c] = value

        def write_nu(e, value):
            staples[nu, mu, e, c] = value

        store_matrix(mat_mul(dagger(one), u_nu), write_mu)
        store_matrix(mat_mul(dagger(two), u_mu), write_nu)
        return carry

    lax.fori_loop(0, 6, plane_body, 0)

    def lower_body(e, carry):
        for mu in range(3):
            acc = [jnp.where(steps == 0, 0.0, pltpu.roll(time_staples[mu, e, c], 1, 0)) for c in range(2)]
            for nu in range(3):
                if nu != mu:
                    pair = dense_shift([staples[mu, nu, e, 0], staples[mu, nu, e, 1]], nu, -1)
                    acc = [acc[c] + pair[c] for c in range(2)]
            state[sum_at(mu, e, 0)] = acc[0]
            state[sum_at(mu, e, 1)] = acc[1]
        return carry

    lax.fori_loop(0, 18, lower_body, 0, unroll=3)


def time_kernel(
    code_ref, dense, edges, state, cot_ref, up_ref, down_ref,
    fm_ref, fup_ref, fdown_ref, moves_ref,
    cots, gates, moved, staples, sums, halo_up, halo_down, forces, rows,
):
    for q in range(4):
        halo_up[:, q, :] = up_ref[:, q * 128:q * 128 + 128].astype(F32)
        halo_down[:, q, :] = down_ref[:, q * 128:q * 128 + 128].astype(F32)
    rows[...] = jnp.zeros_like(rows)
    pack_links(cot_ref, cots)
    lanes = lane_iota(8)
    site_steps = row_iota() % 4
    colour = (lanes // 64 + lanes // 8 % 8 + lanes % 8 + site_steps) % 2
    code = jnp.zeros_like(site_steps)
    for t in range(4):
        code = jnp.where(site_steps == t, code_ref[0, t], code)
    for mu in range(4):
        active = jnp.logical_and(colour == code % 2, jnp.right_shift(code, mu + 1) % 2 == 1)
        gates[mu] = jnp.where(active, 1.0, 0.0)
    for channel, plane in ((0, 0), (1, 1), (3, 2)):
        for c in range(2):
            put_row(rows, channel, c, state[PLANE + 2 * plane + c])
    for mu in range(4):
        for e in range(9):
            for c in range(2):
                forces[mu, e, c] = state[force_at(mu, e, c)]
    steps = row_iota() % 4

    def shift_body(e, carry):
        for nu in range(3):
            halo = halo_pair(halo_down, 16 + nu * 18 + e)
            below = halo_pair(halo_up, 16 + nu * 18 + e)
            for c in range(2):
                moved[nu, e, c] = jnp.where(steps == 3, halo[c], pltpu.roll(dense[nu, e, c], 7, 0))
                sums[nu, e, c] = state[sum_at(nu, e, c)] + jnp.where(steps == 0, below[c], 0.0)
        return carry

    lax.fori_loop(0, 18, shift_body, 0, unroll=3)

    def plane_body(step, carry):
        mu = step // 2
        c = step % 2
        one = load_matrix(lambda e: edges[mu, e, c])
        two = mat_mul(load_matrix(lambda e: dense[3, e, c]), load_matrix(lambda e: moved[mu, e, c]))
        loop = mat_mul(one, dagger(two))
        put_row(rows, jnp.where(mu == 0, 2, mu + 3), c, (loop[0][0][0] + loop[0][1][1] + loop[0][2][2]) / 3.0)
        for e, part in enumerate(anti_parts(loop)):
            forces[mu, e, c] += part
            forces[3, e, c] -= part

        def write(e, value):
            staples[mu, e, c] = value

        store_matrix(mat_mul(dagger(two), load_matrix(lambda e: dense[mu, e, c])), write)
        return carry

    lax.fori_loop(0, 6, plane_body, 0)

    def lower_body(e, carry):
        acc = None
        for mu in range(3):
            pair = dense_shift([staples[mu, e, 0], staples[mu, e, 1]], mu, -1)
            acc = pair if acc is None else [acc[c] + pair[c] for c in range(2)]
        sums[3, e, 0] = acc[0]
        sums[3, e, 1] = acc[1]
        return carry

    lax.fori_loop(0, 18, lower_body, 0, unroll=3)

    def force_body(step, carry):
        mu = step // 2
        c = step % 2
        current = load_matrix(lambda e: dense[mu, e, c])
        omega = mat_mul(current, load_matrix(lambda e: sums[mu, e, c]))
        parts = [part + forces[mu, e, c] for e, part in enumerate(anti_parts(omega))]
        mean = (parts[0] + parts[1] + parts[2]) * (1.0 / 3.0)
        parts = [parts[e] - mean if e < 3 else parts[e] for e in range(9)]
        parts = [part * (1.0 / 12.0) for part in parts]
        applied = anti_mul(parts, current)
        twice = anti_mul(parts, applied)
        gate = gates[mu]
        slope = jnp.zeros_like(gate)
        curve = jnp.zeros_like(gate)
        for e, (part, i, j) in enumerate(ENTRIES):
            weight = cots[mu, e, c]
            slope = slope + weight * applied[part][i][j]
            curve = curve + weight * twice[part][i][j]
            moves_ref[0, mu, e, c] = (gate * applied[part][i][j]).astype(BF16)
            moves_ref[1, mu, e, c] = (gate * twice[part][i][j]).astype(BF16)
        put_row(rows, 8 + mu, c, gate * slope)
        put_row(rows, 12 + mu, c, gate * curve)
        return carry

    lax.fori_loop(0, 8, force_body, 0)
    for t in range(4):
        for q in range(4):
            value = rows[t, q]
            fm_ref[t, :, q * 128:q * 128 + 128] = value.astype(BF16)
            if t > 0:
                fup_ref[t - 1, :, q * 128:q * 128 + 128] = value[0:8].astype(BF16)
            if t < 3:
                fdown_ref[t, :, q * 128:q * 128 + 128] = value[0:8].astype(BF16)


def selectors():
    row = lax.broadcasted_iota(jnp.int32, (432, 72), 0)
    col = lax.broadcasted_iota(jnp.int32, (432, 72), 1)
    group = row // 12
    spread = (group // 4 * 8 + group % 4 == col).astype(F32).astype(BF16)
    keep = (
        lax.broadcasted_iota(jnp.int32, (432, H), 1) // 4 == lax.broadcasted_iota(jnp.int32, (432, H), 0) % 12
    )
    return spread, keep


def panel_kernel(gathered_ref, weights_ref, loops_ref, p1_ref, p2_ref, p3_ref, p4_ref, b2_ref, b3_ref, b4_ref, weights):
    count = gathered_ref.shape[0]

    def read(chip):
        low = gathered_ref[2 * chip].astype(F32)
        high = gathered_ref[2 * chip + 1].astype(F32)
        return special(
            two_rows(lambda e: jnp.concatenate([low[2 * e:2 * e + 2], high[2 * e:2 * e + 2]], axis=0))
        )

    def flat(matrix):
        return tuple(matrix[0][i][j] for i in range(3) for j in range(3)) + tuple(
            imag_of(matrix, i, j) for i in range(3) for j in range(3)
        )

    def chain(chip, state):
        return flat(mat_mul(load_matrix(lambda e: state[e]), read(chip)))

    state = lax.fori_loop(1, count // 2, chain, flat(read(0)))
    loops_ref[0] = (state[0] + state[4] + state[8]) / 3.0
    loops_ref[1] = (state[9] + state[13] + state[17]) / 3.0

    if weights_ref is None:
        for d in range(count):
            block = gathered_ref[d].astype(F32)
            weights[27 * d:27 * d + 27, :] = block[SLABROWS:SLABROWS + 27]
    else:
        weights[...] = weights_ref[...].astype(F32)
    for k in range(TAPS):
        rows = slice(H * k, H * k + H)
        back = slice(H * SWAP[k], H * SWAP[k] + H)
        p2_ref[:, rows] = weights[rows, 0:48].astype(BF16)
        p3_ref[:, rows] = weights[rows, 48:96].astype(BF16)
        p1_ref[:, 8 * k:8 * k + 8] = weights[rows, 96:104].astype(BF16)
        turned = weights[back, :].T
        b2_ref[:, rows] = turned[0:48].astype(BF16)
        b3_ref[:, rows] = turned[48:96].astype(BF16)
    spread, keep = selectors()
    place = (
        lax.broadcasted_iota(jnp.int32, (LANES, H), 0) == 104 + lax.broadcasted_iota(jnp.int32, (LANES, H), 1) % 4
    ).astype(F32).astype(BF16)
    wide = jnp.dot(weights[...].astype(BF16), place, preferred_element_type=F32)
    wide = jnp.where(keep, wide, 0.0).astype(BF16)
    last = lax.dot_general(spread, wide, (((0,), (0,)), ((), ())), preferred_element_type=F32)
    p4_ref[...] = last.astype(BF16)
    for k in range(TAPS):
        b4_ref[:, 8 * k:8 * k + 8] = last[8 * SWAP[k]:8 * SWAP[k] + 8, :].T.astype(BF16)


def panel_kernel_plain(gathered_ref, *rest):
    panel_kernel(gathered_ref, None, *rest)


def chunks_of(value):
    return [value[:, q * 128:q * 128 + 128] for q in range(4)]


def one_shift(chunks, position):
    if position == 0:
        return chunks
    lanes = lane_iota(chunks[0].shape[0])
    sign = 1 if position % 2 == 1 else -1
    if position > 4:
        return [shift_z(chunk, sign, lanes) for chunk in chunks]
    if position > 2:
        return [shift_y(chunk, sign, lanes) for chunk in chunks]
    low = lanes < 64
    rolled = [roll_lanes(chunk, 64) for chunk in chunks]
    if sign > 0:
        return [jnp.where(low, rolled[q], rolled[(q + 1) % 4]) for q in range(4)]
    return [jnp.where(low, rolled[(q + 3) % 4], rolled[q]) for q in range(4)]


def all_shifts(chunks):
    lanes = lane_iota(chunks[0].shape[0])
    y = lanes // 8 % 8
    z = lanes % 8
    low = lanes < 64
    half = [roll_lanes(chunk, 64) for chunk in chunks]
    return [
        chunks,
        [jnp.where(low, half[q], half[(q + 1) % 4]) for q in range(4)],
        [jnp.where(low, half[(q + 3) % 4], half[q]) for q in range(4)],
        [roll_lanes(jnp.where(y == 0, half[q], chunks[q]), -8) for q in range(4)],
        [roll_lanes(jnp.where(y == 7, half[q], chunks[q]), 8) for q in range(4)],
        [roll_lanes(jnp.where(z == 0, roll_lanes(chunk, 8), chunk), -1) for chunk in chunks],
        [roll_lanes(jnp.where(z == 7, roll_lanes(chunk, -8), chunk), 1) for chunk in chunks],
    ]


def span(slice_index, count=1):
    if isinstance(slice_index, int):
        return slice(slice_index * SITES, (slice_index + count) * SITES)
    return pl.ds(pl.multiple_of(slice_index * SITES, SITES), count * SITES)


def slot_of(slot):
    return slice(slot * SITES, (slot + 1) * SITES)


def stack_wide(source, target, index, slot):
    chunks = chunks_of(source[:, span(index)])
    for position, shifted in enumerate(all_shifts(chunks)):
        for q in range(4):
            lanes = slice(slot * SITES + q * 128, slot * SITES + q * 128 + 128)
            target[H * position:H * position + H, lanes] = shifted[q]
    target[7 * H:8 * H, slot_of(slot)] = source[:, span(index + 1)]
    target[8 * H:9 * H, slot_of(slot)] = source[:, span(index - 1)]


def stack_thin(source, target, index, slot):
    chunks = chunks_of(source[:, span(index)])
    ahead = chunks_of(source[:, span(index + 1)])
    behind = chunks_of(source[:, span(index - 1)])
    columns = all_shifts(chunks) + [ahead, behind]
    for q in range(4):
        lanes = slice(slot * SITES + q * 128, slot * SITES + q * 128 + 128)
        target[0:72, lanes] = jnp.concatenate([column[q] for column in columns], axis=0).astype(BF16)


def one_minus_square(value):
    value = value.astype(F32)
    return 1.0 - value * value


def conv_kernel(
    split, fm_ref, below_ref, above_ref, fbelow_ref, fabove_ref, loops_ref,
    p1_ref, p2_ref, p3_ref, p4_ref, b2_ref, b3_ref, b4_ref,
    coeff_ref, grads_ref,
    feats, mixed, h1, h2, h3, parts, lasts, g3, g2, g1, wide, thin, packed,
):
    row8 = lax.broadcasted_iota(jnp.int32, (8, SITES), 0)
    loop_re = jnp.concatenate([loops_ref[0, q:q + 1, :] for q in range(4)], axis=1)
    loop_im = jnp.concatenate([loops_ref[1, q:q + 1, :] for q in range(4)], axis=1)
    loops = jnp.where(row8 == 6, loop_re, jnp.where(row8 == 7, loop_im, 0.0))
    loops = loops.astype(BF16).astype(F32)
    for j in range(3):
        feats[:, span(j)] = fbelow_ref[j].astype(F32) + loops
        feats[:, span(15 + j)] = fabove_ref[j].astype(F32) + loops
    for base, ref in ((3, below_ref), (7, fm_ref), (11, above_ref)):
        for j in range(4):
            value = ref[j].astype(F32)
            feats[:, span(base + j)] = value[0:8] + loops
            mixed[:, span(base + j)] = value[8:16]

    def wide_dot(source, weights, index, slot):
        stack_wide(source, wide, index, slot)
        return jnp.dot(weights[...], wide[:, slot_of(slot)], preferred_element_type=F32)

    def thin_dot(source, weights, index, slot):
        stack_thin(source, thin, index, slot)
        return jnp.dot(weights[...], thin[:, slot_of(slot)], preferred_element_type=F32)

    def layer_one(half, carry):
        for s in range(8):
            index = 1 + 8 * half + s
            h1[:, span(index)] = jnp.tanh(thin_dot(feats, p1_ref, index, s % 4)).astype(BF16)
        return carry

    lax.fori_loop(0, 2, layer_one, 0)

    def layer_two(half, carry):
        for s in range(7):
            index = 2 + 7 * half + s
            h2[:, span(index)] = jnp.tanh(wide_dot(h1, p2_ref, index, s % 4)).astype(BF16)
        return carry

    lax.fori_loop(0, 2, layer_two, 0)

    def layer_three(half, carry):
        for s in range(6):
            index = 3 + 6 * half + s
            out = jnp.tanh(wide_dot(h2, p3_ref, index, s % 4)).astype(BF16)
            h3[:, span(index)] = out
            taps = jnp.dot(p4_ref[...], out, preferred_element_type=F32)
            acc = None
            for position in range(7):
                shifted = one_shift(chunks_of(taps[8 * position:8 * position + 8]), position)
                acc = shifted if acc is None else [a + b for a, b in zip(acc, shifted)]
            parts[0, :, span(index)] = jnp.concatenate(acc, axis=1)
            parts[1, :, span(index)] = taps[56:64]
            parts[2, :, span(index)] = taps[64:72]
        return carry

    lax.fori_loop(0, 2, layer_three, 0)

    for index in range(4, 14):
        coeff = jnp.tanh(parts[0, :, span(index)] + parts[1, :, span(index + 1)] + parts[2, :, span(index - 1)])
        blend = mixed[:, span(index)]
        value = (blend + coeff * pltpu.roll(blend, 4, 0)) * (1.0 - coeff * coeff)
        lasts[:, span(index)] = jnp.where(row8 < 4, value, 0.0).astype(BF16).astype(F32)
        if 7 <= index < 11:
            coeff_ref[index - 7] = coeff

    own = span(7, 4)
    contract = (((1,), (1,)), ((), ()))
    for index in (5, 6, 11, 12, 7, 8, 9, 10):
        out = thin_dot(lasts, b4_ref, index, (index + 1) % 4)
        g3[:, span(index)] = (out * one_minus_square(h3[:, span(index)])).astype(BF16)
    grad_last = lax.dot_general(thin[...], h3[:, own], contract, preferred_element_type=F32)
    for index in (6, 11, 7, 8, 9, 10):
        out = wide_dot(g3, b3_ref, index, (index + 1) % 4)
        g2[:, span(index)] = (out * one_minus_square(h2[:, span(index)])).astype(BF16)
    grad_third = lax.dot_general(wide[...], h2[:, own], contract, preferred_element_type=F32)
    for index in (7, 8, 9, 10):
        out = wide_dot(g2, b2_ref, index, (index + 1) % 4)
        g1[:, slot_of(index - 7)] = (out * one_minus_square(h1[:, span(index)])).astype(BF16)
    grad_second = lax.dot_general(wide[...], h1[:, own], contract, preferred_element_type=F32)
    for index in (7, 8, 9, 10):
        stack_thin(feats, thin, index, index - 7)
    grad_first = lax.dot_general(g1[...], thin[...], contract, preferred_element_type=F32)

    spread, keep = selectors()
    ordered = jnp.concatenate([grad_last[8 * SWAP[k]:8 * SWAP[k] + 8] for k in range(TAPS)], axis=0)
    broad = jnp.dot(spread, ordered.astype(BF16), preferred_element_type=F32)
    broad = jnp.where(keep, broad, 0.0).astype(BF16)
    place = (
        lax.broadcasted_iota(jnp.int32, (H, LANES), 1) == 104 + lax.broadcasted_iota(jnp.int32, (H, LANES), 0) % 4
    ).astype(F32).astype(BF16)
    packed[...] = jnp.dot(broad, place, preferred_element_type=F32)
    for k in range(TAPS):
        rows = slice(H * k, H * k + H)
        back = slice(H * SWAP[k], H * SWAP[k] + H)
        packed[rows, 0:48] = grad_second[back]
        packed[rows, 48:96] = grad_third[back]
        packed[rows, 96:104] = grad_first[:, 8 * k:8 * k + 8]
    if split:
        for d in range(16):
            grads_ref[d] = packed[27 * d:27 * d + 27, :].astype(BF16)
    else:
        grads_ref[...] = packed[...].astype(BF16)


def update_kernel(dense, moves_ref, coeff_ref, out_ref, factors):
    for mu in range(4):
        for t in range(4):
            for c in range(2):
                factors[mu, c, t:t + 1, :] = coeff_ref[t, mu:mu + 1, c * 128:c * 128 + 128]
                factors[mu, c, 4 + t:5 + t, :] = coeff_ref[t, mu:mu + 1, 256 + c * 128:384 + c * 128]

    def body(mu, carry):
        factor = [factors[mu, c] for c in range(2)]
        half = [0.5 * value * value for value in factor]
        for e, (part, i, j) in enumerate(ENTRIES):
            new = [
                dense[mu, e, c]
                + factor[c] * moves_ref[0, mu, e, c].astype(F32)
                + half[c] * moves_ref[1, mu, e, c].astype(F32)
                for c in range(2)
            ]
            out_ref[mu, part, i, j, 0] = jnp.concatenate(
                [new[0][0:4], new[1][0:4], new[0][4:8], new[1][4:8]], axis=1
            )
        return carry

    lax.fori_loop(0, 4, body, 0)


def sum_kernel(widths, parts_ref, first_ref, second_ref, third_ref, last_ref):
    value = parts_ref[0].astype(F32)
    for d in range(1, parts_ref.shape[0]):
        value = value + parts_ref[d].astype(F32)
    offset = 0
    for ref, width in zip((second_ref, third_ref, first_ref, last_ref), widths):
        for r in range(27):
            ref[:, width * r:width * r + width] = value[r:r + 1, offset:offset + width]
        offset += width


def call(body, outs, scratch, places=None, cost=None, limit=LIMIT):
    specs = {}
    if places is not None:
        specs["in_specs"] = [pl.BlockSpec(memory_space=place) for place in places]
    return pl.pallas_call(
        body,
        out_shape=[jax.ShapeDtypeStruct(shape, dtype) for shape, dtype in outs],
        scratch_shapes=[pltpu.VMEM(*item) if isinstance(item, tuple) else item for item in scratch],
        compiler_params=pltpu.CompilerParams(vmem_limit_bytes=limit),
        cost_estimate=cost,
        **specs,
    )


def on_device(links, cotangent, parity, link_subset, w_first, w_second, w_third, w_last):
    count = lax.axis_size("tm")

    def send(value, distance):
        return lax.ppermute(value, "tm", [(i, (i + distance) % count) for i in range(count)])

    widths = (768 // count, 768 // count, 128 // count, 64 // count)
    vmem, smem = pltpu.VMEM, pltpu.SMEM
    field = ((4, 18, 2, 8, LANES), F32)
    space = ((3, 18, 2, 8, LANES), F32)
    edge_rows = ((70, SITES), BF16)
    up, down, dense, edges, staples, slab = call(
        face_kernel,
        [edge_rows, edge_rows, field, space, space, ((12, 4, LANES), F32)],
        [space, ((70, 4, LANES), F32)],
    )(links)
    up = send(up, 1)
    down = send(down, -1)
    (state,) = call(
        space_kernel,
        [((186, 8, LANES), F32)],
        [((3, 3, 18, 2, 8, LANES), F32), ((3, 3, 18, 2, 8, LANES), F32)],
        cost=pl.CostEstimate(flops=4_000_000_000, bytes_accessed=16_000_000, transcendentals=0),
    )(dense, staples)
    core = (lax.axis_index("tm") % 2).astype(jnp.int32)[None]
    (block,) = call(
        functools.partial(block_kernel, widths),
        [((count, BLOCKROWS, LANES), BF16)],
        [((12, 4, LANES), F32), ((BLOCKROWS, LANES), F32)],
        places=(smem,) + (vmem,) * 7 + (pl.ANY,),
    )(core, up, down, slab, w_first, w_second, w_third, w_last, state)
    gathered = lax.all_to_all(block, "tm", split_axis=0, concat_axis=0, tiled=True)
    fm, fup, fdown, moves = call(
        time_kernel,
        [
            ((4, 16, SITES), BF16), ((3, 8, SITES), BF16), ((3, 8, SITES), BF16),
            ((2, 4, 18, 2, 8, LANES), BF16),
        ],
        [
            field, ((4, 8, LANES), F32), space, space, field, ((70, 4, LANES), F32), ((70, 4, LANES), F32),
            ((4, 9, 2, 8, LANES), F32), ((4, 4, 16, LANES), F32),
        ],
        places=(smem,) + (vmem,) * 6,
    )(parity + 2 * link_subset, dense, edges, state, cotangent, up, down)
    below = send(fm, 1)
    above = send(fm, -1)
    fbelow = send(fup, 2)
    fabove = send(fdown, -2)

    panel_outs = [
        ((2, 4, LANES), F32), ((H, 72), BF16), ((H, 432), BF16), ((H, 432), BF16), ((72, H), BF16),
        ((H, 432), BF16), ((H, 432), BF16), ((H, 72), BF16),
    ]
    panel_scratch = [((432, LANES), F32)]
    if count == 16:
        loops, p1, p2, p3, p4, b2, b3, b4 = call(panel_kernel_plain, panel_outs, panel_scratch)(gathered)
    else:
        pieces = []
        offset = 0
        for width, full in zip(widths, (48, 48, 8, 4)):
            piece = gathered[:, SLABROWS:SLABROWS + 27, offset:offset + width]
            pieces.append(piece.reshape(432, full))
            offset += width
        pieces.append(jnp.zeros((432, 20), BF16))
        loops, p1, p2, p3, p4, b2, b3, b4 = call(panel_kernel, panel_outs, panel_scratch)(
            gathered, jnp.concatenate(pieces, axis=1)
        )

    window = 18 * SITES
    coeff, grads = call(
        functools.partial(conv_kernel, count == 16),
        [((4, 8, SITES), F32), ((16, 27, LANES) if count == 16 else (432, LANES), BF16)],
        [
            ((8, window), F32), ((8, window), F32), ((H, window), BF16), ((H, window), BF16), ((H, window), BF16),
            ((3, 8, window), F32), ((8, window), F32), ((H, window), BF16), ((H, window), BF16), ((H, 4 * SITES), BF16),
            ((432, 4 * SITES), BF16), ((72, 4 * SITES), BF16), ((432, LANES), F32),
        ],
        limit=20 * 1024 * 1024,
    )(fm, below, above, fbelow, fabove, loops, p1, p2, p3, p4, b2, b3, b4)
    if count != 16:
        offset = 0
        pieces = []
        for width, full in zip(widths, (48, 48, 8, 4)):
            pieces.append(grads[:, offset:offset + full].reshape(count, 27, width))
            offset += full
        grads = jnp.concatenate(pieces, axis=2)
    grads = lax.all_to_all(grads, "tm", split_axis=0, concat_axis=0, tiled=True)
    (new_links,) = call(
        update_kernel, [(links.shape, F32)], [((4, 2, 8, LANES), F32)]
    )(dense, moves, coeff)
    grad_first, grad_second, grad_third, grad_last = call(
        functools.partial(sum_kernel, widths),
        [((1, 27 * width), F32) for width in (widths[2], widths[0], widths[1], widths[3])],
        [],
    )(grads)
    return (new_links, grad_first, grad_second, grad_third, grad_last)


def solution(mesh):
    placed = (
        P(None, None, None, None, "groups", "tm", None),
        P(None, None, None, None, "groups", "tm", None),
        P("groups", "tm"),
        P("groups", "tm"),
        P("tm"),
        P("tm"),
        P("tm"),
        P("tm"),
    )
    return jax.shard_map(
        on_device,
        mesh=mesh,
        in_specs=placed,
        out_specs=(
            P(None, None, None, None, "groups", "tm", None),
            P("groups", "tm"),
            P("groups", "tm"),
            P("groups", "tm"),
            P("groups", "tm"),
        ),
        check_vma=False,
    )
```

```python
import functools

import jax
import jax.numpy as jnp
from jax import lax
from jax.experimental import pallas as pl
from jax.experimental.pallas import tpu as pltpu
from jax.sharding import PartitionSpec as P

F32 = jnp.float32
BF16 = jnp.bfloat16
TAPS = 9
H = 48
LANES = 128
SITES = 512
PAIRS = ((0, 1), (0, 2), (0, 3), (1, 2), (1, 3), (2, 3))
SWAP = (0, 2, 1, 4, 3, 6, 5, 8, 7)
ENTRIES = tuple((c, i, j) for c in range(2) for i in range(3) for j in range(3))
PLANE = 180
SLABROWS = 24
BLOCKROWS = 64
LIMIT = 8 * 1024 * 1024


def lane_iota(rows):
    return lax.broadcasted_iota(jnp.int32, (rows, LANES), 1)


def row_iota():
    return lax.broadcasted_iota(jnp.int32, (8, LANES), 0)


def roll_lanes(value, amount):
    return pltpu.roll(value, amount % LANES, 1)


def shift_z(chunk, sign, lanes):
    z = lanes % 8
    if sign > 0:
        return jnp.where(z == 7, roll_lanes(chunk, 7), roll_lanes(chunk, -1))
    return jnp.where(z == 0, roll_lanes(chunk, -7), roll_lanes(chunk, 1))


def shift_y(chunk, sign, lanes):
    y = lanes // 8 % 8
    if sign > 0:
        return jnp.where(y == 7, roll_lanes(chunk, 56), roll_lanes(chunk, -8))
    return jnp.where(y == 0, roll_lanes(chunk, -56), roll_lanes(chunk, 8))


def dense_shift(pair, axis, sign):
    lanes = lane_iota(8)
    if axis == 2:
        return [shift_z(chunk, sign, lanes) for chunk in pair]
    if axis == 1:
        return [shift_y(chunk, sign, lanes) for chunk in pair]
    low = lanes < 64
    first, second = [roll_lanes(chunk, 64) for chunk in pair]
    if sign > 0:
        return [jnp.where(low, first, second), jnp.where(low, second, pltpu.roll(first, 4, 0))]
    return [jnp.where(low, pltpu.roll(second, 4, 0), first), jnp.where(low, first, second)]


def pack_pair(value):
    return [
        jnp.concatenate([value[:, c * 128:c * 128 + 128], value[:, 256 + c * 128:384 + c * 128]], axis=0)
        for c in range(2)
    ]


def halo_pair(ref, index):
    top = row_iota() < 4
    pair = []
    for c in range(2):
        low = jnp.broadcast_to(ref[index, c:c + 1, :], (8, LANES))
        high = jnp.broadcast_to(ref[index, 2 + c:3 + c, :], (8, LANES))
        pair.append(jnp.where(top, low, high))
    return pair


def load_matrix(read):
    real = [[read(3 * i + j) for j in range(3)] for i in range(3)]
    imag = [[read(9 + 3 * i + j) for j in range(3)] for i in range(3)]
    return (real, imag, 1)


def dagger(matrix):
    real, imag, sign = matrix
    return (
        [[real[j][i] for j in range(3)] for i in range(3)],
        [[imag[j][i] for j in range(3)] for i in range(3)],
        -sign,
    )


def total(terms, signs):
    value = None
    for term, sign in zip(terms, signs):
        if value is None:
            value = term if sign > 0 else -term
        else:
            value = value + term if sign > 0 else value - term
    return value


def mat_mul(left, right):
    lr, li, ls = left
    rr, ri, rs = right
    same = ls == rs
    height = len(lr)
    real = [[None] * 3 for _ in range(height)]
    imag = [[None] * 3 for _ in range(height)]
    for i in range(height):
        for j in range(3):
            real[i][j] = total(
                [lr[i][k] * rr[k][j] for k in range(3)] + [li[i][k] * ri[k][j] for k in range(3)],
                [1, 1, 1] + [-1 if same else 1] * 3,
            )
            imag[i][j] = total(
                [lr[i][k] * ri[k][j] for k in range(3)] + [li[i][k] * rr[k][j] for k in range(3)],
                [1, 1, 1] + [1 if same else -1] * 3,
            )
    return (real, imag, ls if same else rs)


def imag_of(matrix, i, j):
    return matrix[1][i][j] if matrix[2] > 0 else -matrix[1][i][j]


def store_matrix(matrix, write):
    for i in range(3):
        for j in range(3):
            write(3 * i + j, matrix[0][i][j])
            write(9 + 3 * i + j, imag_of(matrix, i, j))


def two_rows(read):
    real = [[read(3 * i + j) for j in range(3)] for i in range(2)]
    imag = [[read(6 + 3 * i + j) for j in range(3)] for i in range(2)]
    return (real, imag, 1)


def store_rows(matrix, write):
    for i in range(2):
        for j in range(3):
            write(3 * i + j, matrix[0][i][j])
            write(6 + 3 * i + j, imag_of(matrix, i, j))


def special(matrix):
    real, imag, _ = matrix
    last_r, last_i = [], []
    for k in range(3):
        i, j = (k + 1) % 3, (k + 2) % 3
        last_r.append(
            (real[0][i] * real[1][j] - imag[0][i] * imag[1][j])
            - (real[0][j] * real[1][i] - imag[0][j] * imag[1][i])
        )
        last_i.append(
            (real[0][j] * imag[1][i] + imag[0][j] * real[1][i])
            - (real[0][i] * imag[1][j] + imag[0][i] * real[1][j])
        )
    return (real + [last_r], imag + [last_i], 1)


def anti_parts(matrix):
    parts = [2.0 * imag_of(matrix, i, i) for i in range(3)]
    for i, j in ((0, 1), (0, 2), (1, 2)):
        parts.append(matrix[0][i][j] - matrix[0][j][i])
        parts.append(imag_of(matrix, i, j) + imag_of(matrix, j, i))
    return parts


def anti_matrix(parts):
    zero = jnp.zeros_like(parts[0])
    real = [[zero, parts[3], parts[5]], [-parts[3], zero, parts[7]], [-parts[5], -parts[7], zero]]
    imag = [[parts[0], parts[4], parts[6]], [parts[4], parts[1], parts[8]], [parts[6], parts[8], parts[2]]]
    return real, imag


def anti_mul(parts, right):
    real, imag = anti_matrix(parts)
    rr, ri, _ = right
    out_r = [[None] * 3 for _ in range(3)]
    out_i = [[None] * 3 for _ in range(3)]
    for i in range(3):
        for j in range(3):
            value_r = -(imag[i][i] * ri[i][j])
            value_i = imag[i][i] * rr[i][j]
            for k in range(3):
                if k != i:
                    value_r = value_r + real[i][k] * rr[k][j] - imag[i][k] * ri[k][j]
                    value_i = value_i + real[i][k] * ri[k][j] + imag[i][k] * rr[k][j]
            out_r[i][j] = value_r
            out_i[i][j] = value_i
    return (out_r, out_i, 1)


def pack_links(links_ref, dense):
    def body(mu, carry):
        for e, (c, i, j) in enumerate(ENTRIES):
            low, high = pack_pair(links_ref[mu, c, i, j, 0].astype(F32))
            dense[mu, e, 0] = low
            dense[mu, e, 1] = high
        return carry

    lax.fori_loop(0, 4, body, 0)


def face_kernel(links_ref, up_ref, down_ref, dense, edges, staples, slab, moved, rows):
    pack_links(links_ref, dense)

    def shift_body(e, carry):
        pair = [dense[3, e, 0], dense[3, e, 1]]
        for mu in range(3):
            low, high = dense_shift(pair, mu, 1)
            moved[mu, e, 0] = low
            moved[mu, e, 1] = high
        return carry

    lax.fori_loop(0, 18, shift_body, 0, unroll=3)

    def staple_body(step, carry):
        mu = step // 2
        c = step % 2
        u_mu = load_matrix(lambda e: dense[mu, e, c])
        u_t = load_matrix(lambda e: dense[3, e, c])
        edge = mat_mul(u_mu, load_matrix(lambda e: moved[mu, e, c]))

        def write_edge(e, value):
            edges[mu, e, c] = value

        store_matrix(edge, write_edge)

        def write(e, value):
            staples[mu, e, c] = value
            rows[16 + mu * 18 + e, pl.ds(c, 1)] = value[3:4]
            rows[16 + mu * 18 + e, pl.ds(2 + c, 1)] = value[7:8]

        store_matrix(mat_mul(dagger(edge), u_t), write)
        return carry

    lax.fori_loop(0, 6, staple_body, 0)

    def slab_body(c, carry):
        u_t = load_matrix(lambda e: dense[3, e, c])
        ahead = load_matrix(lambda e: pltpu.roll(dense[3, e, c], 7, 0))
        two = mat_mul(u_t, ahead)
        later = tuple(
            [[pltpu.roll(part[i][j], 6, 0) for j in range(3)] for i in range(3)] for part in two[:2]
        ) + (two[2],)
        four = mat_mul((two[0][:2], two[1][:2], two[2]), later)

        def write(e, value):
            slab[e, pl.ds(c, 1)] = value[0:1]
            slab[e, pl.ds(2 + c, 1)] = value[4:5]
            rows[e, pl.ds(c, 1)] = value[0:1]
            rows[e, pl.ds(2 + c, 1)] = value[4:5]

        store_rows(four, write)
        return carry

    lax.fori_loop(0, 2, slab_body, 0)
    for q in range(4):
        up_ref[:, q * 128:q * 128 + 128] = rows[:, q, :].astype(BF16)

    def down_body(e, carry):
        for mu in range(3):
            for c in range(2):
                value = dense[mu, e, c]
                rows[16 + mu * 18 + e, c:c + 1] = value[0:1]
                rows[16 + mu * 18 + e, 2 + c:3 + c] = value[4:5]
        return carry

    lax.fori_loop(0, 18, down_body, 0, unroll=3)
    for q in range(4):
        down_ref[:, q * 128:q * 128 + 128] = rows[:, q, :].astype(BF16)


def block_kernel(
    widths, core_ref, up_ref, down_ref, slab, w1_ref, w2_ref, w3_ref, w4_ref, after_ref, block_ref, other, block
):
    even = core_ref[0] == 0
    up = up_ref[0:16].astype(F32)
    down = down_ref[0:16].astype(F32)
    for q in range(4):
        lanes = slice(q * 128, q * 128 + 128)
        other[:, q, :] = jnp.where(even, down[0:12, lanes], up[0:12, lanes])
    first = two_rows(lambda e: jnp.where(even, slab[e], other[e]))
    second = special(two_rows(lambda e: jnp.where(even, other[e], slab[e])))

    def write(e, value):
        block[2 * e:2 * e + 2, :] = jnp.where(even, value[0:2], value[2:4])

    store_rows(mat_mul(first, second), write)
    block[SLABROWS:BLOCKROWS] = jnp.zeros((BLOCKROWS - SLABROWS, LANES), F32)
    offset = 0
    for ref, width in zip((w2_ref, w3_ref, w1_ref, w4_ref), widths):
        flat = ref[...].astype(F32)
        for r in range(27):
            block[SLABROWS + r:SLABROWS + r + 1, offset:offset + width] = (
                flat[width * r:width * r + width].reshape(1, width)
            )
        offset += width
    value = block[...].astype(BF16)
    for d in range(block_ref.shape[0]):
        block_ref[d] = value


def put_row(rows, channel, c, value):
    for t in range(4):
        rows[t, c, pl.ds(channel, 1), :] = value[t:t + 1]
        rows[t, 2 + c, pl.ds(channel, 1), :] = value[4 + t:5 + t]


def sum_at(mu, e, c):
    return (mu * 18 + e) * 2 + c


def force_at(mu, e, c):
    return 108 + (mu * 9 + e) * 2 + c


def space_kernel(dense, time_staples, state, moved, staples):
    state[108:180] = jnp.zeros((72, 8, LANES), F32)
    steps = row_iota() % 4

    def shift_body(e, carry):
        for nu in range(3):
            pair = [dense[nu, e, 0], dense[nu, e, 1]]
            for mu in range(3):
                if mu != nu:
                    low, high = dense_shift(pair, mu, 1)
                    moved[mu, nu, e, 0] = low
                    moved[mu, nu, e, 1] = high
        return carry

    lax.fori_loop(0, 18, shift_body, 0, unroll=3)

    def plane_body(step, carry):
        plane = step // 2
        c = step % 2
        mu = jnp.where(plane == 2, 1, 0)
        nu = jnp.where(plane == 0, 1, 2)
        u_mu = load_matrix(lambda e: dense[mu, e, c])
        u_nu = load_matrix(lambda e: dense[nu, e, c])
        one = mat_mul(u_mu, load_matrix(lambda e: moved[mu, nu, e, c]))
        two = mat_mul(u_nu, load_matrix(lambda e: moved[nu, mu, e, c]))
        loop = mat_mul(one, dagger(two))
        state[PLANE + step] = (loop[0][0][0] + loop[0][1][1] + loop[0][2][2]) / 3.0
        for e, part in enumerate(anti_parts(loop)):
            state[force_at(mu, e, c)] += part
            state[force_at(nu, e, c)] -= part

        def write_mu(e, value):
            staples[mu, nu, e, c] = value

        def write_nu(e, value):
            staples[nu, mu, e, c] = value

        store_matrix(mat_mul(dagger(one), u_nu), write_mu)
        store_matrix(mat_mul(dagger(two), u_mu), write_nu)
        return carry

    lax.fori_loop(0, 6, plane_body, 0)

    def lower_body(e, carry):
        for mu in range(3):
            acc = [jnp.where(steps == 0, 0.0, pltpu.roll(time_staples[mu, e, c], 1, 0)) for c in range(2)]
            for nu in range(3):
                if nu != mu:
                    pair = dense_shift([staples[mu, nu, e, 0], staples[mu, nu, e, 1]], nu, -1)
                    acc = [acc[c] + pair[c] for c in range(2)]
            state[sum_at(mu, e, 0)] = acc[0]
            state[sum_at(mu, e, 1)] = acc[1]
        return carry

    lax.fori_loop(0, 18, lower_body, 0, unroll=3)


def time_kernel(
    code_ref, dense, edges, state, cot_ref, up_ref, down_ref,
    fm_ref, fup_ref, fdown_ref, moves_ref,
    cots, gates, moved, staples, sums, halo_up, halo_down, forces, rows,
):
    for q in range(4):
        halo_up[:, q, :] = up_ref[:, q * 128:q * 128 + 128].astype(F32)
        halo_down[:, q, :] = down_ref[:, q * 128:q * 128 + 128].astype(F32)
    rows[...] = jnp.zeros_like(rows)
    pack_links(cot_ref, cots)
    lanes = lane_iota(8)
    site_steps = row_iota() % 4
    colour = (lanes // 64 + lanes // 8 % 8 + lanes % 8 + site_steps) % 2
    code = jnp.zeros_like(site_steps)
    for t in range(4):
        code = jnp.where(site_steps == t, code_ref[0, t], code)
    for mu in range(4):
        active = jnp.logical_and(colour == code % 2, jnp.right_shift(code, mu + 1) % 2 == 1)
        gates[mu] = jnp.where(active, 1.0, 0.0)
    for channel, plane in ((0, 0), (1, 1), (3, 2)):
        for c in range(2):
            put_row(rows, channel, c, state[PLANE + 2 * plane + c])
    for mu in range(4):
        for e in range(9):
            for c in range(2):
                forces[mu, e, c] = state[force_at(mu, e, c)]
    steps = row_iota() % 4

    def shift_body(e, carry):
        for nu in range(3):
            halo = halo_pair(halo_down, 16 + nu * 18 + e)
            below = halo_pair(halo_up, 16 + nu * 18 + e)
            for c in range(2):
                moved[nu, e, c] = jnp.where(steps == 3, halo[c], pltpu.roll(dense[nu, e, c], 7, 0))
                sums[nu, e, c] = state[sum_at(nu, e, c)] + jnp.where(steps == 0, below[c], 0.0)
        return carry

    lax.fori_loop(0, 18, shift_body, 0, unroll=3)

    def plane_body(step, carry):
        mu = step // 2
        c = step % 2
        one = load_matrix(lambda e: edges[mu, e, c])
        two = mat_mul(load_matrix(lambda e: dense[3, e, c]), load_matrix(lambda e: moved[mu, e, c]))
        loop = mat_mul(one, dagger(two))
        put_row(rows, jnp.where(mu == 0, 2, mu + 3), c, (loop[0][0][0] + loop[0][1][1] + loop[0][2][2]) / 3.0)
        for e, part in enumerate(anti_parts(loop)):
            forces[mu, e, c] += part
            forces[3, e, c] -= part

        def write(e, value):
            staples[mu, e, c] = value

        store_matrix(mat_mul(dagger(two), load_matrix(lambda e: dense[mu, e, c])), write)
        return carry

    lax.fori_loop(0, 6, plane_body, 0)

    def lower_body(e, carry):
        acc = None
        for mu in range(3):
            pair = dense_shift([staples[mu, e, 0], staples[mu, e, 1]], mu, -1)
            acc = pair if acc is None else [acc[c] + pair[c] for c in range(2)]
        sums[3, e, 0] = acc[0]
        sums[3, e, 1] = acc[1]
        return carry

    lax.fori_loop(0, 18, lower_body, 0, unroll=3)

    def force_body(step, carry):
        mu = step // 2
        c = step % 2
        current = load_matrix(lambda e: dense[mu, e, c])
        omega = mat_mul(current, load_matrix(lambda e: sums[mu, e, c]))
        parts = [part + forces[mu, e, c] for e, part in enumerate(anti_parts(omega))]
        mean = (parts[0] + parts[1] + parts[2]) * (1.0 / 3.0)
        parts = [parts[e] - mean if e < 3 else parts[e] for e in range(9)]
        parts = [part * (1.0 / 12.0) for part in parts]
        applied = anti_mul(parts, current)
        twice = anti_mul(parts, applied)
        gate = gates[mu]
        slope = jnp.zeros_like(gate)
        curve = jnp.zeros_like(gate)
        for e, (part, i, j) in enumerate(ENTRIES):
            weight = cots[mu, e, c]
            slope = slope + weight * applied[part][i][j]
            curve = curve + weight * twice[part][i][j]
            moves_ref[0, mu, e, c] = (gate * applied[part][i][j]).astype(BF16)
            moves_ref[1, mu, e, c] = (gate * twice[part][i][j]).astype(BF16)
        put_row(rows, 8 + mu, c, gate * slope)
        put_row(rows, 12 + mu, c, gate * curve)
        return carry

    lax.fori_loop(0, 8, force_body, 0)
    for t in range(4):
        for q in range(4):
            value = rows[t, q]
            fm_ref[t, :, q * 128:q * 128 + 128] = value.astype(BF16)
            if t > 0:
                fup_ref[t - 1, :, q * 128:q * 128 + 128] = value[0:8].astype(BF16)
            if t < 3:
                fdown_ref[t, :, q * 128:q * 128 + 128] = value[0:8].astype(BF16)


def selectors():
    row = lax.broadcasted_iota(jnp.int32, (432, 72), 0)
    col = lax.broadcasted_iota(jnp.int32, (432, 72), 1)
    group = row // 12
    spread = (group // 4 * 8 + group % 4 == col).astype(F32).astype(BF16)
    keep = (
        lax.broadcasted_iota(jnp.int32, (432, H), 1) // 4 == lax.broadcasted_iota(jnp.int32, (432, H), 0) % 12
    )
    return spread, keep


def panel_kernel(gathered_ref, weights_ref, loops_ref, p1_ref, p2_ref, p3_ref, p4_ref, b2_ref, b3_ref, b4_ref, weights):
    count = gathered_ref.shape[0]

    def read(chip):
        low = gathered_ref[2 * chip].astype(F32)
        high = gathered_ref[2 * chip + 1].astype(F32)
        return special(
            two_rows(lambda e: jnp.concatenate([low[2 * e:2 * e + 2], high[2 * e:2 * e + 2]], axis=0))
        )

    def flat(matrix):
        return tuple(matrix[0][i][j] for i in range(3) for j in range(3)) + tuple(
            imag_of(matrix, i, j) for i in range(3) for j in range(3)
        )

    def chain(chip, state):
        return flat(mat_mul(load_matrix(lambda e: state[e]), read(chip)))

    state = lax.fori_loop(1, count // 2, chain, flat(read(0)))
    loops_ref[0] = (state[0] + state[4] + state[8]) / 3.0
    loops_ref[1] = (state[9] + state[13] + state[17]) / 3.0

    if weights_ref is None:
        for d in range(count):
            block = gathered_ref[d].astype(F32)
            weights[27 * d:27 * d + 27, :] = block[SLABROWS:SLABROWS + 27]
    else:
        weights[...] = weights_ref[...].astype(F32)
    for k in range(TAPS):
        rows = slice(H * k, H * k + H)
        back = slice(H * SWAP[k], H * SWAP[k] + H)
        p2_ref[:, rows] = weights[rows, 0:48].astype(BF16)
        p3_ref[:, rows] = weights[rows, 48:96].astype(BF16)
        p1_ref[:, 8 * k:8 * k + 8] = weights[rows, 96:104].astype(BF16)
        turned = weights[back, :].T
        b2_ref[:, rows] = turned[0:48].astype(BF16)
        b3_ref[:, rows] = turned[48:96].astype(BF16)
    spread, keep = selectors()
    place = (
        lax.broadcasted_iota(jnp.int32, (LANES, H), 0) == 104 + lax.broadcasted_iota(jnp.int32, (LANES, H), 1) % 4
    ).astype(F32).astype(BF16)
    wide = jnp.dot(weights[...].astype(BF16), place, preferred_element_type=F32)
    wide = jnp.where(keep, wide, 0.0).astype(BF16)
    last = lax.dot_general(spread, wide, (((0,), (0,)), ((), ())), preferred_element_type=F32)
    p4_ref[...] = last.astype(BF16)
    for k in range(TAPS):
        b4_ref[:, 8 * k:8 * k + 8] = last[8 * SWAP[k]:8 * SWAP[k] + 8, :].T.astype(BF16)


def panel_kernel_plain(gathered_ref, *rest):
    panel_kernel(gathered_ref, None, *rest)


def chunks_of(value):
    return [value[:, q * 128:q * 128 + 128] for q in range(4)]


def one_shift(chunks, position):
    if position == 0:
        return chunks
    lanes = lane_iota(chunks[0].shape[0])
    sign = 1 if position % 2 == 1 else -1
    if position > 4:
        return [shift_z(chunk, sign, lanes) for chunk in chunks]
    if position > 2:
        return [shift_y(chunk, sign, lanes) for chunk in chunks]
    low = lanes < 64
    rolled = [roll_lanes(chunk, 64) for chunk in chunks]
    if sign > 0:
        return [jnp.where(low, rolled[q], rolled[(q + 1) % 4]) for q in range(4)]
    return [jnp.where(low, rolled[(q + 3) % 4], rolled[q]) for q in range(4)]


def all_shifts(chunks):
    lanes = lane_iota(chunks[0].shape[0])
    y = lanes // 8 % 8
    z = lanes % 8
    low = lanes < 64
    half = [roll_lanes(chunk, 64) for chunk in chunks]
    return [
        chunks,
        [jnp.where(low, half[q], half[(q + 1) % 4]) for q in range(4)],
        [jnp.where(low, half[(q + 3) % 4], half[q]) for q in range(4)],
        [roll_lanes(jnp.where(y == 0, half[q], chunks[q]), -8) for q in range(4)],
        [roll_lanes(jnp.where(y == 7, half[q], chunks[q]), 8) for q in range(4)],
        [roll_lanes(jnp.where(z == 0, roll_lanes(chunk, 8), chunk), -1) for chunk in chunks],
        [roll_lanes(jnp.where(z == 7, roll_lanes(chunk, -8), chunk), 1) for chunk in chunks],
    ]


def span(slice_index, count=1):
    if isinstance(slice_index, int):
        return slice(slice_index * SITES, (slice_index + count) * SITES)
    return pl.ds(pl.multiple_of(slice_index * SITES, SITES), count * SITES)


def slot_of(slot):
    return slice(slot * SITES, (slot + 1) * SITES)


def stack_wide(source, target, index, slot):
    chunks = chunks_of(source[:, span(index)])
    for position, shifted in enumerate(all_shifts(chunks)):
        for q in range(4):
            lanes = slice(slot * SITES + q * 128, slot * SITES + q * 128 + 128)
            target[H * position:H * position + H, lanes] = shifted[q]
    target[7 * H:8 * H, slot_of(slot)] = source[:, span(index + 1)]
    target[8 * H:9 * H, slot_of(slot)] = source[:, span(index - 1)]


def stack_thin(source, target, index, slot):
    chunks = chunks_of(source[:, span(index)])
    ahead = chunks_of(source[:, span(index + 1)])
    behind = chunks_of(source[:, span(index - 1)])
    columns = all_shifts(chunks) + [ahead, behind]
    for q in range(4):
        lanes = slice(slot * SITES + q * 128, slot * SITES + q * 128 + 128)
        target[0:72, lanes] = jnp.concatenate([column[q] for column in columns], axis=0).astype(BF16)


def one_minus_square(value):
    value = value.astype(F32)
    return 1.0 - value * value


def conv_kernel(
    split, fm_ref, below_ref, above_ref, fbelow_ref, fabove_ref, loops_ref,
    p1_ref, p2_ref, p3_ref, p4_ref, b2_ref, b3_ref, b4_ref,
    coeff_ref, grads_ref,
    feats, mixed, h1, h2, h3, parts, lasts, g3, g2, g1, wide, wide_back, wide_first, thin, thin_back, packed,
):
    row8 = lax.broadcasted_iota(jnp.int32, (8, SITES), 0)
    loop_re = jnp.concatenate([loops_ref[0, q:q + 1, :] for q in range(4)], axis=1)
    loop_im = jnp.concatenate([loops_ref[1, q:q + 1, :] for q in range(4)], axis=1)
    loops = jnp.where(row8 == 6, loop_re, jnp.where(row8 == 7, loop_im, 0.0))
    loops = loops.astype(BF16).astype(F32)
    for j in range(3):
        feats[:, span(j)] = fbelow_ref[j].astype(F32) + loops
        feats[:, span(15 + j)] = fabove_ref[j].astype(F32) + loops
    for base, ref in ((3, below_ref), (7, fm_ref), (11, above_ref)):
        for j in range(4):
            value = ref[j].astype(F32)
            feats[:, span(base + j)] = value[0:8] + loops
            mixed[:, span(base + j)] = value[8:16]

    own = span(7, 4)
    contract = (((1,), (1,)), ((), ()))

    def own_slot(index, others):
        return index - 7 if 7 <= index < 11 else 4 + others.index(index)

    def dot(weights, stack, slot):
        return jnp.dot(weights[...], stack[:, slot_of(slot)], preferred_element_type=F32)

    def first_dot(index):
        h1[:, span(index)] = jnp.tanh(dot(p1_ref, thin, index % 4)).astype(BF16)

    def second_dot(index):
        h2[:, span(index)] = jnp.tanh(dot(p2_ref, wide, index % 2)).astype(BF16)

    def third_dot(index):
        h3[:, span(index)] = jnp.tanh(dot(p3_ref, wide, 2 + index % 2)).astype(BF16)

    def taps_of(index):
        taps = jnp.dot(p4_ref[...], h3[:, span(index)], preferred_element_type=F32)
        acc = None
        for position in range(7):
            shifted = one_shift(chunks_of(taps[8 * position:8 * position + 8]), position)
            acc = shifted if acc is None else [a + b for a, b in zip(acc, shifted)]
        parts[0, :, span(index)] = jnp.concatenate(acc, axis=1)
        parts[1, :, span(index)] = taps[56:64]
        parts[2, :, span(index)] = taps[64:72]

    def last_of(index):
        coeff = jnp.tanh(parts[0, :, span(index)] + parts[1, :, span(index + 1)] + parts[2, :, span(index - 1)])
        blend = mixed[:, span(index)]
        value = (blend + coeff * pltpu.roll(blend, 4, 0)) * (1.0 - coeff * coeff)
        lasts[:, span(index)] = jnp.where(row8 < 4, value, 0.0).astype(BF16).astype(F32)
        if 7 <= index < 11:
            coeff_ref[index - 7] = coeff

    halo3, halo2 = (5, 6, 11, 12), (6, 11)

    def back_third(index):
        out = dot(b4_ref, thin_back, own_slot(index, halo3))
        g3[:, span(index)] = (out * one_minus_square(h3[:, span(index)])).astype(BF16)

    def back_second(index):
        out = dot(b3_ref, wide_back, own_slot(index, halo2))
        g2[:, span(index)] = (out * one_minus_square(h2[:, span(index)])).astype(BF16)

    def back_first(index):
        out = dot(b2_ref, wide_first, index - 7)
        g1[:, slot_of(index - 7)] = (out * one_minus_square(h1[:, span(index)])).astype(BF16)

    stages = (
        (0, 1, 17, lambda i: stack_thin(feats, thin, i, i % 4)),
        (1, 1, 17, first_dot),
        (3, 2, 16, lambda i: stack_wide(h1, wide, i, i % 2)),
        (4, 2, 16, second_dot),
        (6, 3, 15, lambda i: stack_wide(h2, wide, i, 2 + i % 2)),
        (7, 3, 15, third_dot),
        (8, 3, 15, taps_of),
        (10, 4, 14, last_of),
        (12, 5, 13, lambda i: stack_thin(lasts, thin_back, i, own_slot(i, halo3))),
        (13, 5, 13, back_third),
        (15, 6, 12, lambda i: stack_wide(g3, wide_back, i, own_slot(i, halo2))),
        (16, 6, 12, back_second),
        (18, 7, 11, lambda i: stack_wide(g2, wide_first, i, i - 7)),
        (19, 7, 11, back_first),
    )
    for step in range(1, 30):
        for delay, low, high, task in reversed(stages):
            if low <= step - delay < high:
                task(step - delay)
        if step == 18:
            for index in (7, 8, 9, 10):
                stack_thin(feats, thin, index, index - 7)
        if step == 23:
            grad_last = lax.dot_general(
                thin_back[:, 0:4 * SITES], h3[:, own], contract, preferred_element_type=F32
            )
        if step == 26:
            grad_third = lax.dot_general(
                wide_back[:, 0:4 * SITES], h2[:, own], contract, preferred_element_type=F32
            )
    grad_second = lax.dot_general(wide_first[...], h1[:, own], contract, preferred_element_type=F32)
    grad_first = lax.dot_general(g1[...], thin[...], contract, preferred_element_type=F32)

    spread, keep = selectors()
    ordered = jnp.concatenate([grad_last[8 * SWAP[k]:8 * SWAP[k] + 8] for k in range(TAPS)], axis=0)
    broad = jnp.dot(spread, ordered.astype(BF16), preferred_element_type=F32)
    broad = jnp.where(keep, broad, 0.0).astype(BF16)
    place = (
        lax.broadcasted_iota(jnp.int32, (H, LANES), 1) == 104 + lax.broadcasted_iota(jnp.int32, (H, LANES), 0) % 4
    ).astype(F32).astype(BF16)
    packed[...] = jnp.dot(broad, place, preferred_element_type=F32)
    for k in range(TAPS):
        rows = slice(H * k, H * k + H)
        back = slice(H * SWAP[k], H * SWAP[k] + H)
        packed[rows, 0:48] = grad_second[back]
        packed[rows, 48:96] = grad_third[back]
        packed[rows, 96:104] = grad_first[:, 8 * k:8 * k + 8]
    if split:
        for d in range(16):
            grads_ref[d] = packed[27 * d:27 * d + 27, :].astype(BF16)
    else:
        grads_ref[...] = packed[...].astype(BF16)


def update_kernel(dense, moves_ref, coeff_ref, out_ref, factors):
    for mu in range(4):
        for t in range(4):
            for c in range(2):
                factors[mu, c, t:t + 1, :] = coeff_ref[t, mu:mu + 1, c * 128:c * 128 + 128]
                factors[mu, c, 4 + t:5 + t, :] = coeff_ref[t, mu:mu + 1, 256 + c * 128:384 + c * 128]

    def body(mu, carry):
        factor = [factors[mu, c] for c in range(2)]
        half = [0.5 * value * value for value in factor]
        for e, (part, i, j) in enumerate(ENTRIES):
            new = [
                dense[mu, e, c]
                + factor[c] * moves_ref[0, mu, e, c].astype(F32)
                + half[c] * moves_ref[1, mu, e, c].astype(F32)
                for c in range(2)
            ]
            out_ref[mu, part, i, j, 0] = jnp.concatenate(
                [new[0][0:4], new[1][0:4], new[0][4:8], new[1][4:8]], axis=1
            )
        return carry

    lax.fori_loop(0, 4, body, 0)


def sum_kernel(widths, parts_ref, first_ref, second_ref, third_ref, last_ref):
    value = parts_ref[0].astype(F32)
    for d in range(1, parts_ref.shape[0]):
        value = value + parts_ref[d].astype(F32)
    offset = 0
    for ref, width in zip((second_ref, third_ref, first_ref, last_ref), widths):
        for r in range(27):
            ref[:, width * r:width * r + width] = value[r:r + 1, offset:offset + width]
        offset += width


def call(body, outs, scratch, places=None, cost=None, limit=LIMIT):
    specs = {}
    if places is not None:
        specs["in_specs"] = [pl.BlockSpec(memory_space=place) for place in places]
    return pl.pallas_call(
        body,
        out_shape=[jax.ShapeDtypeStruct(shape, dtype) for shape, dtype in outs],
        scratch_shapes=[pltpu.VMEM(*item) if isinstance(item, tuple) else item for item in scratch],
        compiler_params=pltpu.CompilerParams(vmem_limit_bytes=limit),
        cost_estimate=cost,
        **specs,
    )


def on_device(links, cotangent, parity, link_subset, w_first, w_second, w_third, w_last):
    count = lax.axis_size("tm")

    def send(value, distance):
        return lax.ppermute(value, "tm", [(i, (i + distance) % count) for i in range(count)])

    widths = (768 // count, 768 // count, 128 // count, 64 // count)
    vmem, smem = pltpu.VMEM, pltpu.SMEM
    field = ((4, 18, 2, 8, LANES), F32)
    space = ((3, 18, 2, 8, LANES), F32)
    edge_rows = ((70, SITES), BF16)
    up, down, dense, edges, staples, slab = call(
        face_kernel,
        [edge_rows, edge_rows, field, space, space, ((12, 4, LANES), F32)],
        [space, ((70, 4, LANES), F32)],
    )(links)
    up = send(up, 1)
    down = send(down, -1)
    (state,) = call(
        space_kernel,
        [((186, 8, LANES), F32)],
        [((3, 3, 18, 2, 8, LANES), F32), ((3, 3, 18, 2, 8, LANES), F32)],
        cost=pl.CostEstimate(flops=4_000_000_000, bytes_accessed=16_000_000, transcendentals=0),
    )(dense, staples)
    core = (lax.axis_index("tm") % 2).astype(jnp.int32)[None]
    (block,) = call(
        functools.partial(block_kernel, widths),
        [((count, BLOCKROWS, LANES), BF16)],
        [((12, 4, LANES), F32), ((BLOCKROWS, LANES), F32)],
        places=(smem,) + (vmem,) * 7 + (pl.ANY,),
    )(core, up, down, slab, w_first, w_second, w_third, w_last, state)
    gathered = lax.all_to_all(block, "tm", split_axis=0, concat_axis=0, tiled=True)
    fm, fup, fdown, moves = call(
        time_kernel,
        [
            ((4, 16, SITES), BF16), ((3, 8, SITES), BF16), ((3, 8, SITES), BF16),
            ((2, 4, 18, 2, 8, LANES), BF16),
        ],
        [
            field, ((4, 8, LANES), F32), space, space, field, ((70, 4, LANES), F32), ((70, 4, LANES), F32),
            ((4, 9, 2, 8, LANES), F32), ((4, 4, 16, LANES), F32),
        ],
        places=(smem,) + (vmem,) * 6,
    )(parity + 2 * link_subset, dense, edges, state, cotangent, up, down)
    below = send(fm, 1)
    above = send(fm, -1)
    fbelow = send(fup, 2)
    fabove = send(fdown, -2)

    panel_outs = [
        ((2, 4, LANES), F32), ((H, 72), BF16), ((H, 432), BF16), ((H, 432), BF16), ((72, H), BF16),
        ((H, 432), BF16), ((H, 432), BF16), ((H, 72), BF16),
    ]
    panel_scratch = [((432, LANES), F32)]
    if count == 16:
        loops, p1, p2, p3, p4, b2, b3, b4 = call(panel_kernel_plain, panel_outs, panel_scratch)(gathered)
    else:
        pieces = []
        offset = 0
        for width, full in zip(widths, (48, 48, 8, 4)):
            piece = gathered[:, SLABROWS:SLABROWS + 27, offset:offset + width]
            pieces.append(piece.reshape(432, full))
            offset += width
        pieces.append(jnp.zeros((432, 20), BF16))
        loops, p1, p2, p3, p4, b2, b3, b4 = call(panel_kernel, panel_outs, panel_scratch)(
            gathered, jnp.concatenate(pieces, axis=1)
        )

    window = 18 * SITES
    coeff, grads = call(
        functools.partial(conv_kernel, count == 16),
        [((4, 8, SITES), F32), ((16, 27, LANES) if count == 16 else (432, LANES), BF16)],
        [
            ((8, window), F32), ((8, window), F32), ((H, window), BF16), ((H, window), BF16), ((H, window), BF16),
            ((3, 8, window), F32), ((8, window), F32), ((H, window), BF16), ((H, window), BF16), ((H, 4 * SITES), BF16),
            ((432, 4 * SITES), BF16), ((432, 6 * SITES), BF16), ((432, 4 * SITES), BF16),
            ((72, 4 * SITES), BF16), ((72, 8 * SITES), BF16), ((432, LANES), F32),
        ],
        limit=20 * 1024 * 1024,
    )(fm, below, above, fbelow, fabove, loops, p1, p2, p3, p4, b2, b3, b4)
    if count != 16:
        offset = 0
        pieces = []
        for width, full in zip(widths, (48, 48, 8, 4)):
            pieces.append(grads[:, offset:offset + full].reshape(count, 27, width))
            offset += full
        grads = jnp.concatenate(pieces, axis=2)
    grads = lax.all_to_all(grads, "tm", split_axis=0, concat_axis=0, tiled=True)
    (new_links,) = call(
        update_kernel, [(links.shape, F32)], [((4, 2, 8, LANES), F32)]
    )(dense, moves, coeff)
    grad_first, grad_second, grad_third, grad_last = call(
        functools.partial(sum_kernel, widths),
        [((1, 27 * width), F32) for width in (widths[2], widths[0], widths[1], widths[3])],
        [],
    )(grads)
    return (new_links, grad_first, grad_second, grad_third, grad_last)


def solution(mesh):
    placed = (
        P(None, None, None, None, "groups", "tm", None),
        P(None, None, None, None, "groups", "tm", None),
        P("groups", "tm"),
        P("groups", "tm"),
        P("tm"),
        P("tm"),
        P("tm"),
        P("tm"),
    )
    return jax.shard_map(
        on_device,
        mesh=mesh,
        in_specs=placed,
        out_specs=(
            P(None, None, None, None, "groups", "tm", None),
            P("groups", "tm"),
            P("groups", "tm"),
            P("groups", "tm"),
            P("groups", "tm"),
        ),
        check_vma=False,
    )
```

```python
import functools

import jax
import jax.numpy as jnp
from jax import lax
from jax.experimental import pallas as pl
from jax.experimental.pallas import tpu as pltpu
from jax.sharding import PartitionSpec as P

F32 = jnp.float32
BF16 = jnp.bfloat16
TAPS = 9
H = 48
LANES = 128
SITES = 512
PAIRS = ((0, 1), (0, 2), (0, 3), (1, 2), (1, 3), (2, 3))
SWAP = (0, 2, 1, 4, 3, 6, 5, 8, 7)
ENTRIES = tuple((c, i, j) for c in range(2) for i in range(3) for j in range(3))
PLANE = 180
SLABROWS = 24
BLOCKROWS = 64
LIMIT = 8 * 1024 * 1024


def lane_iota(rows):
    return lax.broadcasted_iota(jnp.int32, (rows, LANES), 1)


def row_iota():
    return lax.broadcasted_iota(jnp.int32, (8, LANES), 0)


def roll_lanes(value, amount):
    return pltpu.roll(value, amount % LANES, 1)


def shift_z(chunk, sign, lanes):
    z = lanes % 8
    if sign > 0:
        return jnp.where(z == 7, roll_lanes(chunk, 7), roll_lanes(chunk, -1))
    return jnp.where(z == 0, roll_lanes(chunk, -7), roll_lanes(chunk, 1))


def shift_y(chunk, sign, lanes):
    y = lanes // 8 % 8
    if sign > 0:
        return jnp.where(y == 7, roll_lanes(chunk, 56), roll_lanes(chunk, -8))
    return jnp.where(y == 0, roll_lanes(chunk, -56), roll_lanes(chunk, 8))


def dense_shift(pair, axis, sign):
    lanes = lane_iota(8)
    if axis == 2:
        return [shift_z(chunk, sign, lanes) for chunk in pair]
    if axis == 1:
        return [shift_y(chunk, sign, lanes) for chunk in pair]
    low = lanes < 64
    first, second = [roll_lanes(chunk, 64) for chunk in pair]
    if sign > 0:
        return [jnp.where(low, first, second), jnp.where(low, second, pltpu.roll(first, 4, 0))]
    return [jnp.where(low, pltpu.roll(second, 4, 0), first), jnp.where(low, first, second)]


def pack_pair(value):
    return [
        jnp.concatenate([value[:, c * 128:c * 128 + 128], value[:, 256 + c * 128:384 + c * 128]], axis=0)
        for c in range(2)
    ]


def halo_pair(ref, index):
    top = row_iota() < 4
    pair = []
    for c in range(2):
        low = jnp.broadcast_to(ref[index, c:c + 1, :], (8, LANES))
        high = jnp.broadcast_to(ref[index, 2 + c:3 + c, :], (8, LANES))
        pair.append(jnp.where(top, low, high))
    return pair


def load_matrix(read):
    real = [[read(3 * i + j) for j in range(3)] for i in range(3)]
    imag = [[read(9 + 3 * i + j) for j in range(3)] for i in range(3)]
    return (real, imag, 1)


def dagger(matrix):
    real, imag, sign = matrix
    return (
        [[real[j][i] for j in range(3)] for i in range(3)],
        [[imag[j][i] for j in range(3)] for i in range(3)],
        -sign,
    )


def total(terms, signs):
    value = None
    for term, sign in zip(terms, signs):
        if value is None:
            value = term if sign > 0 else -term
        else:
            value = value + term if sign > 0 else value - term
    return value


def mat_mul(left, right):
    lr, li, ls = left
    rr, ri, rs = right
    same = ls == rs
    height = len(lr)
    real = [[None] * 3 for _ in range(height)]
    imag = [[None] * 3 for _ in range(height)]
    for i in range(height):
        for j in range(3):
            real[i][j] = total(
                [lr[i][k] * rr[k][j] for k in range(3)] + [li[i][k] * ri[k][j] for k in range(3)],
                [1, 1, 1] + [-1 if same else 1] * 3,
            )
            imag[i][j] = total(
                [lr[i][k] * ri[k][j] for k in range(3)] + [li[i][k] * rr[k][j] for k in range(3)],
                [1, 1, 1] + [1 if same else -1] * 3,
            )
    return (real, imag, ls if same else rs)


def imag_of(matrix, i, j):
    return matrix[1][i][j] if matrix[2] > 0 else -matrix[1][i][j]


def store_matrix(matrix, write):
    for i in range(3):
        for j in range(3):
            write(3 * i + j, matrix[0][i][j])
            write(9 + 3 * i + j, imag_of(matrix, i, j))


def two_rows(read):
    real = [[read(3 * i + j) for j in range(3)] for i in range(2)]
    imag = [[read(6 + 3 * i + j) for j in range(3)] for i in range(2)]
    return (real, imag, 1)


def store_rows(matrix, write):
    for i in range(2):
        for j in range(3):
            write(3 * i + j, matrix[0][i][j])
            write(6 + 3 * i + j, imag_of(matrix, i, j))


def special(matrix):
    real, imag, _ = matrix
    last_r, last_i = [], []
    for k in range(3):
        i, j = (k + 1) % 3, (k + 2) % 3
        last_r.append(
            (real[0][i] * real[1][j] - imag[0][i] * imag[1][j])
            - (real[0][j] * real[1][i] - imag[0][j] * imag[1][i])
        )
        last_i.append(
            (real[0][j] * imag[1][i] + imag[0][j] * real[1][i])
            - (real[0][i] * imag[1][j] + imag[0][i] * real[1][j])
        )
    return (real + [last_r], imag + [last_i], 1)


def anti_parts(matrix):
    parts = [2.0 * imag_of(matrix, i, i) for i in range(3)]
    for i, j in ((0, 1), (0, 2), (1, 2)):
        parts.append(matrix[0][i][j] - matrix[0][j][i])
        parts.append(imag_of(matrix, i, j) + imag_of(matrix, j, i))
    return parts


def anti_matrix(parts):
    zero = jnp.zeros_like(parts[0])
    real = [[zero, parts[3], parts[5]], [-parts[3], zero, parts[7]], [-parts[5], -parts[7], zero]]
    imag = [[parts[0], parts[4], parts[6]], [parts[4], parts[1], parts[8]], [parts[6], parts[8], parts[2]]]
    return real, imag


def anti_mul(parts, right):
    real, imag = anti_matrix(parts)
    rr, ri, _ = right
    out_r = [[None] * 3 for _ in range(3)]
    out_i = [[None] * 3 for _ in range(3)]
    for i in range(3):
        for j in range(3):
            value_r = -(imag[i][i] * ri[i][j])
            value_i = imag[i][i] * rr[i][j]
            for k in range(3):
                if k != i:
                    value_r = value_r + real[i][k] * rr[k][j] - imag[i][k] * ri[k][j]
                    value_i = value_i + real[i][k] * ri[k][j] + imag[i][k] * rr[k][j]
            out_r[i][j] = value_r
            out_i[i][j] = value_i
    return (out_r, out_i, 1)


def pack_links(links_ref, dense):
    def body(mu, carry):
        for e, (c, i, j) in enumerate(ENTRIES):
            low, high = pack_pair(links_ref[mu, c, i, j, 0].astype(F32))
            dense[mu, e, 0] = low
            dense[mu, e, 1] = high
        return carry

    lax.fori_loop(0, 4, body, 0)


def face_kernel(links_ref, up_ref, down_ref, dense, edges, staples, slab, moved, rows):
    pack_links(links_ref, dense)

    def shift_body(e, carry):
        pair = [dense[3, e, 0], dense[3, e, 1]]
        for mu in range(3):
            low, high = dense_shift(pair, mu, 1)
            moved[mu, e, 0] = low
            moved[mu, e, 1] = high
        return carry

    lax.fori_loop(0, 18, shift_body, 0, unroll=3)

    def staple_body(step, carry):
        mu = step // 2
        c = step % 2
        u_mu = load_matrix(lambda e: dense[mu, e, c])
        u_t = load_matrix(lambda e: dense[3, e, c])
        edge = mat_mul(u_mu, load_matrix(lambda e: moved[mu, e, c]))

        def write_edge(e, value):
            edges[mu, e, c] = value

        store_matrix(edge, write_edge)

        def write(e, value):
            staples[mu, e, c] = value
            rows[16 + mu * 18 + e, pl.ds(c, 1)] = value[3:4]
            rows[16 + mu * 18 + e, pl.ds(2 + c, 1)] = value[7:8]

        store_matrix(mat_mul(dagger(edge), u_t), write)
        return carry

    lax.fori_loop(0, 6, staple_body, 0)

    def slab_body(c, carry):
        u_t = load_matrix(lambda e: dense[3, e, c])
        ahead = load_matrix(lambda e: pltpu.roll(dense[3, e, c], 7, 0))
        two = mat_mul(u_t, ahead)
        later = tuple(
            [[pltpu.roll(part[i][j], 6, 0) for j in range(3)] for i in range(3)] for part in two[:2]
        ) + (two[2],)
        four = mat_mul((two[0][:2], two[1][:2], two[2]), later)

        def write(e, value):
            slab[e, pl.ds(c, 1)] = value[0:1]
            slab[e, pl.ds(2 + c, 1)] = value[4:5]
            rows[e, pl.ds(c, 1)] = value[0:1]
            rows[e, pl.ds(2 + c, 1)] = value[4:5]

        store_rows(four, write)
        return carry

    lax.fori_loop(0, 2, slab_body, 0)
    for q in range(4):
        up_ref[:, q * 128:q * 128 + 128] = rows[:, q, :].astype(BF16)

    def down_body(e, carry):
        for mu in range(3):
            for c in range(2):
                value = dense[mu, e, c]
                rows[16 + mu * 18 + e, c:c + 1] = value[0:1]
                rows[16 + mu * 18 + e, 2 + c:3 + c] = value[4:5]
        return carry

    lax.fori_loop(0, 18, down_body, 0, unroll=3)
    for q in range(4):
        down_ref[:, q * 128:q * 128 + 128] = rows[:, q, :].astype(BF16)


def block_kernel(
    widths, core_ref, up_ref, down_ref, slab, w1_ref, w2_ref, w3_ref, w4_ref, after_ref, block_ref, other, block
):
    even = core_ref[0] == 0
    up = up_ref[0:16].astype(F32)
    down = down_ref[0:16].astype(F32)
    for q in range(4):
        lanes = slice(q * 128, q * 128 + 128)
        other[:, q, :] = jnp.where(even, down[0:12, lanes], up[0:12, lanes])
    first = two_rows(lambda e: jnp.where(even, slab[e], other[e]))
    second = special(two_rows(lambda e: jnp.where(even, other[e], slab[e])))

    def write(e, value):
        block[2 * e:2 * e + 2, :] = jnp.where(even, value[0:2], value[2:4])

    store_rows(mat_mul(first, second), write)
    block[SLABROWS:BLOCKROWS] = jnp.zeros((BLOCKROWS - SLABROWS, LANES), F32)
    offset = 0
    for ref, width in zip((w2_ref, w3_ref, w1_ref, w4_ref), widths):
        flat = ref[...].astype(F32)
        for r in range(27):
            block[SLABROWS + r:SLABROWS + r + 1, offset:offset + width] = (
                flat[width * r:width * r + width].reshape(1, width)
            )
        offset += width
    value = block[...].astype(BF16)
    for d in range(block_ref.shape[0]):
        block_ref[d] = value


def put_row(rows, channel, c, value):
    for t in range(4):
        rows[t, c, pl.ds(channel, 1), :] = value[t:t + 1]
        rows[t, 2 + c, pl.ds(channel, 1), :] = value[4 + t:5 + t]


def sum_at(mu, e, c):
    return (mu * 18 + e) * 2 + c


def force_at(mu, e, c):
    return 108 + (mu * 9 + e) * 2 + c


def space_kernel(dense, time_staples, state, moved, staples):
    state[108:180] = jnp.zeros((72, 8, LANES), F32)
    steps = row_iota() % 4

    def shift_body(e, carry):
        for nu in range(3):
            pair = [dense[nu, e, 0], dense[nu, e, 1]]
            for mu in range(3):
                if mu != nu:
                    low, high = dense_shift(pair, mu, 1)
                    moved[mu, nu, e, 0] = low
                    moved[mu, nu, e, 1] = high
        return carry

    lax.fori_loop(0, 18, shift_body, 0, unroll=3)

    def plane_body(step, carry):
        plane = step // 2
        c = step % 2
        mu = jnp.where(plane == 2, 1, 0)
        nu = jnp.where(plane == 0, 1, 2)
        u_mu = load_matrix(lambda e: dense[mu, e, c])
        u_nu = load_matrix(lambda e: dense[nu, e, c])
        one = mat_mul(u_mu, load_matrix(lambda e: moved[mu, nu, e, c]))
        two = mat_mul(u_nu, load_matrix(lambda e: moved[nu, mu, e, c]))
        loop = mat_mul(one, dagger(two))
        state[PLANE + step] = (loop[0][0][0] + loop[0][1][1] + loop[0][2][2]) / 3.0
        for e, part in enumerate(anti_parts(loop)):
            state[force_at(mu, e, c)] += part
            state[force_at(nu, e, c)] -= part

        def write_mu(e, value):
            staples[mu, nu, e, c] = value

        def write_nu(e, value):
            staples[nu, mu, e, c] = value

        store_matrix(mat_mul(dagger(one), u_nu), write_mu)
        store_matrix(mat_mul(dagger(two), u_mu), write_nu)
        return carry

    lax.fori_loop(0, 6, plane_body, 0)

    def lower_body(e, carry):
        for mu in range(3):
            acc = [jnp.where(steps == 0, 0.0, pltpu.roll(time_staples[mu, e, c], 1, 0)) for c in range(2)]
            for nu in range(3):
                if nu != mu:
                    pair = dense_shift([staples[mu, nu, e, 0], staples[mu, nu, e, 1]], nu, -1)
                    acc = [acc[c] + pair[c] for c in range(2)]
            state[sum_at(mu, e, 0)] = acc[0]
            state[sum_at(mu, e, 1)] = acc[1]
        return carry

    lax.fori_loop(0, 18, lower_body, 0, unroll=3)


def time_kernel(
    code_ref, dense, edges, state, cot_ref, up_ref, down_ref,
    fm_ref, fup_ref, fdown_ref, moves_ref,
    cots, gates, moved, staples, sums, halo_up, halo_down, forces, rows,
):
    for q in range(4):
        halo_up[:, q, :] = up_ref[:, q * 128:q * 128 + 128].astype(F32)
        halo_down[:, q, :] = down_ref[:, q * 128:q * 128 + 128].astype(F32)
    rows[...] = jnp.zeros_like(rows)
    pack_links(cot_ref, cots)
    lanes = lane_iota(8)
    site_steps = row_iota() % 4
    colour = (lanes // 64 + lanes // 8 % 8 + lanes % 8 + site_steps) % 2
    code = jnp.zeros_like(site_steps)
    for t in range(4):
        code = jnp.where(site_steps == t, code_ref[0, t], code)
    for mu in range(4):
        active = jnp.logical_and(colour == code % 2, jnp.right_shift(code, mu + 1) % 2 == 1)
        gates[mu] = jnp.where(active, 1.0, 0.0)
    for channel, plane in ((0, 0), (1, 1), (3, 2)):
        for c in range(2):
            put_row(rows, channel, c, state[PLANE + 2 * plane + c])
    for mu in range(4):
        for e in range(9):
            for c in range(2):
                forces[mu, e, c] = state[force_at(mu, e, c)]
    steps = row_iota() % 4

    def shift_body(e, carry):
        for nu in range(3):
            halo = halo_pair(halo_down, 16 + nu * 18 + e)
            below = halo_pair(halo_up, 16 + nu * 18 + e)
            for c in range(2):
                moved[nu, e, c] = jnp.where(steps == 3, halo[c], pltpu.roll(dense[nu, e, c], 7, 0))
                sums[nu, e, c] = state[sum_at(nu, e, c)] + jnp.where(steps == 0, below[c], 0.0)
        return carry

    lax.fori_loop(0, 18, shift_body, 0, unroll=3)

    def plane_body(step, carry):
        mu = step // 2
        c = step % 2
        one = load_matrix(lambda e: edges[mu, e, c])
        two = mat_mul(load_matrix(lambda e: dense[3, e, c]), load_matrix(lambda e: moved[mu, e, c]))
        loop = mat_mul(one, dagger(two))
        put_row(rows, jnp.where(mu == 0, 2, mu + 3), c, (loop[0][0][0] + loop[0][1][1] + loop[0][2][2]) / 3.0)
        for e, part in enumerate(anti_parts(loop)):
            forces[mu, e, c] += part
            forces[3, e, c] -= part

        def write(e, value):
            staples[mu, e, c] = value

        store_matrix(mat_mul(dagger(two), load_matrix(lambda e: dense[mu, e, c])), write)
        return carry

    lax.fori_loop(0, 6, plane_body, 0)

    def lower_body(e, carry):
        acc = None
        for mu in range(3):
            pair = dense_shift([staples[mu, e, 0], staples[mu, e, 1]], mu, -1)
            acc = pair if acc is None else [acc[c] + pair[c] for c in range(2)]
        sums[3, e, 0] = acc[0]
        sums[3, e, 1] = acc[1]
        return carry

    lax.fori_loop(0, 18, lower_body, 0, unroll=3)

    def force_body(step, carry):
        mu = step // 2
        c = step % 2
        current = load_matrix(lambda e: dense[mu, e, c])
        omega = mat_mul(current, load_matrix(lambda e: sums[mu, e, c]))
        parts = [part + forces[mu, e, c] for e, part in enumerate(anti_parts(omega))]
        mean = (parts[0] + parts[1] + parts[2]) * (1.0 / 3.0)
        parts = [parts[e] - mean if e < 3 else parts[e] for e in range(9)]
        parts = [part * (1.0 / 12.0) for part in parts]
        applied = anti_mul(parts, current)
        twice = anti_mul(parts, applied)
        gate = gates[mu]
        slope = jnp.zeros_like(gate)
        curve = jnp.zeros_like(gate)
        for e, (part, i, j) in enumerate(ENTRIES):
            weight = cots[mu, e, c]
            slope = slope + weight * applied[part][i][j]
            curve = curve + weight * twice[part][i][j]
            moves_ref[0, mu, e, c] = (gate * applied[part][i][j]).astype(BF16)
            moves_ref[1, mu, e, c] = (gate * twice[part][i][j]).astype(BF16)
        put_row(rows, 8 + mu, c, gate * slope)
        put_row(rows, 12 + mu, c, gate * curve)
        return carry

    lax.fori_loop(0, 8, force_body, 0)
    for t in range(4):
        for q in range(4):
            value = rows[t, q]
            fm_ref[t, :, q * 128:q * 128 + 128] = value.astype(BF16)
            if t > 0:
                fup_ref[t - 1, :, q * 128:q * 128 + 128] = value[0:8].astype(BF16)
            if t < 3:
                fdown_ref[t, :, q * 128:q * 128 + 128] = value[0:8].astype(BF16)


def selectors():
    row = lax.broadcasted_iota(jnp.int32, (432, 72), 0)
    col = lax.broadcasted_iota(jnp.int32, (432, 72), 1)
    group = row // 12
    spread = (group // 4 * 8 + group % 4 == col).astype(F32).astype(BF16)
    keep = (
        lax.broadcasted_iota(jnp.int32, (432, H), 1) // 4 == lax.broadcasted_iota(jnp.int32, (432, H), 0) % 12
    )
    return spread, keep


def panel_kernel(gathered_ref, weights_ref, loops_ref, p1_ref, p2_ref, p3_ref, p4_ref, b2_ref, b3_ref, b4_ref, weights):
    count = gathered_ref.shape[0]

    def read(chip):
        low = gathered_ref[2 * chip].astype(F32)
        high = gathered_ref[2 * chip + 1].astype(F32)
        return special(
            two_rows(lambda e: jnp.concatenate([low[2 * e:2 * e + 2], high[2 * e:2 * e + 2]], axis=0))
        )

    def flat(matrix):
        return tuple(matrix[0][i][j] for i in range(3) for j in range(3)) + tuple(
            imag_of(matrix, i, j) for i in range(3) for j in range(3)
        )

    def chain(chip, state):
        return flat(mat_mul(load_matrix(lambda e: state[e]), read(chip)))

    state = lax.fori_loop(1, count // 2, chain, flat(read(0)))
    loops_ref[0] = (state[0] + state[4] + state[8]) / 3.0
    loops_ref[1] = (state[9] + state[13] + state[17]) / 3.0

    if weights_ref is None:
        for d in range(count):
            block = gathered_ref[d].astype(F32)
            weights[27 * d:27 * d + 27, :] = block[SLABROWS:SLABROWS + 27]
    else:
        weights[...] = weights_ref[...].astype(F32)
    for k in range(TAPS):
        rows = slice(H * k, H * k + H)
        back = slice(H * SWAP[k], H * SWAP[k] + H)
        p2_ref[:, rows] = weights[rows, 0:48].astype(BF16)
        p3_ref[:, rows] = weights[rows, 48:96].astype(BF16)
        p1_ref[:, 8 * k:8 * k + 8] = weights[rows, 96:104].astype(BF16)
        turned = weights[back, :].T
        b2_ref[:, rows] = turned[0:48].astype(BF16)
        b3_ref[:, rows] = turned[48:96].astype(BF16)
    spread, keep = selectors()
    place = (
        lax.broadcasted_iota(jnp.int32, (LANES, H), 0) == 104 + lax.broadcasted_iota(jnp.int32, (LANES, H), 1) % 4
    ).astype(F32).astype(BF16)
    wide = jnp.dot(weights[...].astype(BF16), place, preferred_element_type=F32)
    wide = jnp.where(keep, wide, 0.0).astype(BF16)
    last = lax.dot_general(spread, wide, (((0,), (0,)), ((), ())), preferred_element_type=F32)
    p4_ref[...] = last.astype(BF16)
    for k in range(TAPS):
        b4_ref[:, 8 * k:8 * k + 8] = last[8 * SWAP[k]:8 * SWAP[k] + 8, :].T.astype(BF16)


def panel_kernel_plain(gathered_ref, *rest):
    panel_kernel(gathered_ref, None, *rest)


def chunks_of(value):
    return [value[:, q * 128:q * 128 + 128] for q in range(4)]


def one_shift(chunks, position):
    if position == 0:
        return chunks
    lanes = lane_iota(chunks[0].shape[0])
    sign = 1 if position % 2 == 1 else -1
    if position > 4:
        return [shift_z(chunk, sign, lanes) for chunk in chunks]
    if position > 2:
        return [shift_y(chunk, sign, lanes) for chunk in chunks]
    low = lanes < 64
    rolled = [roll_lanes(chunk, 64) for chunk in chunks]
    if sign > 0:
        return [jnp.where(low, rolled[q], rolled[(q + 1) % 4]) for q in range(4)]
    return [jnp.where(low, rolled[(q + 3) % 4], rolled[q]) for q in range(4)]


def all_shifts(chunks):
    lanes = lane_iota(chunks[0].shape[0])
    y = lanes // 8 % 8
    z = lanes % 8
    low = lanes < 64
    half = [roll_lanes(chunk, 64) for chunk in chunks]
    return [
        chunks,
        [jnp.where(low, half[q], half[(q + 1) % 4]) for q in range(4)],
        [jnp.where(low, half[(q + 3) % 4], half[q]) for q in range(4)],
        [roll_lanes(jnp.where(y == 0, half[q], chunks[q]), -8) for q in range(4)],
        [roll_lanes(jnp.where(y == 7, half[q], chunks[q]), 8) for q in range(4)],
        [roll_lanes(jnp.where(z == 0, roll_lanes(chunk, 8), chunk), -1) for chunk in chunks],
        [roll_lanes(jnp.where(z == 7, roll_lanes(chunk, -8), chunk), 1) for chunk in chunks],
    ]


def mask_rows(masks):
    lanes = lane_iota(H)
    y = lanes // 8 % 8
    z = lanes % 8
    for k, chosen in enumerate((lanes < 64, y == 0, y == 7, z == 0, z == 7)):
        picked = jnp.where(chosen, 1.0, 0.0)
        masks[2 * k] = picked.astype(BF16)
        masks[2 * k + 1] = (1.0 - picked).astype(BF16)


def masked_shifts(chunks, masks):
    half = [roll_lanes(chunk, 64) for chunk in chunks]
    low = [chunk * masks[0] for chunk in half]
    high = [chunk * masks[1] for chunk in half]

    def blend(k, first, second):
        return first * masks[2 * k] + second * masks[2 * k + 1]

    return [
        chunks,
        [low[q] + high[(q + 1) % 4] for q in range(4)],
        [low[(q + 3) % 4] + high[q] for q in range(4)],
        [roll_lanes(blend(1, half[q], chunks[q]), -8) for q in range(4)],
        [roll_lanes(blend(2, half[q], chunks[q]), 8) for q in range(4)],
        [roll_lanes(blend(3, roll_lanes(chunk, 8), chunk), -1) for chunk in chunks],
        [roll_lanes(blend(4, roll_lanes(chunk, -8), chunk), 1) for chunk in chunks],
    ]


def span(slice_index, count=1):
    if isinstance(slice_index, int):
        return slice(slice_index * SITES, (slice_index + count) * SITES)
    return pl.ds(pl.multiple_of(slice_index * SITES, SITES), count * SITES)


def slot_of(slot):
    return slice(slot * SITES, (slot + 1) * SITES)


def stack_wide(source, target, index, slot, masks):
    chunks = chunks_of(source[:, span(index)])
    for position, shifted in enumerate(masked_shifts(chunks, masks)):
        for q in range(4):
            lanes = slice(slot * SITES + q * 128, slot * SITES + q * 128 + 128)
            target[H * position:H * position + H, lanes] = shifted[q]
    target[7 * H:8 * H, slot_of(slot)] = source[:, span(index + 1)]
    target[8 * H:9 * H, slot_of(slot)] = source[:, span(index - 1)]


def stack_thin(source, target, index, slot):
    chunks = chunks_of(source[:, span(index)])
    ahead = chunks_of(source[:, span(index + 1)])
    behind = chunks_of(source[:, span(index - 1)])
    columns = all_shifts(chunks) + [ahead, behind]
    for q in range(4):
        lanes = slice(slot * SITES + q * 128, slot * SITES + q * 128 + 128)
        target[0:72, lanes] = jnp.concatenate([column[q] for column in columns], axis=0).astype(BF16)


def one_minus_square(value):
    value = value.astype(F32)
    return 1.0 - value * value


def conv_kernel(
    split, fm_ref, below_ref, above_ref, fbelow_ref, fabove_ref, loops_ref,
    p1_ref, p2_ref, p3_ref, p4_ref, b2_ref, b3_ref, b4_ref,
    coeff_ref, grads_ref,
    feats, mixed, h1, h2, h3, parts, lasts, g3, g2, g1, wide, wide_back, wide_first, thin, thin_back, packed, masks,
):
    mask_rows(masks)
    row8 = lax.broadcasted_iota(jnp.int32, (8, SITES), 0)
    loop_re = jnp.concatenate([loops_ref[0, q:q + 1, :] for q in range(4)], axis=1)
    loop_im = jnp.concatenate([loops_ref[1, q:q + 1, :] for q in range(4)], axis=1)
    loops = jnp.where(row8 == 6, loop_re, jnp.where(row8 == 7, loop_im, 0.0))
    loops = loops.astype(BF16).astype(F32)
    for j in range(3):
        feats[:, span(j)] = fbelow_ref[j].astype(F32) + loops
        feats[:, span(15 + j)] = fabove_ref[j].astype(F32) + loops
    for base, ref in ((3, below_ref), (7, fm_ref), (11, above_ref)):
        for j in range(4):
            value = ref[j].astype(F32)
            feats[:, span(base + j)] = value[0:8] + loops
            mixed[:, span(base + j)] = value[8:16]

    own = span(7, 4)
    contract = (((1,), (1,)), ((), ()))

    def own_slot(index, others):
        return index - 7 if 7 <= index < 11 else 4 + others.index(index)

    def dot(weights, stack, slot):
        return jnp.dot(weights[...], stack[:, slot_of(slot)], preferred_element_type=F32)

    def first_dot(index):
        h1[:, span(index)] = jnp.tanh(dot(p1_ref, thin, index % 4)).astype(BF16)

    def second_dot(index):
        h2[:, span(index)] = jnp.tanh(dot(p2_ref, wide, index % 2)).astype(BF16)

    def third_dot(index):
        h3[:, span(index)] = jnp.tanh(dot(p3_ref, wide, 2 + index % 2)).astype(BF16)

    def taps_of(index):
        taps = jnp.dot(p4_ref[...], h3[:, span(index)], preferred_element_type=F32)
        acc = None
        for position in range(7):
            shifted = one_shift(chunks_of(taps[8 * position:8 * position + 8]), position)
            acc = shifted if acc is None else [a + b for a, b in zip(acc, shifted)]
        parts[0, :, span(index)] = jnp.concatenate(acc, axis=1)
        parts[1, :, span(index)] = taps[56:64]
        parts[2, :, span(index)] = taps[64:72]

    def last_of(index):
        coeff = jnp.tanh(parts[0, :, span(index)] + parts[1, :, span(index + 1)] + parts[2, :, span(index - 1)])
        blend = mixed[:, span(index)]
        value = (blend + coeff * pltpu.roll(blend, 4, 0)) * (1.0 - coeff * coeff)
        lasts[:, span(index)] = jnp.where(row8 < 4, value, 0.0).astype(BF16).astype(F32)
        if 7 <= index < 11:
            coeff_ref[index - 7] = coeff

    halo3, halo2 = (5, 6, 11, 12), (6, 11)

    def back_third(index):
        out = dot(b4_ref, thin_back, own_slot(index, halo3))
        g3[:, span(index)] = (out * one_minus_square(h3[:, span(index)])).astype(BF16)

    def back_second(index):
        out = dot(b3_ref, wide_back, own_slot(index, halo2))
        g2[:, span(index)] = (out * one_minus_square(h2[:, span(index)])).astype(BF16)

    def back_first(index):
        out = dot(b2_ref, wide_first, index - 7)
        g1[:, slot_of(index - 7)] = (out * one_minus_square(h1[:, span(index)])).astype(BF16)

    stages = (
        (0, 1, 17, lambda i: stack_thin(feats, thin, i, i % 4)),
        (1, 1, 17, first_dot),
        (3, 2, 16, lambda i: stack_wide(h1, wide, i, i % 2, masks)),
        (4, 2, 16, second_dot),
        (6, 3, 15, lambda i: stack_wide(h2, wide, i, 2 + i % 2, masks)),
        (7, 3, 15, third_dot),
        (8, 3, 15, taps_of),
        (10, 4, 14, last_of),
        (12, 5, 13, lambda i: stack_thin(lasts, thin_back, i, own_slot(i, halo3))),
        (13, 5, 13, back_third),
        (15, 6, 12, lambda i: stack_wide(g3, wide_back, i, own_slot(i, halo2), masks)),
        (16, 6, 12, back_second),
        (18, 7, 11, lambda i: stack_wide(g2, wide_first, i, i - 7, masks)),
        (19, 7, 11, back_first),
    )
    for step in range(1, 30):
        for delay, low, high, task in reversed(stages):
            if low <= step - delay < high:
                task(step - delay)
        if step == 18:
            for index in (7, 8, 9, 10):
                stack_thin(feats, thin, index, index - 7)
        if step == 23:
            grad_last = lax.dot_general(
                thin_back[:, 0:4 * SITES], h3[:, own], contract, preferred_element_type=F32
            )
        if step == 26:
            grad_third = lax.dot_general(
                wide_back[:, 0:4 * SITES], h2[:, own], contract, preferred_element_type=F32
            )
    grad_second = lax.dot_general(wide_first[...], h1[:, own], contract, preferred_element_type=F32)
    grad_first = lax.dot_general(g1[...], thin[...], contract, preferred_element_type=F32)

    spread, keep = selectors()
    ordered = jnp.concatenate([grad_last[8 * SWAP[k]:8 * SWAP[k] + 8] for k in range(TAPS)], axis=0)
    broad = jnp.dot(spread, ordered.astype(BF16), preferred_element_type=F32)
    broad = jnp.where(keep, broad, 0.0).astype(BF16)
    place = (
        lax.broadcasted_iota(jnp.int32, (H, LANES), 1) == 104 + lax.broadcasted_iota(jnp.int32, (H, LANES), 0) % 4
    ).astype(F32).astype(BF16)
    packed[...] = jnp.dot(broad, place, preferred_element_type=F32)
    for k in range(TAPS):
        rows = slice(H * k, H * k + H)
        back = slice(H * SWAP[k], H * SWAP[k] + H)
        packed[rows, 0:48] = grad_second[back]
        packed[rows, 48:96] = grad_third[back]
        packed[rows, 96:104] = grad_first[:, 8 * k:8 * k + 8]
    if split:
        for d in range(16):
            grads_ref[d] = packed[27 * d:27 * d + 27, :].astype(BF16)
    else:
        grads_ref[...] = packed[...].astype(BF16)


def update_kernel(dense, moves_ref, coeff_ref, out_ref, factors):
    for mu in range(4):
        for t in range(4):
            for c in range(2):
                factors[mu, c, t:t + 1, :] = coeff_ref[t, mu:mu + 1, c * 128:c * 128 + 128]
                factors[mu, c, 4 + t:5 + t, :] = coeff_ref[t, mu:mu + 1, 256 + c * 128:384 + c * 128]

    def body(mu, carry):
        factor = [factors[mu, c] for c in range(2)]
        half = [0.5 * value * value for value in factor]
        for e, (part, i, j) in enumerate(ENTRIES):
            new = [
                dense[mu, e, c]
                + factor[c] * moves_ref[0, mu, e, c].astype(F32)
                + half[c] * moves_ref[1, mu, e, c].astype(F32)
                for c in range(2)
            ]
            out_ref[mu, part, i, j, 0] = jnp.concatenate(
                [new[0][0:4], new[1][0:4], new[0][4:8], new[1][4:8]], axis=1
            )
        return carry

    lax.fori_loop(0, 4, body, 0)


def sum_kernel(widths, parts_ref, first_ref, second_ref, third_ref, last_ref):
    value = parts_ref[0].astype(F32)
    for d in range(1, parts_ref.shape[0]):
        value = value + parts_ref[d].astype(F32)
    offset = 0
    for ref, width in zip((second_ref, third_ref, first_ref, last_ref), widths):
        for r in range(27):
            ref[:, width * r:width * r + width] = value[r:r + 1, offset:offset + width]
        offset += width


def call(body, outs, scratch, places=None, cost=None, limit=LIMIT):
    specs = {}
    if places is not None:
        specs["in_specs"] = [pl.BlockSpec(memory_space=place) for place in places]
    return pl.pallas_call(
        body,
        out_shape=[jax.ShapeDtypeStruct(shape, dtype) for shape, dtype in outs],
        scratch_shapes=[pltpu.VMEM(*item) if isinstance(item, tuple) else item for item in scratch],
        compiler_params=pltpu.CompilerParams(vmem_limit_bytes=limit),
        cost_estimate=cost,
        **specs,
    )


def on_device(links, cotangent, parity, link_subset, w_first, w_second, w_third, w_last):
    count = lax.axis_size("tm")

    def send(value, distance):
        return lax.ppermute(value, "tm", [(i, (i + distance) % count) for i in range(count)])

    widths = (768 // count, 768 // count, 128 // count, 64 // count)
    vmem, smem = pltpu.VMEM, pltpu.SMEM
    field = ((4, 18, 2, 8, LANES), F32)
    space = ((3, 18, 2, 8, LANES), F32)
    edge_rows = ((70, SITES), BF16)
    up, down, dense, edges, staples, slab = call(
        face_kernel,
        [edge_rows, edge_rows, field, space, space, ((12, 4, LANES), F32)],
        [space, ((70, 4, LANES), F32)],
    )(links)
    up = send(up, 1)
    down = send(down, -1)
    (state,) = call(
        space_kernel,
        [((186, 8, LANES), F32)],
        [((3, 3, 18, 2, 8, LANES), F32), ((3, 3, 18, 2, 8, LANES), F32)],
        cost=pl.CostEstimate(flops=4_000_000_000, bytes_accessed=16_000_000, transcendentals=0),
    )(dense, staples)
    core = (lax.axis_index("tm") % 2).astype(jnp.int32)[None]
    (block,) = call(
        functools.partial(block_kernel, widths),
        [((count, BLOCKROWS, LANES), BF16)],
        [((12, 4, LANES), F32), ((BLOCKROWS, LANES), F32)],
        places=(smem,) + (vmem,) * 7 + (pl.ANY,),
    )(core, up, down, slab, w_first, w_second, w_third, w_last, state)
    gathered = lax.all_to_all(block, "tm", split_axis=0, concat_axis=0, tiled=True)
    fm, fup, fdown, moves = call(
        time_kernel,
        [
            ((4, 16, SITES), BF16), ((3, 8, SITES), BF16), ((3, 8, SITES), BF16),
            ((2, 4, 18, 2, 8, LANES), BF16),
        ],
        [
            field, ((4, 8, LANES), F32), space, space, field, ((70, 4, LANES), F32), ((70, 4, LANES), F32),
            ((4, 9, 2, 8, LANES), F32), ((4, 4, 16, LANES), F32),
        ],
        places=(smem,) + (vmem,) * 6,
    )(parity + 2 * link_subset, dense, edges, state, cotangent, up, down)
    below = send(fm, 1)
    above = send(fm, -1)
    fbelow = send(fup, 2)
    fabove = send(fdown, -2)

    panel_outs = [
        ((2, 4, LANES), F32), ((H, 72), BF16), ((H, 432), BF16), ((H, 432), BF16), ((72, H), BF16),
        ((H, 432), BF16), ((H, 432), BF16), ((H, 72), BF16),
    ]
    panel_scratch = [((432, LANES), F32)]
    if count == 16:
        loops, p1, p2, p3, p4, b2, b3, b4 = call(panel_kernel_plain, panel_outs, panel_scratch)(gathered)
    else:
        pieces = []
        offset = 0
        for width, full in zip(widths, (48, 48, 8, 4)):
            piece = gathered[:, SLABROWS:SLABROWS + 27, offset:offset + width]
            pieces.append(piece.reshape(432, full))
            offset += width
        pieces.append(jnp.zeros((432, 20), BF16))
        loops, p1, p2, p3, p4, b2, b3, b4 = call(panel_kernel, panel_outs, panel_scratch)(
            gathered, jnp.concatenate(pieces, axis=1)
        )

    window = 18 * SITES
    coeff, grads = call(
        functools.partial(conv_kernel, count == 16),
        [((4, 8, SITES), F32), ((16, 27, LANES) if count == 16 else (432, LANES), BF16)],
        [
            ((8, window), F32), ((8, window), F32), ((H, window), BF16), ((H, window), BF16), ((H, window), BF16),
            ((3, 8, window), F32), ((8, window), F32), ((H, window), BF16), ((H, window), BF16), ((H, 4 * SITES), BF16),
            ((432, 4 * SITES), BF16), ((432, 6 * SITES), BF16), ((432, 4 * SITES), BF16),
            ((72, 4 * SITES), BF16), ((72, 8 * SITES), BF16), ((432, LANES), F32), ((10, H, LANES), BF16),
        ],
        limit=20 * 1024 * 1024,
    )(fm, below, above, fbelow, fabove, loops, p1, p2, p3, p4, b2, b3, b4)
    if count != 16:
        offset = 0
        pieces = []
        for width, full in zip(widths, (48, 48, 8, 4)):
            pieces.append(grads[:, offset:offset + full].reshape(count, 27, width))
            offset += full
        grads = jnp.concatenate(pieces, axis=2)
    grads = lax.all_to_all(grads, "tm", split_axis=0, concat_axis=0, tiled=True)
    (new_links,) = call(
        update_kernel, [(links.shape, F32)], [((4, 2, 8, LANES), F32)]
    )(dense, moves, coeff)
    grad_first, grad_second, grad_third, grad_last = call(
        functools.partial(sum_kernel, widths),
        [((1, 27 * width), F32) for width in (widths[2], widths[0], widths[1], widths[3])],
        [],
    )(grads)
    return (new_links, grad_first, grad_second, grad_third, grad_last)


def solution(mesh):
    placed = (
        P(None, None, None, None, "groups", "tm", None),
        P(None, None, None, None, "groups", "tm", None),
        P("groups", "tm"),
        P("groups", "tm"),
        P("tm"),
        P("tm"),
        P("tm"),
        P("tm"),
    )
    return jax.shard_map(
        on_device,
        mesh=mesh,
        in_specs=placed,
        out_specs=(
            P(None, None, None, None, "groups", "tm", None),
            P("groups", "tm"),
            P("groups", "tm"),
            P("groups", "tm"),
            P("groups", "tm"),
        ),
        check_vma=False,
    )
```

```python
import functools

import jax
import jax.numpy as jnp
from jax import lax
from jax.experimental import pallas as pl
from jax.experimental.pallas import tpu as pltpu
from jax.sharding import PartitionSpec as P

F32 = jnp.float32
BF16 = jnp.bfloat16
TAPS = 9
H = 48
LANES = 128
SITES = 512
PAIRS = ((0, 1), (0, 2), (0, 3), (1, 2), (1, 3), (2, 3))
SWAP = (0, 2, 1, 4, 3, 6, 5, 8, 7)
ENTRIES = tuple((c, i, j) for c in range(2) for i in range(3) for j in range(3))
PLANE = 180
SLABROWS = 24
BLOCKROWS = 64
LIMIT = 8 * 1024 * 1024


def lane_iota(rows):
    return lax.broadcasted_iota(jnp.int32, (rows, LANES), 1)


def row_iota():
    return lax.broadcasted_iota(jnp.int32, (8, LANES), 0)


def roll_lanes(value, amount):
    return pltpu.roll(value, amount % LANES, 1)


def shift_z(chunk, sign, lanes):
    z = lanes % 8
    if sign > 0:
        return jnp.where(z == 7, roll_lanes(chunk, 7), roll_lanes(chunk, -1))
    return jnp.where(z == 0, roll_lanes(chunk, -7), roll_lanes(chunk, 1))


def shift_y(chunk, sign, lanes):
    y = lanes // 8 % 8
    if sign > 0:
        return jnp.where(y == 7, roll_lanes(chunk, 56), roll_lanes(chunk, -8))
    return jnp.where(y == 0, roll_lanes(chunk, -56), roll_lanes(chunk, 8))


def dense_shift(pair, axis, sign):
    lanes = lane_iota(8)
    if axis == 2:
        return [shift_z(chunk, sign, lanes) for chunk in pair]
    if axis == 1:
        return [shift_y(chunk, sign, lanes) for chunk in pair]
    low = lanes < 64
    first, second = [roll_lanes(chunk, 64) for chunk in pair]
    if sign > 0:
        return [jnp.where(low, first, second), jnp.where(low, second, pltpu.roll(first, 4, 0))]
    return [jnp.where(low, pltpu.roll(second, 4, 0), first), jnp.where(low, first, second)]


def pack_pair(value):
    return [
        jnp.concatenate([value[:, c * 128:c * 128 + 128], value[:, 256 + c * 128:384 + c * 128]], axis=0)
        for c in range(2)
    ]


def halo_pair(ref, index):
    top = row_iota() < 4
    pair = []
    for c in range(2):
        low = jnp.broadcast_to(ref[index, c:c + 1, :], (8, LANES))
        high = jnp.broadcast_to(ref[index, 2 + c:3 + c, :], (8, LANES))
        pair.append(jnp.where(top, low, high))
    return pair


def load_matrix(read):
    real = [[read(3 * i + j) for j in range(3)] for i in range(3)]
    imag = [[read(9 + 3 * i + j) for j in range(3)] for i in range(3)]
    return (real, imag, 1)


def dagger(matrix):
    real, imag, sign = matrix
    return (
        [[real[j][i] for j in range(3)] for i in range(3)],
        [[imag[j][i] for j in range(3)] for i in range(3)],
        -sign,
    )


def total(terms, signs):
    value = None
    for term, sign in zip(terms, signs):
        if value is None:
            value = term if sign > 0 else -term
        else:
            value = value + term if sign > 0 else value - term
    return value


def mat_mul(left, right):
    lr, li, ls = left
    rr, ri, rs = right
    same = ls == rs
    height = len(lr)
    real = [[None] * 3 for _ in range(height)]
    imag = [[None] * 3 for _ in range(height)]
    for i in range(height):
        for j in range(3):
            real[i][j] = total(
                [lr[i][k] * rr[k][j] for k in range(3)] + [li[i][k] * ri[k][j] for k in range(3)],
                [1, 1, 1] + [-1 if same else 1] * 3,
            )
            imag[i][j] = total(
                [lr[i][k] * ri[k][j] for k in range(3)] + [li[i][k] * rr[k][j] for k in range(3)],
                [1, 1, 1] + [1 if same else -1] * 3,
            )
    return (real, imag, ls if same else rs)


def imag_of(matrix, i, j):
    return matrix[1][i][j] if matrix[2] > 0 else -matrix[1][i][j]


def store_matrix(matrix, write):
    for i in range(3):
        for j in range(3):
            write(3 * i + j, matrix[0][i][j])
            write(9 + 3 * i + j, imag_of(matrix, i, j))


def two_rows(read):
    real = [[read(3 * i + j) for j in range(3)] for i in range(2)]
    imag = [[read(6 + 3 * i + j) for j in range(3)] for i in range(2)]
    return (real, imag, 1)


def store_rows(matrix, write):
    for i in range(2):
        for j in range(3):
            write(3 * i + j, matrix[0][i][j])
            write(6 + 3 * i + j, imag_of(matrix, i, j))


def special(matrix):
    real, imag, _ = matrix
    last_r, last_i = [], []
    for k in range(3):
        i, j = (k + 1) % 3, (k + 2) % 3
        last_r.append(
            (real[0][i] * real[1][j] - imag[0][i] * imag[1][j])
            - (real[0][j] * real[1][i] - imag[0][j] * imag[1][i])
        )
        last_i.append(
            (real[0][j] * imag[1][i] + imag[0][j] * real[1][i])
            - (real[0][i] * imag[1][j] + imag[0][i] * real[1][j])
        )
    return (real + [last_r], imag + [last_i], 1)


def anti_parts(matrix):
    parts = [2.0 * imag_of(matrix, i, i) for i in range(3)]
    for i, j in ((0, 1), (0, 2), (1, 2)):
        parts.append(matrix[0][i][j] - matrix[0][j][i])
        parts.append(imag_of(matrix, i, j) + imag_of(matrix, j, i))
    return parts


def anti_matrix(parts):
    zero = jnp.zeros_like(parts[0])
    real = [[zero, parts[3], parts[5]], [-parts[3], zero, parts[7]], [-parts[5], -parts[7], zero]]
    imag = [[parts[0], parts[4], parts[6]], [parts[4], parts[1], parts[8]], [parts[6], parts[8], parts[2]]]
    return real, imag


def anti_mul(parts, right):
    real, imag = anti_matrix(parts)
    rr, ri, _ = right
    out_r = [[None] * 3 for _ in range(3)]
    out_i = [[None] * 3 for _ in range(3)]
    for i in range(3):
        for j in range(3):
            value_r = -(imag[i][i] * ri[i][j])
            value_i = imag[i][i] * rr[i][j]
            for k in range(3):
                if k != i:
                    value_r = value_r + real[i][k] * rr[k][j] - imag[i][k] * ri[k][j]
                    value_i = value_i + real[i][k] * ri[k][j] + imag[i][k] * rr[k][j]
            out_r[i][j] = value_r
            out_i[i][j] = value_i
    return (out_r, out_i, 1)


def pack_links(links_ref, dense):
    def body(mu, carry):
        for e, (c, i, j) in enumerate(ENTRIES):
            low, high = pack_pair(links_ref[mu, c, i, j, 0].astype(F32))
            dense[mu, e, 0] = low
            dense[mu, e, 1] = high
        return carry

    lax.fori_loop(0, 4, body, 0)


def face_kernel(links_ref, up_ref, down_ref, dense, edges, staples, slab, moved, rows):
    pack_links(links_ref, dense)

    def shift_body(e, carry):
        pair = [dense[3, e, 0], dense[3, e, 1]]
        for mu in range(3):
            low, high = dense_shift(pair, mu, 1)
            moved[mu, e, 0] = low
            moved[mu, e, 1] = high
        return carry

    lax.fori_loop(0, 18, shift_body, 0, unroll=3)

    def staple_body(step, carry):
        mu = step // 2
        c = step % 2
        u_mu = load_matrix(lambda e: dense[mu, e, c])
        u_t = load_matrix(lambda e: dense[3, e, c])
        edge = mat_mul(u_mu, load_matrix(lambda e: moved[mu, e, c]))

        def write_edge(e, value):
            edges[mu, e, c] = value

        store_matrix(edge, write_edge)

        def write(e, value):
            staples[mu, e, c] = value
            rows[16 + mu * 18 + e, pl.ds(c, 1)] = value[3:4]
            rows[16 + mu * 18 + e, pl.ds(2 + c, 1)] = value[7:8]

        store_matrix(mat_mul(dagger(edge), u_t), write)
        return carry

    lax.fori_loop(0, 6, staple_body, 0)

    def slab_body(c, carry):
        u_t = load_matrix(lambda e: dense[3, e, c])
        ahead = load_matrix(lambda e: pltpu.roll(dense[3, e, c], 7, 0))
        two = mat_mul(u_t, ahead)
        later = tuple(
            [[pltpu.roll(part[i][j], 6, 0) for j in range(3)] for i in range(3)] for part in two[:2]
        ) + (two[2],)
        four = mat_mul((two[0][:2], two[1][:2], two[2]), later)

        def write(e, value):
            slab[e, pl.ds(c, 1)] = value[0:1]
            slab[e, pl.ds(2 + c, 1)] = value[4:5]
            rows[e, pl.ds(c, 1)] = value[0:1]
            rows[e, pl.ds(2 + c, 1)] = value[4:5]

        store_rows(four, write)
        return carry

    lax.fori_loop(0, 2, slab_body, 0)
    for q in range(4):
        up_ref[:, q * 128:q * 128 + 128] = rows[:, q, :].astype(BF16)

    def down_body(e, carry):
        for mu in range(3):
            for c in range(2):
                value = dense[mu, e, c]
                rows[16 + mu * 18 + e, c:c + 1] = value[0:1]
                rows[16 + mu * 18 + e, 2 + c:3 + c] = value[4:5]
        return carry

    lax.fori_loop(0, 18, down_body, 0, unroll=3)
    for q in range(4):
        down_ref[:, q * 128:q * 128 + 128] = rows[:, q, :].astype(BF16)


def block_kernel(
    widths, place_ref, up_ref, down_ref, slab, w1_ref, w2_ref, w3_ref, w4_ref, after_ref, block_ref, other, block
):
    even = place_ref[0] % 2 == 0
    up = up_ref[0:16].astype(F32)
    down = down_ref[0:16].astype(F32)
    for q in range(4):
        lanes = slice(q * 128, q * 128 + 128)
        other[:, q, :] = jnp.where(even, down[0:12, lanes], up[0:12, lanes])
    first = two_rows(lambda e: jnp.where(even, slab[e], other[e]))
    second = special(two_rows(lambda e: jnp.where(even, other[e], slab[e])))

    def write(e, value):
        block[2 * e:2 * e + 2, :] = jnp.where(even, value[0:2], value[2:4])

    store_rows(mat_mul(first, second), write)
    block[SLABROWS:BLOCKROWS] = jnp.zeros((BLOCKROWS - SLABROWS, LANES), F32)
    offset = 0
    for ref, width in zip((w2_ref, w3_ref, w1_ref, w4_ref), widths):
        flat = ref[...].astype(F32)
        for r in range(27):
            block[SLABROWS + r:SLABROWS + r + 1, offset:offset + width] = (
                flat[width * r:width * r + width].reshape(1, width)
            )
        offset += width
    value = block[...].astype(BF16)
    for d in range(block_ref.shape[0]):
        block_ref[d] = value


def put_row(rows, channel, c, value):
    for t in range(4):
        rows[t, c, pl.ds(channel, 1), :] = value[t:t + 1]
        rows[t, 2 + c, pl.ds(channel, 1), :] = value[4 + t:5 + t]


def sum_at(mu, e, c):
    return (mu * 18 + e) * 2 + c


def force_at(mu, e, c):
    return 108 + (mu * 9 + e) * 2 + c


def space_kernel(dense, time_staples, state, moved, staples):
    state[108:180] = jnp.zeros((72, 8, LANES), F32)
    steps = row_iota() % 4

    def shift_body(e, carry):
        for nu in range(3):
            pair = [dense[nu, e, 0], dense[nu, e, 1]]
            for mu in range(3):
                if mu != nu:
                    low, high = dense_shift(pair, mu, 1)
                    moved[mu, nu, e, 0] = low
                    moved[mu, nu, e, 1] = high
        return carry

    lax.fori_loop(0, 18, shift_body, 0, unroll=3)

    def plane_body(step, carry):
        plane = step // 2
        c = step % 2
        mu = jnp.where(plane == 2, 1, 0)
        nu = jnp.where(plane == 0, 1, 2)
        u_mu = load_matrix(lambda e: dense[mu, e, c])
        u_nu = load_matrix(lambda e: dense[nu, e, c])
        one = mat_mul(u_mu, load_matrix(lambda e: moved[mu, nu, e, c]))
        two = mat_mul(u_nu, load_matrix(lambda e: moved[nu, mu, e, c]))
        loop = mat_mul(one, dagger(two))
        state[PLANE + step] = (loop[0][0][0] + loop[0][1][1] + loop[0][2][2]) / 3.0
        for e, part in enumerate(anti_parts(loop)):
            state[force_at(mu, e, c)] += part
            state[force_at(nu, e, c)] -= part

        def write_mu(e, value):
            staples[mu, nu, e, c] = value

        def write_nu(e, value):
            staples[nu, mu, e, c] = value

        store_matrix(mat_mul(dagger(one), u_nu), write_mu)
        store_matrix(mat_mul(dagger(two), u_mu), write_nu)
        return carry

    lax.fori_loop(0, 6, plane_body, 0)

    def lower_body(e, carry):
        for mu in range(3):
            acc = [jnp.where(steps == 0, 0.0, pltpu.roll(time_staples[mu, e, c], 1, 0)) for c in range(2)]
            for nu in range(3):
                if nu != mu:
                    pair = dense_shift([staples[mu, nu, e, 0], staples[mu, nu, e, 1]], nu, -1)
                    acc = [acc[c] + pair[c] for c in range(2)]
            state[sum_at(mu, e, 0)] = acc[0]
            state[sum_at(mu, e, 1)] = acc[1]
        return carry

    lax.fori_loop(0, 18, lower_body, 0, unroll=3)


def time_kernel(
    code_ref, dense, edges, state, cot_ref, up_ref, down_ref,
    fm_ref, planes_ref, moves_ref,
    cots, gates, moved, staples, sums, halo_up, halo_down, forces, rows,
):
    for q in range(4):
        halo_up[:, q, :] = up_ref[:, q * 128:q * 128 + 128].astype(F32)
        halo_down[:, q, :] = down_ref[:, q * 128:q * 128 + 128].astype(F32)
    rows[...] = jnp.zeros_like(rows)
    pack_links(cot_ref, cots)
    lanes = lane_iota(8)
    site_steps = row_iota() % 4
    colour = (lanes // 64 + lanes // 8 % 8 + lanes % 8 + site_steps) % 2
    code = jnp.zeros_like(site_steps)
    for t in range(4):
        code = jnp.where(site_steps == t, code_ref[0, t], code)
    for mu in range(4):
        active = jnp.logical_and(colour == code % 2, jnp.right_shift(code, mu + 1) % 2 == 1)
        gates[mu] = jnp.where(active, 1.0, 0.0)
    for channel, plane in ((0, 0), (1, 1), (3, 2)):
        for c in range(2):
            put_row(rows, channel, c, state[PLANE + 2 * plane + c])
    for mu in range(4):
        for e in range(9):
            for c in range(2):
                forces[mu, e, c] = state[force_at(mu, e, c)]
    steps = row_iota() % 4

    def shift_body(e, carry):
        for nu in range(3):
            halo = halo_pair(halo_down, 16 + nu * 18 + e)
            below = halo_pair(halo_up, 16 + nu * 18 + e)
            for c in range(2):
                moved[nu, e, c] = jnp.where(steps == 3, halo[c], pltpu.roll(dense[nu, e, c], 7, 0))
                sums[nu, e, c] = state[sum_at(nu, e, c)] + jnp.where(steps == 0, below[c], 0.0)
        return carry

    lax.fori_loop(0, 18, shift_body, 0, unroll=3)

    def plane_body(step, carry):
        mu = step // 2
        c = step % 2
        one = load_matrix(lambda e: edges[mu, e, c])
        two = mat_mul(load_matrix(lambda e: dense[3, e, c]), load_matrix(lambda e: moved[mu, e, c]))
        loop = mat_mul(one, dagger(two))
        put_row(rows, jnp.where(mu == 0, 2, mu + 3), c, (loop[0][0][0] + loop[0][1][1] + loop[0][2][2]) / 3.0)
        for e, part in enumerate(anti_parts(loop)):
            forces[mu, e, c] += part
            forces[3, e, c] -= part

        def write(e, value):
            staples[mu, e, c] = value

        store_matrix(mat_mul(dagger(two), load_matrix(lambda e: dense[mu, e, c])), write)
        return carry

    lax.fori_loop(0, 6, plane_body, 0)

    def lower_body(e, carry):
        acc = None
        for mu in range(3):
            pair = dense_shift([staples[mu, e, 0], staples[mu, e, 1]], mu, -1)
            acc = pair if acc is None else [acc[c] + pair[c] for c in range(2)]
        sums[3, e, 0] = acc[0]
        sums[3, e, 1] = acc[1]
        return carry

    lax.fori_loop(0, 18, lower_body, 0, unroll=3)

    def force_body(step, carry):
        mu = step // 2
        c = step % 2
        current = load_matrix(lambda e: dense[mu, e, c])
        omega = mat_mul(current, load_matrix(lambda e: sums[mu, e, c]))
        parts = [part + forces[mu, e, c] for e, part in enumerate(anti_parts(omega))]
        mean = (parts[0] + parts[1] + parts[2]) * (1.0 / 3.0)
        parts = [parts[e] - mean if e < 3 else parts[e] for e in range(9)]
        parts = [part * (1.0 / 12.0) for part in parts]
        applied = anti_mul(parts, current)
        twice = anti_mul(parts, applied)
        gate = gates[mu]
        slope = jnp.zeros_like(gate)
        curve = jnp.zeros_like(gate)
        for e, (part, i, j) in enumerate(ENTRIES):
            weight = cots[mu, e, c]
            slope = slope + weight * applied[part][i][j]
            curve = curve + weight * twice[part][i][j]
            moves_ref[0, mu, e, c] = (gate * applied[part][i][j]).astype(BF16)
            moves_ref[1, mu, e, c] = (gate * twice[part][i][j]).astype(BF16)
        put_row(rows, 8 + mu, c, gate * slope)
        put_row(rows, 12 + mu, c, gate * curve)
        return carry

    lax.fori_loop(0, 8, force_body, 0)
    for t in range(4):
        for q in range(4):
            value = rows[t, q]
            fm_ref[t, :, q * 128:q * 128 + 128] = value.astype(BF16)
            planes_ref[t, :, q * 128:q * 128 + 128] = value[0:8].astype(BF16)


def selectors():
    row = lax.broadcasted_iota(jnp.int32, (432, 72), 0)
    col = lax.broadcasted_iota(jnp.int32, (432, 72), 1)
    group = row // 12
    spread = (group // 4 * 8 + group % 4 == col).astype(F32).astype(BF16)
    keep = (
        lax.broadcasted_iota(jnp.int32, (432, H), 1) // 4 == lax.broadcasted_iota(jnp.int32, (432, H), 0) % 12
    )
    return spread, keep


def panel_kernel(gathered_ref, weights_ref, loops_ref, p1_ref, p2_ref, p3_ref, p4_ref, b2_ref, b3_ref, b4_ref, weights):
    count = gathered_ref.shape[0]

    def read(chip):
        low = gathered_ref[2 * chip].astype(F32)
        high = gathered_ref[2 * chip + 1].astype(F32)
        return special(
            two_rows(lambda e: jnp.concatenate([low[2 * e:2 * e + 2], high[2 * e:2 * e + 2]], axis=0))
        )

    def flat(matrix):
        return tuple(matrix[0][i][j] for i in range(3) for j in range(3)) + tuple(
            imag_of(matrix, i, j) for i in range(3) for j in range(3)
        )

    def chain(chip, state):
        return flat(mat_mul(load_matrix(lambda e: state[e]), read(chip)))

    state = lax.fori_loop(1, count // 2, chain, flat(read(0)))
    loops_ref[0] = (state[0] + state[4] + state[8]) / 3.0
    loops_ref[1] = (state[9] + state[13] + state[17]) / 3.0

    if weights_ref is None:
        for d in range(count):
            block = gathered_ref[d].astype(F32)
            weights[27 * d:27 * d + 27, :] = block[SLABROWS:SLABROWS + 27]
    else:
        weights[...] = weights_ref[...].astype(F32)
    for k in range(TAPS):
        rows = slice(H * k, H * k + H)
        back = slice(H * SWAP[k], H * SWAP[k] + H)
        p2_ref[:, rows] = weights[rows, 0:48].astype(BF16)
        p3_ref[:, rows] = weights[rows, 48:96].astype(BF16)
        p1_ref[:, 8 * k:8 * k + 8] = weights[rows, 96:104].astype(BF16)
        turned = weights[back, :].T
        b2_ref[:, rows] = turned[0:48].astype(BF16)
        b3_ref[:, rows] = turned[48:96].astype(BF16)
    spread, keep = selectors()
    place = (
        lax.broadcasted_iota(jnp.int32, (LANES, H), 0) == 104 + lax.broadcasted_iota(jnp.int32, (LANES, H), 1) % 4
    ).astype(F32).astype(BF16)
    wide = jnp.dot(weights[...].astype(BF16), place, preferred_element_type=F32)
    wide = jnp.where(keep, wide, 0.0).astype(BF16)
    last = lax.dot_general(spread, wide, (((0,), (0,)), ((), ())), preferred_element_type=F32)
    p4_ref[...] = last.astype(BF16)
    for k in range(TAPS):
        b4_ref[:, 8 * k:8 * k + 8] = last[8 * SWAP[k]:8 * SWAP[k] + 8, :].T.astype(BF16)


def panel_kernel_plain(gathered_ref, *rest):
    panel_kernel(gathered_ref, None, *rest)


def chunks_of(value):
    return [value[:, q * 128:q * 128 + 128] for q in range(4)]


def one_shift(chunks, position):
    if position == 0:
        return chunks
    lanes = lane_iota(chunks[0].shape[0])
    sign = 1 if position % 2 == 1 else -1
    if position > 4:
        return [shift_z(chunk, sign, lanes) for chunk in chunks]
    if position > 2:
        return [shift_y(chunk, sign, lanes) for chunk in chunks]
    low = lanes < 64
    rolled = [roll_lanes(chunk, 64) for chunk in chunks]
    if sign > 0:
        return [jnp.where(low, rolled[q], rolled[(q + 1) % 4]) for q in range(4)]
    return [jnp.where(low, rolled[(q + 3) % 4], rolled[q]) for q in range(4)]


def all_shifts(chunks):
    lanes = lane_iota(chunks[0].shape[0])
    y = lanes // 8 % 8
    z = lanes % 8
    low = lanes < 64
    half = [roll_lanes(chunk, 64) for chunk in chunks]
    return [
        chunks,
        [jnp.where(low, half[q], half[(q + 1) % 4]) for q in range(4)],
        [jnp.where(low, half[(q + 3) % 4], half[q]) for q in range(4)],
        [roll_lanes(jnp.where(y == 0, half[q], chunks[q]), -8) for q in range(4)],
        [roll_lanes(jnp.where(y == 7, half[q], chunks[q]), 8) for q in range(4)],
        [roll_lanes(jnp.where(z == 0, roll_lanes(chunk, 8), chunk), -1) for chunk in chunks],
        [roll_lanes(jnp.where(z == 7, roll_lanes(chunk, -8), chunk), 1) for chunk in chunks],
    ]


def span(slice_index, count=1):
    if isinstance(slice_index, int):
        return slice(slice_index * SITES, (slice_index + count) * SITES)
    return pl.ds(pl.multiple_of(slice_index * SITES, SITES), count * SITES)


def slot_of(slot):
    return slice(slot * SITES, (slot + 1) * SITES)


def stack_wide(source, target, index, slot):
    chunks = chunks_of(source[:, span(index)])
    for position, shifted in enumerate(all_shifts(chunks)):
        for q in range(4):
            lanes = slice(slot * SITES + q * 128, slot * SITES + q * 128 + 128)
            target[H * position:H * position + H, lanes] = shifted[q]
    target[7 * H:8 * H, slot_of(slot)] = source[:, span(index + 1)]
    target[8 * H:9 * H, slot_of(slot)] = source[:, span(index - 1)]


def stack_thin(source, target, index, slot):
    chunks = chunks_of(source[:, span(index)])
    ahead = chunks_of(source[:, span(index + 1)])
    behind = chunks_of(source[:, span(index - 1)])
    columns = all_shifts(chunks) + [ahead, behind]
    for q in range(4):
        lanes = slice(slot * SITES + q * 128, slot * SITES + q * 128 + 128)
        target[0:72, lanes] = jnp.concatenate([column[q] for column in columns], axis=0).astype(BF16)


def one_minus_square(value):
    value = value.astype(F32)
    return 1.0 - value * value


def conv_kernel(
    split, place_ref, fm_ref, near_ref, far_ref, near_chip_ref, far_chip_ref, loops_ref,
    p1_ref, p2_ref, p3_ref, p4_ref, b2_ref, b3_ref, b4_ref,
    coeff_ref, grads_ref,
    feats, mixed, h1, h2, h3, parts, lasts, g3, g2, g1, wide, wide_back, wide_first, thin, thin_back, packed,
):
    row8 = lax.broadcasted_iota(jnp.int32, (8, SITES), 0)
    loop_re = jnp.concatenate([loops_ref[0, q:q + 1, :] for q in range(4)], axis=1)
    loop_im = jnp.concatenate([loops_ref[1, q:q + 1, :] for q in range(4)], axis=1)
    loops = jnp.where(row8 == 6, loop_re, jnp.where(row8 == 7, loop_im, 0.0))
    loops = loops.astype(BF16).astype(F32)
    first_core = place_ref[0] % 2 == 0
    first_chip = place_ref[0] // 2 % 2 == 0
    for j in range(4):
        near, far = near_chip_ref[j].astype(F32), far_chip_ref[j].astype(F32)
        if j > 0:
            feats[:, span(j - 1)] = jnp.where(first_chip, far, near) + loops
        if j < 3:
            feats[:, span(15 + j)] = jnp.where(first_chip, near, far) + loops
        near, far = near_ref[j].astype(F32), far_ref[j].astype(F32)
        below, above = jnp.where(first_core, far, near), jnp.where(first_core, near, far)
        for base, value in ((3, below), (7, fm_ref[j].astype(F32)), (11, above)):
            feats[:, span(base + j)] = value[0:8] + loops
            mixed[:, span(base + j)] = value[8:16]

    own = span(7, 4)
    contract = (((1,), (1,)), ((), ()))

    def own_slot(index, others):
        return index - 7 if 7 <= index < 11 else 4 + others.index(index)

    def dot(weights, stack, slot):
        return jnp.dot(weights[...], stack[:, slot_of(slot)], preferred_element_type=F32)

    def first_dot(index):
        h1[:, span(index)] = jnp.tanh(dot(p1_ref, thin, index % 4)).astype(BF16)

    def second_dot(index):
        h2[:, span(index)] = jnp.tanh(dot(p2_ref, wide, index % 2)).astype(BF16)

    def third_dot(index):
        h3[:, span(index)] = jnp.tanh(dot(p3_ref, wide, 2 + index % 2)).astype(BF16)

    def taps_of(index):
        taps = jnp.dot(p4_ref[...], h3[:, span(index)], preferred_element_type=F32)
        acc = None
        for position in range(7):
            shifted = one_shift(chunks_of(taps[8 * position:8 * position + 8]), position)
            acc = shifted if acc is None else [a + b for a, b in zip(acc, shifted)]
        parts[0, :, span(index)] = jnp.concatenate(acc, axis=1)
        parts[1, :, span(index)] = taps[56:64]
        parts[2, :, span(index)] = taps[64:72]

    def last_of(index):
        coeff = jnp.tanh(parts[0, :, span(index)] + parts[1, :, span(index + 1)] + parts[2, :, span(index - 1)])
        blend = mixed[:, span(index)]
        value = (blend + coeff * pltpu.roll(blend, 4, 0)) * (1.0 - coeff * coeff)
        lasts[:, span(index)] = jnp.where(row8 < 4, value, 0.0).astype(BF16).astype(F32)
        if 7 <= index < 11:
            coeff_ref[index - 7] = coeff

    halo3, halo2 = (5, 6, 11, 12), (6, 11)

    def back_third(index):
        out = dot(b4_ref, thin_back, own_slot(index, halo3))
        g3[:, span(index)] = (out * one_minus_square(h3[:, span(index)])).astype(BF16)

    def back_second(index):
        out = dot(b3_ref, wide_back, own_slot(index, halo2))
        g2[:, span(index)] = (out * one_minus_square(h2[:, span(index)])).astype(BF16)

    def back_first(index):
        out = dot(b2_ref, wide_first, index - 7)
        g1[:, slot_of(index - 7)] = (out * one_minus_square(h1[:, span(index)])).astype(BF16)

    stages = (
        (0, 1, 17, lambda i: stack_thin(feats, thin, i, i % 4)),
        (1, 1, 17, first_dot),
        (3, 2, 16, lambda i: stack_wide(h1, wide, i, i % 2)),
        (4, 2, 16, second_dot),
        (6, 3, 15, lambda i: stack_wide(h2, wide, i, 2 + i % 2)),
        (7, 3, 15, third_dot),
        (8, 3, 15, taps_of),
        (10, 4, 14, last_of),
        (12, 5, 13, lambda i: stack_thin(lasts, thin_back, i, own_slot(i, halo3))),
        (13, 5, 13, back_third),
        (15, 6, 12, lambda i: stack_wide(g3, wide_back, i, own_slot(i, halo2))),
        (16, 6, 12, back_second),
        (18, 7, 11, lambda i: stack_wide(g2, wide_first, i, i - 7)),
        (19, 7, 11, back_first),
    )
    for step in range(1, 30):
        for delay, low, high, task in reversed(stages):
            if low <= step - delay < high:
                task(step - delay)
        if step == 18:
            for index in (7, 8, 9, 10):
                stack_thin(feats, thin, index, index - 7)
        if step == 23:
            grad_last = lax.dot_general(
                thin_back[:, 0:4 * SITES], h3[:, own], contract, preferred_element_type=F32
            )
        if step == 26:
            grad_third = lax.dot_general(
                wide_back[:, 0:4 * SITES], h2[:, own], contract, preferred_element_type=F32
            )
    grad_second = lax.dot_general(wide_first[...], h1[:, own], contract, preferred_element_type=F32)
    grad_first = lax.dot_general(g1[...], thin[...], contract, preferred_element_type=F32)

    spread, keep = selectors()
    ordered = jnp.concatenate([grad_last[8 * SWAP[k]:8 * SWAP[k] + 8] for k in range(TAPS)], axis=0)
    broad = jnp.dot(spread, ordered.astype(BF16), preferred_element_type=F32)
    broad = jnp.where(keep, broad, 0.0).astype(BF16)
    place = (
        lax.broadcasted_iota(jnp.int32, (H, LANES), 1) == 104 + lax.broadcasted_iota(jnp.int32, (H, LANES), 0) % 4
    ).astype(F32).astype(BF16)
    packed[...] = jnp.dot(broad, place, preferred_element_type=F32)
    for k in range(TAPS):
        rows = slice(H * k, H * k + H)
        back = slice(H * SWAP[k], H * SWAP[k] + H)
        packed[rows, 0:48] = grad_second[back]
        packed[rows, 48:96] = grad_third[back]
        packed[rows, 96:104] = grad_first[:, 8 * k:8 * k + 8]
    if split:
        for d in range(16):
            grads_ref[d] = packed[27 * d:27 * d + 27, :].astype(BF16)
    else:
        grads_ref[...] = packed[...].astype(BF16)


def update_kernel(dense, moves_ref, coeff_ref, out_ref, factors):
    for mu in range(4):
        for t in range(4):
            for c in range(2):
                factors[mu, c, t:t + 1, :] = coeff_ref[t, mu:mu + 1, c * 128:c * 128 + 128]
                factors[mu, c, 4 + t:5 + t, :] = coeff_ref[t, mu:mu + 1, 256 + c * 128:384 + c * 128]

    def body(mu, carry):
        factor = [factors[mu, c] for c in range(2)]
        half = [0.5 * value * value for value in factor]
        for e, (part, i, j) in enumerate(ENTRIES):
            new = [
                dense[mu, e, c]
                + factor[c] * moves_ref[0, mu, e, c].astype(F32)
                + half[c] * moves_ref[1, mu, e, c].astype(F32)
                for c in range(2)
            ]
            out_ref[mu, part, i, j, 0] = jnp.concatenate(
                [new[0][0:4], new[1][0:4], new[0][4:8], new[1][4:8]], axis=1
            )
        return carry

    lax.fori_loop(0, 4, body, 0)


def sum_kernel(widths, parts_ref, first_ref, second_ref, third_ref, last_ref):
    value = parts_ref[0].astype(F32)
    for d in range(1, parts_ref.shape[0]):
        value = value + parts_ref[d].astype(F32)
    offset = 0
    for ref, width in zip((second_ref, third_ref, first_ref, last_ref), widths):
        for r in range(27):
            ref[:, width * r:width * r + width] = value[r:r + 1, offset:offset + width]
        offset += width


def call(body, outs, scratch, places=None, cost=None, limit=LIMIT):
    specs = {}
    if places is not None:
        specs["in_specs"] = [pl.BlockSpec(memory_space=place) for place in places]
    return pl.pallas_call(
        body,
        out_shape=[jax.ShapeDtypeStruct(shape, dtype) for shape, dtype in outs],
        scratch_shapes=[pltpu.VMEM(*item) if isinstance(item, tuple) else item for item in scratch],
        compiler_params=pltpu.CompilerParams(vmem_limit_bytes=limit),
        cost_estimate=cost,
        **specs,
    )


def on_device(links, cotangent, parity, link_subset, w_first, w_second, w_third, w_last):
    count = lax.axis_size("tm")

    def send(value, distance):
        return lax.ppermute(value, "tm", [(i, (i + distance) % count) for i in range(count)])

    def swap(value, pairs):
        return lax.ppermute(value, "tm", pairs + [(target, source) for source, target in pairs])

    chips = count // 2
    widths = (768 // count, 768 // count, 128 // count, 64 // count)
    vmem, smem = pltpu.VMEM, pltpu.SMEM
    field = ((4, 18, 2, 8, LANES), F32)
    space = ((3, 18, 2, 8, LANES), F32)
    edge_rows = ((70, SITES), BF16)
    up, down, dense, edges, staples, slab = call(
        face_kernel,
        [edge_rows, edge_rows, field, space, space, ((12, 4, LANES), F32)],
        [space, ((70, 4, LANES), F32)],
    )(links)
    up = send(up, 1)
    down = send(down, -1)
    (state,) = call(
        space_kernel,
        [((186, 8, LANES), F32)],
        [((3, 3, 18, 2, 8, LANES), F32), ((3, 3, 18, 2, 8, LANES), F32)],
        cost=pl.CostEstimate(flops=4_000_000_000, bytes_accessed=16_000_000, transcendentals=0),
    )(dense, staples)
    place = lax.axis_index("tm").astype(jnp.int32)[None]
    (block,) = call(
        functools.partial(block_kernel, widths),
        [((count, BLOCKROWS, LANES), BF16)],
        [((12, 4, LANES), F32), ((BLOCKROWS, LANES), F32)],
        places=(smem,) + (vmem,) * 7 + (pl.ANY,),
    )(place, up, down, slab, w_first, w_second, w_third, w_last, state)
    gathered = lax.all_to_all(block, "tm", split_axis=0, concat_axis=0, tiled=True)
    fm, planes, moves = call(
        time_kernel,
        [
            ((4, 16, SITES), BF16), ((4, 8, SITES), BF16),
            ((2, 4, 18, 2, 8, LANES), BF16),
        ],
        [
            field, ((4, 8, LANES), F32), space, space, field, ((70, 4, LANES), F32), ((70, 4, LANES), F32),
            ((4, 9, 2, 8, LANES), F32), ((4, 4, 16, LANES), F32),
        ],
        places=(smem,) + (vmem,) * 6,
    )(parity + 2 * link_subset, dense, edges, state, cotangent, up, down)
    far_chip = swap(planes, [(2 * c + k, (2 * c + 2 + k) % count) for c in range(1, chips, 2) for k in range(2)])
    far_core = swap(fm, [(i, (i + 1) % count) for i in range(1, count, 2)])
    near_chip = swap(planes, [(2 * c + k, 2 * c + 2 + k) for c in range(0, chips, 2) for k in range(2)])
    near_core = swap(fm, [(i, i + 1) for i in range(0, count, 2)])

    panel_outs = [
        ((2, 4, LANES), F32), ((H, 72), BF16), ((H, 432), BF16), ((H, 432), BF16), ((72, H), BF16),
        ((H, 432), BF16), ((H, 432), BF16), ((H, 72), BF16),
    ]
    panel_scratch = [((432, LANES), F32)]
    if count == 16:
        loops, p1, p2, p3, p4, b2, b3, b4 = call(panel_kernel_plain, panel_outs, panel_scratch)(gathered)
    else:
        pieces = []
        offset = 0
        for width, full in zip(widths, (48, 48, 8, 4)):
            piece = gathered[:, SLABROWS:SLABROWS + 27, offset:offset + width]
            pieces.append(piece.reshape(432, full))
            offset += width
        pieces.append(jnp.zeros((432, 20), BF16))
        loops, p1, p2, p3, p4, b2, b3, b4 = call(panel_kernel, panel_outs, panel_scratch)(
            gathered, jnp.concatenate(pieces, axis=1)
        )

    window = 18 * SITES
    coeff, grads = call(
        functools.partial(conv_kernel, count == 16),
        [((4, 8, SITES), F32), ((16, 27, LANES) if count == 16 else (432, LANES), BF16)],
        [
            ((8, window), F32), ((8, window), F32), ((H, window), BF16), ((H, window), BF16), ((H, window), BF16),
            ((3, 8, window), F32), ((8, window), F32), ((H, window), BF16), ((H, window), BF16), ((H, 4 * SITES), BF16),
            ((432, 4 * SITES), BF16), ((432, 6 * SITES), BF16), ((432, 4 * SITES), BF16),
            ((72, 4 * SITES), BF16), ((72, 8 * SITES), BF16), ((432, LANES), F32),
        ],
        limit=20 * 1024 * 1024,
        places=(smem,) + (vmem,) * 13,
    )(place, fm, near_core, far_core, near_chip, far_chip, loops, p1, p2, p3, p4, b2, b3, b4)
    if count != 16:
        offset = 0
        pieces = []
        for width, full in zip(widths, (48, 48, 8, 4)):
            pieces.append(grads[:, offset:offset + full].reshape(count, 27, width))
            offset += full
        grads = jnp.concatenate(pieces, axis=2)
    grads = lax.all_to_all(grads, "tm", split_axis=0, concat_axis=0, tiled=True)
    (new_links,) = call(
        update_kernel, [(links.shape, F32)], [((4, 2, 8, LANES), F32)]
    )(dense, moves, coeff)
    grad_first, grad_second, grad_third, grad_last = call(
        functools.partial(sum_kernel, widths),
        [((1, 27 * width), F32) for width in (widths[2], widths[0], widths[1], widths[3])],
        [],
    )(grads)
    return (new_links, grad_first, grad_second, grad_third, grad_last)


def solution(mesh):
    placed = (
        P(None, None, None, None, "groups", "tm", None),
        P(None, None, None, None, "groups", "tm", None),
        P("groups", "tm"),
        P("groups", "tm"),
        P("tm"),
        P("tm"),
        P("tm"),
        P("tm"),
    )
    return jax.shard_map(
        on_device,
        mesh=mesh,
        in_specs=placed,
        out_specs=(
            P(None, None, None, None, "groups", "tm", None),
            P("groups", "tm"),
            P("groups", "tm"),
            P("groups", "tm"),
            P("groups", "tm"),
        ),
        check_vma=False,
    )
```

```python
import functools

import jax
import jax.numpy as jnp
from jax import lax
from jax.experimental import pallas as pl
from jax.experimental.pallas import tpu as pltpu
from jax.sharding import PartitionSpec as P

F32 = jnp.float32
BF16 = jnp.bfloat16
TAPS = 9
H = 48
LANES = 128
SITES = 512
PAIRS = ((0, 1), (0, 2), (0, 3), (1, 2), (1, 3), (2, 3))
SWAP = (0, 2, 1, 4, 3, 6, 5, 8, 7)
ENTRIES = tuple((c, i, j) for c in range(2) for i in range(3) for j in range(3))
PLANE = 180
SLABROWS = 24
BLOCKROWS = 64
LIMIT = 8 * 1024 * 1024


def lane_iota(rows):
    return lax.broadcasted_iota(jnp.int32, (rows, LANES), 1)


def row_iota():
    return lax.broadcasted_iota(jnp.int32, (8, LANES), 0)


def roll_lanes(value, amount):
    return pltpu.roll(value, amount % LANES, 1)


def shift_z(chunk, sign, lanes):
    z = lanes % 8
    if sign > 0:
        return jnp.where(z == 7, roll_lanes(chunk, 7), roll_lanes(chunk, -1))
    return jnp.where(z == 0, roll_lanes(chunk, -7), roll_lanes(chunk, 1))


def shift_y(chunk, sign, lanes):
    y = lanes // 8 % 8
    if sign > 0:
        return jnp.where(y == 7, roll_lanes(chunk, 56), roll_lanes(chunk, -8))
    return jnp.where(y == 0, roll_lanes(chunk, -56), roll_lanes(chunk, 8))


def dense_shift(pair, axis, sign):
    lanes = lane_iota(8)
    if axis == 2:
        return [shift_z(chunk, sign, lanes) for chunk in pair]
    if axis == 1:
        return [shift_y(chunk, sign, lanes) for chunk in pair]
    low = lanes < 64
    first, second = [roll_lanes(chunk, 64) for chunk in pair]
    if sign > 0:
        return [jnp.where(low, first, second), jnp.where(low, second, pltpu.roll(first, 4, 0))]
    return [jnp.where(low, pltpu.roll(second, 4, 0), first), jnp.where(low, first, second)]


def pack_pair(value):
    return [
        jnp.concatenate([value[:, c * 128:c * 128 + 128], value[:, 256 + c * 128:384 + c * 128]], axis=0)
        for c in range(2)
    ]


def halo_pair(ref, index):
    top = row_iota() < 4
    pair = []
    for c in range(2):
        low = jnp.broadcast_to(ref[index, c:c + 1, :], (8, LANES))
        high = jnp.broadcast_to(ref[index, 2 + c:3 + c, :], (8, LANES))
        pair.append(jnp.where(top, low, high))
    return pair


def load_matrix(read):
    real = [[read(3 * i + j) for j in range(3)] for i in range(3)]
    imag = [[read(9 + 3 * i + j) for j in range(3)] for i in range(3)]
    return (real, imag, 1)


def dagger(matrix):
    real, imag, sign = matrix
    return (
        [[real[j][i] for j in range(3)] for i in range(3)],
        [[imag[j][i] for j in range(3)] for i in range(3)],
        -sign,
    )


def total(terms, signs):
    value = None
    for term, sign in zip(terms, signs):
        if value is None:
            value = term if sign > 0 else -term
        else:
            value = value + term if sign > 0 else value - term
    return value


def mat_mul(left, right):
    lr, li, ls = left
    rr, ri, rs = right
    same = ls == rs
    height = len(lr)
    real = [[None] * 3 for _ in range(height)]
    imag = [[None] * 3 for _ in range(height)]
    for i in range(height):
        for j in range(3):
            real[i][j] = total(
                [lr[i][k] * rr[k][j] for k in range(3)] + [li[i][k] * ri[k][j] for k in range(3)],
                [1, 1, 1] + [-1 if same else 1] * 3,
            )
            imag[i][j] = total(
                [lr[i][k] * ri[k][j] for k in range(3)] + [li[i][k] * rr[k][j] for k in range(3)],
                [1, 1, 1] + [1 if same else -1] * 3,
            )
    return (real, imag, ls if same else rs)


def imag_of(matrix, i, j):
    return matrix[1][i][j] if matrix[2] > 0 else -matrix[1][i][j]


def store_matrix(matrix, write):
    for i in range(3):
        for j in range(3):
            write(3 * i + j, matrix[0][i][j])
            write(9 + 3 * i + j, imag_of(matrix, i, j))


def two_rows(read):
    real = [[read(3 * i + j) for j in range(3)] for i in range(2)]
    imag = [[read(6 + 3 * i + j) for j in range(3)] for i in range(2)]
    return (real, imag, 1)


def store_rows(matrix, write):
    for i in range(2):
        for j in range(3):
            write(3 * i + j, matrix[0][i][j])
            write(6 + 3 * i + j, imag_of(matrix, i, j))


def special(matrix):
    real, imag, _ = matrix
    last_r, last_i = [], []
    for k in range(3):
        i, j = (k + 1) % 3, (k + 2) % 3
        last_r.append(
            (real[0][i] * real[1][j] - imag[0][i] * imag[1][j])
            - (real[0][j] * real[1][i] - imag[0][j] * imag[1][i])
        )
        last_i.append(
            (real[0][j] * imag[1][i] + imag[0][j] * real[1][i])
            - (real[0][i] * imag[1][j] + imag[0][i] * real[1][j])
        )
    return (real + [last_r], imag + [last_i], 1)


def anti_parts(matrix):
    parts = [2.0 * imag_of(matrix, i, i) for i in range(3)]
    for i, j in ((0, 1), (0, 2), (1, 2)):
        parts.append(matrix[0][i][j] - matrix[0][j][i])
        parts.append(imag_of(matrix, i, j) + imag_of(matrix, j, i))
    return parts


def anti_matrix(parts):
    zero = jnp.zeros_like(parts[0])
    real = [[zero, parts[3], parts[5]], [-parts[3], zero, parts[7]], [-parts[5], -parts[7], zero]]
    imag = [[parts[0], parts[4], parts[6]], [parts[4], parts[1], parts[8]], [parts[6], parts[8], parts[2]]]
    return real, imag


def anti_mul(parts, right):
    real, imag = anti_matrix(parts)
    rr, ri, _ = right
    out_r = [[None] * 3 for _ in range(3)]
    out_i = [[None] * 3 for _ in range(3)]
    for i in range(3):
        for j in range(3):
            value_r = -(imag[i][i] * ri[i][j])
            value_i = imag[i][i] * rr[i][j]
            for k in range(3):
                if k != i:
                    value_r = value_r + real[i][k] * rr[k][j] - imag[i][k] * ri[k][j]
                    value_i = value_i + real[i][k] * ri[k][j] + imag[i][k] * rr[k][j]
            out_r[i][j] = value_r
            out_i[i][j] = value_i
    return (out_r, out_i, 1)


def pack_links(links_ref, dense):
    def body(mu, carry):
        for e, (c, i, j) in enumerate(ENTRIES):
            low, high = pack_pair(links_ref[mu, c, i, j, 0].astype(F32))
            dense[mu, e, 0] = low
            dense[mu, e, 1] = high
        return carry

    lax.fori_loop(0, 4, body, 0)


def face_kernel(links_ref, up_ref, down_ref, dense, edges, staples, slab, moved, rows):
    pack_links(links_ref, dense)

    def shift_body(e, carry):
        pair = [dense[3, e, 0], dense[3, e, 1]]
        for mu in range(3):
            low, high = dense_shift(pair, mu, 1)
            moved[mu, e, 0] = low
            moved[mu, e, 1] = high
        return carry

    lax.fori_loop(0, 18, shift_body, 0, unroll=6)

    def staple_body(step, carry):
        mu = step // 2
        c = step % 2
        u_mu = load_matrix(lambda e: dense[mu, e, c])
        u_t = load_matrix(lambda e: dense[3, e, c])
        edge = mat_mul(u_mu, load_matrix(lambda e: moved[mu, e, c]))

        def write_edge(e, value):
            edges[mu, e, c] = value

        store_matrix(edge, write_edge)

        def write(e, value):
            staples[mu, e, c] = value
            rows[16 + mu * 18 + e, pl.ds(c, 1)] = value[3:4]
            rows[16 + mu * 18 + e, pl.ds(2 + c, 1)] = value[7:8]

        store_matrix(mat_mul(dagger(edge), u_t), write)
        return carry

    lax.fori_loop(0, 6, staple_body, 0, unroll=2)

    def slab_body(c, carry):
        u_t = load_matrix(lambda e: dense[3, e, c])
        ahead = load_matrix(lambda e: pltpu.roll(dense[3, e, c], 7, 0))
        two = mat_mul(u_t, ahead)
        later = tuple(
            [[pltpu.roll(part[i][j], 6, 0) for j in range(3)] for i in range(3)] for part in two[:2]
        ) + (two[2],)
        four = mat_mul((two[0][:2], two[1][:2], two[2]), later)

        def write(e, value):
            slab[e, pl.ds(c, 1)] = value[0:1]
            slab[e, pl.ds(2 + c, 1)] = value[4:5]
            rows[e, pl.ds(c, 1)] = value[0:1]
            rows[e, pl.ds(2 + c, 1)] = value[4:5]

        store_rows(four, write)
        return carry

    lax.fori_loop(0, 2, slab_body, 0)
    for q in range(4):
        up_ref[:, q * 128:q * 128 + 128] = rows[:, q, :].astype(BF16)

    def down_body(e, carry):
        for mu in range(3):
            for c in range(2):
                value = dense[mu, e, c]
                rows[16 + mu * 18 + e, c:c + 1] = value[0:1]
                rows[16 + mu * 18 + e, 2 + c:3 + c] = value[4:5]
        return carry

    lax.fori_loop(0, 18, down_body, 0, unroll=6)
    for q in range(4):
        down_ref[:, q * 128:q * 128 + 128] = rows[:, q, :].astype(BF16)


def block_kernel(
    widths, place_ref, up_ref, down_ref, slab, w1_ref, w2_ref, w3_ref, w4_ref, after_ref, block_ref, other, block
):
    even = place_ref[0] % 2 == 0
    up = up_ref[0:16].astype(F32)
    down = down_ref[0:16].astype(F32)
    for q in range(4):
        lanes = slice(q * 128, q * 128 + 128)
        other[:, q, :] = jnp.where(even, down[0:12, lanes], up[0:12, lanes])
    first = two_rows(lambda e: jnp.where(even, slab[e], other[e]))
    second = special(two_rows(lambda e: jnp.where(even, other[e], slab[e])))

    def write(e, value):
        block[2 * e:2 * e + 2, :] = jnp.where(even, value[0:2], value[2:4])

    store_rows(mat_mul(first, second), write)
    block[SLABROWS:BLOCKROWS] = jnp.zeros((BLOCKROWS - SLABROWS, LANES), F32)
    offset = 0
    for ref, width in zip((w2_ref, w3_ref, w1_ref, w4_ref), widths):
        flat = ref[...].astype(F32)
        for r in range(27):
            block[SLABROWS + r:SLABROWS + r + 1, offset:offset + width] = (
                flat[width * r:width * r + width].reshape(1, width)
            )
        offset += width
    value = block[...].astype(BF16)
    for d in range(block_ref.shape[0]):
        block_ref[d] = value


def put_row(rows, channel, c, value):
    for t in range(4):
        rows[t, c, pl.ds(channel, 1), :] = value[t:t + 1]
        rows[t, 2 + c, pl.ds(channel, 1), :] = value[4 + t:5 + t]


def sum_at(mu, e, c):
    return (mu * 18 + e) * 2 + c


def force_at(mu, e, c):
    return 108 + (mu * 9 + e) * 2 + c


def space_kernel(dense, time_staples, state, moved, staples):
    state[108:180] = jnp.zeros((72, 8, LANES), F32)
    steps = row_iota() % 4

    def shift_body(e, carry):
        for nu in range(3):
            pair = [dense[nu, e, 0], dense[nu, e, 1]]
            for mu in range(3):
                if mu != nu:
                    low, high = dense_shift(pair, mu, 1)
                    moved[mu, nu, e, 0] = low
                    moved[mu, nu, e, 1] = high
        return carry

    lax.fori_loop(0, 18, shift_body, 0, unroll=6)

    def plane_body(step, carry):
        plane = step // 2
        c = step % 2
        mu = jnp.where(plane == 2, 1, 0)
        nu = jnp.where(plane == 0, 1, 2)
        u_mu = load_matrix(lambda e: dense[mu, e, c])
        u_nu = load_matrix(lambda e: dense[nu, e, c])
        one = mat_mul(u_mu, load_matrix(lambda e: moved[mu, nu, e, c]))
        two = mat_mul(u_nu, load_matrix(lambda e: moved[nu, mu, e, c]))
        loop = mat_mul(one, dagger(two))
        state[PLANE + step] = (loop[0][0][0] + loop[0][1][1] + loop[0][2][2]) / 3.0
        for e, part in enumerate(anti_parts(loop)):
            state[force_at(mu, e, c)] += part
            state[force_at(nu, e, c)] -= part

        def write_mu(e, value):
            staples[mu, nu, e, c] = value

        def write_nu(e, value):
            staples[nu, mu, e, c] = value

        store_matrix(mat_mul(dagger(one), u_nu), write_mu)
        store_matrix(mat_mul(dagger(two), u_mu), write_nu)
        return carry

    lax.fori_loop(0, 6, plane_body, 0, unroll=2)

    def lower_body(e, carry):
        for mu in range(3):
            acc = [jnp.where(steps == 0, 0.0, pltpu.roll(time_staples[mu, e, c], 1, 0)) for c in range(2)]
            for nu in range(3):
                if nu != mu:
                    pair = dense_shift([staples[mu, nu, e, 0], staples[mu, nu, e, 1]], nu, -1)
                    acc = [acc[c] + pair[c] for c in range(2)]
            state[sum_at(mu, e, 0)] = acc[0]
            state[sum_at(mu, e, 1)] = acc[1]
        return carry

    lax.fori_loop(0, 18, lower_body, 0, unroll=6)


def time_kernel(
    code_ref, dense, edges, state, cot_ref, up_ref, down_ref,
    fm_ref, planes_ref, moves_ref,
    cots, gates, moved, staples, sums, halo_up, halo_down, forces, rows,
):
    for q in range(4):
        halo_up[:, q, :] = up_ref[:, q * 128:q * 128 + 128].astype(F32)
        halo_down[:, q, :] = down_ref[:, q * 128:q * 128 + 128].astype(F32)
    rows[...] = jnp.zeros_like(rows)
    pack_links(cot_ref, cots)
    lanes = lane_iota(8)
    site_steps = row_iota() % 4
    colour = (lanes // 64 + lanes // 8 % 8 + lanes % 8 + site_steps) % 2
    code = jnp.zeros_like(site_steps)
    for t in range(4):
        code = jnp.where(site_steps == t, code_ref[0, t], code)
    for mu in range(4):
        active = jnp.logical_and(colour == code % 2, jnp.right_shift(code, mu + 1) % 2 == 1)
        gates[mu] = jnp.where(active, 1.0, 0.0)
    for channel, plane in ((0, 0), (1, 1), (3, 2)):
        for c in range(2):
            put_row(rows, channel, c, state[PLANE + 2 * plane + c])
    for mu in range(4):
        for e in range(9):
            for c in range(2):
                forces[mu, e, c] = state[force_at(mu, e, c)]
    steps = row_iota() % 4

    def shift_body(e, carry):
        for nu in range(3):
            halo = halo_pair(halo_down, 16 + nu * 18 + e)
            below = halo_pair(halo_up, 16 + nu * 18 + e)
            for c in range(2):
                moved[nu, e, c] = jnp.where(steps == 3, halo[c], pltpu.roll(dense[nu, e, c], 7, 0))
                sums[nu, e, c] = state[sum_at(nu, e, c)] + jnp.where(steps == 0, below[c], 0.0)
        return carry

    lax.fori_loop(0, 18, shift_body, 0, unroll=6)

    def plane_body(step, carry):
        mu = step // 2
        c = step % 2
        one = load_matrix(lambda e: edges[mu, e, c])
        two = mat_mul(load_matrix(lambda e: dense[3, e, c]), load_matrix(lambda e: moved[mu, e, c]))
        loop = mat_mul(one, dagger(two))
        put_row(rows, jnp.where(mu == 0, 2, mu + 3), c, (loop[0][0][0] + loop[0][1][1] + loop[0][2][2]) / 3.0)
        for e, part in enumerate(anti_parts(loop)):
            forces[mu, e, c] += part
            forces[3, e, c] -= part

        def write(e, value):
            staples[mu, e, c] = value

        store_matrix(mat_mul(dagger(two), load_matrix(lambda e: dense[mu, e, c])), write)
        return carry

    lax.fori_loop(0, 6, plane_body, 0, unroll=2)

    def lower_body(e, carry):
        acc = None
        for mu in range(3):
            pair = dense_shift([staples[mu, e, 0], staples[mu, e, 1]], mu, -1)
            acc = pair if acc is None else [acc[c] + pair[c] for c in range(2)]
        sums[3, e, 0] = acc[0]
        sums[3, e, 1] = acc[1]
        return carry

    lax.fori_loop(0, 18, lower_body, 0, unroll=6)

    def force_body(step, carry):
        mu = step // 2
        c = step % 2
        current = load_matrix(lambda e: dense[mu, e, c])
        omega = mat_mul(current, load_matrix(lambda e: sums[mu, e, c]))
        parts = [part + forces[mu, e, c] for e, part in enumerate(anti_parts(omega))]
        mean = (parts[0] + parts[1] + parts[2]) * (1.0 / 3.0)
        parts = [parts[e] - mean if e < 3 else parts[e] for e in range(9)]
        parts = [part * (1.0 / 12.0) for part in parts]
        applied = anti_mul(parts, current)
        twice = anti_mul(parts, applied)
        gate = gates[mu]
        slope = jnp.zeros_like(gate)
        curve = jnp.zeros_like(gate)
        for e, (part, i, j) in enumerate(ENTRIES):
            weight = cots[mu, e, c]
            slope = slope + weight * applied[part][i][j]
            curve = curve + weight * twice[part][i][j]
            moves_ref[0, mu, e, c] = (gate * applied[part][i][j]).astype(BF16)
            moves_ref[1, mu, e, c] = (gate * twice[part][i][j]).astype(BF16)
        put_row(rows, 8 + mu, c, gate * slope)
        put_row(rows, 12 + mu, c, gate * curve)
        return carry

    lax.fori_loop(0, 8, force_body, 0, unroll=2)
    for t in range(4):
        for q in range(4):
            value = rows[t, q]
            fm_ref[t, :, q * 128:q * 128 + 128] = value.astype(BF16)
            planes_ref[t, :, q * 128:q * 128 + 128] = value[0:8].astype(BF16)


def selectors():
    row = lax.broadcasted_iota(jnp.int32, (432, 72), 0)
    col = lax.broadcasted_iota(jnp.int32, (432, 72), 1)
    group = row // 12
    spread = (group // 4 * 8 + group % 4 == col).astype(F32).astype(BF16)
    keep = (
        lax.broadcasted_iota(jnp.int32, (432, H), 1) // 4 == lax.broadcasted_iota(jnp.int32, (432, H), 0) % 12
    )
    return spread, keep


def panel_kernel(gathered_ref, weights_ref, loops_ref, p1_ref, p2_ref, p3_ref, p4_ref, b2_ref, b3_ref, b4_ref, weights):
    count = gathered_ref.shape[0]

    def read(chip):
        low = gathered_ref[2 * chip].astype(F32)
        high = gathered_ref[2 * chip + 1].astype(F32)
        return special(
            two_rows(lambda e: jnp.concatenate([low[2 * e:2 * e + 2], high[2 * e:2 * e + 2]], axis=0))
        )

    def flat(matrix):
        return tuple(matrix[0][i][j] for i in range(3) for j in range(3)) + tuple(
            imag_of(matrix, i, j) for i in range(3) for j in range(3)
        )

    def chain(chip, state):
        return flat(mat_mul(load_matrix(lambda e: state[e]), read(chip)))

    state = lax.fori_loop(1, count // 2, chain, flat(read(0)))
    loops_ref[0] = (state[0] + state[4] + state[8]) / 3.0
    loops_ref[1] = (state[9] + state[13] + state[17]) / 3.0

    if weights_ref is None:
        for d in range(count):
            block = gathered_ref[d].astype(F32)
            weights[27 * d:27 * d + 27, :] = block[SLABROWS:SLABROWS + 27]
    else:
        weights[...] = weights_ref[...].astype(F32)
    for k in range(TAPS):
        rows = slice(H * k, H * k + H)
        back = slice(H * SWAP[k], H * SWAP[k] + H)
        p2_ref[:, rows] = weights[rows, 0:48].astype(BF16)
        p3_ref[:, rows] = weights[rows, 48:96].astype(BF16)
        p1_ref[:, 8 * k:8 * k + 8] = weights[rows, 96:104].astype(BF16)
        turned = weights[back, :].T
        b2_ref[:, rows] = turned[0:48].astype(BF16)
        b3_ref[:, rows] = turned[48:96].astype(BF16)
    spread, keep = selectors()
    place = (
        lax.broadcasted_iota(jnp.int32, (LANES, H), 0) == 104 + lax.broadcasted_iota(jnp.int32, (LANES, H), 1) % 4
    ).astype(F32).astype(BF16)
    wide = jnp.dot(weights[...].astype(BF16), place, preferred_element_type=F32)
    wide = jnp.where(keep, wide, 0.0).astype(BF16)
    last = lax.dot_general(spread, wide, (((0,), (0,)), ((), ())), preferred_element_type=F32)
    p4_ref[...] = last.astype(BF16)
    for k in range(TAPS):
        b4_ref[:, 8 * k:8 * k + 8] = last[8 * SWAP[k]:8 * SWAP[k] + 8, :].T.astype(BF16)


def panel_kernel_plain(gathered_ref, *rest):
    panel_kernel(gathered_ref, None, *rest)


def chunks_of(value):
    return [value[:, q * 128:q * 128 + 128] for q in range(4)]


def one_shift(chunks, position):
    if position == 0:
        return chunks
    lanes = lane_iota(chunks[0].shape[0])
    sign = 1 if position % 2 == 1 else -1
    if position > 4:
        return [shift_z(chunk, sign, lanes) for chunk in chunks]
    if position > 2:
        return [shift_y(chunk, sign, lanes) for chunk in chunks]
    low = lanes < 64
    rolled = [roll_lanes(chunk, 64) for chunk in chunks]
    if sign > 0:
        return [jnp.where(low, rolled[q], rolled[(q + 1) % 4]) for q in range(4)]
    return [jnp.where(low, rolled[(q + 3) % 4], rolled[q]) for q in range(4)]


def all_shifts(chunks):
    lanes = lane_iota(chunks[0].shape[0])
    y = lanes // 8 % 8
    z = lanes % 8
    low = lanes < 64
    half = [roll_lanes(chunk, 64) for chunk in chunks]
    return [
        chunks,
        [jnp.where(low, half[q], half[(q + 1) % 4]) for q in range(4)],
        [jnp.where(low, half[(q + 3) % 4], half[q]) for q in range(4)],
        [roll_lanes(jnp.where(y == 0, half[q], chunks[q]), -8) for q in range(4)],
        [roll_lanes(jnp.where(y == 7, half[q], chunks[q]), 8) for q in range(4)],
        [roll_lanes(jnp.where(z == 0, roll_lanes(chunk, 8), chunk), -1) for chunk in chunks],
        [roll_lanes(jnp.where(z == 7, roll_lanes(chunk, -8), chunk), 1) for chunk in chunks],
    ]


def span(slice_index, count=1):
    if isinstance(slice_index, int):
        return slice(slice_index * SITES, (slice_index + count) * SITES)
    return pl.ds(pl.multiple_of(slice_index * SITES, SITES), count * SITES)


def slot_of(slot):
    return slice(slot * SITES, (slot + 1) * SITES)


def stack_wide(source, target, index, slot):
    chunks = chunks_of(source[:, span(index)])
    for position, shifted in enumerate(all_shifts(chunks)):
        for q in range(4):
            lanes = slice(slot * SITES + q * 128, slot * SITES + q * 128 + 128)
            target[H * position:H * position + H, lanes] = shifted[q]
    target[7 * H:8 * H, slot_of(slot)] = source[:, span(index + 1)]
    target[8 * H:9 * H, slot_of(slot)] = source[:, span(index - 1)]


def stack_thin(source, target, index, slot):
    chunks = chunks_of(source[:, span(index)])
    ahead = chunks_of(source[:, span(index + 1)])
    behind = chunks_of(source[:, span(index - 1)])
    columns = all_shifts(chunks) + [ahead, behind]
    for q in range(4):
        lanes = slice(slot * SITES + q * 128, slot * SITES + q * 128 + 128)
        target[0:72, lanes] = jnp.concatenate([column[q] for column in columns], axis=0).astype(BF16)


def one_minus_square(value):
    value = value.astype(F32)
    return 1.0 - value * value


def conv_kernel(
    split, place_ref, fm_ref, near_ref, far_ref, near_chip_ref, far_chip_ref, loops_ref,
    p1_ref, p2_ref, p3_ref, p4_ref, b2_ref, b3_ref, b4_ref,
    coeff_ref, grads_ref,
    feats, mixed, h1, h2, h3, parts, lasts, g3, g2, g1, wide, wide_back, wide_first, thin, thin_back, packed,
):
    row8 = lax.broadcasted_iota(jnp.int32, (8, SITES), 0)
    loop_re = jnp.concatenate([loops_ref[0, q:q + 1, :] for q in range(4)], axis=1)
    loop_im = jnp.concatenate([loops_ref[1, q:q + 1, :] for q in range(4)], axis=1)
    loops = jnp.where(row8 == 6, loop_re, jnp.where(row8 == 7, loop_im, 0.0))
    loops = loops.astype(BF16).astype(F32)
    first_core = place_ref[0] % 2 == 0
    first_chip = place_ref[0] // 2 % 2 == 0
    for j in range(4):
        near, far = near_chip_ref[j].astype(F32), far_chip_ref[j].astype(F32)
        if j > 0:
            feats[:, span(j - 1)] = jnp.where(first_chip, far, near) + loops
        if j < 3:
            feats[:, span(15 + j)] = jnp.where(first_chip, near, far) + loops
        near, far = near_ref[j].astype(F32), far_ref[j].astype(F32)
        below, above = jnp.where(first_core, far, near), jnp.where(first_core, near, far)
        for base, value in ((3, below), (7, fm_ref[j].astype(F32)), (11, above)):
            feats[:, span(base + j)] = value[0:8] + loops
            mixed[:, span(base + j)] = value[8:16]

    own = span(7, 4)
    contract = (((1,), (1,)), ((), ()))

    def own_slot(index, others):
        return index - 7 if 7 <= index < 11 else 4 + others.index(index)

    def dot(weights, stack, slot):
        return jnp.dot(weights[...], stack[:, slot_of(slot)], preferred_element_type=F32)

    def first_dot(index):
        h1[:, span(index)] = jnp.tanh(dot(p1_ref, thin, index % 4)).astype(BF16)

    def second_dot(index):
        h2[:, span(index)] = jnp.tanh(dot(p2_ref, wide, index % 2)).astype(BF16)

    def third_dot(index):
        h3[:, span(index)] = jnp.tanh(dot(p3_ref, wide, 2 + index % 2)).astype(BF16)

    def taps_of(index):
        taps = jnp.dot(p4_ref[...], h3[:, span(index)], preferred_element_type=F32)
        acc = None
        for position in range(7):
            shifted = one_shift(chunks_of(taps[8 * position:8 * position + 8]), position)
            acc = shifted if acc is None else [a + b for a, b in zip(acc, shifted)]
        parts[0, :, span(index)] = jnp.concatenate(acc, axis=1)
        parts[1, :, span(index)] = taps[56:64]
        parts[2, :, span(index)] = taps[64:72]

    def last_of(index):
        coeff = jnp.tanh(parts[0, :, span(index)] + parts[1, :, span(index + 1)] + parts[2, :, span(index - 1)])
        blend = mixed[:, span(index)]
        value = (blend + coeff * pltpu.roll(blend, 4, 0)) * (1.0 - coeff * coeff)
        lasts[:, span(index)] = jnp.where(row8 < 4, value, 0.0).astype(BF16).astype(F32)
        if 7 <= index < 11:
            coeff_ref[index - 7] = coeff

    halo3, halo2 = (5, 6, 11, 12), (6, 11)

    def back_third(index):
        out = dot(b4_ref, thin_back, own_slot(index, halo3))
        g3[:, span(index)] = (out * one_minus_square(h3[:, span(index)])).astype(BF16)

    def back_second(index):
        out = dot(b3_ref, wide_back, own_slot(index, halo2))
        g2[:, span(index)] = (out * one_minus_square(h2[:, span(index)])).astype(BF16)

    def back_first(index):
        out = dot(b2_ref, wide_first, index - 7)
        g1[:, slot_of(index - 7)] = (out * one_minus_square(h1[:, span(index)])).astype(BF16)

    stages = (
        (0, 1, 17, lambda i: stack_thin(feats, thin, i, i % 4)),
        (1, 1, 17, first_dot),
        (3, 2, 16, lambda i: stack_wide(h1, wide, i, i % 2)),
        (4, 2, 16, second_dot),
        (6, 3, 15, lambda i: stack_wide(h2, wide, i, 2 + i % 2)),
        (7, 3, 15, third_dot),
        (8, 3, 15, taps_of),
        (10, 4, 14, last_of),
        (12, 5, 13, lambda i: stack_thin(lasts, thin_back, i, own_slot(i, halo3))),
        (13, 5, 13, back_third),
        (15, 6, 12, lambda i: stack_wide(g3, wide_back, i, own_slot(i, halo2))),
        (16, 6, 12, back_second),
        (18, 7, 11, lambda i: stack_wide(g2, wide_first, i, i - 7)),
        (19, 7, 11, back_first),
    )
    for step in range(1, 30):
        for delay, low, high, task in reversed(stages):
            if low <= step - delay < high:
                task(step - delay)
        if step == 18:
            for index in (7, 8, 9, 10):
                stack_thin(feats, thin, index, index - 7)
        if step == 23:
            grad_last = lax.dot_general(
                thin_back[:, 0:4 * SITES], h3[:, own], contract, preferred_element_type=F32
            )
            spread, keep = selectors()
            ordered = jnp.concatenate([grad_last[8 * SWAP[k]:8 * SWAP[k] + 8] for k in range(TAPS)], axis=0)
            broad = jnp.dot(spread, ordered.astype(BF16), preferred_element_type=F32)
        if step == 24:
            broad = jnp.where(keep, broad, 0.0).astype(BF16)
            place = (
                lax.broadcasted_iota(jnp.int32, (H, LANES), 1)
                == 104 + lax.broadcasted_iota(jnp.int32, (H, LANES), 0) % 4
            ).astype(F32).astype(BF16)
            packed[...] = jnp.dot(broad, place, preferred_element_type=F32)
        if step == 26:
            grad_third = lax.dot_general(
                wide_back[:, 0:4 * SITES], h2[:, own], contract, preferred_element_type=F32
            )
        if step == 27:
            for k in range(TAPS):
                packed[H * k:H * k + H, 48:96] = grad_third[H * SWAP[k]:H * SWAP[k] + H]
    grad_second = lax.dot_general(wide_first[...], h1[:, own], contract, preferred_element_type=F32)
    grad_first = lax.dot_general(g1[...], thin[...], contract, preferred_element_type=F32)
    for k in range(TAPS):
        rows = slice(H * k, H * k + H)
        packed[rows, 0:48] = grad_second[H * SWAP[k]:H * SWAP[k] + H]
        packed[rows, 96:104] = grad_first[:, 8 * k:8 * k + 8]
    if split:
        for d in range(16):
            grads_ref[d] = packed[27 * d:27 * d + 27, :].astype(BF16)
    else:
        grads_ref[...] = packed[...].astype(BF16)


def update_kernel(dense, moves_ref, coeff_ref, out_ref, factors):
    for mu in range(4):
        for t in range(4):
            for c in range(2):
                factors[mu, c, t:t + 1, :] = coeff_ref[t, mu:mu + 1, c * 128:c * 128 + 128]
                factors[mu, c, 4 + t:5 + t, :] = coeff_ref[t, mu:mu + 1, 256 + c * 128:384 + c * 128]

    def body(mu, carry):
        factor = [factors[mu, c] for c in range(2)]
        half = [0.5 * value * value for value in factor]
        for e, (part, i, j) in enumerate(ENTRIES):
            new = [
                dense[mu, e, c]
                + factor[c] * moves_ref[0, mu, e, c].astype(F32)
                + half[c] * moves_ref[1, mu, e, c].astype(F32)
                for c in range(2)
            ]
            out_ref[mu, part, i, j, 0] = jnp.concatenate(
                [new[0][0:4], new[1][0:4], new[0][4:8], new[1][4:8]], axis=1
            )
        return carry

    lax.fori_loop(0, 4, body, 0)


def sum_kernel(widths, parts_ref, first_ref, second_ref, third_ref, last_ref):
    value = parts_ref[0].astype(F32)
    for d in range(1, parts_ref.shape[0]):
        value = value + parts_ref[d].astype(F32)
    offset = 0
    for ref, width in zip((second_ref, third_ref, first_ref, last_ref), widths):
        for r in range(27):
            ref[:, width * r:width * r + width] = value[r:r + 1, offset:offset + width]
        offset += width


def call(body, outs, scratch, places=None, cost=None, limit=LIMIT):
    specs = {}
    if places is not None:
        specs["in_specs"] = [pl.BlockSpec(memory_space=place) for place in places]
    return pl.pallas_call(
        body,
        out_shape=[jax.ShapeDtypeStruct(shape, dtype) for shape, dtype in outs],
        scratch_shapes=[pltpu.VMEM(*item) if isinstance(item, tuple) else item for item in scratch],
        compiler_params=pltpu.CompilerParams(vmem_limit_bytes=limit),
        cost_estimate=cost,
        **specs,
    )


def on_device(links, cotangent, parity, link_subset, w_first, w_second, w_third, w_last):
    count = lax.axis_size("tm")

    def send(value, distance):
        return lax.ppermute(value, "tm", [(i, (i + distance) % count) for i in range(count)])

    def swap(value, pairs):
        return lax.ppermute(value, "tm", pairs + [(target, source) for source, target in pairs])

    chips = count // 2
    widths = (768 // count, 768 // count, 128 // count, 64 // count)
    vmem, smem = pltpu.VMEM, pltpu.SMEM
    field = ((4, 18, 2, 8, LANES), F32)
    space = ((3, 18, 2, 8, LANES), F32)
    edge_rows = ((70, SITES), BF16)
    up, down, dense, edges, staples, slab = call(
        face_kernel,
        [edge_rows, edge_rows, field, space, space, ((12, 4, LANES), F32)],
        [space, ((70, 4, LANES), F32)],
    )(links)
    up = send(up, 1)
    down = send(down, -1)
    (state,) = call(
        space_kernel,
        [((186, 8, LANES), F32)],
        [((3, 3, 18, 2, 8, LANES), F32), ((3, 3, 18, 2, 8, LANES), F32)],
        cost=pl.CostEstimate(flops=4_000_000_000, bytes_accessed=16_000_000, transcendentals=0),
    )(dense, staples)
    place = lax.axis_index("tm").astype(jnp.int32)[None]
    (block,) = call(
        functools.partial(block_kernel, widths),
        [((count, BLOCKROWS, LANES), BF16)],
        [((12, 4, LANES), F32), ((BLOCKROWS, LANES), F32)],
        places=(smem,) + (vmem,) * 7 + (pl.ANY,),
    )(place, up, down, slab, w_first, w_second, w_third, w_last, state)
    gathered = lax.all_to_all(block, "tm", split_axis=0, concat_axis=0, tiled=True)
    fm, planes, moves = call(
        time_kernel,
        [
            ((4, 16, SITES), BF16), ((4, 8, SITES), BF16),
            ((2, 4, 18, 2, 8, LANES), BF16),
        ],
        [
            field, ((4, 8, LANES), F32), space, space, field, ((70, 4, LANES), F32), ((70, 4, LANES), F32),
            ((4, 9, 2, 8, LANES), F32), ((4, 4, 16, LANES), F32),
        ],
        places=(smem,) + (vmem,) * 6,
    )(parity + 2 * link_subset, dense, edges, state, cotangent, up, down)
    far_chip = swap(planes, [(2 * c + k, (2 * c + 2 + k) % count) for c in range(1, chips, 2) for k in range(2)])
    far_core = swap(fm, [(i, (i + 1) % count) for i in range(1, count, 2)])
    near_chip = swap(planes, [(2 * c + k, 2 * c + 2 + k) for c in range(0, chips, 2) for k in range(2)])
    near_core = swap(fm, [(i, i + 1) for i in range(0, count, 2)])

    panel_outs = [
        ((2, 4, LANES), F32), ((H, 72), BF16), ((H, 432), BF16), ((H, 432), BF16), ((72, H), BF16),
        ((H, 432), BF16), ((H, 432), BF16), ((H, 72), BF16),
    ]
    panel_scratch = [((432, LANES), F32)]
    if count == 16:
        loops, p1, p2, p3, p4, b2, b3, b4 = call(panel_kernel_plain, panel_outs, panel_scratch)(gathered)
    else:
        pieces = []
        offset = 0
        for width, full in zip(widths, (48, 48, 8, 4)):
            piece = gathered[:, SLABROWS:SLABROWS + 27, offset:offset + width]
            pieces.append(piece.reshape(432, full))
            offset += width
        pieces.append(jnp.zeros((432, 20), BF16))
        loops, p1, p2, p3, p4, b2, b3, b4 = call(panel_kernel, panel_outs, panel_scratch)(
            gathered, jnp.concatenate(pieces, axis=1)
        )

    window = 18 * SITES
    coeff, grads = call(
        functools.partial(conv_kernel, count == 16),
        [((4, 8, SITES), F32), ((16, 27, LANES) if count == 16 else (432, LANES), BF16)],
        [
            ((8, window), F32), ((8, window), F32), ((H, window), BF16), ((H, window), BF16), ((H, window), BF16),
            ((3, 8, window), F32), ((8, window), F32), ((H, window), BF16), ((H, window), BF16), ((H, 4 * SITES), BF16),
            ((432, 4 * SITES), BF16), ((432, 6 * SITES), BF16), ((432, 4 * SITES), BF16),
            ((72, 4 * SITES), BF16), ((72, 8 * SITES), BF16), ((432, LANES), F32),
        ],
        limit=20 * 1024 * 1024,
        places=(smem,) + (vmem,) * 13,
    )(place, fm, near_core, far_core, near_chip, far_chip, loops, p1, p2, p3, p4, b2, b3, b4)
    if count != 16:
        offset = 0
        pieces = []
        for width, full in zip(widths, (48, 48, 8, 4)):
            pieces.append(grads[:, offset:offset + full].reshape(count, 27, width))
            offset += full
        grads = jnp.concatenate(pieces, axis=2)
    grads = lax.all_to_all(grads, "tm", split_axis=0, concat_axis=0, tiled=True)
    (new_links,) = call(
        update_kernel, [(links.shape, F32)], [((4, 2, 8, LANES), F32)]
    )(dense, moves, coeff)
    grad_first, grad_second, grad_third, grad_last = call(
        functools.partial(sum_kernel, widths),
        [((1, 27 * width), F32) for width in (widths[2], widths[0], widths[1], widths[3])],
        [],
    )(grads)
    return (new_links, grad_first, grad_second, grad_third, grad_last)


def solution(mesh):
    placed = (
        P(None, None, None, None, "groups", "tm", None),
        P(None, None, None, None, "groups", "tm", None),
        P("groups", "tm"),
        P("groups", "tm"),
        P("tm"),
        P("tm"),
        P("tm"),
        P("tm"),
    )
    return jax.shard_map(
        on_device,
        mesh=mesh,
        in_specs=placed,
        out_specs=(
            P(None, None, None, None, "groups", "tm", None),
            P("groups", "tm"),
            P("groups", "tm"),
            P("groups", "tm"),
            P("groups", "tm"),
        ),
        check_vma=False,
    )
```

```python
import functools

import jax
import jax.numpy as jnp
from jax import lax
from jax.experimental import pallas as pl
from jax.experimental.pallas import tpu as pltpu
from jax.sharding import PartitionSpec as P

F32 = jnp.float32
BF16 = jnp.bfloat16
TAPS = 9
H = 48
LANES = 128
SITES = 512
PAIRS = ((0, 1), (0, 2), (0, 3), (1, 2), (1, 3), (2, 3))
SWAP = (0, 2, 1, 4, 3, 6, 5, 8, 7)
ENTRIES = tuple((c, i, j) for c in range(2) for i in range(3) for j in range(3))
PLANE = 180
SLABROWS = 24
BLOCKROWS = 64
LIMIT = 8 * 1024 * 1024


def lane_iota(rows):
    return lax.broadcasted_iota(jnp.int32, (rows, LANES), 1)


def row_iota():
    return lax.broadcasted_iota(jnp.int32, (8, LANES), 0)


def roll_lanes(value, amount):
    return pltpu.roll(value, amount % LANES, 1)


def shift_z(chunk, sign, lanes):
    z = lanes % 8
    if sign > 0:
        return jnp.where(z == 7, roll_lanes(chunk, 7), roll_lanes(chunk, -1))
    return jnp.where(z == 0, roll_lanes(chunk, -7), roll_lanes(chunk, 1))


def shift_y(chunk, sign, lanes):
    y = lanes // 8 % 8
    if sign > 0:
        return jnp.where(y == 7, roll_lanes(chunk, 56), roll_lanes(chunk, -8))
    return jnp.where(y == 0, roll_lanes(chunk, -56), roll_lanes(chunk, 8))


def dense_shift(pair, axis, sign):
    lanes = lane_iota(8)
    if axis == 2:
        return [shift_z(chunk, sign, lanes) for chunk in pair]
    if axis == 1:
        return [shift_y(chunk, sign, lanes) for chunk in pair]
    low = lanes < 64
    first, second = [roll_lanes(chunk, 64) for chunk in pair]
    if sign > 0:
        return [jnp.where(low, first, second), jnp.where(low, second, pltpu.roll(first, 4, 0))]
    return [jnp.where(low, pltpu.roll(second, 4, 0), first), jnp.where(low, first, second)]


def pack_pair(value):
    return [
        jnp.concatenate([value[:, c * 128:c * 128 + 128], value[:, 256 + c * 128:384 + c * 128]], axis=0)
        for c in range(2)
    ]


def halo_pair(ref, index):
    top = row_iota() < 4
    pair = []
    for c in range(2):
        low = jnp.broadcast_to(ref[index, c:c + 1, :], (8, LANES))
        high = jnp.broadcast_to(ref[index, 2 + c:3 + c, :], (8, LANES))
        pair.append(jnp.where(top, low, high))
    return pair


def load_matrix(read):
    real = [[read(3 * i + j) for j in range(3)] for i in range(3)]
    imag = [[read(9 + 3 * i + j) for j in range(3)] for i in range(3)]
    return (real, imag, 1)


def dagger(matrix):
    real, imag, sign = matrix
    return (
        [[real[j][i] for j in range(3)] for i in range(3)],
        [[imag[j][i] for j in range(3)] for i in range(3)],
        -sign,
    )


def total(terms, signs):
    value = None
    for term, sign in zip(terms, signs):
        if value is None:
            value = term if sign > 0 else -term
        else:
            value = value + term if sign > 0 else value - term
    return value


def mat_mul(left, right):
    lr, li, ls = left
    rr, ri, rs = right
    same = ls == rs
    height = len(lr)
    real = [[None] * 3 for _ in range(height)]
    imag = [[None] * 3 for _ in range(height)]
    for i in range(height):
        for j in range(3):
            real[i][j] = total(
                [lr[i][k] * rr[k][j] for k in range(3)] + [li[i][k] * ri[k][j] for k in range(3)],
                [1, 1, 1] + [-1 if same else 1] * 3,
            )
            imag[i][j] = total(
                [lr[i][k] * ri[k][j] for k in range(3)] + [li[i][k] * rr[k][j] for k in range(3)],
                [1, 1, 1] + [1 if same else -1] * 3,
            )
    return (real, imag, ls if same else rs)


def imag_of(matrix, i, j):
    return matrix[1][i][j] if matrix[2] > 0 else -matrix[1][i][j]


def store_matrix(matrix, write):
    for i in range(3):
        for j in range(3):
            write(3 * i + j, matrix[0][i][j])
            write(9 + 3 * i + j, imag_of(matrix, i, j))


def two_rows(read):
    real = [[read(3 * i + j) for j in range(3)] for i in range(2)]
    imag = [[read(6 + 3 * i + j) for j in range(3)] for i in range(2)]
    return (real, imag, 1)


def store_rows(matrix, write):
    for i in range(2):
        for j in range(3):
            write(3 * i + j, matrix[0][i][j])
            write(6 + 3 * i + j, imag_of(matrix, i, j))


def special(matrix):
    real, imag, _ = matrix
    last_r, last_i = [], []
    for k in range(3):
        i, j = (k + 1) % 3, (k + 2) % 3
        last_r.append(
            (real[0][i] * real[1][j] - imag[0][i] * imag[1][j])
            - (real[0][j] * real[1][i] - imag[0][j] * imag[1][i])
        )
        last_i.append(
            (real[0][j] * imag[1][i] + imag[0][j] * real[1][i])
            - (real[0][i] * imag[1][j] + imag[0][i] * real[1][j])
        )
    return (real + [last_r], imag + [last_i], 1)


def anti_parts(matrix):
    parts = [2.0 * imag_of(matrix, i, i) for i in range(3)]
    for i, j in ((0, 1), (0, 2), (1, 2)):
        parts.append(matrix[0][i][j] - matrix[0][j][i])
        parts.append(imag_of(matrix, i, j) + imag_of(matrix, j, i))
    return parts


def anti_matrix(parts):
    zero = jnp.zeros_like(parts[0])
    real = [[zero, parts[3], parts[5]], [-parts[3], zero, parts[7]], [-parts[5], -parts[7], zero]]
    imag = [[parts[0], parts[4], parts[6]], [parts[4], parts[1], parts[8]], [parts[6], parts[8], parts[2]]]
    return real, imag


def anti_mul(parts, right):
    real, imag = anti_matrix(parts)
    rr, ri, _ = right
    out_r = [[None] * 3 for _ in range(3)]
    out_i = [[None] * 3 for _ in range(3)]
    for i in range(3):
        for j in range(3):
            value_r = -(imag[i][i] * ri[i][j])
            value_i = imag[i][i] * rr[i][j]
            for k in range(3):
                if k != i:
                    value_r = value_r + real[i][k] * rr[k][j] - imag[i][k] * ri[k][j]
                    value_i = value_i + real[i][k] * ri[k][j] + imag[i][k] * rr[k][j]
            out_r[i][j] = value_r
            out_i[i][j] = value_i
    return (out_r, out_i, 1)


def pack_links(links_ref, dense):
    def body(mu, carry):
        for e, (c, i, j) in enumerate(ENTRIES):
            low, high = pack_pair(links_ref[mu, c, i, j, 0].astype(F32))
            dense[mu, e, 0] = low
            dense[mu, e, 1] = high
        return carry

    lax.fori_loop(0, 4, body, 0)


def face_kernel(links_ref, up_ref, down_ref, dense, edges, staples, slab, moved, rows):
    pack_links(links_ref, dense)

    def shift_body(e, carry):
        pair = [dense[3, e, 0], dense[3, e, 1]]
        for mu in range(3):
            low, high = dense_shift(pair, mu, 1)
            moved[mu, e, 0] = low
            moved[mu, e, 1] = high
        return carry

    lax.fori_loop(0, 18, shift_body, 0, unroll=6)

    def staple_body(step, carry):
        mu = step // 2
        c = step % 2
        u_mu = load_matrix(lambda e: dense[mu, e, c])
        u_t = load_matrix(lambda e: dense[3, e, c])
        edge = mat_mul(u_mu, load_matrix(lambda e: moved[mu, e, c]))

        def write_edge(e, value):
            edges[mu, e, c] = value

        store_matrix(edge, write_edge)

        def write(e, value):
            staples[mu, e, c] = value
            rows[16 + mu * 18 + e, pl.ds(c, 1)] = value[3:4]
            rows[16 + mu * 18 + e, pl.ds(2 + c, 1)] = value[7:8]

        store_matrix(mat_mul(dagger(edge), u_t), write)
        return carry

    lax.fori_loop(0, 6, staple_body, 0, unroll=2)

    def slab_body(c, carry):
        u_t = load_matrix(lambda e: dense[3, e, c])
        ahead = load_matrix(lambda e: pltpu.roll(dense[3, e, c], 7, 0))
        two = mat_mul(u_t, ahead)
        later = tuple(
            [[pltpu.roll(part[i][j], 6, 0) for j in range(3)] for i in range(3)] for part in two[:2]
        ) + (two[2],)
        four = mat_mul((two[0][:2], two[1][:2], two[2]), later)

        def write(e, value):
            slab[e, pl.ds(c, 1)] = value[0:1]
            slab[e, pl.ds(2 + c, 1)] = value[4:5]
            rows[e, pl.ds(c, 1)] = value[0:1]
            rows[e, pl.ds(2 + c, 1)] = value[4:5]

        store_rows(four, write)
        return carry

    lax.fori_loop(0, 2, slab_body, 0)
    for q in range(4):
        up_ref[:, q * 128:q * 128 + 128] = rows[:, q, :].astype(BF16)

    def down_body(e, carry):
        for mu in range(3):
            for c in range(2):
                value = dense[mu, e, c]
                rows[16 + mu * 18 + e, c:c + 1] = value[0:1]
                rows[16 + mu * 18 + e, 2 + c:3 + c] = value[4:5]
        return carry

    lax.fori_loop(0, 18, down_body, 0, unroll=6)
    for q in range(4):
        down_ref[:, q * 128:q * 128 + 128] = rows[:, q, :].astype(BF16)


def block_kernel(
    widths, place_ref, up_ref, down_ref, slab, w1_ref, w2_ref, w3_ref, w4_ref, after_ref, block_ref, other, block
):
    even = place_ref[0] % 2 == 0
    up = up_ref[0:16].astype(F32)
    down = down_ref[0:16].astype(F32)
    for q in range(4):
        lanes = slice(q * 128, q * 128 + 128)
        other[:, q, :] = jnp.where(even, down[0:12, lanes], up[0:12, lanes])
    first = two_rows(lambda e: jnp.where(even, slab[e], other[e]))
    second = special(two_rows(lambda e: jnp.where(even, other[e], slab[e])))

    def write(e, value):
        block[2 * e:2 * e + 2, :] = jnp.where(even, value[0:2], value[2:4])

    store_rows(mat_mul(first, second), write)
    block[SLABROWS:BLOCKROWS] = jnp.zeros((BLOCKROWS - SLABROWS, LANES), F32)
    offset = 0
    for ref, width in zip((w2_ref, w3_ref, w1_ref, w4_ref), widths):
        flat = ref[...].astype(F32)
        for r in range(27):
            block[SLABROWS + r:SLABROWS + r + 1, offset:offset + width] = (
                flat[width * r:width * r + width].reshape(1, width)
            )
        offset += width
    value = block[...].astype(BF16)
    for d in range(block_ref.shape[0]):
        block_ref[d] = value


def put_row(rows, channel, c, value):
    for t in range(4):
        rows[t, c, pl.ds(channel, 1), :] = value[t:t + 1]
        rows[t, 2 + c, pl.ds(channel, 1), :] = value[4 + t:5 + t]


def sum_at(mu, e, c):
    return (mu * 18 + e) * 2 + c


def force_at(mu, e, c):
    return 108 + (mu * 9 + e) * 2 + c


def space_kernel(dense, time_staples, state, moved, staples):
    state[108:180] = jnp.zeros((72, 8, LANES), F32)
    steps = row_iota() % 4

    def shift_body(e, carry):
        for nu in range(3):
            pair = [dense[nu, e, 0], dense[nu, e, 1]]
            for mu in range(3):
                if mu != nu:
                    low, high = dense_shift(pair, mu, 1)
                    moved[mu, nu, e, 0] = low
                    moved[mu, nu, e, 1] = high
        return carry

    lax.fori_loop(0, 18, shift_body, 0, unroll=6)

    def plane_body(step, carry):
        plane = step // 2
        c = step % 2
        mu = jnp.where(plane == 2, 1, 0)
        nu = jnp.where(plane == 0, 1, 2)
        u_mu = load_matrix(lambda e: dense[mu, e, c])
        u_nu = load_matrix(lambda e: dense[nu, e, c])
        one = mat_mul(u_mu, load_matrix(lambda e: moved[mu, nu, e, c]))
        two = mat_mul(u_nu, load_matrix(lambda e: moved[nu, mu, e, c]))
        loop = mat_mul(one, dagger(two))
        state[PLANE + step] = (loop[0][0][0] + loop[0][1][1] + loop[0][2][2]) / 3.0
        for e, part in enumerate(anti_parts(loop)):
            state[force_at(mu, e, c)] += part
            state[force_at(nu, e, c)] -= part

        def write_mu(e, value):
            staples[mu, nu, e, c] = value

        def write_nu(e, value):
            staples[nu, mu, e, c] = value

        store_matrix(mat_mul(dagger(one), u_nu), write_mu)
        store_matrix(mat_mul(dagger(two), u_mu), write_nu)
        return carry

    lax.fori_loop(0, 6, plane_body, 0, unroll=2)

    def lower_body(e, carry):
        for mu in range(3):
            acc = [jnp.where(steps == 0, 0.0, pltpu.roll(time_staples[mu, e, c], 1, 0)) for c in range(2)]
            for nu in range(3):
                if nu != mu:
                    pair = dense_shift([staples[mu, nu, e, 0], staples[mu, nu, e, 1]], nu, -1)
                    acc = [acc[c] + pair[c] for c in range(2)]
            state[sum_at(mu, e, 0)] = acc[0]
            state[sum_at(mu, e, 1)] = acc[1]
        return carry

    lax.fori_loop(0, 18, lower_body, 0, unroll=6)


def time_kernel(
    code_ref, dense, edges, state, cot_ref, up_ref, down_ref,
    fm_ref, planes_ref, moves_ref,
    cots, gates, moved, staples, sums, halo_up, halo_down, forces, rows,
):
    for q in range(4):
        halo_up[:, q, :] = up_ref[:, q * 128:q * 128 + 128].astype(F32)
        halo_down[:, q, :] = down_ref[:, q * 128:q * 128 + 128].astype(F32)
    rows[...] = jnp.zeros_like(rows)
    pack_links(cot_ref, cots)
    lanes = lane_iota(8)
    site_steps = row_iota() % 4
    colour = (lanes // 64 + lanes // 8 % 8 + lanes % 8 + site_steps) % 2
    code = jnp.zeros_like(site_steps)
    for t in range(4):
        code = jnp.where(site_steps == t, code_ref[0, t], code)
    for mu in range(4):
        active = jnp.logical_and(colour == code % 2, jnp.right_shift(code, mu + 1) % 2 == 1)
        gates[mu] = jnp.where(active, 1.0, 0.0)
    for channel, plane in ((0, 0), (1, 1), (3, 2)):
        for c in range(2):
            put_row(rows, channel, c, state[PLANE + 2 * plane + c])
    for mu in range(4):
        for e in range(9):
            for c in range(2):
                forces[mu, e, c] = state[force_at(mu, e, c)]
    steps = row_iota() % 4

    def shift_body(e, carry):
        for nu in range(3):
            halo = halo_pair(halo_down, 16 + nu * 18 + e)
            below = halo_pair(halo_up, 16 + nu * 18 + e)
            for c in range(2):
                moved[nu, e, c] = jnp.where(steps == 3, halo[c], pltpu.roll(dense[nu, e, c], 7, 0))
                sums[nu, e, c] = state[sum_at(nu, e, c)] + jnp.where(steps == 0, below[c], 0.0)
        return carry

    lax.fori_loop(0, 18, shift_body, 0, unroll=6)

    def plane_body(step, carry):
        mu = step // 2
        c = step % 2
        one = load_matrix(lambda e: edges[mu, e, c])
        two = mat_mul(load_matrix(lambda e: dense[3, e, c]), load_matrix(lambda e: moved[mu, e, c]))
        loop = mat_mul(one, dagger(two))
        put_row(rows, jnp.where(mu == 0, 2, mu + 3), c, (loop[0][0][0] + loop[0][1][1] + loop[0][2][2]) / 3.0)
        for e, part in enumerate(anti_parts(loop)):
            forces[mu, e, c] += part
            forces[3, e, c] -= part

        def write(e, value):
            staples[mu, e, c] = value

        store_matrix(mat_mul(dagger(two), load_matrix(lambda e: dense[mu, e, c])), write)
        return carry

    lax.fori_loop(0, 6, plane_body, 0, unroll=2)

    def lower_body(e, carry):
        acc = None
        for mu in range(3):
            pair = dense_shift([staples[mu, e, 0], staples[mu, e, 1]], mu, -1)
            acc = pair if acc is None else [acc[c] + pair[c] for c in range(2)]
        sums[3, e, 0] = acc[0]
        sums[3, e, 1] = acc[1]
        return carry

    lax.fori_loop(0, 18, lower_body, 0, unroll=6)

    def force_body(step, carry):
        mu = step // 2
        c = step % 2
        current = load_matrix(lambda e: dense[mu, e, c])
        omega = mat_mul(current, load_matrix(lambda e: sums[mu, e, c]))
        parts = [part + forces[mu, e, c] for e, part in enumerate(anti_parts(omega))]
        mean = (parts[0] + parts[1] + parts[2]) * (1.0 / 3.0)
        parts = [parts[e] - mean if e < 3 else parts[e] for e in range(9)]
        parts = [part * (1.0 / 12.0) for part in parts]
        applied = anti_mul(parts, current)
        twice = anti_mul(parts, applied)
        gate = gates[mu]
        slope = jnp.zeros_like(gate)
        curve = jnp.zeros_like(gate)
        for e, (part, i, j) in enumerate(ENTRIES):
            weight = cots[mu, e, c]
            slope = slope + weight * applied[part][i][j]
            curve = curve + weight * twice[part][i][j]
            moves_ref[0, mu, e, c] = (gate * applied[part][i][j]).astype(BF16)
            moves_ref[1, mu, e, c] = (gate * twice[part][i][j]).astype(BF16)
        put_row(rows, 8 + mu, c, gate * slope)
        put_row(rows, 12 + mu, c, gate * curve)
        return carry

    lax.fori_loop(0, 8, force_body, 0, unroll=2)
    for t in range(4):
        for q in range(4):
            value = rows[t, q]
            fm_ref[t, :, q * 128:q * 128 + 128] = value.astype(BF16)
            planes_ref[t, :, q * 128:q * 128 + 128] = value[0:8].astype(BF16)


def selectors():
    row = lax.broadcasted_iota(jnp.int32, (432, 72), 0)
    col = lax.broadcasted_iota(jnp.int32, (432, 72), 1)
    group = row // 12
    spread = (group // 4 * 8 + group % 4 == col).astype(F32).astype(BF16)
    keep = (
        lax.broadcasted_iota(jnp.int32, (432, H), 1) // 4 == lax.broadcasted_iota(jnp.int32, (432, H), 0) % 12
    )
    return spread, keep


def panel_kernel(gathered_ref, weights_ref, loops_ref, p1_ref, p2_ref, p3_ref, p4_ref, b2_ref, b3_ref, b4_ref, weights):
    count = gathered_ref.shape[0]

    def read(chip):
        low = gathered_ref[2 * chip].astype(F32)
        high = gathered_ref[2 * chip + 1].astype(F32)
        return special(
            two_rows(lambda e: jnp.concatenate([low[2 * e:2 * e + 2], high[2 * e:2 * e + 2]], axis=0))
        )

    def flat(matrix):
        return tuple(matrix[0][i][j] for i in range(3) for j in range(3)) + tuple(
            imag_of(matrix, i, j) for i in range(3) for j in range(3)
        )

    def chain(chip, state):
        return flat(mat_mul(load_matrix(lambda e: state[e]), read(chip)))

    state = lax.fori_loop(1, count // 2, chain, flat(read(0)))
    loops_ref[0] = (state[0] + state[4] + state[8]) / 3.0
    loops_ref[1] = (state[9] + state[13] + state[17]) / 3.0

    if weights_ref is None:
        for d in range(count):
            block = gathered_ref[d].astype(F32)
            weights[27 * d:27 * d + 27, :] = block[SLABROWS:SLABROWS + 27]
    else:
        weights[...] = weights_ref[...].astype(F32)
    for k in range(TAPS):
        rows = slice(H * k, H * k + H)
        back = slice(H * SWAP[k], H * SWAP[k] + H)
        p2_ref[:, rows] = weights[rows, 0:48].astype(BF16)
        p3_ref[:, rows] = weights[rows, 48:96].astype(BF16)
        p1_ref[:, 8 * k:8 * k + 8] = weights[rows, 96:104].astype(BF16)
        turned = weights[back, :].T
        b2_ref[:, rows] = turned[0:48].astype(BF16)
        b3_ref[:, rows] = turned[48:96].astype(BF16)
    spread, keep = selectors()
    place = (
        lax.broadcasted_iota(jnp.int32, (LANES, H), 0) == 104 + lax.broadcasted_iota(jnp.int32, (LANES, H), 1) % 4
    ).astype(F32).astype(BF16)
    wide = jnp.dot(weights[...].astype(BF16), place, preferred_element_type=F32)
    wide = jnp.where(keep, wide, 0.0).astype(BF16)
    last = lax.dot_general(spread, wide, (((0,), (0,)), ((), ())), preferred_element_type=F32)
    p4_ref[...] = last.astype(BF16)
    for k in range(TAPS):
        b4_ref[:, 8 * k:8 * k + 8] = last[8 * SWAP[k]:8 * SWAP[k] + 8, :].T.astype(BF16)


def panel_kernel_plain(gathered_ref, *rest):
    panel_kernel(gathered_ref, None, *rest)


def chunks_of(value):
    return [value[:, q * 128:q * 128 + 128] for q in range(4)]


def one_shift(chunks, position):
    if position == 0:
        return chunks
    lanes = lane_iota(chunks[0].shape[0])
    sign = 1 if position % 2 == 1 else -1
    if position > 4:
        return [shift_z(chunk, sign, lanes) for chunk in chunks]
    if position > 2:
        return [shift_y(chunk, sign, lanes) for chunk in chunks]
    low = lanes < 64
    rolled = [roll_lanes(chunk, 64) for chunk in chunks]
    if sign > 0:
        return [jnp.where(low, rolled[q], rolled[(q + 1) % 4]) for q in range(4)]
    return [jnp.where(low, rolled[(q + 3) % 4], rolled[q]) for q in range(4)]


def all_shifts(chunks):
    lanes = lane_iota(chunks[0].shape[0])
    y = lanes // 8 % 8
    z = lanes % 8
    low = lanes < 64
    half = [roll_lanes(chunk, 64) for chunk in chunks]
    return [
        chunks,
        [jnp.where(low, half[q], half[(q + 1) % 4]) for q in range(4)],
        [jnp.where(low, half[(q + 3) % 4], half[q]) for q in range(4)],
        [roll_lanes(jnp.where(y == 0, half[q], chunks[q]), -8) for q in range(4)],
        [roll_lanes(jnp.where(y == 7, half[q], chunks[q]), 8) for q in range(4)],
        [roll_lanes(jnp.where(z == 0, roll_lanes(chunk, 8), chunk), -1) for chunk in chunks],
        [roll_lanes(jnp.where(z == 7, roll_lanes(chunk, -8), chunk), 1) for chunk in chunks],
    ]


def span(slice_index, count=1):
    if isinstance(slice_index, int):
        return slice(slice_index * SITES, (slice_index + count) * SITES)
    return pl.ds(pl.multiple_of(slice_index * SITES, SITES), count * SITES)


def slot_of(slot):
    return slice(slot * SITES, (slot + 1) * SITES)


def wide_dot(weights, source, index, kept=None, slot=0):
    shifts = all_shifts(chunks_of(source[:, span(index)]))
    ahead, behind = source[:, span(index + 1)], source[:, span(index - 1)]
    outs = []
    for half in range(2):
        lanes = slice(256 * half, 256 * half + 256)
        columns = [jnp.concatenate(shifted[2 * half:2 * half + 2], axis=1) for shifted in shifts]
        stack = jnp.concatenate(columns + [ahead[:, lanes], behind[:, lanes]], axis=0)
        if kept is not None:
            kept[:, slot * SITES + 256 * half:slot * SITES + 256 * half + 256] = stack
        outs.append(jnp.dot(weights[...], stack, preferred_element_type=F32))
    return jnp.concatenate(outs, axis=1)


def thin_stack(source, index):
    ahead = chunks_of(source[:, span(index + 1)])
    behind = chunks_of(source[:, span(index - 1)])
    columns = all_shifts(chunks_of(source[:, span(index)])) + [ahead, behind]
    return jnp.concatenate(
        [jnp.concatenate([column[q] for column in columns], axis=0).astype(BF16) for q in range(4)], axis=1
    )


def one_minus_square(value):
    value = value.astype(F32)
    return 1.0 - value * value


def conv_kernel(
    split, place_ref, fm_ref, near_ref, far_ref, near_chip_ref, far_chip_ref, loops_ref,
    p1_ref, p2_ref, p3_ref, p4_ref, b2_ref, b3_ref, b4_ref,
    coeff_ref, grads_ref,
    feats, mixed, h1, h2, h3, parts, lasts, g3, g2, g1, wide_back, wide_first, thin, thin_back, packed,
):
    row8 = lax.broadcasted_iota(jnp.int32, (8, SITES), 0)
    loop_re = jnp.concatenate([loops_ref[0, q:q + 1, :] for q in range(4)], axis=1)
    loop_im = jnp.concatenate([loops_ref[1, q:q + 1, :] for q in range(4)], axis=1)
    loops = jnp.where(row8 == 6, loop_re, jnp.where(row8 == 7, loop_im, 0.0))
    loops = loops.astype(BF16).astype(F32)
    first_core = place_ref[0] % 2 == 0
    first_chip = place_ref[0] // 2 % 2 == 0
    for j in range(4):
        near, far = near_chip_ref[j].astype(F32), far_chip_ref[j].astype(F32)
        if j > 0:
            feats[:, span(j - 1)] = jnp.where(first_chip, far, near) + loops
        if j < 3:
            feats[:, span(15 + j)] = jnp.where(first_chip, near, far) + loops
        near, far = near_ref[j].astype(F32), far_ref[j].astype(F32)
        below, above = jnp.where(first_core, far, near), jnp.where(first_core, near, far)
        for base, value in ((3, below), (7, fm_ref[j].astype(F32)), (11, above)):
            feats[:, span(base + j)] = value[0:8] + loops
            mixed[:, span(base + j)] = value[8:16]

    own = span(7, 4)
    contract = (((1,), (1,)), ((), ()))

    def kept_slot(index):
        return index - 7 if 7 <= index < 11 else None

    def first_layer(index):
        stack = thin_stack(feats, index)
        if kept_slot(index) is not None:
            thin[:, slot_of(index - 7)] = stack
        out = jnp.dot(p1_ref[...], stack, preferred_element_type=F32)
        h1[:, span(index)] = jnp.tanh(out).astype(BF16)

    def second_layer(index):
        h2[:, span(index)] = jnp.tanh(wide_dot(p2_ref, h1, index)).astype(BF16)

    def third_layer(index):
        h3[:, span(index)] = jnp.tanh(wide_dot(p3_ref, h2, index)).astype(BF16)

    def taps_of(index):
        taps = jnp.dot(p4_ref[...], h3[:, span(index)], preferred_element_type=F32)
        acc = None
        for position in range(7):
            shifted = one_shift(chunks_of(taps[8 * position:8 * position + 8]), position)
            acc = shifted if acc is None else [a + b for a, b in zip(acc, shifted)]
        parts[0, :, span(index)] = jnp.concatenate(acc, axis=1)
        parts[1, :, span(index)] = taps[56:64]
        parts[2, :, span(index)] = taps[64:72]

    def last_of(index):
        coeff = jnp.tanh(parts[0, :, span(index)] + parts[1, :, span(index + 1)] + parts[2, :, span(index - 1)])
        blend = mixed[:, span(index)]
        value = (blend + coeff * pltpu.roll(blend, 4, 0)) * (1.0 - coeff * coeff)
        lasts[:, span(index)] = jnp.where(row8 < 4, value, 0.0).astype(BF16).astype(F32)
        if 7 <= index < 11:
            coeff_ref[index - 7] = coeff

    def back_third(index):
        stack = thin_stack(lasts, index)
        if kept_slot(index) is not None:
            thin_back[:, slot_of(index - 7)] = stack
        out = jnp.dot(b4_ref[...], stack, preferred_element_type=F32)
        g3[:, span(index)] = (out * one_minus_square(h3[:, span(index)])).astype(BF16)

    def back_second(index):
        slot = kept_slot(index)
        out = wide_dot(b3_ref, g3, index, None if slot is None else wide_back, slot or 0)
        g2[:, span(index)] = (out * one_minus_square(h2[:, span(index)])).astype(BF16)

    def back_first(index):
        out = wide_dot(b2_ref, g2, index, wide_first, index - 7)
        g1[:, slot_of(index - 7)] = (out * one_minus_square(h1[:, span(index)])).astype(BF16)

    stages = (
        (0, 1, 17, first_layer),
        (2, 2, 16, second_layer),
        (4, 3, 15, third_layer),
        (5, 3, 15, taps_of),
        (7, 4, 14, last_of),
        (9, 5, 13, back_third),
        (11, 6, 12, back_second),
        (13, 7, 11, back_first),
    )
    for step in range(1, 24):
        for delay, low, high, task in reversed(stages):
            if low <= step - delay < high:
                task(step - delay)
        if step == 19:
            grad_last = lax.dot_general(
                thin_back[...], h3[:, own], contract, preferred_element_type=F32
            )
            spread, keep = selectors()
            ordered = jnp.concatenate([grad_last[8 * SWAP[k]:8 * SWAP[k] + 8] for k in range(TAPS)], axis=0)
            broad = jnp.dot(spread, ordered.astype(BF16), preferred_element_type=F32)
        if step == 20:
            broad = jnp.where(keep, broad, 0.0).astype(BF16)
            place = (
                lax.broadcasted_iota(jnp.int32, (H, LANES), 1)
                == 104 + lax.broadcasted_iota(jnp.int32, (H, LANES), 0) % 4
            ).astype(F32).astype(BF16)
            packed[...] = jnp.dot(broad, place, preferred_element_type=F32)
        if step == 21:
            grad_third = lax.dot_general(
                wide_back[...], h2[:, own], contract, preferred_element_type=F32
            )
        if step == 22:
            for k in range(TAPS):
                packed[H * k:H * k + H, 48:96] = grad_third[H * SWAP[k]:H * SWAP[k] + H]
    grad_second = lax.dot_general(wide_first[...], h1[:, own], contract, preferred_element_type=F32)
    grad_first = lax.dot_general(g1[...], thin[...], contract, preferred_element_type=F32)
    for k in range(TAPS):
        rows = slice(H * k, H * k + H)
        packed[rows, 0:48] = grad_second[H * SWAP[k]:H * SWAP[k] + H]
        packed[rows, 96:104] = grad_first[:, 8 * k:8 * k + 8]
    if split:
        for d in range(16):
            grads_ref[d] = packed[27 * d:27 * d + 27, :].astype(BF16)
    else:
        grads_ref[...] = packed[...].astype(BF16)


def update_kernel(dense, moves_ref, coeff_ref, out_ref, factors):
    for mu in range(4):
        for t in range(4):
            for c in range(2):
                factors[mu, c, t:t + 1, :] = coeff_ref[t, mu:mu + 1, c * 128:c * 128 + 128]
                factors[mu, c, 4 + t:5 + t, :] = coeff_ref[t, mu:mu + 1, 256 + c * 128:384 + c * 128]

    def body(mu, carry):
        factor = [factors[mu, c] for c in range(2)]
        half = [0.5 * value * value for value in factor]
        for e, (part, i, j) in enumerate(ENTRIES):
            new = [
                dense[mu, e, c]
                + factor[c] * moves_ref[0, mu, e, c].astype(F32)
                + half[c] * moves_ref[1, mu, e, c].astype(F32)
                for c in range(2)
            ]
            out_ref[mu, part, i, j, 0] = jnp.concatenate(
                [new[0][0:4], new[1][0:4], new[0][4:8], new[1][4:8]], axis=1
            )
        return carry

    lax.fori_loop(0, 4, body, 0)


def sum_kernel(widths, parts_ref, first_ref, second_ref, third_ref, last_ref):
    value = parts_ref[0].astype(F32)
    for d in range(1, parts_ref.shape[0]):
        value = value + parts_ref[d].astype(F32)
    offset = 0
    for ref, width in zip((second_ref, third_ref, first_ref, last_ref), widths):
        for r in range(27):
            ref[:, width * r:width * r + width] = value[r:r + 1, offset:offset + width]
        offset += width


def call(body, outs, scratch, places=None, cost=None, limit=LIMIT):
    specs = {}
    if places is not None:
        specs["in_specs"] = [pl.BlockSpec(memory_space=place) for place in places]
    return pl.pallas_call(
        body,
        out_shape=[jax.ShapeDtypeStruct(shape, dtype) for shape, dtype in outs],
        scratch_shapes=[pltpu.VMEM(*item) if isinstance(item, tuple) else item for item in scratch],
        compiler_params=pltpu.CompilerParams(vmem_limit_bytes=limit),
        cost_estimate=cost,
        **specs,
    )


def on_device(links, cotangent, parity, link_subset, w_first, w_second, w_third, w_last):
    count = lax.axis_size("tm")

    def send(value, distance):
        return lax.ppermute(value, "tm", [(i, (i + distance) % count) for i in range(count)])

    def swap(value, pairs):
        return lax.ppermute(value, "tm", pairs + [(target, source) for source, target in pairs])

    chips = count // 2
    widths = (768 // count, 768 // count, 128 // count, 64 // count)
    vmem, smem = pltpu.VMEM, pltpu.SMEM
    field = ((4, 18, 2, 8, LANES), F32)
    space = ((3, 18, 2, 8, LANES), F32)
    edge_rows = ((70, SITES), BF16)
    up, down, dense, edges, staples, slab = call(
        face_kernel,
        [edge_rows, edge_rows, field, space, space, ((12, 4, LANES), F32)],
        [space, ((70, 4, LANES), F32)],
    )(links)
    up = send(up, 1)
    down = send(down, -1)
    (state,) = call(
        space_kernel,
        [((186, 8, LANES), F32)],
        [((3, 3, 18, 2, 8, LANES), F32), ((3, 3, 18, 2, 8, LANES), F32)],
        cost=pl.CostEstimate(flops=4_000_000_000, bytes_accessed=16_000_000, transcendentals=0),
    )(dense, staples)
    place = lax.axis_index("tm").astype(jnp.int32)[None]
    (block,) = call(
        functools.partial(block_kernel, widths),
        [((count, BLOCKROWS, LANES), BF16)],
        [((12, 4, LANES), F32), ((BLOCKROWS, LANES), F32)],
        places=(smem,) + (vmem,) * 7 + (pl.ANY,),
    )(place, up, down, slab, w_first, w_second, w_third, w_last, state)
    gathered = lax.all_to_all(block, "tm", split_axis=0, concat_axis=0, tiled=True)
    fm, planes, moves = call(
        time_kernel,
        [
            ((4, 16, SITES), BF16), ((4, 8, SITES), BF16),
            ((2, 4, 18, 2, 8, LANES), BF16),
        ],
        [
            field, ((4, 8, LANES), F32), space, space, field, ((70, 4, LANES), F32), ((70, 4, LANES), F32),
            ((4, 9, 2, 8, LANES), F32), ((4, 4, 16, LANES), F32),
        ],
        places=(smem,) + (vmem,) * 6,
    )(parity + 2 * link_subset, dense, edges, state, cotangent, up, down)
    far_chip = swap(planes, [(2 * c + k, (2 * c + 2 + k) % count) for c in range(1, chips, 2) for k in range(2)])
    far_core = swap(fm, [(i, (i + 1) % count) for i in range(1, count, 2)])
    near_chip = swap(planes, [(2 * c + k, 2 * c + 2 + k) for c in range(0, chips, 2) for k in range(2)])
    near_core = swap(fm, [(i, i + 1) for i in range(0, count, 2)])

    panel_outs = [
        ((2, 4, LANES), F32), ((H, 72), BF16), ((H, 432), BF16), ((H, 432), BF16), ((72, H), BF16),
        ((H, 432), BF16), ((H, 432), BF16), ((H, 72), BF16),
    ]
    panel_scratch = [((432, LANES), F32)]
    if count == 16:
        loops, p1, p2, p3, p4, b2, b3, b4 = call(panel_kernel_plain, panel_outs, panel_scratch)(gathered)
    else:
        pieces = []
        offset = 0
        for width, full in zip(widths, (48, 48, 8, 4)):
            piece = gathered[:, SLABROWS:SLABROWS + 27, offset:offset + width]
            pieces.append(piece.reshape(432, full))
            offset += width
        pieces.append(jnp.zeros((432, 20), BF16))
        loops, p1, p2, p3, p4, b2, b3, b4 = call(panel_kernel, panel_outs, panel_scratch)(
            gathered, jnp.concatenate(pieces, axis=1)
        )

    window = 18 * SITES
    coeff, grads = call(
        functools.partial(conv_kernel, count == 16),
        [((4, 8, SITES), F32), ((16, 27, LANES) if count == 16 else (432, LANES), BF16)],
        [
            ((8, window), F32), ((8, window), F32), ((H, window), BF16), ((H, window), BF16), ((H, window), BF16),
            ((3, 8, window), F32), ((8, window), F32), ((H, window), BF16), ((H, window), BF16), ((H, 4 * SITES), BF16),
            ((432, 4 * SITES), BF16), ((432, 4 * SITES), BF16), ((72, 4 * SITES), BF16), ((72, 4 * SITES), BF16),
            ((432, LANES), F32),
        ],
        limit=20 * 1024 * 1024,
        places=(smem,) + (vmem,) * 13,
    )(place, fm, near_core, far_core, near_chip, far_chip, loops, p1, p2, p3, p4, b2, b3, b4)
    if count != 16:
        offset = 0
        pieces = []
        for width, full in zip(widths, (48, 48, 8, 4)):
            pieces.append(grads[:, offset:offset + full].reshape(count, 27, width))
            offset += full
        grads = jnp.concatenate(pieces, axis=2)
    grads = lax.all_to_all(grads, "tm", split_axis=0, concat_axis=0, tiled=True)
    (new_links,) = call(
        update_kernel, [(links.shape, F32)], [((4, 2, 8, LANES), F32)]
    )(dense, moves, coeff)
    grad_first, grad_second, grad_third, grad_last = call(
        functools.partial(sum_kernel, widths),
        [((1, 27 * width), F32) for width in (widths[2], widths[0], widths[1], widths[3])],
        [],
    )(grads)
    return (new_links, grad_first, grad_second, grad_third, grad_last)


def solution(mesh):
    placed = (
        P(None, None, None, None, "groups", "tm", None),
        P(None, None, None, None, "groups", "tm", None),
        P("groups", "tm"),
        P("groups", "tm"),
        P("tm"),
        P("tm"),
        P("tm"),
        P("tm"),
    )
    return jax.shard_map(
        on_device,
        mesh=mesh,
        in_specs=placed,
        out_specs=(
            P(None, None, None, None, "groups", "tm", None),
            P("groups", "tm"),
            P("groups", "tm"),
            P("groups", "tm"),
            P("groups", "tm"),
        ),
        check_vma=False,
    )
```

```python
import functools

import jax
import jax.numpy as jnp
from jax import lax
from jax.experimental import pallas as pl
from jax.experimental.pallas import tpu as pltpu
from jax.sharding import PartitionSpec as P

F32 = jnp.float32
BF16 = jnp.bfloat16
TAPS = 9
H = 48
LANES = 128
SITES = 512
PAIRS = ((0, 1), (0, 2), (0, 3), (1, 2), (1, 3), (2, 3))
STACKED = (2, 3, 4, 5, 6)
AFTER = (0, 1, 7, 8)
SWAP = (0, 2, 1, 4, 3, 6, 5, 8, 7)
ENTRIES = tuple((c, i, j) for c in range(2) for i in range(3) for j in range(3))
PLANE = 180
SLABROWS = 24
BLOCKROWS = 64
LIMIT = 8 * 1024 * 1024


def lane_iota(rows):
    return lax.broadcasted_iota(jnp.int32, (rows, LANES), 1)


def row_iota():
    return lax.broadcasted_iota(jnp.int32, (8, LANES), 0)


def roll_lanes(value, amount):
    return pltpu.roll(value, amount % LANES, 1)


def shift_z(chunk, sign, lanes):
    z = lanes % 8
    if sign > 0:
        return jnp.where(z == 7, roll_lanes(chunk, 7), roll_lanes(chunk, -1))
    return jnp.where(z == 0, roll_lanes(chunk, -7), roll_lanes(chunk, 1))


def shift_y(chunk, sign, lanes):
    y = lanes // 8 % 8
    if sign > 0:
        return jnp.where(y == 7, roll_lanes(chunk, 56), roll_lanes(chunk, -8))
    return jnp.where(y == 0, roll_lanes(chunk, -56), roll_lanes(chunk, 8))


def dense_shift(pair, axis, sign):
    lanes = lane_iota(8)
    if axis == 2:
        return [shift_z(chunk, sign, lanes) for chunk in pair]
    if axis == 1:
        return [shift_y(chunk, sign, lanes) for chunk in pair]
    low = lanes < 64
    first, second = [roll_lanes(chunk, 64) for chunk in pair]
    if sign > 0:
        return [jnp.where(low, first, second), jnp.where(low, second, pltpu.roll(first, 4, 0))]
    return [jnp.where(low, pltpu.roll(second, 4, 0), first), jnp.where(low, first, second)]


def pack_pair(value):
    return [
        jnp.concatenate([value[:, c * 128:c * 128 + 128], value[:, 256 + c * 128:384 + c * 128]], axis=0)
        for c in range(2)
    ]


def halo_pair(ref, index):
    top = row_iota() < 4
    pair = []
    for c in range(2):
        low = jnp.broadcast_to(ref[index, c:c + 1, :], (8, LANES))
        high = jnp.broadcast_to(ref[index, 2 + c:3 + c, :], (8, LANES))
        pair.append(jnp.where(top, low, high))
    return pair


def load_matrix(read):
    real = [[read(3 * i + j) for j in range(3)] for i in range(3)]
    imag = [[read(9 + 3 * i + j) for j in range(3)] for i in range(3)]
    return (real, imag, 1)


def dagger(matrix):
    real, imag, sign = matrix
    return (
        [[real[j][i] for j in range(3)] for i in range(3)],
        [[imag[j][i] for j in range(3)] for i in range(3)],
        -sign,
    )


def total(terms, signs):
    value = None
    for term, sign in zip(terms, signs):
        if value is None:
            value = term if sign > 0 else -term
        else:
            value = value + term if sign > 0 else value - term
    return value


def mat_mul(left, right):
    lr, li, ls = left
    rr, ri, rs = right
    same = ls == rs
    height = len(lr)
    real = [[None] * 3 for _ in range(height)]
    imag = [[None] * 3 for _ in range(height)]
    for i in range(height):
        for j in range(3):
            real[i][j] = total(
                [lr[i][k] * rr[k][j] for k in range(3)] + [li[i][k] * ri[k][j] for k in range(3)],
                [1, 1, 1] + [-1 if same else 1] * 3,
            )
            imag[i][j] = total(
                [lr[i][k] * ri[k][j] for k in range(3)] + [li[i][k] * rr[k][j] for k in range(3)],
                [1, 1, 1] + [1 if same else -1] * 3,
            )
    return (real, imag, ls if same else rs)


def imag_of(matrix, i, j):
    return matrix[1][i][j] if matrix[2] > 0 else -matrix[1][i][j]


def store_matrix(matrix, write):
    for i in range(3):
        for j in range(3):
            write(3 * i + j, matrix[0][i][j])
            write(9 + 3 * i + j, imag_of(matrix, i, j))


def two_rows(read):
    real = [[read(3 * i + j) for j in range(3)] for i in range(2)]
    imag = [[read(6 + 3 * i + j) for j in range(3)] for i in range(2)]
    return (real, imag, 1)


def store_rows(matrix, write):
    for i in range(2):
        for j in range(3):
            write(3 * i + j, matrix[0][i][j])
            write(6 + 3 * i + j, imag_of(matrix, i, j))


def special(matrix):
    real, imag, _ = matrix
    last_r, last_i = [], []
    for k in range(3):
        i, j = (k + 1) % 3, (k + 2) % 3
        last_r.append(
            (real[0][i] * real[1][j] - imag[0][i] * imag[1][j])
            - (real[0][j] * real[1][i] - imag[0][j] * imag[1][i])
        )
        last_i.append(
            (real[0][j] * imag[1][i] + imag[0][j] * real[1][i])
            - (real[0][i] * imag[1][j] + imag[0][i] * real[1][j])
        )
    return (real + [last_r], imag + [last_i], 1)


def anti_parts(matrix):
    parts = [2.0 * imag_of(matrix, i, i) for i in range(3)]
    for i, j in ((0, 1), (0, 2), (1, 2)):
        parts.append(matrix[0][i][j] - matrix[0][j][i])
        parts.append(imag_of(matrix, i, j) + imag_of(matrix, j, i))
    return parts


def anti_matrix(parts):
    zero = jnp.zeros_like(parts[0])
    real = [[zero, parts[3], parts[5]], [-parts[3], zero, parts[7]], [-parts[5], -parts[7], zero]]
    imag = [[parts[0], parts[4], parts[6]], [parts[4], parts[1], parts[8]], [parts[6], parts[8], parts[2]]]
    return real, imag


def anti_mul(parts, right):
    real, imag = anti_matrix(parts)
    rr, ri, _ = right
    out_r = [[None] * 3 for _ in range(3)]
    out_i = [[None] * 3 for _ in range(3)]
    for i in range(3):
        for j in range(3):
            value_r = -(imag[i][i] * ri[i][j])
            value_i = imag[i][i] * rr[i][j]
            for k in range(3):
                if k != i:
                    value_r = value_r + real[i][k] * rr[k][j] - imag[i][k] * ri[k][j]
                    value_i = value_i + real[i][k] * ri[k][j] + imag[i][k] * rr[k][j]
            out_r[i][j] = value_r
            out_i[i][j] = value_i
    return (out_r, out_i, 1)


def pack_links(links_ref, dense):
    def body(mu, carry):
        for e, (c, i, j) in enumerate(ENTRIES):
            low, high = pack_pair(links_ref[mu, c, i, j, 0].astype(F32))
            dense[mu, e, 0] = low
            dense[mu, e, 1] = high
        return carry

    lax.fori_loop(0, 4, body, 0)


def face_kernel(links_ref, up_ref, down_ref, dense, edges, staples, slab, moved, rows):
    pack_links(links_ref, dense)

    def shift_body(e, carry):
        pair = [dense[3, e, 0], dense[3, e, 1]]
        for mu in range(3):
            low, high = dense_shift(pair, mu, 1)
            moved[mu, e, 0] = low
            moved[mu, e, 1] = high
        return carry

    lax.fori_loop(0, 18, shift_body, 0, unroll=6)

    def staple_body(step, carry):
        mu = step // 2
        c = step % 2
        u_mu = load_matrix(lambda e: dense[mu, e, c])
        u_t = load_matrix(lambda e: dense[3, e, c])
        edge = mat_mul(u_mu, load_matrix(lambda e: moved[mu, e, c]))

        def write_edge(e, value):
            edges[mu, e, c] = value

        store_matrix(edge, write_edge)

        def write(e, value):
            staples[mu, e, c] = value
            rows[16 + mu * 18 + e, pl.ds(c, 1)] = value[3:4]
            rows[16 + mu * 18 + e, pl.ds(2 + c, 1)] = value[7:8]

        store_matrix(mat_mul(dagger(edge), u_t), write)
        return carry

    lax.fori_loop(0, 6, staple_body, 0, unroll=2)

    def slab_body(c, carry):
        u_t = load_matrix(lambda e: dense[3, e, c])
        ahead = load_matrix(lambda e: pltpu.roll(dense[3, e, c], 7, 0))
        two = mat_mul(u_t, ahead)
        later = tuple(
            [[pltpu.roll(part[i][j], 6, 0) for j in range(3)] for i in range(3)] for part in two[:2]
        ) + (two[2],)
        four = mat_mul((two[0][:2], two[1][:2], two[2]), later)

        def write(e, value):
            slab[e, pl.ds(c, 1)] = value[0:1]
            slab[e, pl.ds(2 + c, 1)] = value[4:5]
            rows[e, pl.ds(c, 1)] = value[0:1]
            rows[e, pl.ds(2 + c, 1)] = value[4:5]

        store_rows(four, write)
        return carry

    lax.fori_loop(0, 2, slab_body, 0)
    for q in range(4):
        up_ref[:, q * 128:q * 128 + 128] = rows[:, q, :].astype(BF16)

    def down_body(e, carry):
        for mu in range(3):
            for c in range(2):
                value = dense[mu, e, c]
                rows[16 + mu * 18 + e, c:c + 1] = value[0:1]
                rows[16 + mu * 18 + e, 2 + c:3 + c] = value[4:5]
        return carry

    lax.fori_loop(0, 18, down_body, 0, unroll=6)
    for q in range(4):
        down_ref[:, q * 128:q * 128 + 128] = rows[:, q, :].astype(BF16)


def block_kernel(
    widths, place_ref, up_ref, down_ref, slab, w1_ref, w2_ref, w3_ref, w4_ref, after_ref, block_ref, other, block
):
    even = place_ref[0] % 2 == 0
    up = up_ref[0:16].astype(F32)
    down = down_ref[0:16].astype(F32)
    for q in range(4):
        lanes = slice(q * 128, q * 128 + 128)
        other[:, q, :] = jnp.where(even, down[0:12, lanes], up[0:12, lanes])
    first = two_rows(lambda e: jnp.where(even, slab[e], other[e]))
    second = special(two_rows(lambda e: jnp.where(even, other[e], slab[e])))

    def write(e, value):
        block[2 * e:2 * e + 2, :] = jnp.where(even, value[0:2], value[2:4])

    store_rows(mat_mul(first, second), write)
    block[SLABROWS:BLOCKROWS] = jnp.zeros((BLOCKROWS - SLABROWS, LANES), F32)
    offset = 0
    for ref, width in zip((w2_ref, w3_ref, w1_ref, w4_ref), widths):
        flat = ref[...].astype(F32)
        for r in range(27):
            block[SLABROWS + r:SLABROWS + r + 1, offset:offset + width] = (
                flat[width * r:width * r + width].reshape(1, width)
            )
        offset += width
    value = block[...].astype(BF16)
    for d in range(block_ref.shape[0]):
        block_ref[d] = value


def put_row(rows, channel, c, value):
    for t in range(4):
        rows[t, c, pl.ds(channel, 1), :] = value[t:t + 1]
        rows[t, 2 + c, pl.ds(channel, 1), :] = value[4 + t:5 + t]


def sum_at(mu, e, c):
    return (mu * 18 + e) * 2 + c


def force_at(mu, e, c):
    return 108 + (mu * 9 + e) * 2 + c


def space_kernel(dense, time_staples, state, moved, staples):
    state[108:180] = jnp.zeros((72, 8, LANES), F32)
    steps = row_iota() % 4

    def shift_body(e, carry):
        for nu in range(3):
            pair = [dense[nu, e, 0], dense[nu, e, 1]]
            for mu in range(3):
                if mu != nu:
                    low, high = dense_shift(pair, mu, 1)
                    moved[mu, nu, e, 0] = low
                    moved[mu, nu, e, 1] = high
        return carry

    lax.fori_loop(0, 18, shift_body, 0, unroll=6)

    def plane_body(step, carry):
        plane = step // 2
        c = step % 2
        mu = jnp.where(plane == 2, 1, 0)
        nu = jnp.where(plane == 0, 1, 2)
        u_mu = load_matrix(lambda e: dense[mu, e, c])
        u_nu = load_matrix(lambda e: dense[nu, e, c])
        one = mat_mul(u_mu, load_matrix(lambda e: moved[mu, nu, e, c]))
        two = mat_mul(u_nu, load_matrix(lambda e: moved[nu, mu, e, c]))
        loop = mat_mul(one, dagger(two))
        state[PLANE + step] = (loop[0][0][0] + loop[0][1][1] + loop[0][2][2]) / 3.0
        for e, part in enumerate(anti_parts(loop)):
            state[force_at(mu, e, c)] += part
            state[force_at(nu, e, c)] -= part

        def write_mu(e, value):
            staples[mu, nu, e, c] = value

        def write_nu(e, value):
            staples[nu, mu, e, c] = value

        store_matrix(mat_mul(dagger(one), u_nu), write_mu)
        store_matrix(mat_mul(dagger(two), u_mu), write_nu)
        return carry

    lax.fori_loop(0, 6, plane_body, 0, unroll=2)

    def lower_body(e, carry):
        for mu in range(3):
            acc = [jnp.where(steps == 0, 0.0, pltpu.roll(time_staples[mu, e, c], 1, 0)) for c in range(2)]
            for nu in range(3):
                if nu != mu:
                    pair = dense_shift([staples[mu, nu, e, 0], staples[mu, nu, e, 1]], nu, -1)
                    acc = [acc[c] + pair[c] for c in range(2)]
            state[sum_at(mu, e, 0)] = acc[0]
            state[sum_at(mu, e, 1)] = acc[1]
        return carry

    lax.fori_loop(0, 18, lower_body, 0, unroll=6)


def time_kernel(
    code_ref, dense, edges, state, cot_ref, up_ref, down_ref,
    fm_ref, planes_ref, moves_ref,
    cots, gates, moved, staples, sums, halo_up, halo_down, forces, rows,
):
    for q in range(4):
        halo_up[:, q, :] = up_ref[:, q * 128:q * 128 + 128].astype(F32)
        halo_down[:, q, :] = down_ref[:, q * 128:q * 128 + 128].astype(F32)
    rows[...] = jnp.zeros_like(rows)
    pack_links(cot_ref, cots)
    lanes = lane_iota(8)
    site_steps = row_iota() % 4
    colour = (lanes // 64 + lanes // 8 % 8 + lanes % 8 + site_steps) % 2
    code = jnp.zeros_like(site_steps)
    for t in range(4):
        code = jnp.where(site_steps == t, code_ref[0, t], code)
    for mu in range(4):
        active = jnp.logical_and(colour == code % 2, jnp.right_shift(code, mu + 1) % 2 == 1)
        gates[mu] = jnp.where(active, 1.0, 0.0)
    for channel, plane in ((0, 0), (1, 1), (3, 2)):
        for c in range(2):
            put_row(rows, channel, c, state[PLANE + 2 * plane + c])
    for mu in range(4):
        for e in range(9):
            for c in range(2):
                forces[mu, e, c] = state[force_at(mu, e, c)]
    steps = row_iota() % 4

    def shift_body(e, carry):
        for nu in range(3):
            halo = halo_pair(halo_down, 16 + nu * 18 + e)
            below = halo_pair(halo_up, 16 + nu * 18 + e)
            for c in range(2):
                moved[nu, e, c] = jnp.where(steps == 3, halo[c], pltpu.roll(dense[nu, e, c], 7, 0))
                sums[nu, e, c] = state[sum_at(nu, e, c)] + jnp.where(steps == 0, below[c], 0.0)
        return carry

    lax.fori_loop(0, 18, shift_body, 0, unroll=6)

    def plane_body(step, carry):
        mu = step // 2
        c = step % 2
        one = load_matrix(lambda e: edges[mu, e, c])
        two = mat_mul(load_matrix(lambda e: dense[3, e, c]), load_matrix(lambda e: moved[mu, e, c]))
        loop = mat_mul(one, dagger(two))
        put_row(rows, jnp.where(mu == 0, 2, mu + 3), c, (loop[0][0][0] + loop[0][1][1] + loop[0][2][2]) / 3.0)
        for e, part in enumerate(anti_parts(loop)):
            forces[mu, e, c] += part
            forces[3, e, c] -= part

        def write(e, value):
            staples[mu, e, c] = value

        store_matrix(mat_mul(dagger(two), load_matrix(lambda e: dense[mu, e, c])), write)
        return carry

    lax.fori_loop(0, 6, plane_body, 0, unroll=2)

    def lower_body(e, carry):
        acc = None
        for mu in range(3):
            pair = dense_shift([staples[mu, e, 0], staples[mu, e, 1]], mu, -1)
            acc = pair if acc is None else [acc[c] + pair[c] for c in range(2)]
        sums[3, e, 0] = acc[0]
        sums[3, e, 1] = acc[1]
        return carry

    lax.fori_loop(0, 18, lower_body, 0, unroll=6)

    def force_body(step, carry):
        mu = step // 2
        c = step % 2
        current = load_matrix(lambda e: dense[mu, e, c])
        omega = mat_mul(current, load_matrix(lambda e: sums[mu, e, c]))
        parts = [part + forces[mu, e, c] for e, part in enumerate(anti_parts(omega))]
        mean = (parts[0] + parts[1] + parts[2]) * (1.0 / 3.0)
        parts = [parts[e] - mean if e < 3 else parts[e] for e in range(9)]
        parts = [part * (1.0 / 12.0) for part in parts]
        applied = anti_mul(parts, current)
        twice = anti_mul(parts, applied)
        gate = gates[mu]
        slope = jnp.zeros_like(gate)
        curve = jnp.zeros_like(gate)
        for e, (part, i, j) in enumerate(ENTRIES):
            weight = cots[mu, e, c]
            slope = slope + weight * applied[part][i][j]
            curve = curve + weight * twice[part][i][j]
            moves_ref[0, mu, e, c] = (gate * applied[part][i][j]).astype(BF16)
            moves_ref[1, mu, e, c] = (gate * twice[part][i][j]).astype(BF16)
        put_row(rows, 8 + mu, c, gate * slope)
        put_row(rows, 12 + mu, c, gate * curve)
        return carry

    lax.fori_loop(0, 8, force_body, 0, unroll=2)
    for t in range(4):
        for q in range(4):
            value = rows[t, q]
            fm_ref[t, :, q * 128:q * 128 + 128] = value.astype(BF16)
            planes_ref[t, :, q * 128:q * 128 + 128] = value[0:8].astype(BF16)


def selectors():
    row = lax.broadcasted_iota(jnp.int32, (432, 72), 0)
    col = lax.broadcasted_iota(jnp.int32, (432, 72), 1)
    group = row // 12
    spread = (group // 4 * 8 + group % 4 == col).astype(F32).astype(BF16)
    keep = (
        lax.broadcasted_iota(jnp.int32, (432, H), 1) // 4 == lax.broadcasted_iota(jnp.int32, (432, H), 0) % 12
    )
    return spread, keep


def panel_kernel(
    gathered_ref, weights_ref, loops_ref, p1_ref, p4_ref, b4_ref,
    s2_ref, s3_ref, t2_ref, t3_ref, a2_ref, a3_ref, c2_ref, c3_ref, weights,
):
    count = gathered_ref.shape[0]

    def read(chip):
        low = gathered_ref[2 * chip].astype(F32)
        high = gathered_ref[2 * chip + 1].astype(F32)
        return special(
            two_rows(lambda e: jnp.concatenate([low[2 * e:2 * e + 2], high[2 * e:2 * e + 2]], axis=0))
        )

    def flat(matrix):
        return tuple(matrix[0][i][j] for i in range(3) for j in range(3)) + tuple(
            imag_of(matrix, i, j) for i in range(3) for j in range(3)
        )

    def chain(chip, state):
        return flat(mat_mul(load_matrix(lambda e: state[e]), read(chip)))

    state = lax.fori_loop(1, count // 2, chain, flat(read(0)))
    loops_ref[0] = (state[0] + state[4] + state[8]) / 3.0
    loops_ref[1] = (state[9] + state[13] + state[17]) / 3.0

    if weights_ref is None:
        for d in range(count):
            block = gathered_ref[d].astype(F32)
            weights[27 * d:27 * d + 27, :] = block[SLABROWS:SLABROWS + 27]
    else:
        weights[...] = weights_ref[...].astype(F32)
    for k in range(TAPS):
        rows = slice(H * k, H * k + H)
        back = slice(H * SWAP[k], H * SWAP[k] + H)
        p1_ref[:, 8 * k:8 * k + 8] = weights[rows, 96:104].astype(BF16)
        turned = weights[back, :].T
        pieces = (weights[rows, 0:48], weights[rows, 48:96], turned[0:48], turned[48:96])
        if k in STACKED:
            place = slice(H * STACKED.index(k), H * STACKED.index(k) + H)
            for ref, piece in zip((s2_ref, s3_ref, t2_ref, t3_ref), pieces):
                ref[:, place] = piece.astype(BF16)
        else:
            place = slice(H * AFTER.index(k), H * AFTER.index(k) + H)
            for ref, piece in zip((a2_ref, a3_ref, c2_ref, c3_ref), pieces):
                ref[place, :] = piece.astype(BF16)
    spread, keep = selectors()
    place = (
        lax.broadcasted_iota(jnp.int32, (LANES, H), 0) == 104 + lax.broadcasted_iota(jnp.int32, (LANES, H), 1) % 4
    ).astype(F32).astype(BF16)
    wide = jnp.dot(weights[...].astype(BF16), place, preferred_element_type=F32)
    wide = jnp.where(keep, wide, 0.0).astype(BF16)
    last = lax.dot_general(spread, wide, (((0,), (0,)), ((), ())), preferred_element_type=F32)
    p4_ref[...] = last.astype(BF16)
    for k in range(TAPS):
        b4_ref[:, 8 * k:8 * k + 8] = last[8 * SWAP[k]:8 * SWAP[k] + 8, :].T.astype(BF16)


def panel_kernel_plain(gathered_ref, *rest):
    panel_kernel(gathered_ref, None, *rest)


def chunks_of(value):
    return [value[:, q * 128:q * 128 + 128] for q in range(4)]


def one_shift(chunks, position):
    if position == 0:
        return chunks
    lanes = lane_iota(chunks[0].shape[0])
    sign = 1 if position % 2 == 1 else -1
    if position > 4:
        return [shift_z(chunk, sign, lanes) for chunk in chunks]
    if position > 2:
        return [shift_y(chunk, sign, lanes) for chunk in chunks]
    low = lanes < 64
    rolled = [roll_lanes(chunk, 64) for chunk in chunks]
    if sign > 0:
        return [jnp.where(low, rolled[q], rolled[(q + 1) % 4]) for q in range(4)]
    return [jnp.where(low, rolled[(q + 3) % 4], rolled[q]) for q in range(4)]


def all_shifts(chunks):
    lanes = lane_iota(chunks[0].shape[0])
    y = lanes // 8 % 8
    z = lanes % 8
    low = lanes < 64
    half = [roll_lanes(chunk, 64) for chunk in chunks]
    return [
        chunks,
        [jnp.where(low, half[q], half[(q + 1) % 4]) for q in range(4)],
        [jnp.where(low, half[(q + 3) % 4], half[q]) for q in range(4)],
        [roll_lanes(jnp.where(y == 0, half[q], chunks[q]), -8) for q in range(4)],
        [roll_lanes(jnp.where(y == 7, half[q], chunks[q]), 8) for q in range(4)],
        [roll_lanes(jnp.where(z == 0, roll_lanes(chunk, 8), chunk), -1) for chunk in chunks],
        [roll_lanes(jnp.where(z == 7, roll_lanes(chunk, -8), chunk), 1) for chunk in chunks],
    ]


def span(slice_index, count=1):
    if isinstance(slice_index, int):
        return slice(slice_index * SITES, (slice_index + count) * SITES)
    return pl.ds(pl.multiple_of(slice_index * SITES, SITES), count * SITES)


def slot_of(slot):
    return slice(slot * SITES, (slot + 1) * SITES)


def wide_mix(stacked, after, source, index, low, high, mixes, kept=None):
    slot = slot_of(index % 4)
    if index == low - 1:
        mixes[2, :, slot] = jnp.dot(after[144:192, :], source[:, span(index)], preferred_element_type=F32)
        return
    if index == high:
        mixes[1, :, slot] = jnp.dot(after[96:144, :], source[:, span(index)], preferred_element_type=F32)
        return
    shifts = all_shifts(chunks_of(source[:, span(index)]))
    outs = []
    for half in range(2):
        columns = [jnp.concatenate(shifted[2 * half:2 * half + 2], axis=1) for shifted in shifts]
        stack = jnp.concatenate([columns[k] for k in STACKED], axis=0)
        if kept is not None:
            lanes = slice((index - 7) * SITES + 256 * half, (index - 7) * SITES + 256 * half + 256)
            kept[0:7 * H, lanes] = jnp.concatenate(columns, axis=0)
        outs.append(jnp.dot(stacked[...], stack, preferred_element_type=F32))
    terms = jnp.dot(after[...], source[:, span(index)], preferred_element_type=F32)
    moved = jnp.concatenate(one_shift(chunks_of(terms[48:96]), 1), axis=1)
    mixes[0, :, slot] = jnp.concatenate(outs, axis=1) + terms[0:48] + moved
    mixes[1, :, slot] = terms[96:144]
    mixes[2, :, slot] = terms[144:192]


def wide_sum(mixes, index):
    return (
        mixes[0, :, slot_of(index % 4)]
        + mixes[1, :, slot_of((index + 1) % 4)]
        + mixes[2, :, slot_of((index - 1) % 4)]
    )


def thin_stack(source, index):
    ahead = chunks_of(source[:, span(index + 1)])
    behind = chunks_of(source[:, span(index - 1)])
    columns = all_shifts(chunks_of(source[:, span(index)])) + [ahead, behind]
    return jnp.concatenate(
        [jnp.concatenate([column[q] for column in columns], axis=0).astype(BF16) for q in range(4)], axis=1
    )


def one_minus_square(value):
    value = value.astype(F32)
    return 1.0 - value * value


def conv_kernel(
    split, place_ref, fm_ref, near_ref, far_ref, near_chip_ref, far_chip_ref, loops_ref,
    p1_ref, p4_ref, b4_ref, s2_ref, s3_ref, t2_ref, t3_ref, a2_ref, a3_ref, c2_ref, c3_ref,
    coeff_ref, grads_ref,
    feats, mixed, h1, h2, h3, parts, lasts, g3, g2, g1, wide_back, wide_first, thin, thin_back, packed, mixes,
):
    row8 = lax.broadcasted_iota(jnp.int32, (8, SITES), 0)
    loop_re = jnp.concatenate([loops_ref[0, q:q + 1, :] for q in range(4)], axis=1)
    loop_im = jnp.concatenate([loops_ref[1, q:q + 1, :] for q in range(4)], axis=1)
    loops = jnp.where(row8 == 6, loop_re, jnp.where(row8 == 7, loop_im, 0.0))
    loops = loops.astype(BF16).astype(F32)
    first_core = place_ref[0] % 2 == 0
    first_chip = place_ref[0] // 2 % 2 == 0
    for j in range(4):
        near, far = near_chip_ref[j].astype(F32), far_chip_ref[j].astype(F32)
        if j > 0:
            feats[:, span(j - 1)] = jnp.where(first_chip, far, near) + loops
        if j < 3:
            feats[:, span(15 + j)] = jnp.where(first_chip, near, far) + loops
        near, far = near_ref[j].astype(F32), far_ref[j].astype(F32)
        below, above = jnp.where(first_core, far, near), jnp.where(first_core, near, far)
        for base, value in ((3, below), (7, fm_ref[j].astype(F32)), (11, above)):
            feats[:, span(base + j)] = value[0:8] + loops
            mixed[:, span(base + j)] = value[8:16]

    own = span(7, 4)
    contract = (((1,), (1,)), ((), ()))

    def kept_slot(index):
        return index - 7 if 7 <= index < 11 else None

    def first_layer(index):
        stack = thin_stack(feats, index)
        if kept_slot(index) is not None:
            thin[:, slot_of(index - 7)] = stack
        out = jnp.dot(p1_ref[...], stack, preferred_element_type=F32)
        h1[:, span(index)] = jnp.tanh(out).astype(BF16)

    def second_mix(index):
        wide_mix(s2_ref, a2_ref, h1, index, 2, 16, mixes.at[0])

    def second_layer(index):
        h2[:, span(index)] = jnp.tanh(wide_sum(mixes.at[0], index)).astype(BF16)

    def third_mix(index):
        wide_mix(s3_ref, a3_ref, h2, index, 3, 15, mixes.at[1])

    def third_layer(index):
        h3[:, span(index)] = jnp.tanh(wide_sum(mixes.at[1], index)).astype(BF16)

    def taps_of(index):
        taps = jnp.dot(p4_ref[...], h3[:, span(index)], preferred_element_type=F32)
        acc = None
        for position in range(7):
            shifted = one_shift(chunks_of(taps[8 * position:8 * position + 8]), position)
            acc = shifted if acc is None else [a + b for a, b in zip(acc, shifted)]
        parts[0, :, span(index)] = jnp.concatenate(acc, axis=1)
        parts[1, :, span(index)] = taps[56:64]
        parts[2, :, span(index)] = taps[64:72]

    def last_of(index):
        coeff = jnp.tanh(parts[0, :, span(index)] + parts[1, :, span(index + 1)] + parts[2, :, span(index - 1)])
        blend = mixed[:, span(index)]
        value = (blend + coeff * pltpu.roll(blend, 4, 0)) * (1.0 - coeff * coeff)
        lasts[:, span(index)] = jnp.where(row8 < 4, value, 0.0).astype(BF16).astype(F32)
        if 7 <= index < 11:
            coeff_ref[index - 7] = coeff

    def back_third(index):
        stack = thin_stack(lasts, index)
        if kept_slot(index) is not None:
            thin_back[:, slot_of(index - 7)] = stack
        out = jnp.dot(b4_ref[...], stack, preferred_element_type=F32)
        g3[:, span(index)] = (out * one_minus_square(h3[:, span(index)])).astype(BF16)

    def keep_times(source, kept, index):
        kept[7 * H:8 * H, slot_of(index - 7)] = source[:, span(index + 1)]
        kept[8 * H:9 * H, slot_of(index - 7)] = source[:, span(index - 1)]

    def back_second_mix(index):
        wide_mix(t3_ref, c3_ref, g3, index, 6, 12, mixes.at[2], wide_back if 7 <= index < 11 else None)

    def back_second(index):
        if 7 <= index < 11:
            keep_times(g3, wide_back, index)
        out = wide_sum(mixes.at[2], index)
        g2[:, span(index)] = (out * one_minus_square(h2[:, span(index)])).astype(BF16)

    def back_first_mix(index):
        wide_mix(t2_ref, c2_ref, g2, index, 7, 11, mixes.at[3], wide_first if 7 <= index < 11 else None)

    def back_first(index):
        keep_times(g2, wide_first, index)
        out = wide_sum(mixes.at[3], index)
        g1[:, slot_of(index - 7)] = (out * one_minus_square(h1[:, span(index)])).astype(BF16)

    stages = (
        (0, 1, 17, first_layer),
        (1, 1, 17, second_mix),
        (3, 2, 16, second_layer),
        (4, 2, 16, third_mix),
        (6, 3, 15, third_layer),
        (7, 3, 15, taps_of),
        (9, 4, 14, last_of),
        (11, 5, 13, back_third),
        (12, 5, 13, back_second_mix),
        (14, 6, 12, back_second),
        (15, 6, 12, back_first_mix),
        (17, 7, 11, back_first),
    )
    for step in range(1, 28):
        for delay, low, high, task in reversed(stages):
            if low <= step - delay < high:
                task(step - delay)
        if step == 21:
            grad_last = lax.dot_general(
                thin_back[...], h3[:, own], contract, preferred_element_type=F32
            )
            spread, keep = selectors()
            ordered = jnp.concatenate([grad_last[8 * SWAP[k]:8 * SWAP[k] + 8] for k in range(TAPS)], axis=0)
            broad = jnp.dot(spread, ordered.astype(BF16), preferred_element_type=F32)
        if step == 22:
            broad = jnp.where(keep, broad, 0.0).astype(BF16)
            place = (
                lax.broadcasted_iota(jnp.int32, (H, LANES), 1)
                == 104 + lax.broadcasted_iota(jnp.int32, (H, LANES), 0) % 4
            ).astype(F32).astype(BF16)
            packed[...] = jnp.dot(broad, place, preferred_element_type=F32)
        if step == 24:
            grad_third = lax.dot_general(
                wide_back[...], h2[:, own], contract, preferred_element_type=F32
            )
        if step == 25:
            for k in range(TAPS):
                packed[H * k:H * k + H, 48:96] = grad_third[H * SWAP[k]:H * SWAP[k] + H]
    grad_second = lax.dot_general(wide_first[...], h1[:, own], contract, preferred_element_type=F32)
    grad_first = lax.dot_general(g1[...], thin[...], contract, preferred_element_type=F32)
    for k in range(TAPS):
        rows = slice(H * k, H * k + H)
        packed[rows, 0:48] = grad_second[H * SWAP[k]:H * SWAP[k] + H]
        packed[rows, 96:104] = grad_first[:, 8 * k:8 * k + 8]
    if split:
        for d in range(16):
            grads_ref[d] = packed[27 * d:27 * d + 27, :].astype(BF16)
    else:
        grads_ref[...] = packed[...].astype(BF16)


def update_kernel(dense, moves_ref, coeff_ref, out_ref, factors):
    for mu in range(4):
        for t in range(4):
            for c in range(2):
                factors[mu, c, t:t + 1, :] = coeff_ref[t, mu:mu + 1, c * 128:c * 128 + 128]
                factors[mu, c, 4 + t:5 + t, :] = coeff_ref[t, mu:mu + 1, 256 + c * 128:384 + c * 128]

    def body(mu, carry):
        factor = [factors[mu, c] for c in range(2)]
        half = [0.5 * value * value for value in factor]
        for e, (part, i, j) in enumerate(ENTRIES):
            new = [
                dense[mu, e, c]
                + factor[c] * moves_ref[0, mu, e, c].astype(F32)
                + half[c] * moves_ref[1, mu, e, c].astype(F32)
                for c in range(2)
            ]
            out_ref[mu, part, i, j, 0] = jnp.concatenate(
                [new[0][0:4], new[1][0:4], new[0][4:8], new[1][4:8]], axis=1
            )
        return carry

    lax.fori_loop(0, 4, body, 0)


def sum_kernel(widths, parts_ref, first_ref, second_ref, third_ref, last_ref):
    value = parts_ref[0].astype(F32)
    for d in range(1, parts_ref.shape[0]):
        value = value + parts_ref[d].astype(F32)
    offset = 0
    for ref, width in zip((second_ref, third_ref, first_ref, last_ref), widths):
        for r in range(27):
            ref[:, width * r:width * r + width] = value[r:r + 1, offset:offset + width]
        offset += width


def call(body, outs, scratch, places=None, cost=None, limit=LIMIT):
    specs = {}
    if places is not None:
        specs["in_specs"] = [pl.BlockSpec(memory_space=place) for place in places]
    return pl.pallas_call(
        body,
        out_shape=[jax.ShapeDtypeStruct(shape, dtype) for shape, dtype in outs],
        scratch_shapes=[pltpu.VMEM(*item) if isinstance(item, tuple) else item for item in scratch],
        compiler_params=pltpu.CompilerParams(vmem_limit_bytes=limit),
        cost_estimate=cost,
        **specs,
    )


def on_device(links, cotangent, parity, link_subset, w_first, w_second, w_third, w_last):
    count = lax.axis_size("tm")

    def send(value, distance):
        return lax.ppermute(value, "tm", [(i, (i + distance) % count) for i in range(count)])

    def swap(value, pairs):
        return lax.ppermute(value, "tm", pairs + [(target, source) for source, target in pairs])

    chips = count // 2
    widths = (768 // count, 768 // count, 128 // count, 64 // count)
    vmem, smem = pltpu.VMEM, pltpu.SMEM
    field = ((4, 18, 2, 8, LANES), F32)
    space = ((3, 18, 2, 8, LANES), F32)
    edge_rows = ((70, SITES), BF16)
    up, down, dense, edges, staples, slab = call(
        face_kernel,
        [edge_rows, edge_rows, field, space, space, ((12, 4, LANES), F32)],
        [space, ((70, 4, LANES), F32)],
    )(links)
    up = send(up, 1)
    down = send(down, -1)
    (state,) = call(
        space_kernel,
        [((186, 8, LANES), F32)],
        [((3, 3, 18, 2, 8, LANES), F32), ((3, 3, 18, 2, 8, LANES), F32)],
        cost=pl.CostEstimate(flops=4_000_000_000, bytes_accessed=16_000_000, transcendentals=0),
    )(dense, staples)
    place = lax.axis_index("tm").astype(jnp.int32)[None]
    (block,) = call(
        functools.partial(block_kernel, widths),
        [((count, BLOCKROWS, LANES), BF16)],
        [((12, 4, LANES), F32), ((BLOCKROWS, LANES), F32)],
        places=(smem,) + (vmem,) * 7 + (pl.ANY,),
    )(place, up, down, slab, w_first, w_second, w_third, w_last, state)
    gathered = lax.all_to_all(block, "tm", split_axis=0, concat_axis=0, tiled=True)
    fm, planes, moves = call(
        time_kernel,
        [
            ((4, 16, SITES), BF16), ((4, 8, SITES), BF16),
            ((2, 4, 18, 2, 8, LANES), BF16),
        ],
        [
            field, ((4, 8, LANES), F32), space, space, field, ((70, 4, LANES), F32), ((70, 4, LANES), F32),
            ((4, 9, 2, 8, LANES), F32), ((4, 4, 16, LANES), F32),
        ],
        places=(smem,) + (vmem,) * 6,
    )(parity + 2 * link_subset, dense, edges, state, cotangent, up, down)
    far_chip = swap(planes, [(2 * c + k, (2 * c + 2 + k) % count) for c in range(1, chips, 2) for k in range(2)])
    far_core = swap(fm, [(i, (i + 1) % count) for i in range(1, count, 2)])
    near_chip = swap(planes, [(2 * c + k, 2 * c + 2 + k) for c in range(0, chips, 2) for k in range(2)])
    near_core = swap(fm, [(i, i + 1) for i in range(0, count, 2)])

    panel_outs = [
        ((2, 4, LANES), F32), ((H, 72), BF16), ((72, H), BF16), ((H, 72), BF16),
    ] + [((H, 240), BF16)] * 4 + [((192, H), BF16)] * 4
    panel_scratch = [((432, LANES), F32)]
    if count == 16:
        loops, *panels = call(panel_kernel_plain, panel_outs, panel_scratch)(gathered)
    else:
        pieces = []
        offset = 0
        for width, full in zip(widths, (48, 48, 8, 4)):
            piece = gathered[:, SLABROWS:SLABROWS + 27, offset:offset + width]
            pieces.append(piece.reshape(432, full))
            offset += width
        pieces.append(jnp.zeros((432, 20), BF16))
        loops, *panels = call(panel_kernel, panel_outs, panel_scratch)(
            gathered, jnp.concatenate(pieces, axis=1)
        )

    window = 18 * SITES
    coeff, grads = call(
        functools.partial(conv_kernel, count == 16),
        [((4, 8, SITES), F32), ((16, 27, LANES) if count == 16 else (432, LANES), BF16)],
        [
            ((8, window), F32), ((8, window), F32), ((H, window), BF16), ((H, window), BF16), ((H, window), BF16),
            ((3, 8, window), F32), ((8, window), F32), ((H, window), BF16), ((H, window), BF16), ((H, 4 * SITES), BF16),
            ((432, 4 * SITES), BF16), ((432, 4 * SITES), BF16), ((72, 4 * SITES), BF16), ((72, 4 * SITES), BF16),
            ((432, LANES), F32), ((4, 3, H, 4 * SITES), F32),
        ],
        limit=20 * 1024 * 1024,
        places=(smem,) + (vmem,) * 17,
    )(place, fm, near_core, far_core, near_chip, far_chip, loops, *panels)
    if count != 16:
        offset = 0
        pieces = []
        for width, full in zip(widths, (48, 48, 8, 4)):
            pieces.append(grads[:, offset:offset + full].reshape(count, 27, width))
            offset += full
        grads = jnp.concatenate(pieces, axis=2)
    grads = lax.all_to_all(grads, "tm", split_axis=0, concat_axis=0, tiled=True)
    (new_links,) = call(
        update_kernel, [(links.shape, F32)], [((4, 2, 8, LANES), F32)]
    )(dense, moves, coeff)
    grad_first, grad_second, grad_third, grad_last = call(
        functools.partial(sum_kernel, widths),
        [((1, 27 * width), F32) for width in (widths[2], widths[0], widths[1], widths[3])],
        [],
    )(grads)
    return (new_links, grad_first, grad_second, grad_third, grad_last)


def solution(mesh):
    placed = (
        P(None, None, None, None, "groups", "tm", None),
        P(None, None, None, None, "groups", "tm", None),
        P("groups", "tm"),
        P("groups", "tm"),
        P("tm"),
        P("tm"),
        P("tm"),
        P("tm"),
    )
    return jax.shard_map(
        on_device,
        mesh=mesh,
        in_specs=placed,
        out_specs=(
            P(None, None, None, None, "groups", "tm", None),
            P("groups", "tm"),
            P("groups", "tm"),
            P("groups", "tm"),
            P("groups", "tm"),
        ),
        check_vma=False,
    )
```

```python
import functools

import jax
import jax.numpy as jnp
from jax import lax
from jax.experimental import pallas as pl
from jax.experimental.pallas import tpu as pltpu
from jax.sharding import PartitionSpec as P

F32 = jnp.float32
BF16 = jnp.bfloat16
TAPS = 9
H = 48
LANES = 128
SITES = 512
PAIRS = ((0, 1), (0, 2), (0, 3), (1, 2), (1, 3), (2, 3))
SWAP = (0, 2, 1, 4, 3, 6, 5, 8, 7)
ENTRIES = tuple((c, i, j) for c in range(2) for i in range(3) for j in range(3))
PLANE = 180
SLABROWS = 24
BLOCKROWS = 64
LIMIT = 8 * 1024 * 1024


def lane_iota(rows):
    return lax.broadcasted_iota(jnp.int32, (rows, LANES), 1)


def row_iota():
    return lax.broadcasted_iota(jnp.int32, (8, LANES), 0)


def roll_lanes(value, amount):
    return pltpu.roll(value, amount % LANES, 1)


def shift_z(chunk, sign, lanes):
    z = lanes % 8
    if sign > 0:
        return jnp.where(z == 7, roll_lanes(chunk, 7), roll_lanes(chunk, -1))
    return jnp.where(z == 0, roll_lanes(chunk, -7), roll_lanes(chunk, 1))


def shift_y(chunk, sign, lanes):
    y = lanes // 8 % 8
    if sign > 0:
        return jnp.where(y == 7, roll_lanes(chunk, 56), roll_lanes(chunk, -8))
    return jnp.where(y == 0, roll_lanes(chunk, -56), roll_lanes(chunk, 8))


def dense_shift(pair, axis, sign):
    lanes = lane_iota(8)
    if axis == 2:
        return [shift_z(chunk, sign, lanes) for chunk in pair]
    if axis == 1:
        return [shift_y(chunk, sign, lanes) for chunk in pair]
    low = lanes < 64
    first, second = [roll_lanes(chunk, 64) for chunk in pair]
    if sign > 0:
        return [jnp.where(low, first, second), jnp.where(low, second, pltpu.roll(first, 4, 0))]
    return [jnp.where(low, pltpu.roll(second, 4, 0), first), jnp.where(low, first, second)]


def pack_pair(value):
    return [
        jnp.concatenate([value[:, c * 128:c * 128 + 128], value[:, 256 + c * 128:384 + c * 128]], axis=0)
        for c in range(2)
    ]


def halo_pair(ref, index):
    top = row_iota() < 4
    pair = []
    for c in range(2):
        low = jnp.broadcast_to(ref[index, c:c + 1, :], (8, LANES))
        high = jnp.broadcast_to(ref[index, 2 + c:3 + c, :], (8, LANES))
        pair.append(jnp.where(top, low, high))
    return pair


def load_matrix(read):
    real = [[read(3 * i + j) for j in range(3)] for i in range(3)]
    imag = [[read(9 + 3 * i + j) for j in range(3)] for i in range(3)]
    return (real, imag, 1)


def dagger(matrix):
    real, imag, sign = matrix
    return (
        [[real[j][i] for j in range(3)] for i in range(3)],
        [[imag[j][i] for j in range(3)] for i in range(3)],
        -sign,
    )


def total(terms, signs):
    value = None
    for term, sign in zip(terms, signs):
        if value is None:
            value = term if sign > 0 else -term
        else:
            value = value + term if sign > 0 else value - term
    return value


def mat_mul(left, right):
    lr, li, ls = left
    rr, ri, rs = right
    same = ls == rs
    height = len(lr)
    real = [[None] * 3 for _ in range(height)]
    imag = [[None] * 3 for _ in range(height)]
    for i in range(height):
        for j in range(3):
            real[i][j] = total(
                [lr[i][k] * rr[k][j] for k in range(3)] + [li[i][k] * ri[k][j] for k in range(3)],
                [1, 1, 1] + [-1 if same else 1] * 3,
            )
            imag[i][j] = total(
                [lr[i][k] * ri[k][j] for k in range(3)] + [li[i][k] * rr[k][j] for k in range(3)],
                [1, 1, 1] + [1 if same else -1] * 3,
            )
    return (real, imag, ls if same else rs)


def imag_of(matrix, i, j):
    return matrix[1][i][j] if matrix[2] > 0 else -matrix[1][i][j]


def store_matrix(matrix, write):
    for i in range(3):
        for j in range(3):
            write(3 * i + j, matrix[0][i][j])
            write(9 + 3 * i + j, imag_of(matrix, i, j))


def two_rows(read):
    real = [[read(3 * i + j) for j in range(3)] for i in range(2)]
    imag = [[read(6 + 3 * i + j) for j in range(3)] for i in range(2)]
    return (real, imag, 1)


def store_rows(matrix, write):
    for i in range(2):
        for j in range(3):
            write(3 * i + j, matrix[0][i][j])
            write(6 + 3 * i + j, imag_of(matrix, i, j))


def special(matrix):
    real, imag, _ = matrix
    last_r, last_i = [], []
    for k in range(3):
        i, j = (k + 1) % 3, (k + 2) % 3
        last_r.append(
            (real[0][i] * real[1][j] - imag[0][i] * imag[1][j])
            - (real[0][j] * real[1][i] - imag[0][j] * imag[1][i])
        )
        last_i.append(
            (real[0][j] * imag[1][i] + imag[0][j] * real[1][i])
            - (real[0][i] * imag[1][j] + imag[0][i] * real[1][j])
        )
    return (real + [last_r], imag + [last_i], 1)


def anti_parts(matrix):
    parts = [2.0 * imag_of(matrix, i, i) for i in range(3)]
    for i, j in ((0, 1), (0, 2), (1, 2)):
        parts.append(matrix[0][i][j] - matrix[0][j][i])
        parts.append(imag_of(matrix, i, j) + imag_of(matrix, j, i))
    return parts


def anti_matrix(parts):
    zero = jnp.zeros_like(parts[0])
    real = [[zero, parts[3], parts[5]], [-parts[3], zero, parts[7]], [-parts[5], -parts[7], zero]]
    imag = [[parts[0], parts[4], parts[6]], [parts[4], parts[1], parts[8]], [parts[6], parts[8], parts[2]]]
    return real, imag


def anti_mul(parts, right):
    real, imag = anti_matrix(parts)
    rr, ri, _ = right
    out_r = [[None] * 3 for _ in range(3)]
    out_i = [[None] * 3 for _ in range(3)]
    for i in range(3):
        for j in range(3):
            value_r = -(imag[i][i] * ri[i][j])
            value_i = imag[i][i] * rr[i][j]
            for k in range(3):
                if k != i:
                    value_r = value_r + real[i][k] * rr[k][j] - imag[i][k] * ri[k][j]
                    value_i = value_i + real[i][k] * ri[k][j] + imag[i][k] * rr[k][j]
            out_r[i][j] = value_r
            out_i[i][j] = value_i
    return (out_r, out_i, 1)


def pack_links(links_ref, dense):
    def body(mu, carry):
        for e, (c, i, j) in enumerate(ENTRIES):
            low, high = pack_pair(links_ref[mu, c, i, j, 0].astype(F32))
            dense[mu, e, 0] = low
            dense[mu, e, 1] = high
        return carry

    lax.fori_loop(0, 4, body, 0)


def face_kernel(links_ref, up_ref, down_ref, dense, edges, staples, slab, moved, rows):
    pack_links(links_ref, dense)

    def shift_body(e, carry):
        pair = [dense[3, e, 0], dense[3, e, 1]]
        for mu in range(3):
            low, high = dense_shift(pair, mu, 1)
            moved[mu, e, 0] = low
            moved[mu, e, 1] = high
        return carry

    lax.fori_loop(0, 18, shift_body, 0, unroll=6)

    def staple_body(step, carry):
        mu = step // 2
        c = step % 2
        u_mu = load_matrix(lambda e: dense[mu, e, c])
        u_t = load_matrix(lambda e: dense[3, e, c])
        edge = mat_mul(u_mu, load_matrix(lambda e: moved[mu, e, c]))

        def write_edge(e, value):
            edges[mu, e, c] = value

        store_matrix(edge, write_edge)

        def write(e, value):
            staples[mu, e, c] = value
            rows[16 + mu * 18 + e, pl.ds(c, 1)] = value[3:4]
            rows[16 + mu * 18 + e, pl.ds(2 + c, 1)] = value[7:8]

        store_matrix(mat_mul(dagger(edge), u_t), write)
        return carry

    lax.fori_loop(0, 6, staple_body, 0, unroll=2)

    def slab_body(c, carry):
        u_t = load_matrix(lambda e: dense[3, e, c])
        ahead = load_matrix(lambda e: pltpu.roll(dense[3, e, c], 7, 0))
        two = mat_mul(u_t, ahead)
        later = tuple(
            [[pltpu.roll(part[i][j], 6, 0) for j in range(3)] for i in range(3)] for part in two[:2]
        ) + (two[2],)
        four = mat_mul((two[0][:2], two[1][:2], two[2]), later)

        def write(e, value):
            slab[e, pl.ds(c, 1)] = value[0:1]
            slab[e, pl.ds(2 + c, 1)] = value[4:5]
            rows[e, pl.ds(c, 1)] = value[0:1]
            rows[e, pl.ds(2 + c, 1)] = value[4:5]

        store_rows(four, write)
        return carry

    lax.fori_loop(0, 2, slab_body, 0)
    for q in range(4):
        up_ref[:, q * 128:q * 128 + 128] = rows[:, q, :].astype(BF16)

    def down_body(e, carry):
        for mu in range(3):
            for c in range(2):
                value = dense[mu, e, c]
                rows[16 + mu * 18 + e, c:c + 1] = value[0:1]
                rows[16 + mu * 18 + e, 2 + c:3 + c] = value[4:5]
        return carry

    lax.fori_loop(0, 18, down_body, 0, unroll=6)
    for q in range(4):
        down_ref[:, q * 128:q * 128 + 128] = rows[:, q, :].astype(BF16)


def block_kernel(
    widths, place_ref, up_ref, down_ref, slab, w1_ref, w2_ref, w3_ref, w4_ref, after_ref, block_ref, other, block
):
    even = place_ref[0] % 2 == 0
    up = up_ref[0:16].astype(F32)
    down = down_ref[0:16].astype(F32)
    for q in range(4):
        lanes = slice(q * 128, q * 128 + 128)
        other[:, q, :] = jnp.where(even, down[0:12, lanes], up[0:12, lanes])
    first = two_rows(lambda e: jnp.where(even, slab[e], other[e]))
    second = special(two_rows(lambda e: jnp.where(even, other[e], slab[e])))

    def write(e, value):
        block[2 * e:2 * e + 2, :] = jnp.where(even, value[0:2], value[2:4])

    store_rows(mat_mul(first, second), write)
    block[SLABROWS:BLOCKROWS] = jnp.zeros((BLOCKROWS - SLABROWS, LANES), F32)
    offset = 0
    for ref, width in zip((w2_ref, w3_ref, w1_ref, w4_ref), widths):
        flat = ref[...].astype(F32)
        for r in range(27):
            block[SLABROWS + r:SLABROWS + r + 1, offset:offset + width] = (
                flat[width * r:width * r + width].reshape(1, width)
            )
        offset += width
    value = block[...].astype(BF16)
    for d in range(block_ref.shape[0]):
        block_ref[d] = value


def put_row(rows, channel, c, value):
    for t in range(4):
        rows[t, c, pl.ds(channel, 1), :] = value[t:t + 1]
        rows[t, 2 + c, pl.ds(channel, 1), :] = value[4 + t:5 + t]


def sum_at(mu, e, c):
    return (mu * 18 + e) * 2 + c


def force_at(mu, e, c):
    return 108 + (mu * 9 + e) * 2 + c


def space_kernel(dense, time_staples, state, moved, staples):
    state[108:180] = jnp.zeros((72, 8, LANES), F32)
    steps = row_iota() % 4

    def shift_body(e, carry):
        for nu in range(3):
            pair = [dense[nu, e, 0], dense[nu, e, 1]]
            for mu in range(3):
                if mu != nu:
                    low, high = dense_shift(pair, mu, 1)
                    moved[mu, nu, e, 0] = low
                    moved[mu, nu, e, 1] = high
        return carry

    lax.fori_loop(0, 18, shift_body, 0, unroll=6)

    def plane_body(step, carry):
        plane = step // 2
        c = step % 2
        mu = jnp.where(plane == 2, 1, 0)
        nu = jnp.where(plane == 0, 1, 2)
        u_mu = load_matrix(lambda e: dense[mu, e, c])
        u_nu = load_matrix(lambda e: dense[nu, e, c])
        one = mat_mul(u_mu, load_matrix(lambda e: moved[mu, nu, e, c]))
        two = mat_mul(u_nu, load_matrix(lambda e: moved[nu, mu, e, c]))
        loop = mat_mul(one, dagger(two))
        state[PLANE + step] = (loop[0][0][0] + loop[0][1][1] + loop[0][2][2]) / 3.0
        for e, part in enumerate(anti_parts(loop)):
            state[force_at(mu, e, c)] += part
            state[force_at(nu, e, c)] -= part

        def write_mu(e, value):
            staples[mu, nu, e, c] = value

        def write_nu(e, value):
            staples[nu, mu, e, c] = value

        store_matrix(mat_mul(dagger(one), u_nu), write_mu)
        store_matrix(mat_mul(dagger(two), u_mu), write_nu)
        return carry

    lax.fori_loop(0, 6, plane_body, 0, unroll=2)

    def lower_body(e, carry):
        for mu in range(3):
            acc = [jnp.where(steps == 0, 0.0, pltpu.roll(time_staples[mu, e, c], 1, 0)) for c in range(2)]
            for nu in range(3):
                if nu != mu:
                    pair = dense_shift([staples[mu, nu, e, 0], staples[mu, nu, e, 1]], nu, -1)
                    acc = [acc[c] + pair[c] for c in range(2)]
            state[sum_at(mu, e, 0)] = acc[0]
            state[sum_at(mu, e, 1)] = acc[1]
        return carry

    lax.fori_loop(0, 18, lower_body, 0, unroll=6)


def time_kernel(
    code_ref, dense, edges, state, cot_ref, up_ref, down_ref,
    fm_ref, planes_ref, moves_ref,
    cots, gates, moved, staples, sums, halo_up, halo_down, forces, rows,
):
    for q in range(4):
        halo_up[:, q, :] = up_ref[:, q * 128:q * 128 + 128].astype(F32)
        halo_down[:, q, :] = down_ref[:, q * 128:q * 128 + 128].astype(F32)
    rows[...] = jnp.zeros_like(rows)
    pack_links(cot_ref, cots)
    lanes = lane_iota(8)
    site_steps = row_iota() % 4
    colour = (lanes // 64 + lanes // 8 % 8 + lanes % 8 + site_steps) % 2
    code = jnp.zeros_like(site_steps)
    for t in range(4):
        code = jnp.where(site_steps == t, code_ref[0, t], code)
    for mu in range(4):
        active = jnp.logical_and(colour == code % 2, jnp.right_shift(code, mu + 1) % 2 == 1)
        gates[mu] = jnp.where(active, 1.0, 0.0)
    for channel, plane in ((0, 0), (1, 1), (3, 2)):
        for c in range(2):
            put_row(rows, channel, c, state[PLANE + 2 * plane + c])
    for mu in range(4):
        for e in range(9):
            for c in range(2):
                forces[mu, e, c] = state[force_at(mu, e, c)]
    steps = row_iota() % 4

    def shift_body(e, carry):
        for nu in range(3):
            halo = halo_pair(halo_down, 16 + nu * 18 + e)
            below = halo_pair(halo_up, 16 + nu * 18 + e)
            for c in range(2):
                moved[nu, e, c] = jnp.where(steps == 3, halo[c], pltpu.roll(dense[nu, e, c], 7, 0))
                sums[nu, e, c] = state[sum_at(nu, e, c)] + jnp.where(steps == 0, below[c], 0.0)
        return carry

    lax.fori_loop(0, 18, shift_body, 0, unroll=6)

    def plane_body(step, carry):
        mu = step // 2
        c = step % 2
        one = load_matrix(lambda e: edges[mu, e, c])
        two = mat_mul(load_matrix(lambda e: dense[3, e, c]), load_matrix(lambda e: moved[mu, e, c]))
        loop = mat_mul(one, dagger(two))
        put_row(rows, jnp.where(mu == 0, 2, mu + 3), c, (loop[0][0][0] + loop[0][1][1] + loop[0][2][2]) / 3.0)
        for e, part in enumerate(anti_parts(loop)):
            forces[mu, e, c] += part
            forces[3, e, c] -= part

        def write(e, value):
            staples[mu, e, c] = value

        store_matrix(mat_mul(dagger(two), load_matrix(lambda e: dense[mu, e, c])), write)
        return carry

    lax.fori_loop(0, 6, plane_body, 0, unroll=2)

    def lower_body(e, carry):
        acc = None
        for mu in range(3):
            pair = dense_shift([staples[mu, e, 0], staples[mu, e, 1]], mu, -1)
            acc = pair if acc is None else [acc[c] + pair[c] for c in range(2)]
        sums[3, e, 0] = acc[0]
        sums[3, e, 1] = acc[1]
        return carry

    lax.fori_loop(0, 18, lower_body, 0, unroll=6)

    def force_body(step, carry):
        mu = step // 2
        c = step % 2
        current = load_matrix(lambda e: dense[mu, e, c])
        omega = mat_mul(current, load_matrix(lambda e: sums[mu, e, c]))
        parts = [part + forces[mu, e, c] for e, part in enumerate(anti_parts(omega))]
        mean = (parts[0] + parts[1] + parts[2]) * (1.0 / 3.0)
        parts = [parts[e] - mean if e < 3 else parts[e] for e in range(9)]
        parts = [part * (1.0 / 12.0) for part in parts]
        applied = anti_mul(parts, current)
        twice = anti_mul(parts, applied)
        gate = gates[mu]
        slope = jnp.zeros_like(gate)
        curve = jnp.zeros_like(gate)
        for e, (part, i, j) in enumerate(ENTRIES):
            weight = cots[mu, e, c]
            slope = slope + weight * applied[part][i][j]
            curve = curve + weight * twice[part][i][j]
            moves_ref[0, mu, e, c] = (gate * applied[part][i][j]).astype(BF16)
            moves_ref[1, mu, e, c] = (gate * twice[part][i][j]).astype(BF16)
        put_row(rows, 8 + mu, c, gate * slope)
        put_row(rows, 12 + mu, c, gate * curve)
        return carry

    lax.fori_loop(0, 8, force_body, 0, unroll=2)
    for t in range(4):
        for q in range(4):
            value = rows[t, q]
            fm_ref[t, :, q * 128:q * 128 + 128] = value.astype(BF16)
            planes_ref[t, :, q * 128:q * 128 + 128] = value[0:8].astype(BF16)


def selectors():
    row = lax.broadcasted_iota(jnp.int32, (432, 72), 0)
    col = lax.broadcasted_iota(jnp.int32, (432, 72), 1)
    group = row // 12
    spread = (group // 4 * 8 + group % 4 == col).astype(F32).astype(BF16)
    keep = (
        lax.broadcasted_iota(jnp.int32, (432, H), 1) // 4 == lax.broadcasted_iota(jnp.int32, (432, H), 0) % 12
    )
    return spread, keep


def panel_kernel(gathered_ref, weights_ref, loops_ref, p1_ref, p2_ref, p3_ref, p4_ref, b2_ref, b3_ref, b4_ref, weights):
    count = gathered_ref.shape[0]

    def read(chip):
        low = gathered_ref[2 * chip].astype(F32)
        high = gathered_ref[2 * chip + 1].astype(F32)
        return special(
            two_rows(lambda e: jnp.concatenate([low[2 * e:2 * e + 2], high[2 * e:2 * e + 2]], axis=0))
        )

    def flat(matrix):
        return tuple(matrix[0][i][j] for i in range(3) for j in range(3)) + tuple(
            imag_of(matrix, i, j) for i in range(3) for j in range(3)
        )

    def chain(chip, state):
        return flat(mat_mul(load_matrix(lambda e: state[e]), read(chip)))

    state = lax.fori_loop(1, count // 2, chain, flat(read(0)))
    loops_ref[0] = (state[0] + state[4] + state[8]) / 3.0
    loops_ref[1] = (state[9] + state[13] + state[17]) / 3.0

    if weights_ref is None:
        for d in range(count):
            block = gathered_ref[d].astype(F32)
            weights[27 * d:27 * d + 27, :] = block[SLABROWS:SLABROWS + 27]
    else:
        weights[...] = weights_ref[...].astype(F32)
    for k in range(TAPS):
        rows = slice(H * k, H * k + H)
        back = slice(H * SWAP[k], H * SWAP[k] + H)
        p2_ref[:, rows] = weights[rows, 0:48].astype(BF16)
        p3_ref[:, rows] = weights[rows, 48:96].astype(BF16)
        p1_ref[:, 8 * k:8 * k + 8] = weights[rows, 96:104].astype(BF16)
        turned = weights[back, :].T
        b2_ref[:, rows] = turned[0:48].astype(BF16)
        b3_ref[:, rows] = turned[48:96].astype(BF16)
    spread, keep = selectors()
    place = (
        lax.broadcasted_iota(jnp.int32, (LANES, H), 0) == 104 + lax.broadcasted_iota(jnp.int32, (LANES, H), 1) % 4
    ).astype(F32).astype(BF16)
    wide = jnp.dot(weights[...].astype(BF16), place, preferred_element_type=F32)
    wide = jnp.where(keep, wide, 0.0).astype(BF16)
    last = lax.dot_general(spread, wide, (((0,), (0,)), ((), ())), preferred_element_type=F32)
    p4_ref[...] = last.astype(BF16)
    for k in range(TAPS):
        b4_ref[:, 8 * k:8 * k + 8] = last[8 * SWAP[k]:8 * SWAP[k] + 8, :].T.astype(BF16)


def panel_kernel_plain(gathered_ref, *rest):
    panel_kernel(gathered_ref, None, *rest)


def chunks_of(value):
    return [value[:, q * 128:q * 128 + 128] for q in range(4)]


def one_shift(chunks, position):
    if position == 0:
        return chunks
    lanes = lane_iota(chunks[0].shape[0])
    sign = 1 if position % 2 == 1 else -1
    if position > 4:
        return [shift_z(chunk, sign, lanes) for chunk in chunks]
    if position > 2:
        return [shift_y(chunk, sign, lanes) for chunk in chunks]
    low = lanes < 64
    rolled = [roll_lanes(chunk, 64) for chunk in chunks]
    if sign > 0:
        return [jnp.where(low, rolled[q], rolled[(q + 1) % 4]) for q in range(4)]
    return [jnp.where(low, rolled[(q + 3) % 4], rolled[q]) for q in range(4)]


def all_shifts(chunks):
    lanes = lane_iota(chunks[0].shape[0])
    y = lanes // 8 % 8
    z = lanes % 8
    low = lanes < 64
    half = [roll_lanes(chunk, 64) for chunk in chunks]
    return [
        chunks,
        [jnp.where(low, half[q], half[(q + 1) % 4]) for q in range(4)],
        [jnp.where(low, half[(q + 3) % 4], half[q]) for q in range(4)],
        [roll_lanes(jnp.where(y == 0, half[q], chunks[q]), -8) for q in range(4)],
        [roll_lanes(jnp.where(y == 7, half[q], chunks[q]), 8) for q in range(4)],
        [roll_lanes(jnp.where(z == 0, roll_lanes(chunk, 8), chunk), -1) for chunk in chunks],
        [roll_lanes(jnp.where(z == 7, roll_lanes(chunk, -8), chunk), 1) for chunk in chunks],
    ]


def span(slice_index, count=1):
    if isinstance(slice_index, int):
        return slice(slice_index * SITES, (slice_index + count) * SITES)
    return pl.ds(pl.multiple_of(slice_index * SITES, SITES), count * SITES)


def slot_of(slot):
    return slice(slot * SITES, (slot + 1) * SITES)


def wide_dot(weights, source, index, kept=None, slot=0):
    shifts = all_shifts(chunks_of(source[:, span(index)]))
    ahead, behind = source[:, span(index + 1)], source[:, span(index - 1)]
    outs = []
    for half in range(2):
        lanes = slice(256 * half, 256 * half + 256)
        columns = [jnp.concatenate(shifted[2 * half:2 * half + 2], axis=1) for shifted in shifts]
        stack = jnp.concatenate(columns + [ahead[:, lanes], behind[:, lanes]], axis=0)
        if kept is not None:
            kept[0:432, slot * SITES + 256 * half:slot * SITES + 256 * half + 256] = stack
        outs.append(jnp.dot(weights[...], stack, preferred_element_type=F32))
    return jnp.concatenate(outs, axis=1)


def turned_back(value):
    return jnp.concatenate([value[:, 128 * q:128 * q + 128].T for q in range(4)], axis=0)


def thin_stack(source, index):
    ahead = chunks_of(source[:, span(index + 1)])
    behind = chunks_of(source[:, span(index - 1)])
    columns = all_shifts(chunks_of(source[:, span(index)])) + [ahead, behind]
    return jnp.concatenate(
        [jnp.concatenate([column[q] for column in columns], axis=0).astype(BF16) for q in range(4)], axis=1
    )


def one_minus_square(value):
    value = value.astype(F32)
    return 1.0 - value * value


def conv_kernel(
    split, place_ref, fm_ref, near_ref, far_ref, near_chip_ref, far_chip_ref, loops_ref,
    p1_ref, p2_ref, p3_ref, p4_ref, b2_ref, b3_ref, b4_ref,
    coeff_ref, grads_ref,
    feats, mixed, h1, h2, h3, parts, lasts, g3, g2, g1, wide_back, wide_first, thin, thin_back, packed,
):
    wide_back[432:512, :] = jnp.zeros((80, 4 * SITES), BF16)
    wide_first[432:512, :] = jnp.zeros((80, 4 * SITES), BF16)
    row8 = lax.broadcasted_iota(jnp.int32, (8, SITES), 0)
    loop_re = jnp.concatenate([loops_ref[0, q:q + 1, :] for q in range(4)], axis=1)
    loop_im = jnp.concatenate([loops_ref[1, q:q + 1, :] for q in range(4)], axis=1)
    loops = jnp.where(row8 == 6, loop_re, jnp.where(row8 == 7, loop_im, 0.0))
    loops = loops.astype(BF16).astype(F32)
    first_core = place_ref[0] % 2 == 0
    first_chip = place_ref[0] // 2 % 2 == 0
    for j in range(4):
        near, far = near_chip_ref[j].astype(F32), far_chip_ref[j].astype(F32)
        if j > 0:
            feats[:, span(j - 1)] = jnp.where(first_chip, far, near) + loops
        if j < 3:
            feats[:, span(15 + j)] = jnp.where(first_chip, near, far) + loops
        near, far = near_ref[j].astype(F32), far_ref[j].astype(F32)
        below, above = jnp.where(first_core, far, near), jnp.where(first_core, near, far)
        for base, value in ((3, below), (7, fm_ref[j].astype(F32)), (11, above)):
            feats[:, span(base + j)] = value[0:8] + loops
            mixed[:, span(base + j)] = value[8:16]

    own = span(7, 4)
    contract = (((1,), (1,)), ((), ()))

    def kept_slot(index):
        return index - 7 if 7 <= index < 11 else None

    def first_layer(index):
        stack = thin_stack(feats, index)
        if kept_slot(index) is not None:
            thin[:, slot_of(index - 7)] = stack
        out = jnp.dot(p1_ref[...], stack, preferred_element_type=F32)
        h1[:, span(index)] = jnp.tanh(out).astype(BF16)

    def second_layer(index):
        h2[:, span(index)] = jnp.tanh(wide_dot(p2_ref, h1, index)).astype(BF16)

    def third_layer(index):
        h3[:, span(index)] = jnp.tanh(wide_dot(p3_ref, h2, index)).astype(BF16)

    def taps_of(index):
        taps = jnp.dot(p4_ref[...], h3[:, span(index)], preferred_element_type=F32)
        acc = None
        for position in range(7):
            shifted = one_shift(chunks_of(taps[8 * position:8 * position + 8]), position)
            acc = shifted if acc is None else [a + b for a, b in zip(acc, shifted)]
        parts[0, :, span(index)] = jnp.concatenate(acc, axis=1)
        parts[1, :, span(index)] = taps[56:64]
        parts[2, :, span(index)] = taps[64:72]

    def last_of(index):
        coeff = jnp.tanh(parts[0, :, span(index)] + parts[1, :, span(index + 1)] + parts[2, :, span(index - 1)])
        blend = mixed[:, span(index)]
        value = (blend + coeff * pltpu.roll(blend, 4, 0)) * (1.0 - coeff * coeff)
        lasts[:, span(index)] = jnp.where(row8 < 4, value, 0.0).astype(BF16).astype(F32)
        if 7 <= index < 11:
            coeff_ref[index - 7] = coeff

    def back_third(index):
        stack = thin_stack(lasts, index)
        if kept_slot(index) is not None:
            thin_back[:, slot_of(index - 7)] = stack
        out = jnp.dot(b4_ref[...], stack, preferred_element_type=F32)
        g3[:, span(index)] = (out * one_minus_square(h3[:, span(index)])).astype(BF16)

    def back_second(index):
        slot = kept_slot(index)
        out = wide_dot(b3_ref, g3, index, None if slot is None else wide_back, slot or 0)
        g2[:, span(index)] = (out * one_minus_square(h2[:, span(index)])).astype(BF16)

    def back_first(index):
        out = wide_dot(b2_ref, g2, index, wide_first, index - 7)
        g1[:, slot_of(index - 7)] = (out * one_minus_square(h1[:, span(index)])).astype(BF16)

    stages = (
        (0, 1, 17, first_layer),
        (2, 2, 16, second_layer),
        (4, 3, 15, third_layer),
        (5, 3, 15, taps_of),
        (7, 4, 14, last_of),
        (9, 5, 13, back_third),
        (11, 6, 12, back_second),
        (13, 7, 11, back_first),
    )
    for step in range(1, 24):
        for delay, low, high, task in reversed(stages):
            if low <= step - delay < high:
                task(step - delay)
        if step == 19:
            grad_last = lax.dot_general(
                thin_back[...], h3[:, own], contract, preferred_element_type=F32
            )
            spread, keep = selectors()
            ordered = jnp.concatenate([grad_last[8 * SWAP[k]:8 * SWAP[k] + 8] for k in range(TAPS)], axis=0)
            broad = jnp.dot(spread, ordered.astype(BF16), preferred_element_type=F32)
        if step == 20:
            broad = jnp.where(keep, broad, 0.0).astype(BF16)
            place = (
                lax.broadcasted_iota(jnp.int32, (H, LANES), 1)
                == 104 + lax.broadcasted_iota(jnp.int32, (H, LANES), 0) % 4
            ).astype(F32).astype(BF16)
            packed[...] = jnp.dot(broad, place, preferred_element_type=F32)
        if step == 21:
            grad_third = turned_back(
                lax.dot_general(h2[:, own], wide_back[...], contract, preferred_element_type=F32)
            )
        if step == 22:
            for k in range(TAPS):
                packed[H * k:H * k + H, 48:96] = grad_third[H * SWAP[k]:H * SWAP[k] + H]
    grad_second = turned_back(
        lax.dot_general(h1[:, own], wide_first[...], contract, preferred_element_type=F32)
    )
    grad_first = lax.dot_general(g1[...], thin[...], contract, preferred_element_type=F32)
    for k in range(TAPS):
        rows = slice(H * k, H * k + H)
        packed[rows, 0:48] = grad_second[H * SWAP[k]:H * SWAP[k] + H]
        packed[rows, 96:104] = grad_first[:, 8 * k:8 * k + 8]
    if split:
        for d in range(16):
            grads_ref[d] = packed[27 * d:27 * d + 27, :].astype(BF16)
    else:
        grads_ref[...] = packed[...].astype(BF16)


def update_kernel(dense, moves_ref, coeff_ref, out_ref, factors):
    for mu in range(4):
        for t in range(4):
            for c in range(2):
                factors[mu, c, t:t + 1, :] = coeff_ref[t, mu:mu + 1, c * 128:c * 128 + 128]
                factors[mu, c, 4 + t:5 + t, :] = coeff_ref[t, mu:mu + 1, 256 + c * 128:384 + c * 128]

    def body(mu, carry):
        factor = [factors[mu, c] for c in range(2)]
        half = [0.5 * value * value for value in factor]
        for e, (part, i, j) in enumerate(ENTRIES):
            new = [
                dense[mu, e, c]
                + factor[c] * moves_ref[0, mu, e, c].astype(F32)
                + half[c] * moves_ref[1, mu, e, c].astype(F32)
                for c in range(2)
            ]
            out_ref[mu, part, i, j, 0] = jnp.concatenate(
                [new[0][0:4], new[1][0:4], new[0][4:8], new[1][4:8]], axis=1
            )
        return carry

    lax.fori_loop(0, 4, body, 0)


def sum_kernel(widths, parts_ref, first_ref, second_ref, third_ref, last_ref):
    value = parts_ref[0].astype(F32)
    for d in range(1, parts_ref.shape[0]):
        value = value + parts_ref[d].astype(F32)
    offset = 0
    for ref, width in zip((second_ref, third_ref, first_ref, last_ref), widths):
        for r in range(27):
            ref[:, width * r:width * r + width] = value[r:r + 1, offset:offset + width]
        offset += width


def call(body, outs, scratch, places=None, cost=None, limit=LIMIT):
    specs = {}
    if places is not None:
        specs["in_specs"] = [pl.BlockSpec(memory_space=place) for place in places]
    return pl.pallas_call(
        body,
        out_shape=[jax.ShapeDtypeStruct(shape, dtype) for shape, dtype in outs],
        scratch_shapes=[pltpu.VMEM(*item) if isinstance(item, tuple) else item for item in scratch],
        compiler_params=pltpu.CompilerParams(vmem_limit_bytes=limit),
        cost_estimate=cost,
        **specs,
    )


def on_device(links, cotangent, parity, link_subset, w_first, w_second, w_third, w_last):
    count = lax.axis_size("tm")

    def send(value, distance):
        return lax.ppermute(value, "tm", [(i, (i + distance) % count) for i in range(count)])

    def swap(value, pairs):
        return lax.ppermute(value, "tm", pairs + [(target, source) for source, target in pairs])

    chips = count // 2
    widths = (768 // count, 768 // count, 128 // count, 64 // count)
    vmem, smem = pltpu.VMEM, pltpu.SMEM
    field = ((4, 18, 2, 8, LANES), F32)
    space = ((3, 18, 2, 8, LANES), F32)
    edge_rows = ((70, SITES), BF16)
    up, down, dense, edges, staples, slab = call(
        face_kernel,
        [edge_rows, edge_rows, field, space, space, ((12, 4, LANES), F32)],
        [space, ((70, 4, LANES), F32)],
    )(links)
    up = send(up, 1)
    down = send(down, -1)
    (state,) = call(
        space_kernel,
        [((186, 8, LANES), F32)],
        [((3, 3, 18, 2, 8, LANES), F32), ((3, 3, 18, 2, 8, LANES), F32)],
        cost=pl.CostEstimate(flops=4_000_000_000, bytes_accessed=16_000_000, transcendentals=0),
    )(dense, staples)
    place = lax.axis_index("tm").astype(jnp.int32)[None]
    (block,) = call(
        functools.partial(block_kernel, widths),
        [((count, BLOCKROWS, LANES), BF16)],
        [((12, 4, LANES), F32), ((BLOCKROWS, LANES), F32)],
        places=(smem,) + (vmem,) * 7 + (pl.ANY,),
    )(place, up, down, slab, w_first, w_second, w_third, w_last, state)
    gathered = lax.all_to_all(block, "tm", split_axis=0, concat_axis=0, tiled=True)
    fm, planes, moves = call(
        time_kernel,
        [
            ((4, 16, SITES), BF16), ((4, 8, SITES), BF16),
            ((2, 4, 18, 2, 8, LANES), BF16),
        ],
        [
            field, ((4, 8, LANES), F32), space, space, field, ((70, 4, LANES), F32), ((70, 4, LANES), F32),
            ((4, 9, 2, 8, LANES), F32), ((4, 4, 16, LANES), F32),
        ],
        places=(smem,) + (vmem,) * 6,
    )(parity + 2 * link_subset, dense, edges, state, cotangent, up, down)
    far_chip = swap(planes, [(2 * c + k, (2 * c + 2 + k) % count) for c in range(1, chips, 2) for k in range(2)])
    far_core = swap(fm, [(i, (i + 1) % count) for i in range(1, count, 2)])
    near_chip = swap(planes, [(2 * c + k, 2 * c + 2 + k) for c in range(0, chips, 2) for k in range(2)])
    near_core = swap(fm, [(i, i + 1) for i in range(0, count, 2)])

    panel_outs = [
        ((2, 4, LANES), F32), ((H, 72), BF16), ((H, 432), BF16), ((H, 432), BF16), ((72, H), BF16),
        ((H, 432), BF16), ((H, 432), BF16), ((H, 72), BF16),
    ]
    panel_scratch = [((432, LANES), F32)]
    if count == 16:
        loops, p1, p2, p3, p4, b2, b3, b4 = call(panel_kernel_plain, panel_outs, panel_scratch)(gathered)
    else:
        pieces = []
        offset = 0
        for width, full in zip(widths, (48, 48, 8, 4)):
            piece = gathered[:, SLABROWS:SLABROWS + 27, offset:offset + width]
            pieces.append(piece.reshape(432, full))
            offset += width
        pieces.append(jnp.zeros((432, 20), BF16))
        loops, p1, p2, p3, p4, b2, b3, b4 = call(panel_kernel, panel_outs, panel_scratch)(
            gathered, jnp.concatenate(pieces, axis=1)
        )

    window = 18 * SITES
    coeff, grads = call(
        functools.partial(conv_kernel, count == 16),
        [((4, 8, SITES), F32), ((16, 27, LANES) if count == 16 else (432, LANES), BF16)],
        [
            ((8, window), F32), ((8, window), F32), ((H, window), BF16), ((H, window), BF16), ((H, window), BF16),
            ((3, 8, window), F32), ((8, window), F32), ((H, window), BF16), ((H, window), BF16), ((H, 4 * SITES), BF16),
            ((512, 4 * SITES), BF16), ((512, 4 * SITES), BF16), ((72, 4 * SITES), BF16), ((72, 4 * SITES), BF16),
            ((432, LANES), F32),
        ],
        limit=20 * 1024 * 1024,
        places=(smem,) + (vmem,) * 13,
    )(place, fm, near_core, far_core, near_chip, far_chip, loops, p1, p2, p3, p4, b2, b3, b4)
    if count != 16:
        offset = 0
        pieces = []
        for width, full in zip(widths, (48, 48, 8, 4)):
            pieces.append(grads[:, offset:offset + full].reshape(count, 27, width))
            offset += full
        grads = jnp.concatenate(pieces, axis=2)
    grads = lax.all_to_all(grads, "tm", split_axis=0, concat_axis=0, tiled=True)
    (new_links,) = call(
        update_kernel, [(links.shape, F32)], [((4, 2, 8, LANES), F32)]
    )(dense, moves, coeff)
    grad_first, grad_second, grad_third, grad_last = call(
        functools.partial(sum_kernel, widths),
        [((1, 27 * width), F32) for width in (widths[2], widths[0], widths[1], widths[3])],
        [],
    )(grads)
    return (new_links, grad_first, grad_second, grad_third, grad_last)


def solution(mesh):
    placed = (
        P(None, None, None, None, "groups", "tm", None),
        P(None, None, None, None, "groups", "tm", None),
        P("groups", "tm"),
        P("groups", "tm"),
        P("tm"),
        P("tm"),
        P("tm"),
        P("tm"),
    )
    return jax.shard_map(
        on_device,
        mesh=mesh,
        in_specs=placed,
        out_specs=(
            P(None, None, None, None, "groups", "tm", None),
            P("groups", "tm"),
            P("groups", "tm"),
            P("groups", "tm"),
            P("groups", "tm"),
        ),
        check_vma=False,
    )
```

```python
import functools

import jax
import jax.numpy as jnp
from jax import lax
from jax.experimental import pallas as pl
from jax.experimental.pallas import tpu as pltpu
from jax.sharding import PartitionSpec as P

F32 = jnp.float32
BF16 = jnp.bfloat16
TAPS = 9
H = 48
LANES = 128
SITES = 512
PAIRS = ((0, 1), (0, 2), (0, 3), (1, 2), (1, 3), (2, 3))
SWAP = (0, 2, 1, 4, 3, 6, 5, 8, 7)
ENTRIES = tuple((c, i, j) for c in range(2) for i in range(3) for j in range(3))
PLANE = 180
SLABROWS = 24
BLOCKROWS = 64
LIMIT = 8 * 1024 * 1024


def lane_iota(rows):
    return lax.broadcasted_iota(jnp.int32, (rows, LANES), 1)


def row_iota():
    return lax.broadcasted_iota(jnp.int32, (8, LANES), 0)


def roll_lanes(value, amount):
    return pltpu.roll(value, amount % LANES, 1)


def shift_z(chunk, sign, lanes):
    z = lanes % 8
    if sign > 0:
        return jnp.where(z == 7, roll_lanes(chunk, 7), roll_lanes(chunk, -1))
    return jnp.where(z == 0, roll_lanes(chunk, -7), roll_lanes(chunk, 1))


def shift_y(chunk, sign, lanes):
    y = lanes // 8 % 8
    if sign > 0:
        return jnp.where(y == 7, roll_lanes(chunk, 56), roll_lanes(chunk, -8))
    return jnp.where(y == 0, roll_lanes(chunk, -56), roll_lanes(chunk, 8))


def dense_shift(pair, axis, sign):
    lanes = lane_iota(8)
    if axis == 2:
        return [shift_z(chunk, sign, lanes) for chunk in pair]
    if axis == 1:
        return [shift_y(chunk, sign, lanes) for chunk in pair]
    low = lanes < 64
    first, second = [roll_lanes(chunk, 64) for chunk in pair]
    if sign > 0:
        return [jnp.where(low, first, second), jnp.where(low, second, pltpu.roll(first, 4, 0))]
    return [jnp.where(low, pltpu.roll(second, 4, 0), first), jnp.where(low, first, second)]


def pack_pair(value):
    return [
        jnp.concatenate([value[:, c * 128:c * 128 + 128], value[:, 256 + c * 128:384 + c * 128]], axis=0)
        for c in range(2)
    ]


def halo_pair(ref, index):
    top = row_iota() < 4
    pair = []
    for c in range(2):
        low = jnp.broadcast_to(ref[index, c:c + 1, :], (8, LANES))
        high = jnp.broadcast_to(ref[index, 2 + c:3 + c, :], (8, LANES))
        pair.append(jnp.where(top, low, high))
    return pair


def load_matrix(read):
    real = [[read(3 * i + j) for j in range(3)] for i in range(3)]
    imag = [[read(9 + 3 * i + j) for j in range(3)] for i in range(3)]
    return (real, imag, 1)


def dagger(matrix):
    real, imag, sign = matrix
    return (
        [[real[j][i] for j in range(3)] for i in range(3)],
        [[imag[j][i] for j in range(3)] for i in range(3)],
        -sign,
    )


def total(terms, signs):
    value = None
    for term, sign in zip(terms, signs):
        if value is None:
            value = term if sign > 0 else -term
        else:
            value = value + term if sign > 0 else value - term
    return value


def mat_mul(left, right):
    lr, li, ls = left
    rr, ri, rs = right
    same = ls == rs
    height = len(lr)
    real = [[None] * 3 for _ in range(height)]
    imag = [[None] * 3 for _ in range(height)]
    for i in range(height):
        for j in range(3):
            real[i][j] = total(
                [lr[i][k] * rr[k][j] for k in range(3)] + [li[i][k] * ri[k][j] for k in range(3)],
                [1, 1, 1] + [-1 if same else 1] * 3,
            )
            imag[i][j] = total(
                [lr[i][k] * ri[k][j] for k in range(3)] + [li[i][k] * rr[k][j] for k in range(3)],
                [1, 1, 1] + [1 if same else -1] * 3,
            )
    return (real, imag, ls if same else rs)


def imag_of(matrix, i, j):
    return matrix[1][i][j] if matrix[2] > 0 else -matrix[1][i][j]


def store_matrix(matrix, write):
    for i in range(3):
        for j in range(3):
            write(3 * i + j, matrix[0][i][j])
            write(9 + 3 * i + j, imag_of(matrix, i, j))


def two_rows(read):
    real = [[read(3 * i + j) for j in range(3)] for i in range(2)]
    imag = [[read(6 + 3 * i + j) for j in range(3)] for i in range(2)]
    return (real, imag, 1)


def store_rows(matrix, write):
    for i in range(2):
        for j in range(3):
            write(3 * i + j, matrix[0][i][j])
            write(6 + 3 * i + j, imag_of(matrix, i, j))


def special(matrix):
    real, imag, _ = matrix
    last_r, last_i = [], []
    for k in range(3):
        i, j = (k + 1) % 3, (k + 2) % 3
        last_r.append(
            (real[0][i] * real[1][j] - imag[0][i] * imag[1][j])
            - (real[0][j] * real[1][i] - imag[0][j] * imag[1][i])
        )
        last_i.append(
            (real[0][j] * imag[1][i] + imag[0][j] * real[1][i])
            - (real[0][i] * imag[1][j] + imag[0][i] * real[1][j])
        )
    return (real + [last_r], imag + [last_i], 1)


def anti_parts(matrix):
    parts = [2.0 * imag_of(matrix, i, i) for i in range(3)]
    for i, j in ((0, 1), (0, 2), (1, 2)):
        parts.append(matrix[0][i][j] - matrix[0][j][i])
        parts.append(imag_of(matrix, i, j) + imag_of(matrix, j, i))
    return parts


def anti_matrix(parts):
    zero = jnp.zeros_like(parts[0])
    real = [[zero, parts[3], parts[5]], [-parts[3], zero, parts[7]], [-parts[5], -parts[7], zero]]
    imag = [[parts[0], parts[4], parts[6]], [parts[4], parts[1], parts[8]], [parts[6], parts[8], parts[2]]]
    return real, imag


def anti_mul(parts, right):
    real, imag = anti_matrix(parts)
    rr, ri, _ = right
    out_r = [[None] * 3 for _ in range(3)]
    out_i = [[None] * 3 for _ in range(3)]
    for i in range(3):
        for j in range(3):
            value_r = -(imag[i][i] * ri[i][j])
            value_i = imag[i][i] * rr[i][j]
            for k in range(3):
                if k != i:
                    value_r = value_r + real[i][k] * rr[k][j] - imag[i][k] * ri[k][j]
                    value_i = value_i + real[i][k] * ri[k][j] + imag[i][k] * rr[k][j]
            out_r[i][j] = value_r
            out_i[i][j] = value_i
    return (out_r, out_i, 1)


def pack_links(links_ref, dense):
    def body(mu, carry):
        for e, (c, i, j) in enumerate(ENTRIES):
            low, high = pack_pair(links_ref[mu, c, i, j, 0].astype(F32))
            dense[mu, e, 0] = low
            dense[mu, e, 1] = high
        return carry

    lax.fori_loop(0, 4, body, 0)


def face_kernel(links_ref, up_ref, down_ref, dense, edges, staples, slab, moved, rows):
    pack_links(links_ref, dense)

    def shift_body(e, carry):
        pair = [dense[3, e, 0], dense[3, e, 1]]
        for mu in range(3):
            low, high = dense_shift(pair, mu, 1)
            moved[mu, e, 0] = low
            moved[mu, e, 1] = high
        return carry

    lax.fori_loop(0, 18, shift_body, 0, unroll=9)

    def staple_body(step, carry):
        mu = step // 2
        c = step % 2
        u_mu = load_matrix(lambda e: dense[mu, e, c])
        u_t = load_matrix(lambda e: dense[3, e, c])
        edge = mat_mul(u_mu, load_matrix(lambda e: moved[mu, e, c]))

        def write_edge(e, value):
            edges[mu, e, c] = value

        store_matrix(edge, write_edge)

        def write(e, value):
            staples[mu, e, c] = value
            rows[16 + mu * 18 + e, pl.ds(c, 1)] = value[3:4]
            rows[16 + mu * 18 + e, pl.ds(2 + c, 1)] = value[7:8]

        store_matrix(mat_mul(dagger(edge), u_t), write)
        return carry

    lax.fori_loop(0, 6, staple_body, 0, unroll=3)

    def slab_body(c, carry):
        u_t = load_matrix(lambda e: dense[3, e, c])
        ahead = load_matrix(lambda e: pltpu.roll(dense[3, e, c], 7, 0))
        two = mat_mul(u_t, ahead)
        later = tuple(
            [[pltpu.roll(part[i][j], 6, 0) for j in range(3)] for i in range(3)] for part in two[:2]
        ) + (two[2],)
        four = mat_mul((two[0][:2], two[1][:2], two[2]), later)

        def write(e, value):
            slab[e, pl.ds(c, 1)] = value[0:1]
            slab[e, pl.ds(2 + c, 1)] = value[4:5]
            rows[e, pl.ds(c, 1)] = value[0:1]
            rows[e, pl.ds(2 + c, 1)] = value[4:5]

        store_rows(four, write)
        return carry

    lax.fori_loop(0, 2, slab_body, 0)
    for q in range(4):
        up_ref[:, q * 128:q * 128 + 128] = rows[:, q, :].astype(BF16)

    def down_body(e, carry):
        for mu in range(3):
            for c in range(2):
                value = dense[mu, e, c]
                rows[16 + mu * 18 + e, c:c + 1] = value[0:1]
                rows[16 + mu * 18 + e, 2 + c:3 + c] = value[4:5]
        return carry

    lax.fori_loop(0, 18, down_body, 0, unroll=9)
    for q in range(4):
        down_ref[:, q * 128:q * 128 + 128] = rows[:, q, :].astype(BF16)


def block_kernel(
    widths, place_ref, up_ref, down_ref, slab, w1_ref, w2_ref, w3_ref, w4_ref, after_ref, block_ref, other, block
):
    even = place_ref[0] % 2 == 0
    up = up_ref[0:16].astype(F32)
    down = down_ref[0:16].astype(F32)
    for q in range(4):
        lanes = slice(q * 128, q * 128 + 128)
        other[:, q, :] = jnp.where(even, down[0:12, lanes], up[0:12, lanes])
    first = two_rows(lambda e: jnp.where(even, slab[e], other[e]))
    second = special(two_rows(lambda e: jnp.where(even, other[e], slab[e])))

    def write(e, value):
        block[2 * e:2 * e + 2, :] = jnp.where(even, value[0:2], value[2:4])

    store_rows(mat_mul(first, second), write)
    block[SLABROWS:BLOCKROWS] = jnp.zeros((BLOCKROWS - SLABROWS, LANES), F32)
    offset = 0
    for ref, width in zip((w2_ref, w3_ref, w1_ref, w4_ref), widths):
        flat = ref[...].astype(F32)
        for r in range(27):
            block[SLABROWS + r:SLABROWS + r + 1, offset:offset + width] = (
                flat[width * r:width * r + width].reshape(1, width)
            )
        offset += width
    value = block[...].astype(BF16)
    for d in range(block_ref.shape[0]):
        block_ref[d] = value


def put_row(rows, channel, c, value):
    for t in range(4):
        rows[t, c, pl.ds(channel, 1), :] = value[t:t + 1]
        rows[t, 2 + c, pl.ds(channel, 1), :] = value[4 + t:5 + t]


def sum_at(mu, e, c):
    return (mu * 18 + e) * 2 + c


def force_at(mu, e, c):
    return 108 + (mu * 9 + e) * 2 + c


def space_kernel(dense, time_staples, state, moved, staples):
    state[108:180] = jnp.zeros((72, 8, LANES), F32)
    steps = row_iota() % 4

    def shift_body(e, carry):
        for nu in range(3):
            pair = [dense[nu, e, 0], dense[nu, e, 1]]
            for mu in range(3):
                if mu != nu:
                    low, high = dense_shift(pair, mu, 1)
                    moved[mu, nu, e, 0] = low
                    moved[mu, nu, e, 1] = high
        return carry

    lax.fori_loop(0, 18, shift_body, 0, unroll=9)

    def plane_body(step, carry):
        plane = step // 2
        c = step % 2
        mu = jnp.where(plane == 2, 1, 0)
        nu = jnp.where(plane == 0, 1, 2)
        u_mu = load_matrix(lambda e: dense[mu, e, c])
        u_nu = load_matrix(lambda e: dense[nu, e, c])
        one = mat_mul(u_mu, load_matrix(lambda e: moved[mu, nu, e, c]))
        two = mat_mul(u_nu, load_matrix(lambda e: moved[nu, mu, e, c]))
        loop = mat_mul(one, dagger(two))
        state[PLANE + step] = (loop[0][0][0] + loop[0][1][1] + loop[0][2][2]) / 3.0
        for e, part in enumerate(anti_parts(loop)):
            state[force_at(mu, e, c)] += part
            state[force_at(nu, e, c)] -= part

        def write_mu(e, value):
            staples[mu, nu, e, c] = value

        def write_nu(e, value):
            staples[nu, mu, e, c] = value

        store_matrix(mat_mul(dagger(one), u_nu), write_mu)
        store_matrix(mat_mul(dagger(two), u_mu), write_nu)
        return carry

    lax.fori_loop(0, 6, plane_body, 0, unroll=3)

    def lower_body(e, carry):
        for mu in range(3):
            acc = [jnp.where(steps == 0, 0.0, pltpu.roll(time_staples[mu, e, c], 1, 0)) for c in range(2)]
            for nu in range(3):
                if nu != mu:
                    pair = dense_shift([staples[mu, nu, e, 0], staples[mu, nu, e, 1]], nu, -1)
                    acc = [acc[c] + pair[c] for c in range(2)]
            state[sum_at(mu, e, 0)] = acc[0]
            state[sum_at(mu, e, 1)] = acc[1]
        return carry

    lax.fori_loop(0, 18, lower_body, 0, unroll=9)


def time_kernel(
    code_ref, dense, edges, state, cot_ref, up_ref, down_ref,
    fm_ref, planes_ref, moves_ref,
    cots, gates, moved, staples, sums, halo_up, halo_down, forces, rows,
):
    for q in range(4):
        halo_up[:, q, :] = up_ref[:, q * 128:q * 128 + 128].astype(F32)
        halo_down[:, q, :] = down_ref[:, q * 128:q * 128 + 128].astype(F32)
    rows[...] = jnp.zeros_like(rows)
    pack_links(cot_ref, cots)
    lanes = lane_iota(8)
    site_steps = row_iota() % 4
    colour = (lanes // 64 + lanes // 8 % 8 + lanes % 8 + site_steps) % 2
    code = jnp.zeros_like(site_steps)
    for t in range(4):
        code = jnp.where(site_steps == t, code_ref[0, t], code)
    for mu in range(4):
        active = jnp.logical_and(colour == code % 2, jnp.right_shift(code, mu + 1) % 2 == 1)
        gates[mu] = jnp.where(active, 1.0, 0.0)
    for channel, plane in ((0, 0), (1, 1), (3, 2)):
        for c in range(2):
            put_row(rows, channel, c, state[PLANE + 2 * plane + c])
    for mu in range(4):
        for e in range(9):
            for c in range(2):
                forces[mu, e, c] = state[force_at(mu, e, c)]
    steps = row_iota() % 4

    def shift_body(e, carry):
        for nu in range(3):
            halo = halo_pair(halo_down, 16 + nu * 18 + e)
            below = halo_pair(halo_up, 16 + nu * 18 + e)
            for c in range(2):
                moved[nu, e, c] = jnp.where(steps == 3, halo[c], pltpu.roll(dense[nu, e, c], 7, 0))
                sums[nu, e, c] = state[sum_at(nu, e, c)] + jnp.where(steps == 0, below[c], 0.0)
        return carry

    lax.fori_loop(0, 18, shift_body, 0, unroll=9)

    def plane_body(step, carry):
        mu = step // 2
        c = step % 2
        one = load_matrix(lambda e: edges[mu, e, c])
        two = mat_mul(load_matrix(lambda e: dense[3, e, c]), load_matrix(lambda e: moved[mu, e, c]))
        loop = mat_mul(one, dagger(two))
        put_row(rows, jnp.where(mu == 0, 2, mu + 3), c, (loop[0][0][0] + loop[0][1][1] + loop[0][2][2]) / 3.0)
        for e, part in enumerate(anti_parts(loop)):
            forces[mu, e, c] += part
            forces[3, e, c] -= part

        def write(e, value):
            staples[mu, e, c] = value

        store_matrix(mat_mul(dagger(two), load_matrix(lambda e: dense[mu, e, c])), write)
        return carry

    lax.fori_loop(0, 6, plane_body, 0, unroll=3)

    def lower_body(e, carry):
        acc = None
        for mu in range(3):
            pair = dense_shift([staples[mu, e, 0], staples[mu, e, 1]], mu, -1)
            acc = pair if acc is None else [acc[c] + pair[c] for c in range(2)]
        sums[3, e, 0] = acc[0]
        sums[3, e, 1] = acc[1]
        return carry

    lax.fori_loop(0, 18, lower_body, 0, unroll=9)

    def force_body(step, carry):
        mu = step // 2
        c = step % 2
        current = load_matrix(lambda e: dense[mu, e, c])
        omega = mat_mul(current, load_matrix(lambda e: sums[mu, e, c]))
        parts = [part + forces[mu, e, c] for e, part in enumerate(anti_parts(omega))]
        mean = (parts[0] + parts[1] + parts[2]) * (1.0 / 3.0)
        parts = [parts[e] - mean if e < 3 else parts[e] for e in range(9)]
        parts = [part * (1.0 / 12.0) for part in parts]
        applied = anti_mul(parts, current)
        twice = anti_mul(parts, applied)
        gate = gates[mu]
        slope = jnp.zeros_like(gate)
        curve = jnp.zeros_like(gate)
        for e, (part, i, j) in enumerate(ENTRIES):
            weight = cots[mu, e, c]
            slope = slope + weight * applied[part][i][j]
            curve = curve + weight * twice[part][i][j]
            moves_ref[0, mu, e, c] = (gate * applied[part][i][j]).astype(BF16)
            moves_ref[1, mu, e, c] = (gate * twice[part][i][j]).astype(BF16)
        put_row(rows, 8 + mu, c, gate * slope)
        put_row(rows, 12 + mu, c, gate * curve)
        return carry

    lax.fori_loop(0, 8, force_body, 0, unroll=4)
    for t in range(4):
        for q in range(4):
            value = rows[t, q]
            fm_ref[t, :, q * 128:q * 128 + 128] = value.astype(BF16)
            planes_ref[t, :, q * 128:q * 128 + 128] = value[0:8].astype(BF16)


def selectors():
    row = lax.broadcasted_iota(jnp.int32, (432, 72), 0)
    col = lax.broadcasted_iota(jnp.int32, (432, 72), 1)
    group = row // 12
    spread = (group // 4 * 8 + group % 4 == col).astype(F32).astype(BF16)
    keep = (
        lax.broadcasted_iota(jnp.int32, (432, H), 1) // 4 == lax.broadcasted_iota(jnp.int32, (432, H), 0) % 12
    )
    return spread, keep


def panel_kernel(gathered_ref, weights_ref, loops_ref, p1_ref, p2_ref, p3_ref, p4_ref, b2_ref, b3_ref, b4_ref, weights):
    count = gathered_ref.shape[0]

    def read(chip):
        low = gathered_ref[2 * chip].astype(F32)
        high = gathered_ref[2 * chip + 1].astype(F32)
        return special(
            two_rows(lambda e: jnp.concatenate([low[2 * e:2 * e + 2], high[2 * e:2 * e + 2]], axis=0))
        )

    def flat(matrix):
        return tuple(matrix[0][i][j] for i in range(3) for j in range(3)) + tuple(
            imag_of(matrix, i, j) for i in range(3) for j in range(3)
        )

    def chain(chip, state):
        return flat(mat_mul(load_matrix(lambda e: state[e]), read(chip)))

    state = lax.fori_loop(1, count // 2, chain, flat(read(0)))
    loops_ref[0] = (state[0] + state[4] + state[8]) / 3.0
    loops_ref[1] = (state[9] + state[13] + state[17]) / 3.0

    if weights_ref is None:
        for d in range(count):
            block = gathered_ref[d].astype(F32)
            weights[27 * d:27 * d + 27, :] = block[SLABROWS:SLABROWS + 27]
    else:
        weights[...] = weights_ref[...].astype(F32)
    for k in range(TAPS):
        rows = slice(H * k, H * k + H)
        back = slice(H * SWAP[k], H * SWAP[k] + H)
        p2_ref[:, rows] = weights[rows, 0:48].astype(BF16)
        p3_ref[:, rows] = weights[rows, 48:96].astype(BF16)
        p1_ref[:, 8 * k:8 * k + 8] = weights[rows, 96:104].astype(BF16)
        turned = weights[back, :].T
        b2_ref[:, rows] = turned[0:48].astype(BF16)
        b3_ref[:, rows] = turned[48:96].astype(BF16)
    spread, keep = selectors()
    place = (
        lax.broadcasted_iota(jnp.int32, (LANES, H), 0) == 104 + lax.broadcasted_iota(jnp.int32, (LANES, H), 1) % 4
    ).astype(F32).astype(BF16)
    wide = jnp.dot(weights[...].astype(BF16), place, preferred_element_type=F32)
    wide = jnp.where(keep, wide, 0.0).astype(BF16)
    last = lax.dot_general(spread, wide, (((0,), (0,)), ((), ())), preferred_element_type=F32)
    p4_ref[...] = last.astype(BF16)
    for k in range(TAPS):
        b4_ref[:, 8 * k:8 * k + 8] = last[8 * SWAP[k]:8 * SWAP[k] + 8, :].T.astype(BF16)


def panel_kernel_plain(gathered_ref, *rest):
    panel_kernel(gathered_ref, None, *rest)


def chunks_of(value):
    return [value[:, q * 128:q * 128 + 128] for q in range(4)]


def one_shift(chunks, position):
    if position == 0:
        return chunks
    lanes = lane_iota(chunks[0].shape[0])
    sign = 1 if position % 2 == 1 else -1
    if position > 4:
        return [shift_z(chunk, sign, lanes) for chunk in chunks]
    if position > 2:
        return [shift_y(chunk, sign, lanes) for chunk in chunks]
    low = lanes < 64
    rolled = [roll_lanes(chunk, 64) for chunk in chunks]
    if sign > 0:
        return [jnp.where(low, rolled[q], rolled[(q + 1) % 4]) for q in range(4)]
    return [jnp.where(low, rolled[(q + 3) % 4], rolled[q]) for q in range(4)]


def all_shifts(chunks):
    lanes = lane_iota(chunks[0].shape[0])
    y = lanes // 8 % 8
    z = lanes % 8
    low = lanes < 64
    half = [roll_lanes(chunk, 64) for chunk in chunks]
    return [
        chunks,
        [jnp.where(low, half[q], half[(q + 1) % 4]) for q in range(4)],
        [jnp.where(low, half[(q + 3) % 4], half[q]) for q in range(4)],
        [roll_lanes(jnp.where(y == 0, half[q], chunks[q]), -8) for q in range(4)],
        [roll_lanes(jnp.where(y == 7, half[q], chunks[q]), 8) for q in range(4)],
        [roll_lanes(jnp.where(z == 0, roll_lanes(chunk, 8), chunk), -1) for chunk in chunks],
        [roll_lanes(jnp.where(z == 7, roll_lanes(chunk, -8), chunk), 1) for chunk in chunks],
    ]


def span(slice_index, count=1):
    if isinstance(slice_index, int):
        return slice(slice_index * SITES, (slice_index + count) * SITES)
    return pl.ds(pl.multiple_of(slice_index * SITES, SITES), count * SITES)


def slot_of(slot):
    return slice(slot * SITES, (slot + 1) * SITES)


def wide_dot(weights, source, index, kept=None, slot=0):
    shifts = all_shifts(chunks_of(source[:, span(index)]))
    ahead, behind = source[:, span(index + 1)], source[:, span(index - 1)]
    outs = []
    for half in range(2):
        lanes = slice(256 * half, 256 * half + 256)
        columns = [jnp.concatenate(shifted[2 * half:2 * half + 2], axis=1) for shifted in shifts]
        stack = jnp.concatenate(columns + [ahead[:, lanes], behind[:, lanes]], axis=0)
        if kept is not None:
            kept[:, slot * SITES + 256 * half:slot * SITES + 256 * half + 256] = stack
        outs.append(jnp.dot(weights[...], stack, preferred_element_type=F32))
    return jnp.concatenate(outs, axis=1)


def thin_stack(source, index):
    ahead = chunks_of(source[:, span(index + 1)])
    behind = chunks_of(source[:, span(index - 1)])
    columns = all_shifts(chunks_of(source[:, span(index)])) + [ahead, behind]
    return jnp.concatenate(
        [jnp.concatenate([column[q] for column in columns], axis=0).astype(BF16) for q in range(4)], axis=1
    )


def one_minus_square(value):
    value = value.astype(F32)
    return 1.0 - value * value


def conv_kernel(
    split, place_ref, fm_ref, near_ref, far_ref, near_chip_ref, far_chip_ref, loops_ref,
    p1_ref, p2_ref, p3_ref, p4_ref, b2_ref, b3_ref, b4_ref,
    coeff_ref, grads_ref,
    feats, mixed, h1, h2, h3, parts, lasts, g3, g2, g1, wide_back, wide_first, thin, thin_back, packed,
):
    row8 = lax.broadcasted_iota(jnp.int32, (8, SITES), 0)
    loop_re = jnp.concatenate([loops_ref[0, q:q + 1, :] for q in range(4)], axis=1)
    loop_im = jnp.concatenate([loops_ref[1, q:q + 1, :] for q in range(4)], axis=1)
    loops = jnp.where(row8 == 6, loop_re, jnp.where(row8 == 7, loop_im, 0.0))
    loops = loops.astype(BF16).astype(F32)
    first_core = place_ref[0] % 2 == 0
    first_chip = place_ref[0] // 2 % 2 == 0
    for j in range(4):
        near, far = near_chip_ref[j].astype(F32), far_chip_ref[j].astype(F32)
        if j > 0:
            feats[:, span(j - 1)] = jnp.where(first_chip, far, near) + loops
        if j < 3:
            feats[:, span(15 + j)] = jnp.where(first_chip, near, far) + loops
        near, far = near_ref[j].astype(F32), far_ref[j].astype(F32)
        below, above = jnp.where(first_core, far, near), jnp.where(first_core, near, far)
        for base, value in ((3, below), (7, fm_ref[j].astype(F32)), (11, above)):
            feats[:, span(base + j)] = value[0:8] + loops
            mixed[:, span(base + j)] = value[8:16]

    own = span(7, 4)
    contract = (((1,), (1,)), ((), ()))

    def kept_slot(index):
        return index - 7 if 7 <= index < 11 else None

    def first_layer(index):
        stack = thin_stack(feats, index)
        if kept_slot(index) is not None:
            thin[:, slot_of(index - 7)] = stack
        out = jnp.dot(p1_ref[...], stack, preferred_element_type=F32)
        h1[:, span(index)] = jnp.tanh(out).astype(BF16)

    def second_layer(index):
        h2[:, span(index)] = jnp.tanh(wide_dot(p2_ref, h1, index)).astype(BF16)

    def third_layer(index):
        h3[:, span(index)] = jnp.tanh(wide_dot(p3_ref, h2, index)).astype(BF16)

    def taps_of(index):
        taps = jnp.dot(p4_ref[...], h3[:, span(index)], preferred_element_type=F32)
        acc = None
        for position in range(7):
            shifted = one_shift(chunks_of(taps[8 * position:8 * position + 8]), position)
            acc = shifted if acc is None else [a + b for a, b in zip(acc, shifted)]
        parts[0, :, span(index)] = jnp.concatenate(acc, axis=1)
        parts[1, :, span(index)] = taps[56:64]
        parts[2, :, span(index)] = taps[64:72]

    def last_of(index):
        coeff = jnp.tanh(parts[0, :, span(index)] + parts[1, :, span(index + 1)] + parts[2, :, span(index - 1)])
        blend = mixed[:, span(index)]
        value = (blend + coeff * pltpu.roll(blend, 4, 0)) * (1.0 - coeff * coeff)
        lasts[:, span(index)] = jnp.where(row8 < 4, value, 0.0).astype(BF16).astype(F32)
        if 7 <= index < 11:
            coeff_ref[index - 7] = coeff

    def back_third(index):
        stack = thin_stack(lasts, index)
        if kept_slot(index) is not None:
            thin_back[:, slot_of(index - 7)] = stack
        out = jnp.dot(b4_ref[...], stack, preferred_element_type=F32)
        g3[:, span(index)] = (out * one_minus_square(h3[:, span(index)])).astype(BF16)

    def back_second(index):
        slot = kept_slot(index)
        out = wide_dot(b3_ref, g3, index, None if slot is None else wide_back, slot or 0)
        g2[:, span(index)] = (out * one_minus_square(h2[:, span(index)])).astype(BF16)

    def back_first(index):
        out = wide_dot(b2_ref, g2, index, wide_first, index - 7)
        g1[:, slot_of(index - 7)] = (out * one_minus_square(h1[:, span(index)])).astype(BF16)

    stages = (
        (0, 1, 17, first_layer),
        (2, 2, 16, second_layer),
        (4, 3, 15, third_layer),
        (5, 3, 15, taps_of),
        (7, 4, 14, last_of),
        (9, 5, 13, back_third),
        (11, 6, 12, back_second),
        (13, 7, 11, back_first),
    )
    for step in range(1, 24):
        for delay, low, high, task in reversed(stages):
            if low <= step - delay < high:
                task(step - delay)
        if step == 19:
            grad_last = lax.dot_general(
                thin_back[...], h3[:, own], contract, preferred_element_type=F32
            )
            spread, keep = selectors()
            ordered = jnp.concatenate([grad_last[8 * SWAP[k]:8 * SWAP[k] + 8] for k in range(TAPS)], axis=0)
            broad = jnp.dot(spread, ordered.astype(BF16), preferred_element_type=F32)
        if step == 20:
            broad = jnp.where(keep, broad, 0.0).astype(BF16)
            place = (
                lax.broadcasted_iota(jnp.int32, (H, LANES), 1)
                == 104 + lax.broadcasted_iota(jnp.int32, (H, LANES), 0) % 4
            ).astype(F32).astype(BF16)
            packed[...] = jnp.dot(broad, place, preferred_element_type=F32)
        if step == 21:
            grad_third = lax.dot_general(
                wide_back[...], h2[:, own], contract, preferred_element_type=F32
            )
        if step == 22:
            for k in range(TAPS):
                packed[H * k:H * k + H, 48:96] = grad_third[H * SWAP[k]:H * SWAP[k] + H]
    grad_second = lax.dot_general(wide_first[...], h1[:, own], contract, preferred_element_type=F32)
    grad_first = lax.dot_general(g1[...], thin[...], contract, preferred_element_type=F32)
    for k in range(TAPS):
        rows = slice(H * k, H * k + H)
        packed[rows, 0:48] = grad_second[H * SWAP[k]:H * SWAP[k] + H]
        packed[rows, 96:104] = grad_first[:, 8 * k:8 * k + 8]
    if split:
        for d in range(16):
            grads_ref[d] = packed[27 * d:27 * d + 27, :].astype(BF16)
    else:
        grads_ref[...] = packed[...].astype(BF16)


def update_kernel(dense, moves_ref, coeff_ref, out_ref, factors):
    for mu in range(4):
        for t in range(4):
            for c in range(2):
                factors[mu, c, t:t + 1, :] = coeff_ref[t, mu:mu + 1, c * 128:c * 128 + 128]
                factors[mu, c, 4 + t:5 + t, :] = coeff_ref[t, mu:mu + 1, 256 + c * 128:384 + c * 128]

    def body(mu, carry):
        factor = [factors[mu, c] for c in range(2)]
        half = [0.5 * value * value for value in factor]
        for e, (part, i, j) in enumerate(ENTRIES):
            new = [
                dense[mu, e, c]
                + factor[c] * moves_ref[0, mu, e, c].astype(F32)
                + half[c] * moves_ref[1, mu, e, c].astype(F32)
                for c in range(2)
            ]
            out_ref[mu, part, i, j, 0] = jnp.concatenate(
                [new[0][0:4], new[1][0:4], new[0][4:8], new[1][4:8]], axis=1
            )
        return carry

    lax.fori_loop(0, 4, body, 0)


def sum_kernel(widths, parts_ref, first_ref, second_ref, third_ref, last_ref):
    value = parts_ref[0].astype(F32)
    for d in range(1, parts_ref.shape[0]):
        value = value + parts_ref[d].astype(F32)
    offset = 0
    for ref, width in zip((second_ref, third_ref, first_ref, last_ref), widths):
        for r in range(27):
            ref[:, width * r:width * r + width] = value[r:r + 1, offset:offset + width]
        offset += width


def call(body, outs, scratch, places=None, cost=None, limit=LIMIT):
    specs = {}
    if places is not None:
        specs["in_specs"] = [pl.BlockSpec(memory_space=place) for place in places]
    return pl.pallas_call(
        body,
        out_shape=[jax.ShapeDtypeStruct(shape, dtype) for shape, dtype in outs],
        scratch_shapes=[pltpu.VMEM(*item) if isinstance(item, tuple) else item for item in scratch],
        compiler_params=pltpu.CompilerParams(vmem_limit_bytes=limit),
        cost_estimate=cost,
        **specs,
    )


def on_device(links, cotangent, parity, link_subset, w_first, w_second, w_third, w_last):
    count = lax.axis_size("tm")

    def send(value, distance):
        return lax.ppermute(value, "tm", [(i, (i + distance) % count) for i in range(count)])

    def swap(value, pairs):
        return lax.ppermute(value, "tm", pairs + [(target, source) for source, target in pairs])

    chips = count // 2
    widths = (768 // count, 768 // count, 128 // count, 64 // count)
    vmem, smem = pltpu.VMEM, pltpu.SMEM
    field = ((4, 18, 2, 8, LANES), F32)
    space = ((3, 18, 2, 8, LANES), F32)
    edge_rows = ((70, SITES), BF16)
    up, down, dense, edges, staples, slab = call(
        face_kernel,
        [edge_rows, edge_rows, field, space, space, ((12, 4, LANES), F32)],
        [space, ((70, 4, LANES), F32)],
    )(links)
    up = send(up, 1)
    down = send(down, -1)
    (state,) = call(
        space_kernel,
        [((186, 8, LANES), F32)],
        [((3, 3, 18, 2, 8, LANES), F32), ((3, 3, 18, 2, 8, LANES), F32)],
        cost=pl.CostEstimate(flops=4_000_000_000, bytes_accessed=16_000_000, transcendentals=0),
    )(dense, staples)
    place = lax.axis_index("tm").astype(jnp.int32)[None]
    (block,) = call(
        functools.partial(block_kernel, widths),
        [((count, BLOCKROWS, LANES), BF16)],
        [((12, 4, LANES), F32), ((BLOCKROWS, LANES), F32)],
        places=(smem,) + (vmem,) * 7 + (pl.ANY,),
    )(place, up, down, slab, w_first, w_second, w_third, w_last, state)
    gathered = lax.all_to_all(block, "tm", split_axis=0, concat_axis=0, tiled=True)
    fm, planes, moves = call(
        time_kernel,
        [
            ((4, 16, SITES), BF16), ((4, 8, SITES), BF16),
            ((2, 4, 18, 2, 8, LANES), BF16),
        ],
        [
            field, ((4, 8, LANES), F32), space, space, field, ((70, 4, LANES), F32), ((70, 4, LANES), F32),
            ((4, 9, 2, 8, LANES), F32), ((4, 4, 16, LANES), F32),
        ],
        places=(smem,) + (vmem,) * 6,
    )(parity + 2 * link_subset, dense, edges, state, cotangent, up, down)
    far_chip = swap(planes, [(2 * c + k, (2 * c + 2 + k) % count) for c in range(1, chips, 2) for k in range(2)])
    far_core = swap(fm, [(i, (i + 1) % count) for i in range(1, count, 2)])
    near_chip = swap(planes, [(2 * c + k, 2 * c + 2 + k) for c in range(0, chips, 2) for k in range(2)])
    near_core = swap(fm, [(i, i + 1) for i in range(0, count, 2)])

    panel_outs = [
        ((2, 4, LANES), F32), ((H, 72), BF16), ((H, 432), BF16), ((H, 432), BF16), ((72, H), BF16),
        ((H, 432), BF16), ((H, 432), BF16), ((H, 72), BF16),
    ]
    panel_scratch = [((432, LANES), F32)]
    if count == 16:
        loops, p1, p2, p3, p4, b2, b3, b4 = call(panel_kernel_plain, panel_outs, panel_scratch)(gathered)
    else:
        pieces = []
        offset = 0
        for width, full in zip(widths, (48, 48, 8, 4)):
            piece = gathered[:, SLABROWS:SLABROWS + 27, offset:offset + width]
            pieces.append(piece.reshape(432, full))
            offset += width
        pieces.append(jnp.zeros((432, 20), BF16))
        loops, p1, p2, p3, p4, b2, b3, b4 = call(panel_kernel, panel_outs, panel_scratch)(
            gathered, jnp.concatenate(pieces, axis=1)
        )

    window = 18 * SITES
    coeff, grads = call(
        functools.partial(conv_kernel, count == 16),
        [((4, 8, SITES), F32), ((16, 27, LANES) if count == 16 else (432, LANES), BF16)],
        [
            ((8, window), F32), ((8, window), F32), ((H, window), BF16), ((H, window), BF16), ((H, window), BF16),
            ((3, 8, window), F32), ((8, window), F32), ((H, window), BF16), ((H, window), BF16), ((H, 4 * SITES), BF16),
            ((432, 4 * SITES), BF16), ((432, 4 * SITES), BF16), ((72, 4 * SITES), BF16), ((72, 4 * SITES), BF16),
            ((432, LANES), F32),
        ],
        limit=20 * 1024 * 1024,
        places=(smem,) + (vmem,) * 13,
    )(place, fm, near_core, far_core, near_chip, far_chip, loops, p1, p2, p3, p4, b2, b3, b4)
    if count != 16:
        offset = 0
        pieces = []
        for width, full in zip(widths, (48, 48, 8, 4)):
            pieces.append(grads[:, offset:offset + full].reshape(count, 27, width))
            offset += full
        grads = jnp.concatenate(pieces, axis=2)
    grads = lax.all_to_all(grads, "tm", split_axis=0, concat_axis=0, tiled=True)
    (new_links,) = call(
        update_kernel, [(links.shape, F32)], [((4, 2, 8, LANES), F32)]
    )(dense, moves, coeff)
    grad_first, grad_second, grad_third, grad_last = call(
        functools.partial(sum_kernel, widths),
        [((1, 27 * width), F32) for width in (widths[2], widths[0], widths[1], widths[3])],
        [],
    )(grads)
    return (new_links, grad_first, grad_second, grad_third, grad_last)


def solution(mesh):
    placed = (
        P(None, None, None, None, "groups", "tm", None),
        P(None, None, None, None, "groups", "tm", None),
        P("groups", "tm"),
        P("groups", "tm"),
        P("tm"),
        P("tm"),
        P("tm"),
        P("tm"),
    )
    return jax.shard_map(
        on_device,
        mesh=mesh,
        in_specs=placed,
        out_specs=(
            P(None, None, None, None, "groups", "tm", None),
            P("groups", "tm"),
            P("groups", "tm"),
            P("groups", "tm"),
            P("groups", "tm"),
        ),
        check_vma=False,
    )
```
